32 devices in a mesh: dp: 16 (over z, y, x), seq: 2 (over core).
Axes of the slice: x: 2, y: 2, z: 4, core: 2. Of those that a mesh axis runs over, the one named last changes fastest.
Arguments:
- patches: bfloat16 [48, 1024, 512], P('dp', 'seq'), may hold values from -6 to 6
- text_rows: bfloat16 [48, 77, 512], P('dp'), may hold values from -6 to 6
- lengths: int32 [48], P('dp'), may hold values from 5 to 77, as said below
- first_gain: bfloat16 [512], P(('dp', 'seq')), may hold values from 0.099609375 to 1.8984375
- first_shift: bfloat16 [512], P(('dp', 'seq')), may hold values from -3 to 3
- in_weight: bfloat16 [512, 1536], P(('dp', 'seq')), may hold values from -0.25 to 0.25
- query_bias: bfloat16 [512], P(('dp', 'seq')), may hold values from -3 to 3
- value_bias: bfloat16 [512], P(('dp', 'seq')), may hold values from -0.1796875 to 0.1796875
- out_weight: bfloat16 [512, 512], P(('dp', 'seq')), may hold values from -0.5 to 0.5
- branch_bias: bfloat16 [512], P(('dp', 'seq')), may hold values from -3 to 3
- second_gain: bfloat16 [512], P(('dp', 'seq')), may hold values from 0.099609375 to 1.8984375
- second_shift: bfloat16 [512], P(('dp', 'seq')), may hold values from -3 to 3
- up_weight: bfloat16 [512, 2048], P(('dp', 'seq')), may hold values from -0.25 to 0.25
- up_bias: bfloat16 [2048], P(('dp', 'seq')), may hold values from -3 to 3
- down_weight: bfloat16 [2048, 512], P(('dp', 'seq')), may hold values from -0.125 to 0.125
- down_bias: bfloat16 [512], P(('dp', 'seq')), may hold values from -3 to 3
- patch_cotangent: bfloat16 [48, 1024, 512], P('dp', 'seq'), may hold values from -6 to 6
- text_cotangent: bfloat16 [48, 77, 512], P('dp'), may hold values from -6 to 6
Outputs:
- out_patches: bfloat16 [48, 1024, 512], P('dp', 'seq')
- out_text: bfloat16 [48, 77, 512], P('dp')
- grad_patches: bfloat16 [48, 1024, 512], P('dp', 'seq')
- grad_text: bfloat16 [48, 77, 512], P('dp')
- first_gain_grad: float32 [512], P(('dp', 'seq'))
- first_shift_grad: float32 [512], P(('dp', 'seq'))
- in_weight_grad: float32 [512, 1536], P(('dp', 'seq'))
- query_bias_grad: float32 [512], P(('dp', 'seq'))
- value_bias_grad: float32 [512], P(('dp', 'seq'))
- out_weight_grad: float32 [512, 512], P(('dp', 'seq'))
- branch_bias_grad: float32 [512], P(('dp', 'seq'))
- second_gain_grad: float32 [512], P(('dp', 'seq'))
- second_shift_grad: float32 [512], P(('dp', 'seq'))
- up_weight_grad: float32 [512, 2048], P(('dp', 'seq'))
- up_bias_grad: float32 [2048], P(('dp', 'seq'))
- down_weight_grad: float32 [2048, 512], P(('dp', 'seq'))
- down_bias_grad: float32 [512], P(('dp', 'seq'))
The draws below stay inside these ranges and needn't reach their ends.
Inputs may be any that keep to these rules, and one draw needn't show every extreme that they name: `lengths`: in every draw one item uses all 77 language slots and another uses 5.
All inputs are finite; a program needn't handle non-finite values.
Results may differ from the reference program's by a relative error of at most 0.014.
Values may be sent and summed in bfloat16 or wider, within the bound.
A program may use at most 192 MiB of HBM per device.

```python
import math
import jax
import jax.numpy as jnp
from jax import lax

D = 512
HEADS = 8
HD = 64
FF = 2048
TEXT = 77
PATCHES = 1024
ITEMS = 48


def draw_lengths(key, part):
    key = jax.random.fold_in(key, 11)
    drawn_lengths = jax.random.randint(jax.random.fold_in(key, 1), (ITEMS,), 5, TEXT + 1)
    full_place = jax.random.randint(jax.random.fold_in(key, 2), (), 0, ITEMS)
    offset_draw = jax.random.randint(jax.random.fold_in(key, 3), (), 1, ITEMS)
    short_place = (full_place + offset_draw) % ITEMS
    drawn_lengths = drawn_lengths.at[full_place].set(TEXT)
    drawn_lengths = drawn_lengths.at[short_place].set(5)
    return drawn_lengths.astype(jnp.int32)


def block_levels(stream_key, shape, pieces, low, high):
    def one(axis_at, blocks):
        heights = jax.random.uniform(jax.random.fold_in(jax.random.fold_in(stream_key, 6), axis_at), (blocks,), jnp.float32, low / len(pieces), high / len(pieces))
        return jnp.repeat(jnp.exp(heights), shape[axis_at] // blocks).reshape((-1,) + (1,) * (len(shape) - axis_at - 1))

    loudness = one(*pieces[0])
    for cut in pieces[1:]:
        loudness = loudness * one(*cut)
    return loudness


def normal_values(key, dims, deviation, most, split=(), dtype=jnp.bfloat16):
    gain = block_levels(key, dims, split, -0.22, 0.18) if split else 1.0
    array = jax.random.normal(key, dims, jnp.float32) * deviation * gain
    return jnp.minimum(jnp.maximum(array, -most), most).astype(dtype)


def setup_inputs(seed: int = 0) -> dict:
    key_of = jax.random.split(jax.random.key(seed), 19)
    patches = normal_values(key_of[0], (ITEMS, PATCHES, D), 1.0, 6.0, ((0, 16), (1, 2)))
    text_rows = normal_values(key_of[1], (ITEMS, TEXT, D), 1.0, 6.0, ((0, 16),))
    lengths = draw_lengths(jax.random.fold_in(key_of[18], 71), 0)
    first_gain = jnp.clip(1.0 + 0.18 * jax.random.normal(key_of[3], (D,), jnp.float32), 0.099609375, 1.8984375).astype(jnp.bfloat16)
    first_shift = normal_values(key_of[4], (D,), 0.5, 3.0, ((0, 32),))
    in_weight = normal_values(key_of[5], (D, 3 * D), D ** -0.5, 0.25, ((0, 32),))
    query_bias = normal_values(key_of[6], (D,), 0.5, 3.0, ((0, 32),))
    value_bias = normal_values(key_of[7], (D,), 0.03, 0.1796875, ((0, 32),))
    out_weight = normal_values(key_of[8], (D, D), (D // 4) ** -0.5, 0.5, ((0, 32),))
    branch_bias = normal_values(key_of[9], (D,), 0.5, 3.0, ((0, 32),))
    second_gain = jnp.clip(1.0 + 0.18 * jax.random.normal(key_of[10], (D,), jnp.float32), 0.099609375, 1.8984375).astype(jnp.bfloat16)
    second_shift = normal_values(key_of[11], (D,), 0.5, 3.0, ((0, 32),))
    up_weight = normal_values(key_of[12], (D, FF), D ** -0.5, 0.25, ((0, 32),))
    up_bias = normal_values(key_of[13], (FF,), 0.5, 3.0, ((0, 32),))
    down_weight = normal_values(key_of[14], (FF, D), FF ** -0.5, 0.125, ((0, 32),))
    down_bias = normal_values(key_of[15], (D,), 0.5, 3.0, ((0, 32),))
    patch_cotangent = normal_values(key_of[16], (ITEMS, PATCHES, D), 1.0, 6.0, ((0, 16), (1, 2)))
    text_cotangent = normal_values(key_of[17], (ITEMS, TEXT, D), 1.0, 6.0, ((0, 16),))
    return dict(patches=patches, text_rows=text_rows, lengths=lengths, first_gain=first_gain, first_shift=first_shift, in_weight=in_weight, query_bias=query_bias, value_bias=value_bias, out_weight=out_weight, branch_bias=branch_bias, second_gain=second_gain, second_shift=second_shift, up_weight=up_weight, up_bias=up_bias, down_weight=down_weight, down_bias=down_bias, patch_cotangent=patch_cotangent, text_cotangent=text_cotangent)


@jax.custom_vjp
def low(v):
    return lax.optimization_barrier(v.astype(jnp.bfloat16)).astype(jnp.float32)

@jax.custom_vjp
def low_back(v):
    return v

def low_keep(v):
    return (low(v), None)

def low_pass(kept, grad):
    return (grad,)

def back_keep(v):
    return (v, None)

def back_low(kept, grad):
    return (low(grad),)
low.defvjp(low_keep, low_pass)
low_back.defvjp(back_keep, back_low)
EPSILON = 1e-05
NEG_FILL = -1e+30

def product(left_side, right_side):
    return jnp.dot(left_side, right_side, precision=lax.Precision.HIGHEST, preferred_element_type=jnp.float32)

def normalize(token_rows, gain_vec, shift_vec):
    row_mean = lax.optimization_barrier(jnp.mean(token_rows, axis=-1, keepdims=True))
    centred = token_rows - row_mean
    variance = lax.optimization_barrier(jnp.mean(centred * centred, axis=-1, keepdims=True))
    return centred * lax.rsqrt(variance + EPSILON) * gain_vec + shift_vec

def layer(params, patch_rows, text_part, length):
    first_gain, first_shift, in_weight, query_bias, value_bias, out_weight, branch_bias, second_gain, second_shift, up_weight, up_bias, down_weight, down_bias = params
    token_rows = jnp.concatenate([patch_rows, text_part], 0)
    row_count = token_rows.shape[0]
    first_in = low(normalize(token_rows, first_gain, first_shift))
    projected = product(first_in, in_weight)
    queries = low_back(low(projected[:, :D] + query_bias))
    key_rows = low_back(low(projected[:, D:2 * D]))
    values = low_back(low(projected[:, 2 * D:] + value_bias))
    head_query = queries.reshape(row_count, HEADS, HD)
    head_key = key_rows.reshape(row_count, HEADS, HD)
    head_value = values.reshape(row_count, HEADS, HD)
    score_scale = 1.0 / math.sqrt(HD)
    scores = jnp.einsum('qhe,khe->hqk', head_query, head_key, precision=lax.Precision.HIGHEST) * score_scale
    key_valid = jnp.concatenate([jnp.ones((PATCHES,), jnp.bool_), jnp.arange(TEXT) < length])
    scores = low_back(jnp.where(key_valid[None, None, :], scores, NEG_FILL))
    probs = low(jax.nn.softmax(scores, axis=-1))
    mixed_heads = jnp.einsum('hqk,khe->qhe', probs, head_value, precision=lax.Precision.HIGHEST)
    attended = low_back(low(mixed_heads.reshape(row_count, D)))
    branch = low_back(product(attended, out_weight) + branch_bias)
    middle = token_rows + branch
    second_in = low(normalize(middle, second_gain, second_shift))
    hidden_pre = low_back(product(second_in, up_weight) + up_bias)
    hidden = low(jax.nn.gelu(hidden_pre, approximate=False))
    return middle + product(hidden, down_weight) + down_bias

def reference(patches, text_rows, lengths, first_gain, first_shift, in_weight, query_bias, value_bias, out_weight, branch_bias, second_gain, second_shift, up_weight, up_bias, down_weight, down_bias, patch_cotangent, text_cotangent):
    params = tuple((member.astype(jnp.float32) for member in (first_gain, first_shift, in_weight, query_bias, value_bias, out_weight, branch_bias, second_gain, second_shift, up_weight, up_bias, down_weight, down_bias)))

    def step(totals, packed):
        patch_rows, text_part, length, patch_grad, text_grad = packed

        def apply_layer(params_in, patch_in, text_in):
            return layer(params_in, patch_in, text_in, length)
        result, pullback = jax.vjp(apply_layer, params, patch_rows.astype(jnp.float32), text_part.astype(jnp.float32))
        cotangent = jnp.concatenate([patch_grad, text_grad], 0).astype(jnp.float32)
        param_grads, patch_back, text_back = pullback(cotangent)
        totals = jax.tree.map(lambda total_sum, new_term: total_sum + new_term, totals, param_grads)
        per_item = (result[:PATCHES].astype(jnp.bfloat16), result[PATCHES:].astype(jnp.bfloat16), patch_back.astype(jnp.bfloat16), text_back.astype(jnp.bfloat16))
        return (totals, per_item)
    zero_grads = jax.tree.map(jnp.zeros_like, params)
    totals, per_item = lax.scan(step, zero_grads, (patches, text_rows, lengths, patch_cotangent, text_cotangent))
    return (per_item[0], per_item[1], per_item[2], per_item[3], totals[0], totals[1], totals[2], totals[3], totals[4], totals[5], totals[6], totals[7], totals[8], totals[9], totals[10], totals[11], totals[12])
```

```python
import functools
import math

import jax
import jax.numpy as jnp
from jax import lax
from jax.experimental import pallas as pl
from jax.experimental.pallas import tpu as pltpu
from jax.sharding import PartitionSpec as P

HEADS = 8
EPSILON = 1e-05
NEG_FILL = -1e30
LOG2E = math.log2(math.e)
LN2 = math.log(2.0)
ROW_TILE = 16
LANES = 128
MESH = pl.DeviceIdType.MESH
f32, bf16 = jnp.float32, jnp.bfloat16

GAIN1, SHIFT1, QBIAS, VBIAS, BRANCH, GAIN2, SHIFT2, DOWNB = range(8)


def round_up(value, unit):
    return -(-value // unit) * unit


def mm(a, b):
    return lax.dot_general(a, b, (((1,), (0,)), ((), ())), preferred_element_type=f32)


def mm_t(a, b):
    return lax.dot_general(a, b, (((1,), (1,)), ((), ())), preferred_element_type=f32)


def t_mm(a, b):
    return lax.dot_general(a, b, (((0,), (0,)), ((), ())), preferred_element_type=f32)


def compiler_params(**more):
    return pltpu.CompilerParams(vmem_limit_bytes=60 * 2**20, **more)


WHOLE = pl.BlockSpec(memory_space=pltpu.VMEM)


class Place:
    def __init__(self, depth, seq_size):
        self.depth, self.seq_size = depth, seq_size
        index = lax.axis_index("dp") * seq_size + lax.axis_index("seq")
        self.core = lax.rem(index, 2)
        self.x = lax.rem(index // 2, 2)
        self.y = lax.rem(index // 4, 2)
        self.z = index // 8
        core = self.core
        flip_x, flip_y = 1 - self.x, 1 - self.y
        x_first = self.x * core + flip_x * (1 - core)
        y_first = self.y * (1 - core) + flip_y * core
        x_second = self.x * (1 - core) + flip_x * core
        y_second = self.y * core + flip_y * (1 - core)
        self.columns = (
            (self.y, self.x),
            (y_first, x_first),
            (y_second, x_second),
            (flip_y, flip_x),
        )

    def device(self, z, y, x, core):
        index = ((z * 2 + y) * 2 + x) * 2 + core
        return (index // self.seq_size, lax.rem(index, self.seq_size))

    def layer(self, k):
        return lax.rem(self.z + self.depth - k, self.depth)

    def ahead(self, k):
        return lax.rem(self.z + k, self.depth)

    def first(self):
        return self.device(self.z, *self.columns[1], self.core)

    def second(self):
        return self.device(self.z, *self.columns[2], self.core)

    def other_core(self):
        return self.device(self.z, self.y, self.x, 1 - self.core)

    def above(self, k):
        return self.device(self.ahead(k), self.y, self.x, self.core)

    def greet(self):
        barrier = pltpu.get_barrier_semaphore()
        friends = [self.above(k) for k in range(1, self.depth)]
        friends += [self.first(), self.second(), self.other_core()]
        for friend in friends:
            pl.semaphore_signal(barrier, inc=1, device_id=friend, device_id_type=MESH)
        pl.semaphore_wait(barrier, len(friends))


def remote(src, dst, send, recv, device):
    return pltpu.make_async_remote_copy(
        src_ref=src, dst_ref=dst, send_sem=send, recv_sem=recv, device_id=device, device_id_type=MESH
    )


class Gather:
    def __init__(self, place, shard, full, out, into, local):
        self.place, self.shard, self.full, self.out, self.into, self.local = place, shard, full, out, into, local
        self.sends = []

    def block(self, k, column, core):
        y, x = self.place.columns[column]
        return self.full.at[self.place.layer(k), y, x, core]

    def copy(self, src, dst, lane, k, device):
        return remote(src, dst, self.out.at[lane, k], self.into.at[lane, k], device)

    def send(self, src, dst, lane, k, device):
        copy = self.copy(src, dst, lane, k, device)
        copy.start()
        self.sends.append(copy)

    def arrived(self, lane, k, column, core):
        here = self.block(k, column, core)
        self.copy(here, here, lane, k, self.place.other_core()).wait_recv()
        return here

    def start(self):
        place = self.place
        mine = self.block(0, 0, place.core)
        self.own = pltpu.make_async_copy(self.shard, mine, self.local)
        self.own.start()
        for k in range(1, place.depth):
            self.send(self.shard, mine, 0, k, place.above(k))
        self.forward_line(0)

    def forward_line(self, k):
        place = self.place
        here = self.arrived(0, k, 0, place.core) if k else self.block(0, 0, place.core)
        src = here if k else self.shard
        self.send(src, here, 1, k, place.first())
        self.send(src, here, 2, k, place.second())
        self.send(src, here, 4, k, place.other_core())

    def forward_first(self, k):
        here = self.arrived(1, k, 1, self.place.core)
        self.send(here, here, 3, k, self.place.second())
        self.send(here, here, 5, k, self.place.other_core())

    def forward_second(self, half, k):
        here = self.arrived(2 + half, k, 2 + half, self.place.core)
        self.send(here, here, 6 + half, k, self.place.other_core())

    def finish(self):
        for column in range(4):
            for k in range(self.place.depth):
                self.arrived(4 + column, k, column, 1 - self.place.core)
        self.own.wait()
        for copy in self.sends:
            copy.wait_send()


def gather_sems(depth):
    sems = pltpu.SemaphoreType.DMA
    return [sems((8, depth)), sems((8, depth)), sems]


def gather_kernel(seq_size, arrays, *refs):
    shards, fulls, sems = refs[:arrays], refs[arrays : 2 * arrays], refs[2 * arrays :]
    place = Place(fulls[0].shape[0], seq_size)
    place.greet()
    moves = [Gather(place, shards[n], fulls[n], *sems[3 * n : 3 * n + 3]) for n in range(arrays)]
    for move in moves:
        move.start()
    for k in range(1, place.depth):
        for move in moves:
            move.forward_line(k)
    for k in range(place.depth):
        for move in moves:
            move.forward_first(k)
    for half in range(2):
        for k in range(place.depth):
            for move in moves:
                move.forward_second(half, k)
    for move in moves:
        move.finish()


def gather(shards, devices, seq_size, number):
    depth = devices // 8
    fulls = pl.pallas_call(
        functools.partial(gather_kernel, seq_size, len(shards)),
        out_shape=[jax.ShapeDtypeStruct((depth, 2, 2, 2) + shard.shape, shard.dtype) for shard in shards],
        in_specs=[WHOLE] * len(shards),
        out_specs=[WHOLE] * len(shards),
        scratch_shapes=gather_sems(depth) * len(shards),
        compiler_params=compiler_params(collective_id=number, has_side_effects=True),
        name="gather",
    )(*shards)
    return [full.reshape(-1, full.shape[-1]) for full in fulls]


class Reduce:
    def __init__(self, place, part, total, from_core, held, from_second, pair, from_first, line, from_line, out, into):
        self.place, self.part, self.total = place, part, total
        self.from_core, self.held, self.from_second, self.pair = from_core, held, from_second, pair
        self.from_first, self.line, self.from_line = from_first, line, from_line
        self.out, self.into = out, into

    def copy(self, src, dst, lane, device):
        return remote(src, dst, self.out.at[lane], self.into.at[lane], device)

    def core_copies(self):
        core = self.place.core
        return [self.copy(self.part.at[:, :, :, 1 - core], self.from_core, 0, self.place.other_core())]

    def second_copies(self):
        columns = self.place.columns
        return [
            self.copy(self.held.at[:, columns[2 + k][0], columns[2 + k][1]], self.from_second.at[k], 1 + k,
                      self.place.second())
            for k in range(2)
        ]

    def first_copies(self):
        return [self.copy(self.pair.at[1], self.from_first, 3, self.place.first())]

    def line_copies(self):
        place = self.place
        return [
            self.copy(self.line.at[place.ahead(k)], self.from_line.at[k - 1], 3 + k, place.above(k))
            for k in range(1, place.depth)
        ]

    def start(self, copies):
        for copy in copies:
            copy.start()

    def wait(self, copies):
        for copy in copies:
            copy.wait()

    def add_core(self):
        self.wait(self.core_copies())
        own = self.part[:, :, :, self.place.core]
        self.held[...] = (own.astype(f32) + self.from_core[...].astype(f32)).astype(bf16)

    def add_second(self):
        self.wait(self.second_copies())
        for k in range(2):
            y, x = self.place.columns[k]
            self.pair[k] = (self.held[:, y, x].astype(f32) + self.from_second[k].astype(f32)).astype(bf16)

    def add_first(self):
        self.wait(self.first_copies())
        self.line[...] = (self.pair[0].astype(f32) + self.from_first[...].astype(f32)).astype(bf16)

    def add_line(self):
        self.wait(self.line_copies())
        result = self.line[self.place.z].astype(f32)
        for k in range(self.place.depth - 1):
            result = result + self.from_line[k].astype(f32)
        self.total[...] = result


REDUCE_SCRATCH = 9


def reduce_scratch(depth, rows, cols):
    shapes = [(depth, 2, 2), (depth, 2, 2), (2, depth), (2, depth), (depth,), (depth,), (depth - 1,)]
    sems = pltpu.SemaphoreType.DMA
    return [pltpu.VMEM(shape + (rows, cols), bf16) for shape in shapes] + [sems((3 + depth,))] * 2


def reduce_kernel(seq_size, arrays, *refs):
    parts, totals, scratch = refs[:arrays], refs[arrays : 2 * arrays], refs[2 * arrays :]
    place = Place(parts[0].shape[0], seq_size)
    place.greet()
    sums = [
        Reduce(place, parts[n], totals[n], *scratch[REDUCE_SCRATCH * n : REDUCE_SCRATCH * (n + 1)])
        for n in range(arrays)
    ]
    for one in sums:
        one.start(one.core_copies())
    for one in sums:
        one.add_core()
        one.start(one.second_copies())
    for one in sums:
        one.add_second()
        one.start(one.first_copies())
    for one in sums:
        one.add_first()
        one.start(one.line_copies())
    for one in sums:
        one.add_line()


def reduce(parts, devices, seq_size, number):
    depth = devices // 8
    sizes = [(part.shape[0] // devices, part.shape[1]) for part in parts]
    return pl.pallas_call(
        functools.partial(reduce_kernel, seq_size, len(parts)),
        out_shape=[jax.ShapeDtypeStruct(size, f32) for size in sizes],
        in_specs=[WHOLE] * len(parts),
        out_specs=[WHOLE] * len(parts),
        scratch_shapes=sum([reduce_scratch(depth, *size) for size in sizes], []),
        compiler_params=compiler_params(collective_id=number, has_side_effects=True),
        name="reduce",
    )(*[part.reshape((depth, 2, 2, 2) + size) for part, size in zip(parts, sizes)])


def norm_rows(rows):
    centred = rows - jnp.mean(rows, axis=1, keepdims=True)
    inverse = lax.rsqrt(jnp.mean(centred * centred, axis=1, keepdims=True) + EPSILON)
    return centred * inverse, inverse


def norm_back(grad, scaled, inverse, gain):
    inner = grad * gain
    return inverse * (
        inner
        - jnp.mean(inner, axis=1, keepdims=True)
        - scaled * jnp.mean(inner * scaled, axis=1, keepdims=True)
    )


def gelu_both(v):
    power = jnp.exp2(v * v * (-0.5 * LOG2E))
    base = 1.0 + (0.3275911 / math.sqrt(2.0)) * jnp.abs(v)
    t = pl.reciprocal(base, approx=True)
    t = t * (2.0 - base * t)
    series = 0.5 * 1.061405429
    for factor in (-1.453152027, 1.421413741, -0.284496736, 0.254829592):
        series = series * t + 0.5 * factor
    tail = series * t * power
    cdf = jnp.where(v >= 0, 1.0 - tail, tail)
    return v * cdf, cdf + v * power * (1.0 / math.sqrt(2.0 * math.pi))


def column_sum(rows):
    return jnp.sum(rows.astype(f32), axis=0, keepdims=True)


def to_columns(rows):
    count, width = rows.shape
    return jnp.transpose(jnp.concatenate([rows, jnp.zeros((LANES - count, width), f32)], axis=0)).astype(bf16)


def qkv_kernel(x_ref, w_ref, vec_ref, q_ref, k_ref, v_ref):
    width = x_ref.shape[2]
    scaled, _ = norm_rows(x_ref[0].astype(f32))
    first_in = (scaled * vec_ref[GAIN1 : GAIN1 + 1] + vec_ref[SHIFT1 : SHIFT1 + 1]).astype(bf16)
    scale = LOG2E / math.sqrt(width // HEADS)
    q = mm(first_in, w_ref[:, :width]) + vec_ref[QBIAS : QBIAS + 1]
    q_ref[0] = (q * scale).astype(bf16)
    k_ref[0] = mm(first_in, w_ref[:, width : 2 * width]).astype(bf16)
    v = mm(first_in, w_ref[:, 2 * width : 3 * width]) + vec_ref[VBIAS : VBIAS + 1]
    v_ref[0] = v.astype(bf16)


def qkv(x, weight, vecs):
    block = pl.BlockSpec((1,) + x.shape[1:], lambda i: (i, 0, 0))
    return pl.pallas_call(
        qkv_kernel,
        grid=(x.shape[0],),
        in_specs=[block, WHOLE, WHOLE],
        out_specs=[block] * 3,
        out_shape=[jax.ShapeDtypeStruct(x.shape, bf16)] * 3,
        compiler_params=compiler_params(),
        name="qkv",
    )(x, weight, vecs)


def collect(dst, refs, patch, text):
    count, width = len(refs), refs[0].shape[2]
    for r, ref in enumerate(refs):
        dst[r * patch : (r + 1) * patch, :width] = ref[0, :patch, :]
        at = count * patch + r * text
        dst[at : at + text, :width] = ref[0, patch:, :]
    filled = count * (patch + text)
    if dst.shape[0] > filled:
        dst[filled:, :width] = jnp.zeros((dst.shape[0] - filled, width), dst.dtype)


def attend_kernel(count, patch, head, *refs):
    q_ref, k_refs, v_refs = refs[0], refs[1 : 1 + count], refs[1 + count : 1 + 2 * count]
    bias_ref, out_ref, log_ref, keys, values = refs[1 + 2 * count :]
    width = q_ref.shape[2]
    text = q_ref.shape[1] - patch
    collect(keys, k_refs, patch, text)
    collect(values, v_refs, patch, text)
    values[:, width:] = jnp.ones((values.shape[0], values.shape[1] - width), bf16)
    q = q_ref[0]
    lane = lax.broadcasted_iota(jnp.int32, (1, width), 1) // head
    out = logs = None
    for h in range(width // head):
        q_head = jnp.where(lane == h, q, jnp.zeros_like(q))
        scores = mm_t(q_head, keys[...]) + bias_ref[0]
        top = jnp.max(scores, axis=1, keepdims=True)
        powers = jnp.exp2(scores - top).astype(bf16)
        mixed = mm(powers, values[...])
        total = mixed[:, width:]
        head_out = mixed[:, :width] * (1.0 / total)
        head_log = top + jnp.log2(total)
        out = head_out if out is None else jnp.where(lane == h, head_out, out)
        logs = head_log if logs is None else jnp.where(lane == h, head_log, logs)
    out_ref[0] = out.astype(bf16)
    log_ref[0] = logs


def attend(q, keys, values, bias, patch, head, width):
    items, _, model = q.shape
    count, span = len(keys), bias.shape[-1]
    block = pl.BlockSpec((1, q.shape[1], width), lambda i, p: (i, 0, p))
    return pl.pallas_call(
        functools.partial(attend_kernel, count, patch, head),
        grid=(items, model // width),
        in_specs=[block] * (1 + 2 * count) + [pl.BlockSpec((1, 1, span), lambda i, p: (i, 0, 0))],
        out_specs=[block, block],
        out_shape=[jax.ShapeDtypeStruct(q.shape, bf16), jax.ShapeDtypeStruct(q.shape, f32)],
        scratch_shapes=[pltpu.VMEM((span, width), bf16), pltpu.VMEM((span, 2 * width), bf16)],
        compiler_params=compiler_params(),
        name="attend",
    )(q, *keys, *values, bias)


def attend_back_kernel(count, patch, head, *refs):
    q_ref, k_refs, v_refs = refs[0], refs[1 : 1 + count], refs[1 + count : 1 + 2 * count]
    bias_ref, out_ref, log_ref, grad_ref, dq_ref = refs[1 + 2 * count : 6 + 2 * count]
    dk_refs, dv_refs = refs[6 + 2 * count : 6 + 3 * count], refs[6 + 3 * count : 6 + 4 * count]
    keys, values = refs[6 + 4 * count :]
    width = q_ref.shape[2]
    text = q_ref.shape[1] - patch
    collect(keys, k_refs, patch, text)
    collect(values, v_refs, patch, text)
    q, grad = q_ref[0], grad_ref[0]
    lane = lax.broadcasted_iota(jnp.int32, (1, width), 1) // head
    row = lax.broadcasted_iota(jnp.int32, (width, 1), 0) // head
    inner = grad.astype(f32) * out_ref[0].astype(f32)
    dq = dk = dv = None
    for h in range(width // head):
        mine = lane == h
        q_head = jnp.where(mine, q, jnp.zeros_like(q))
        grad_head = jnp.where(mine, grad, jnp.zeros_like(grad))
        delta = jnp.sum(jnp.where(mine, inner, 0.0), axis=1, keepdims=True)
        scores = mm_t(q_head, keys[...]) + bias_ref[0]
        probs = jnp.exp2(scores - log_ref[0, :, h * head : h * head + 1])
        grad_probs = mm_t(grad_head, values[...])
        grad_scores = (probs * (grad_probs - delta)).astype(bf16)
        dv_head = t_mm(grad, probs.astype(bf16))
        dk_head = t_mm(q, grad_scores)
        dq_head = mm(grad_scores, keys[...])
        dq = dq_head if dq is None else jnp.where(mine, dq_head, dq)
        dk = dk_head if dk is None else jnp.where(row == h, dk_head, dk)
        dv = dv_head if dv is None else jnp.where(row == h, dv_head, dv)
    dq_ref[0] = (dq * (1.0 / math.sqrt(head))).astype(bf16)
    for grads, parts in ((dk * LN2, dk_refs), (dv, dv_refs)):
        grads = jnp.transpose(grads).astype(bf16)
        for r in range(count):
            parts[r][0, :patch, :] = grads[r * patch : (r + 1) * patch]
            at = count * patch + r * text
            parts[r][0, patch:, :] = grads[at : at + text]


def attend_back(q, keys, values, bias, attended, logs, grad_att, patch, head, width):
    items, _, model = q.shape
    count, span = len(keys), bias.shape[-1]
    block = pl.BlockSpec((1, q.shape[1], width), lambda i, p: (i, 0, p))
    grads = pl.pallas_call(
        functools.partial(attend_back_kernel, count, patch, head),
        grid=(items, model // width),
        in_specs=[block] * (1 + 2 * count) + [pl.BlockSpec((1, 1, span), lambda i, p: (i, 0, 0))] + [block] * 3,
        out_specs=[block] * (1 + 2 * count),
        out_shape=[jax.ShapeDtypeStruct(q.shape, bf16)] * (1 + 2 * count),
        scratch_shapes=[pltpu.VMEM((span, width), bf16), pltpu.VMEM((span, width), bf16)],
        compiler_params=compiler_params(),
        name="attend_back",
    )(q, *keys, *values, bias, attended, logs, grad_att)
    return grads[0], grads[1 : 1 + count], grads[1 + count :]


def ffn_kernel(steps, chunk, x_ref, at_ref, dy_ref, w_ref, wd_ref, vec_ref,
               res_ref, gb_ref, ga_ref, part_ref, down_ref, second_s, hidden_s, pre_s, sums_s):
    step = pl.program_id(0)
    block = x_ref.shape[0] // steps
    rows = pl.ds(pl.multiple_of(step * block, ROW_TILE), block)
    model, units = x_ref.shape[1], wd_ref.shape[0]
    gain = vec_ref[GAIN2 : GAIN2 + 1]
    w_out = w_ref[:, units:]
    up_bias = jnp.transpose(wd_ref[:, model:].astype(f32))[:1]
    middle = x_ref[rows, :].astype(f32) + (mm(at_ref[rows, :], w_out) + vec_ref[BRANCH : BRANCH + 1])
    scaled, inverse = norm_rows(middle)
    second_in = (scaled * gain + vec_ref[SHIFT2 : SHIFT2 + 1]).astype(bf16)
    second_s[rows, :] = second_in
    dy = dy_ref[rows, :]
    result = middle + vec_ref[DOWNB : DOWNB + 1]
    grad_second = jnp.zeros_like(middle)
    for c in range(units // chunk):
        cols = slice(c * chunk, (c + 1) * chunk)
        value, slope = gelu_both(mm(second_in, w_ref[:, cols]) + up_bias[:, cols])
        hidden = value.astype(bf16)
        hidden_s[rows, cols] = hidden
        grad_pre = (mm_t(dy, wd_ref[cols, :model]) * slope).astype(bf16)
        pre_s[rows, cols] = grad_pre
        result = result + mm(hidden, wd_ref[cols, :model])
        grad_second = grad_second + mm_t(grad_pre, w_ref[:, cols])
    res_ref[rows, :] = result.astype(bf16)
    grad_branch = (dy.astype(f32) + norm_back(grad_second, scaled, inverse, gain)).astype(bf16)
    gb_ref[rows, :] = grad_branch
    ga_ref[rows, :] = mm_t(grad_branch, w_out).astype(bf16)

    @pl.when(step == 0)
    def _():
        sums_s[...] = jnp.zeros_like(sums_s)

    for at, grad in ((BRANCH, grad_branch), (GAIN2, grad_second * scaled), (SHIFT2, grad_second), (DOWNB, dy)):
        sums_s[at : at + 1, :] += column_sum(grad)

    @pl.when(step == steps - 1)
    def _():
        for c in range(units // model):
            cols = slice(c * model, (c + 1) * model)
            grad_pre = pre_s[:, cols]
            part_ref[:, cols] = t_mm(second_s[...], grad_pre).astype(bf16)
            down_ref[cols, :model] = jnp.transpose(t_mm(dy_ref[...], hidden_s[:, cols])).astype(bf16)
            down_ref[cols, model:] = to_columns(column_sum(grad_pre))
        part_ref[:, units : units + model] = t_mm(at_ref[...], gb_ref[...]).astype(bf16)
        part_ref[:, units + model :] = to_columns(sums_s[...])


def ffn(x, attended, dy, weights, w_down, vecs):
    rows, model = x.shape
    units = w_down.shape[0]
    steps = 3
    return pl.pallas_call(
        functools.partial(ffn_kernel, steps, 512),
        grid=(steps,),
        in_specs=[WHOLE] * 6,
        out_specs=[WHOLE] * 5,
        out_shape=[jax.ShapeDtypeStruct((rows, model), bf16)] * 3
        + [
            jax.ShapeDtypeStruct((model, units + model + LANES), bf16),
            jax.ShapeDtypeStruct((units, model + LANES), bf16),
        ],
        scratch_shapes=[
            pltpu.VMEM((rows, model), bf16),
            pltpu.VMEM((rows, units), bf16),
            pltpu.VMEM((rows, units), bf16),
            pltpu.VMEM((8, model), f32),
        ],
        compiler_params=compiler_params(),
        name="ffn",
    )(x, attended, dy, weights, w_down, vecs)


def in_back_kernel(steps, count, *refs):
    x_ref, gb_ref, w_ref, vec_ref, dq_ref = refs[:5]
    dk_refs, dv_refs = refs[5 : 5 + count], refs[5 + count : 5 + 2 * count]
    grad_ref, part_ref, first_s, mixed_s, sums_s = refs[5 + 2 * count :]
    step = pl.program_id(0)
    block = x_ref.shape[0] // steps
    rows = pl.ds(pl.multiple_of(step * block, ROW_TILE), block)
    model = x_ref.shape[1]
    gain = vec_ref[GAIN1 : GAIN1 + 1]
    scaled, inverse = norm_rows(x_ref[rows, :].astype(f32))
    first_s[rows, :] = (scaled * gain + vec_ref[SHIFT1 : SHIFT1 + 1]).astype(bf16)
    dq = dq_ref[rows, :]
    dk = sum(ref[rows, :].astype(f32) for ref in dk_refs).astype(bf16)
    dv = sum(ref[rows, :].astype(f32) for ref in dv_refs).astype(bf16)
    mixed_s[rows, :model] = dq
    mixed_s[rows, model : 2 * model] = dk
    mixed_s[rows, 2 * model :] = dv
    grad_first = mm_t(mixed_s[rows, :], w_ref[...])
    grad = gb_ref[rows, :].astype(f32) + norm_back(grad_first, scaled, inverse, gain)
    grad_ref[rows, :] = grad.astype(bf16)

    @pl.when(step == 0)
    def _():
        sums_s[...] = jnp.zeros_like(sums_s)

    for at, value in ((GAIN1, grad_first * scaled), (SHIFT1, grad_first), (QBIAS, dq), (VBIAS, dv)):
        sums_s[at : at + 1, :] += column_sum(value)

    @pl.when(step == steps - 1)
    def _():
        for c in range(3):
            cols = slice(c * model, (c + 1) * model)
            part_ref[:, cols] = t_mm(first_s[...], mixed_s[:, cols]).astype(bf16)
        part_ref[:, 3 * model :] = to_columns(sums_s[...])


def in_back(x, grad_branch, weight, vecs, dq, dks, dvs):
    rows, model = x.shape
    count, steps = len(dks), 3
    return pl.pallas_call(
        functools.partial(in_back_kernel, steps, count),
        grid=(steps,),
        in_specs=[WHOLE] * (5 + 2 * count),
        out_specs=[WHOLE] * 2,
        out_shape=[
            jax.ShapeDtypeStruct((rows, model), bf16),
            jax.ShapeDtypeStruct((model, 3 * model + LANES), bf16),
        ],
        scratch_shapes=[
            pltpu.VMEM((rows, model), bf16),
            pltpu.VMEM((rows, 3 * model), bf16),
            pltpu.VMEM((8, model), f32),
        ],
        compiler_params=compiler_params(),
        name="in_back",
    )(x, grad_branch, weight, vecs, dq, *dks, *dvs)


def per_device(
    seq_size,
    devices,
    patches,
    text_rows,
    lengths,
    first_gain,
    first_shift,
    in_weight,
    query_bias,
    value_bias,
    out_weight,
    branch_bias,
    second_gain,
    second_shift,
    up_weight,
    up_bias,
    down_weight,
    down_bias,
    patch_cotangent,
    text_cotangent,
):
    items, patch, model = patches.shape
    slots = text_rows.shape[1]
    units = up_weight.shape[1]
    head = model // HEADS
    width = min(LANES, model)
    share = -(-slots // seq_size)
    text = round_up(share, ROW_TILE)
    seq = lax.axis_index("seq")

    def rows_of(patch_rows, slot_rows):
        padded = jnp.pad(slot_rows, ((0, 0), (0, share * seq_size - slots), (0, 0)))
        mine = lax.dynamic_slice_in_dim(padded, seq * share, share, 1)
        mine = jnp.pad(mine, ((0, 0), (0, text - share), (0, 0)))
        return jnp.concatenate([patch_rows, mine], axis=1)

    def rotate(array, step):
        if step == 0:
            return array
        return lax.ppermute(array, "seq", [((i + step) % seq_size, i) for i in range(seq_size)])

    def rotate_back(array, step):
        if step == 0:
            return array
        return lax.ppermute(array, "seq", [(i, (i + step) % seq_size) for i in range(seq_size)])

    vec_shard = jnp.stack(
        [first_gain, first_shift, query_bias, value_bias, branch_bias, second_gain, second_shift, down_bias], axis=1
    )
    vec_shard = jnp.pad(vec_shard, ((0, 0), (0, LANES - vec_shard.shape[1])))
    (first,) = gather([jnp.concatenate([in_weight, vec_shard], axis=1)], devices, seq_size, 0)
    up_column = jnp.pad(up_bias[:, None], ((0, 0), (0, LANES - 1)))
    weights, w_down = gather(
        [jnp.concatenate([up_weight, out_weight], axis=1), jnp.concatenate([down_weight, up_column], axis=1)],
        devices,
        seq_size,
        1,
    )
    vecs = first[:, 3 * model :].astype(f32).T

    x = rows_of(patches, text_rows)
    dy = rows_of(patch_cotangent, text_cotangent)
    in_full = first[:, : 3 * model]
    q, k, v = qkv(x, in_full, vecs)
    keys = [rotate(k, r) for r in range(seq_size)]
    values = [rotate(v, r) for r in range(seq_size)]

    spans = []
    for r in range(seq_size):
        slot = lax.rem(seq + r, seq_size) * share + jnp.arange(text)
        spans.append((jnp.arange(text) < share)[None, :] & (slot[None, :] < lengths[:, None]))
    valid = jnp.concatenate([jnp.ones((items, patch * seq_size), jnp.bool_)] + spans, axis=1)
    span = round_up(valid.shape[1], LANES)
    valid = jnp.pad(valid, ((0, 0), (0, span - valid.shape[1])))
    bias = jnp.where(valid, 0.0, NEG_FILL).astype(f32)[:, None, :]

    attended, logs = attend(q, keys, values, bias, patch, head, width)
    flat = (items * x.shape[1], model)
    result, grad_branch, grad_att, part, down_part = ffn(
        x.reshape(flat), attended.reshape(flat), dy.reshape(flat), weights, w_down, vecs
    )
    sums, down_sums = reduce([part, down_part], devices, seq_size, 2)
    dq, dks, dvs = attend_back(
        q, keys, values, bias, attended, logs, grad_att.reshape(x.shape), patch, head, width
    )
    dks = [rotate_back(part, r).reshape(flat) for r, part in enumerate(dks)]
    dvs = [rotate_back(part, r).reshape(flat) for r, part in enumerate(dvs)]
    grad_rows, in_part = in_back(x.reshape(flat), grad_branch, in_full, vecs, dq.reshape(flat), dks, dvs)
    (in_sums,) = reduce([in_part], devices, seq_size, 3)

    def split(rows):
        rows = rows.reshape(x.shape)
        own = rows[:, patch : patch + share]
        blocks = [rotate(own, r) for r in range(seq_size)]
        order = jnp.stack(blocks, axis=1)
        order = jnp.roll(order, seq, axis=1)
        return rows[:, :patch], order.reshape(items, -1, model)[:, :slots]

    out_patches, out_text = split(result)
    grad_patches, grad_text = split(grad_rows)
    vec1 = in_sums[:, 3 * model :].T
    vec2 = sums[:, units + model :].T
    return (
        out_patches,
        out_text,
        grad_patches,
        grad_text,
        vec1[GAIN1],
        vec1[SHIFT1],
        in_sums[:, : 3 * model],
        vec1[QBIAS],
        vec1[VBIAS],
        sums[:, units : units + model],
        vec2[BRANCH],
        vec2[GAIN2],
        vec2[SHIFT2],
        sums[:, :units],
        down_sums[:, model],
        down_sums[:, :model],
        vec2[DOWNB],
    )


def solution(mesh):
    both = ("dp", "seq")
    rows, slots, vector, matrix = P("dp", "seq", None), P("dp", None, None), P(both), P(both, None)
    weights = (vector, vector, matrix, vector, vector, matrix, vector, vector, vector, matrix, vector, matrix, vector)
    return jax.shard_map(
        functools.partial(per_device, mesh.shape["seq"], mesh.size),
        mesh=mesh,
        in_specs=(rows, slots, P("dp")) + weights + (rows, slots),
        out_specs=(rows, slots, rows, slots) + weights,
        check_vma=False,
    )
```

```python
import functools
import math

import jax
import jax.numpy as jnp
from jax import lax
from jax.experimental import pallas as pl
from jax.experimental.pallas import tpu as pltpu
from jax.sharding import PartitionSpec as P

HEADS = 8
EPSILON = 1e-05
NEG_FILL = -1e30
LOG2E = math.log2(math.e)
LN2 = math.log(2.0)
ROW_TILE = 16
LANES = 128
MESH = pl.DeviceIdType.MESH
f32, bf16 = jnp.float32, jnp.bfloat16

GAIN1, SHIFT1, QBIAS, VBIAS, BRANCH, GAIN2, SHIFT2, DOWNB = range(8)


def round_up(value, unit):
    return -(-value // unit) * unit


def mm(a, b):
    return lax.dot_general(a, b, (((1,), (0,)), ((), ())), preferred_element_type=f32)


def mm_t(a, b):
    return lax.dot_general(a, b, (((1,), (1,)), ((), ())), preferred_element_type=f32)


def t_mm(a, b):
    return lax.dot_general(a, b, (((0,), (0,)), ((), ())), preferred_element_type=f32)


def compiler_params(**more):
    return pltpu.CompilerParams(vmem_limit_bytes=60 * 2**20, **more)


WHOLE = pl.BlockSpec(memory_space=pltpu.VMEM)
ANY = pl.BlockSpec(memory_space=pl.ANY)


class Place:
    def __init__(self, depth, seq_size):
        self.depth, self.seq_size = depth, seq_size
        index = lax.axis_index("dp") * seq_size + lax.axis_index("seq")
        self.core = lax.rem(index, 2)
        self.x = lax.rem(index // 2, 2)
        self.y = lax.rem(index // 4, 2)
        self.z = index // 8
        core = self.core
        flip_x, flip_y = 1 - self.x, 1 - self.y
        x_first = self.x * core + flip_x * (1 - core)
        y_first = self.y * (1 - core) + flip_y * core
        x_second = self.x * (1 - core) + flip_x * core
        y_second = self.y * core + flip_y * (1 - core)
        self.columns = (
            (self.y, self.x),
            (y_first, x_first),
            (y_second, x_second),
            (flip_y, flip_x),
        )

    def device(self, z, y, x, core):
        index = ((z * 2 + y) * 2 + x) * 2 + core
        return (index // self.seq_size, lax.rem(index, self.seq_size))

    def layer(self, k):
        return lax.rem(self.z + self.depth - k, self.depth)

    def ahead(self, k):
        return lax.rem(self.z + k, self.depth)

    def first(self):
        return self.device(self.z, *self.columns[1], self.core)

    def second(self):
        return self.device(self.z, *self.columns[2], self.core)

    def other_core(self):
        return self.device(self.z, self.y, self.x, 1 - self.core)

    def above(self, k):
        return self.device(self.ahead(k), self.y, self.x, self.core)

    def mate(self, step):
        return (lax.axis_index("dp"), lax.rem(lax.axis_index("seq") + self.seq_size - step, self.seq_size))

    def greet(self):
        barrier = pltpu.get_barrier_semaphore()
        friends = [self.above(k) for k in range(1, self.depth)]
        friends += [self.first(), self.second(), self.other_core()]
        friends += [self.mate(step) for step in range(1, self.seq_size)]
        for friend in friends:
            pl.semaphore_signal(barrier, inc=1, device_id=friend, device_id_type=MESH)
        pl.semaphore_wait(barrier, len(friends))


def remote(src, dst, send, recv, device):
    return pltpu.make_async_remote_copy(
        src_ref=src, dst_ref=dst, send_sem=send, recv_sem=recv, device_id=device, device_id_type=MESH
    )


class Gather:
    def __init__(self, place, shard, full, out, into, local):
        self.place, self.shard, self.full, self.out, self.into, self.local = place, shard, full, out, into, local

    def block(self, k, column, core):
        y, x = self.place.columns[column]
        return self.full.at[self.place.layer(k), y, x, core]

    def copy(self, src, dst, lane, k, device):
        return remote(src, dst, self.out.at[lane, k], self.into.at[lane, k], device)

    def send(self, src, dst, lane, k, device):
        self.copy(src, dst, lane, k, device).start()

    def arrived(self, lane, k, column, core):
        here = self.block(k, column, core)
        self.copy(here, here, lane, k, self.place.other_core()).wait_recv()
        return here

    def start(self):
        place = self.place
        mine = self.block(0, 0, place.core)
        pltpu.make_async_copy(self.shard, mine, self.local).start()
        for k in range(1, place.depth):
            self.send(self.shard, mine, 0, k, place.above(k))
        self.forward_line(0)

    def forward_line(self, k):
        place = self.place
        here = self.arrived(0, k, 0, place.core) if k else self.block(0, 0, place.core)
        src = here if k else self.shard
        self.send(src, here, 1, k, place.first())
        self.send(src, here, 2, k, place.second())
        self.send(src, here, 4, k, place.other_core())

    def forward_first(self, k):
        here = self.arrived(1, k, 1, self.place.core)
        self.send(here, here, 3, k, self.place.second())
        self.send(here, here, 5, k, self.place.other_core())

    def forward_second(self, half, k):
        here = self.arrived(2 + half, k, 2 + half, self.place.core)
        self.send(here, here, 6 + half, k, self.place.other_core())

    def finish(self):
        for column in range(4):
            for k in range(self.place.depth):
                self.arrived(4 + column, k, column, 1 - self.place.core)
        mine = self.block(0, 0, self.place.core)
        pltpu.make_async_copy(self.shard, mine, self.local).wait()
        for lane in range(8):
            for k in range(self.place.depth):
                if lane or k:
                    self.copy(mine, mine, lane, k, self.place.other_core()).wait_send()


def gather_sems(depth):
    sems = pltpu.SemaphoreType.DMA
    return [sems((8, depth)), sems((8, depth)), sems]


class Reduce:
    def __init__(self, place, part, total, from_core, held, from_second, pair, from_first, line, from_line, out, into):
        self.place, self.part, self.total = place, part, total
        self.from_core, self.held, self.from_second, self.pair = from_core, held, from_second, pair
        self.from_first, self.line, self.from_line = from_first, line, from_line
        self.out, self.into = out, into

    def copy(self, src, dst, lane, device):
        return remote(src, dst, self.out.at[lane], self.into.at[lane], device)

    def core_copies(self):
        core = self.place.core
        return [self.copy(self.part.at[:, :, :, 1 - core], self.from_core, 0, self.place.other_core())]

    def second_copies(self):
        columns = self.place.columns
        return [
            self.copy(self.held.at[:, columns[2 + k][0], columns[2 + k][1]], self.from_second.at[k], 1 + k,
                      self.place.second())
            for k in range(2)
        ]

    def first_copies(self):
        return [self.copy(self.pair.at[1], self.from_first, 3, self.place.first())]

    def line_copies(self):
        place = self.place
        return [
            self.copy(self.line.at[place.ahead(k)], self.from_line.at[k - 1], 3 + k, place.above(k))
            for k in range(1, place.depth)
        ]

    def start(self, copies):
        for copy in copies:
            copy.start()

    def wait(self, copies):
        for copy in copies:
            copy.wait()

    def add_core(self):
        self.wait(self.core_copies())
        own = self.part[:, :, :, self.place.core]
        self.held[...] = (own.astype(f32) + self.from_core[...].astype(f32)).astype(bf16)

    def add_second(self):
        self.wait(self.second_copies())
        for k in range(2):
            y, x = self.place.columns[k]
            self.pair[k] = (self.held[:, y, x].astype(f32) + self.from_second[k].astype(f32)).astype(bf16)

    def add_first(self):
        self.wait(self.first_copies())
        self.line[...] = (self.pair[0].astype(f32) + self.from_first[...].astype(f32)).astype(bf16)

    def add_line(self):
        self.wait(self.line_copies())
        result = self.line[self.place.z].astype(f32)
        for k in range(self.place.depth - 1):
            result = result + self.from_line[k].astype(f32)
        self.total[...] = result


REDUCE_SCRATCH = 9


def reduce_scratch(depth, rows, cols):
    shapes = [(depth, 2, 2), (depth, 2, 2), (2, depth), (2, depth), (depth,), (depth,), (depth - 1,)]
    sems = pltpu.SemaphoreType.DMA
    return [pltpu.VMEM(shape + (rows, cols), bf16) for shape in shapes] + [sems((3 + depth,))] * 2


def reduce_kernel(seq_size, arrays, *refs):
    parts, totals, scratch = refs[:arrays], refs[arrays : 2 * arrays], refs[2 * arrays :]
    place = Place(parts[0].shape[0], seq_size)
    place.greet()
    sums = [
        Reduce(place, parts[n], totals[n], *scratch[REDUCE_SCRATCH * n : REDUCE_SCRATCH * (n + 1)])
        for n in range(arrays)
    ]
    for one in sums:
        one.start(one.core_copies())
    for one in sums:
        one.add_core()
        one.start(one.second_copies())
    for one in sums:
        one.add_second()
        one.start(one.first_copies())
    for one in sums:
        one.add_first()
        one.start(one.line_copies())
    for one in sums:
        one.add_line()


def reduce(parts, devices, seq_size, number):
    depth = devices // 8
    sizes = [(part.shape[0] // devices, part.shape[1]) for part in parts]
    return pl.pallas_call(
        functools.partial(reduce_kernel, seq_size, len(parts)),
        out_shape=[jax.ShapeDtypeStruct(size, f32) for size in sizes],
        in_specs=[WHOLE] * len(parts),
        out_specs=[WHOLE] * len(parts),
        scratch_shapes=sum([reduce_scratch(depth, *size) for size in sizes], []),
        compiler_params=compiler_params(collective_id=number, has_side_effects=True),
        name="reduce",
    )(*[part.reshape((depth, 2, 2, 2) + size) for part, size in zip(parts, sizes)])


def norm_rows(rows):
    centred = rows - jnp.mean(rows, axis=1, keepdims=True)
    inverse = lax.rsqrt(jnp.mean(centred * centred, axis=1, keepdims=True) + EPSILON)
    return centred * inverse, inverse


def norm_back(grad, scaled, inverse, gain):
    inner = grad * gain
    return inverse * (
        inner
        - jnp.mean(inner, axis=1, keepdims=True)
        - scaled * jnp.mean(inner * scaled, axis=1, keepdims=True)
    )


def gelu_both(v):
    power = jnp.exp2(v * v * (-0.5 * LOG2E))
    base = 1.0 + (0.3275911 / math.sqrt(2.0)) * jnp.abs(v)
    t = pl.reciprocal(base, approx=True)
    t = t * (2.0 - base * t)
    series = 0.5 * 1.061405429
    for factor in (-1.453152027, 1.421413741, -0.284496736, 0.254829592):
        series = series * t + 0.5 * factor
    tail = series * t * power
    cdf = jnp.where(v >= 0, 1.0 - tail, tail)
    return v * cdf, cdf + v * power * (1.0 / math.sqrt(2.0 * math.pi))


def column_sum(rows):
    return jnp.sum(rows.astype(f32), axis=0, keepdims=True)


def to_columns(rows):
    count, width = rows.shape
    return jnp.transpose(jnp.concatenate([rows, jnp.zeros((LANES - count, width), f32)], axis=0)).astype(bf16)


def own_text(ref, item, text, seq):
    slots, width = ref.shape[1:]
    own = jnp.zeros((text, width), ref.dtype)
    for r in range(-(-slots // text)):
        share = ref[item, r * text : min(slots, (r + 1) * text), :]
        if share.shape[0] < text:
            share = jnp.concatenate([share, jnp.zeros((text - share.shape[0], width), ref.dtype)], axis=0)
        own = jnp.where(seq == r, share, own)
    return own


def as_column(row, count):
    length = row.shape[1] // count
    rows = [row[:, n * length : (n + 1) * length].astype(f32) for n in range(count)]
    rows = jnp.concatenate(rows + [jnp.zeros((LANES - count, length), f32)], axis=0)
    rows = jnp.concatenate([rows, jnp.zeros((LANES, LANES - length), f32)], axis=1)
    return jnp.transpose(rows)[:length].astype(bf16)


def front_kernel(seq_size, text, *refs):
    shard_ref, vec_ref, up_bias_ref, down_ref, x_ref, slot_ref = refs[:6]
    outs = refs[6 : 11 + 2 * seq_size]
    w_full, vecs, side_ref, xtext_ref, q_ref = outs[:5]
    k_refs, v_refs = outs[5 : 5 + seq_size], outs[5 + seq_size :]
    shard, out, into, local, kv_out, kv_in = refs[11 + 2 * seq_size :]
    items, patch, model = x_ref.shape
    wide = shard_ref.shape[1]
    place = Place(w_full.shape[0], seq_size)
    seq = lax.axis_index("seq")
    place.greet()
    shard[:, :wide] = shard_ref[...]
    shard[:, wide:] = as_column(vec_ref[...], 8)
    move = Gather(place, shard, w_full, out, into, local)
    move.start()
    side_ref[:, :model] = down_ref[...]
    side_ref[:, model:] = as_column(up_bias_ref[...], 1)
    for i in range(items):
        xtext_ref[i] = own_text(slot_ref, i, text, seq)
    for k in range(1, place.depth):
        move.forward_line(k)
    for k in range(place.depth):
        move.forward_first(k)
    for half in range(2):
        for k in range(place.depth):
            move.forward_second(half, k)
    move.finish()
    rows = w_full.shape[0] * 8 * w_full.shape[4]
    weight = w_full[...].reshape(rows, w_full.shape[5])
    table = jnp.transpose(weight[:, wide:].astype(f32))
    vecs[...] = table
    scale = LOG2E / math.sqrt(model // HEADS)
    copies = []
    for i in range(items):
        scaled, _ = norm_rows(jnp.concatenate([x_ref[i], xtext_ref[i]], axis=0).astype(f32))
        first_in = (scaled * table[GAIN1 : GAIN1 + 1] + table[SHIFT1 : SHIFT1 + 1]).astype(bf16)
        k_refs[0][i] = mm(first_in, weight[:, model : 2 * model]).astype(bf16)
        v = mm(first_in, weight[:, 2 * model : 3 * model]) + table[VBIAS : VBIAS + 1]
        v_refs[0][i] = v.astype(bf16)
        for r in range(1, seq_size):
            for n, ref in enumerate((k_refs, v_refs)):
                at = (2 * i + n) * seq_size + r
                copies.append(remote(ref[0].at[i], ref[r].at[i], kv_out.at[at], kv_in.at[at], place.mate(r)))
                copies[-1].start()
        q = mm(first_in, weight[:, :model]) + table[QBIAS : QBIAS + 1]
        q_ref[i] = (q * scale).astype(bf16)
    for copy in copies:
        copy.wait()


def front(in_weight, vectors, up_bias, down_weight, patches, text_rows, text, devices, seq_size):
    items, patch, model = patches.shape
    depth = devices // 8
    rows, cols = in_weight.shape
    tokens = jax.ShapeDtypeStruct((items, patch + text, model), bf16)
    sems = pltpu.SemaphoreType.DMA
    outs = pl.pallas_call(
        functools.partial(front_kernel, seq_size, text),
        in_specs=[WHOLE] * 6,
        out_specs=[WHOLE] * (5 + 2 * seq_size),
        out_shape=[
            jax.ShapeDtypeStruct((depth, 2, 2, 2, rows, cols + LANES), bf16),
            jax.ShapeDtypeStruct((LANES, model), f32),
            jax.ShapeDtypeStruct((down_weight.shape[0], model + LANES), bf16),
            jax.ShapeDtypeStruct((items, text, model), bf16),
            tokens,
        ]
        + [tokens] * (2 * seq_size),
        scratch_shapes=[pltpu.VMEM((rows, cols + LANES), bf16)]
        + gather_sems(depth)
        + [sems((2 * items * seq_size,)), sems((2 * items * seq_size,))],
        compiler_params=compiler_params(collective_id=0, has_side_effects=True),
        name="front",
    )(in_weight, vectors, up_bias, down_weight, patches, text_rows)
    full = outs[0].reshape(model, cols + LANES)
    return full, outs[1], outs[2], outs[3], outs[4], outs[5 : 5 + seq_size], outs[5 + seq_size :]


def collect(dst, refs, patch, text):
    count, width = len(refs), refs[0].shape[2]
    for r, ref in enumerate(refs):
        dst[r * patch : (r + 1) * patch, :width] = ref[0, :patch, :]
        at = count * patch + r * text
        dst[at : at + text, :width] = ref[0, patch:, :]
    filled = count * (patch + text)
    if dst.shape[0] > filled:
        dst[filled:, :width] = jnp.zeros((dst.shape[0] - filled, width), dst.dtype)


def gather_turns(move, depth):
    turns = {}

    def add(turn, *action):
        turns.setdefault(turn, []).append(action)

    for k in range(depth):
        quarter = 4 * k // depth
        if k:
            add((1, 1, 3, 4)[quarter], move.forward_line, k)
        add((3, 4, 5, 6)[quarter], move.forward_first, k)
        add((4, 5, 6, 7)[quarter], move.forward_second, 0, k)
        add((6, 7, 8, 9)[quarter], move.forward_second, 1, k)
    return turns


def attend_kernel(count, patch, head, seq_size, *refs):
    q_ref, k_refs, v_refs = refs[0], refs[1 : 1 + count], refs[1 + count : 1 + 2 * count]
    bias_ref, shard_a, shard_b, out_ref, log_ref, full_a, full_b, keys, values = refs[1 + 2 * count : 10 + 2 * count]
    sems = refs[10 + 2 * count :]
    width = q_ref.shape[2]
    text = q_ref.shape[1] - patch
    place = Place(full_a.shape[0], seq_size)
    turn = pl.program_id(0) * pl.num_programs(1) + pl.program_id(1)
    last = pl.num_programs(0) * pl.num_programs(1) - 1
    moves = [Gather(place, shard_a, full_a, *sems[:3]), Gather(place, shard_b, full_b, *sems[3:])]

    @pl.when(turn == 0)
    def _():
        place.greet()
        for move in moves:
            move.start()

    turns = [gather_turns(move, place.depth) for move in moves]
    for at in sorted(turns[0]):

        @pl.when(turn == at)
        def _(at=at):
            for pair in zip(*[each[at] for each in turns]):
                for action in pair:
                    action[0](*action[1:])

    collect(keys, k_refs, patch, text)
    collect(values, v_refs, patch, text)
    values[:, width:] = jnp.ones((values.shape[0], values.shape[1] - width), bf16)
    q = q_ref[0]
    lane = lax.broadcasted_iota(jnp.int32, (1, width), 1) // head
    out = logs = None
    for h in range(width // head):
        q_head = jnp.where(lane == h, q, jnp.zeros_like(q))
        scores = mm_t(q_head, keys[...]) + bias_ref[0]
        top = jnp.max(scores, axis=1, keepdims=True)
        powers = jnp.exp2(scores - top).astype(bf16)
        mixed = mm(powers, values[...])
        total = mixed[:, width:]
        head_out = mixed[:, :width] * (1.0 / total)
        head_log = top + jnp.log2(total)
        out = head_out if out is None else jnp.where(lane == h, head_out, out)
        logs = head_log if logs is None else jnp.where(lane == h, head_log, logs)
    out_ref[0] = out.astype(bf16)
    log_ref[0] = logs

    @pl.when(turn == last)
    def _():
        for move in moves:
            move.finish()


def attend(q, keys, values, bias, shards, patch, head, width, devices, seq_size):
    items, _, model = q.shape
    count, span = len(keys), bias.shape[-1]
    depth = devices // 8
    block = pl.BlockSpec((1, q.shape[1], width), lambda i, p: (i, 0, p))
    outs = pl.pallas_call(
        functools.partial(attend_kernel, count, patch, head, seq_size),
        grid=(items, model // width),
        in_specs=[block] * (1 + 2 * count) + [pl.BlockSpec((1, 1, span), lambda i, p: (i, 0, 0))] + [ANY] * 2,
        out_specs=[block, block, ANY, ANY],
        out_shape=[jax.ShapeDtypeStruct(q.shape, bf16), jax.ShapeDtypeStruct(q.shape, f32)]
        + [jax.ShapeDtypeStruct((depth, 2, 2, 2) + shard.shape, shard.dtype) for shard in shards],
        scratch_shapes=[pltpu.VMEM((span, width), bf16), pltpu.VMEM((span, 2 * width), bf16)]
        + gather_sems(depth) * 2,
        compiler_params=compiler_params(collective_id=1, has_side_effects=True),
        name="attend",
    )(q, *keys, *values, bias, *shards)
    return outs[0], outs[1], [full.reshape(-1, full.shape[-1]) for full in outs[2:]]


def attend_back_kernel(count, patch, head, *refs):
    q_ref, k_refs, v_refs = refs[0], refs[1 : 1 + count], refs[1 + count : 1 + 2 * count]
    bias_ref, log_ref, grad_ref, dq_ref = refs[1 + 2 * count : 5 + 2 * count]
    dk_refs, dv_refs = refs[5 + 2 * count : 5 + 3 * count], refs[5 + 3 * count : 5 + 4 * count]
    keys, values = refs[5 + 4 * count :]
    width = q_ref.shape[2]
    text = q_ref.shape[1] - patch
    collect(keys, k_refs, patch, text)
    collect(values, v_refs, patch, text)
    q, grad = q_ref[0], grad_ref[0]
    lane = lax.broadcasted_iota(jnp.int32, (1, width), 1) // head
    row = lax.broadcasted_iota(jnp.int32, (width, 1), 0) // head
    dq = dk = dv = None
    for h in range(width // head):
        mine = lane == h
        q_head = jnp.where(mine, q, jnp.zeros_like(q))
        grad_head = jnp.where(mine, grad, jnp.zeros_like(grad))
        scores = mm_t(q_head, keys[...]) + bias_ref[0]
        probs = jnp.exp2(scores - log_ref[0, :, h * head : h * head + 1])
        grad_probs = mm_t(grad_head, values[...])
        delta = jnp.sum(probs * grad_probs, axis=1, keepdims=True)
        grad_scores = (probs * (grad_probs - delta)).astype(bf16)
        dv_head = t_mm(grad, probs.astype(bf16))
        dk_head = t_mm(q, grad_scores)
        dq_head = mm(grad_scores, keys[...])
        dq = dq_head if dq is None else jnp.where(mine, dq_head, dq)
        dk = dk_head if dk is None else jnp.where(row == h, dk_head, dk)
        dv = dv_head if dv is None else jnp.where(row == h, dv_head, dv)
    dq_ref[0] = (dq * (1.0 / math.sqrt(head))).astype(bf16)
    for grads, parts in ((dk * LN2, dk_refs), (dv, dv_refs)):
        grads = jnp.transpose(grads).astype(bf16)
        for r in range(count):
            parts[r][0, :patch, :] = grads[r * patch : (r + 1) * patch]
            at = count * patch + r * text
            parts[r][0, patch:, :] = grads[at : at + text]


def attend_back(q, keys, values, bias, logs, grad_att, patch, head, width):
    items, _, model = q.shape
    count, span = len(keys), bias.shape[-1]
    block = pl.BlockSpec((1, q.shape[1], width), lambda i, p: (i, 0, p))
    grads = pl.pallas_call(
        functools.partial(attend_back_kernel, count, patch, head),
        grid=(items, model // width),
        in_specs=[block] * (1 + 2 * count) + [pl.BlockSpec((1, 1, span), lambda i, p: (i, 0, 0))] + [block] * 2,
        out_specs=[block] * (1 + 2 * count),
        out_shape=[jax.ShapeDtypeStruct(q.shape, bf16)] * (1 + 2 * count),
        scratch_shapes=[pltpu.VMEM((span, width), bf16), pltpu.VMEM((span, width), bf16)],
        compiler_params=compiler_params(),
        name="attend_back",
    )(q, *keys, *values, bias, logs, grad_att)
    return grads[0], grads[1 : 1 + count], grads[1 + count :]


def ffn_kernel(steps, chunk, x_ref, at_ref, dy_ref, w_ref, wd_ref, vec_ref,
               res_ref, gb_ref, ga_ref, part_ref, down_ref, second_s, hidden_s, pre_s, sums_s):
    step = pl.program_id(0)
    block = x_ref.shape[0] // steps
    rows = pl.ds(pl.multiple_of(step * block, ROW_TILE), block)
    model, units = x_ref.shape[1], wd_ref.shape[0]
    gain = vec_ref[GAIN2 : GAIN2 + 1]
    w_out = w_ref[:, units:]
    up_bias = jnp.transpose(wd_ref[:, model:].astype(f32))[:1]
    middle = x_ref[rows, :].astype(f32) + (mm(at_ref[rows, :], w_out) + vec_ref[BRANCH : BRANCH + 1])
    scaled, inverse = norm_rows(middle)
    second_in = (scaled * gain + vec_ref[SHIFT2 : SHIFT2 + 1]).astype(bf16)
    second_s[rows, :] = second_in
    dy = dy_ref[rows, :]
    result = middle + vec_ref[DOWNB : DOWNB + 1]
    grad_second = jnp.zeros_like(middle)
    for c in range(units // chunk):
        cols = slice(c * chunk, (c + 1) * chunk)
        value, slope = gelu_both(mm(second_in, w_ref[:, cols]) + up_bias[:, cols])
        hidden = value.astype(bf16)
        hidden_s[rows, cols] = hidden
        grad_pre = (mm_t(dy, wd_ref[cols, :model]) * slope).astype(bf16)
        pre_s[rows, cols] = grad_pre
        result = result + mm(hidden, wd_ref[cols, :model])
        grad_second = grad_second + mm_t(grad_pre, w_ref[:, cols])
    res_ref[rows, :] = result.astype(bf16)
    grad_branch = (dy.astype(f32) + norm_back(grad_second, scaled, inverse, gain)).astype(bf16)
    gb_ref[rows, :] = grad_branch
    ga_ref[rows, :] = mm_t(grad_branch, w_out).astype(bf16)

    @pl.when(step == 0)
    def _():
        sums_s[...] = jnp.zeros_like(sums_s)

    for at, grad in ((BRANCH, grad_branch), (GAIN2, grad_second * scaled), (SHIFT2, grad_second), (DOWNB, dy)):
        sums_s[at : at + 1, :] += column_sum(grad)

    @pl.when(step == steps - 1)
    def _():
        for c in range(units // model):
            cols = slice(c * model, (c + 1) * model)
            grad_pre = pre_s[:, cols]
            part_ref[:, cols] = t_mm(second_s[...], grad_pre).astype(bf16)
            down_ref[cols, :model] = jnp.transpose(t_mm(dy_ref[...], hidden_s[:, cols])).astype(bf16)
            down_ref[cols, model:] = to_columns(column_sum(grad_pre))
        part_ref[:, units : units + model] = t_mm(at_ref[...], gb_ref[...]).astype(bf16)
        part_ref[:, units + model :] = to_columns(sums_s[...])


def ffn(x, attended, dy, weights, w_down, vecs):
    rows, model = x.shape
    units = w_down.shape[0]
    steps = 3
    return pl.pallas_call(
        functools.partial(ffn_kernel, steps, 512),
        grid=(steps,),
        in_specs=[WHOLE] * 6,
        out_specs=[WHOLE] * 5,
        out_shape=[jax.ShapeDtypeStruct((rows, model), bf16)] * 3
        + [
            jax.ShapeDtypeStruct((model, units + model + LANES), bf16),
            jax.ShapeDtypeStruct((units, model + LANES), bf16),
        ],
        scratch_shapes=[
            pltpu.VMEM((rows, model), bf16),
            pltpu.VMEM((rows, units), bf16),
            pltpu.VMEM((rows, units), bf16),
            pltpu.VMEM((8, model), f32),
        ],
        compiler_params=compiler_params(),
        name="ffn",
    )(x, attended, dy, weights, w_down, vecs)


def in_back_kernel(steps, count, *refs):
    x_ref, gb_ref, w_ref, vec_ref, dq_ref = refs[:5]
    dk_refs, dv_refs = refs[5 : 5 + count], refs[5 + count : 5 + 2 * count]
    grad_ref, part_ref, first_s, mixed_s, sums_s = refs[5 + 2 * count :]
    step = pl.program_id(0)
    block = x_ref.shape[0] // steps
    rows = pl.ds(pl.multiple_of(step * block, ROW_TILE), block)
    model = x_ref.shape[1]
    gain = vec_ref[GAIN1 : GAIN1 + 1]
    scaled, inverse = norm_rows(x_ref[rows, :].astype(f32))
    first_s[rows, :] = (scaled * gain + vec_ref[SHIFT1 : SHIFT1 + 1]).astype(bf16)
    dq = dq_ref[rows, :]
    dk = sum(ref[rows, :].astype(f32) for ref in dk_refs).astype(bf16)
    dv = sum(ref[rows, :].astype(f32) for ref in dv_refs).astype(bf16)
    mixed_s[rows, :model] = dq
    mixed_s[rows, model : 2 * model] = dk
    mixed_s[rows, 2 * model :] = dv
    grad_first = mm_t(mixed_s[rows, :], w_ref[...])
    grad = gb_ref[rows, :].astype(f32) + norm_back(grad_first, scaled, inverse, gain)
    grad_ref[rows, :] = grad.astype(bf16)

    @pl.when(step == 0)
    def _():
        sums_s[...] = jnp.zeros_like(sums_s)

    for at, value in ((GAIN1, grad_first * scaled), (SHIFT1, grad_first), (QBIAS, dq), (VBIAS, dv)):
        sums_s[at : at + 1, :] += column_sum(value)

    @pl.when(step == steps - 1)
    def _():
        for c in range(3):
            cols = slice(c * model, (c + 1) * model)
            part_ref[:, cols] = t_mm(first_s[...], mixed_s[:, cols]).astype(bf16)
        part_ref[:, 3 * model :] = to_columns(sums_s[...])


def in_back(x, grad_branch, weight, vecs, dq, dks, dvs):
    rows, model = x.shape
    count, steps = len(dks), 3
    return pl.pallas_call(
        functools.partial(in_back_kernel, steps, count),
        grid=(steps,),
        in_specs=[WHOLE] * (5 + 2 * count),
        out_specs=[WHOLE] * 2,
        out_shape=[
            jax.ShapeDtypeStruct((rows, model), bf16),
            jax.ShapeDtypeStruct((model, 3 * model + LANES), bf16),
        ],
        scratch_shapes=[
            pltpu.VMEM((rows, model), bf16),
            pltpu.VMEM((rows, 3 * model), bf16),
            pltpu.VMEM((8, model), f32),
        ],
        compiler_params=compiler_params(),
        name="in_back",
    )(x, grad_branch, weight, vecs, dq, *dks, *dvs)


def per_device(
    seq_size,
    devices,
    patches,
    text_rows,
    lengths,
    first_gain,
    first_shift,
    in_weight,
    query_bias,
    value_bias,
    out_weight,
    branch_bias,
    second_gain,
    second_shift,
    up_weight,
    up_bias,
    down_weight,
    down_bias,
    patch_cotangent,
    text_cotangent,
):
    items, patch, model = patches.shape
    slots = text_rows.shape[1]
    units = up_weight.shape[1]
    head = model // HEADS
    width = min(LANES, model)
    text = round_up(-(-slots // seq_size), ROW_TILE)
    seq = lax.axis_index("seq")

    def rotate(array, step):
        if step == 0:
            return array
        return lax.ppermute(array, "seq", [((i + step) % seq_size, i) for i in range(seq_size)])

    def rotate_back(array, step):
        if step == 0:
            return array
        return lax.ppermute(array, "seq", [(i, (i + step) % seq_size) for i in range(seq_size)])

    vectors = [first_gain, first_shift, query_bias, value_bias, branch_bias, second_gain, second_shift, down_bias]
    in_full, vecs, side_shard, x_text, q, keys, values = front(
        in_weight, jnp.concatenate(vectors)[None], up_bias[None], down_weight, patches, text_rows, text, devices, seq_size
    )
    shards = [jnp.concatenate([up_weight, out_weight], axis=1), side_shard]

    slot_pad = ((0, 0), (0, text * seq_size - slots), (0, 0))
    dy_text = lax.dynamic_slice_in_dim(jnp.pad(text_cotangent, slot_pad), seq * text, text, 1)
    dy = jnp.concatenate([patch_cotangent, dy_text], axis=1)
    x = jnp.concatenate([patches, x_text], axis=1)

    spans = []
    for r in range(seq_size):
        slot = lax.rem(seq + r, seq_size) * text + jnp.arange(text)
        spans.append(slot[None, :] < lengths[:, None])
    valid = jnp.concatenate([jnp.ones((items, patch * seq_size), jnp.bool_)] + spans, axis=1)
    span = round_up(valid.shape[1], LANES)
    valid = jnp.pad(valid, ((0, 0), (0, span - valid.shape[1])))
    bias = jnp.where(valid, 0.0, NEG_FILL).astype(f32)[:, None, :]

    attended, logs, (weights, w_down) = attend(
        q, keys, values, bias, shards, patch, head, width, devices, seq_size
    )
    flat = (items * x.shape[1], model)
    result, grad_branch, grad_att, part, down_part = ffn(
        x.reshape(flat), attended.reshape(flat), dy.reshape(flat), weights, w_down, vecs
    )
    sums, down_sums = reduce([part, down_part], devices, seq_size, 2)
    dq, dks, dvs = attend_back(
        q, keys, values, bias, logs, grad_att.reshape(x.shape), patch, head, width
    )
    dks = [rotate_back(part, r).reshape(flat) for r, part in enumerate(dks)]
    dvs = [rotate_back(part, r).reshape(flat) for r, part in enumerate(dvs)]
    grad_rows, in_part = in_back(x.reshape(flat), grad_branch, in_full[:, : 3 * model], vecs, dq.reshape(flat), dks, dvs)
    (in_sums,) = reduce([in_part], devices, seq_size, 3)

    def split(rows):
        rows = rows.reshape(x.shape)
        own = rows[:, patch:]
        blocks = [rotate(own, r) for r in range(seq_size)]
        order = jnp.stack(blocks, axis=1)
        order = jnp.roll(order, seq, axis=1)
        return rows[:, :patch], order.reshape(items, -1, model)[:, :slots]

    out_patches, out_text = split(result)
    grad_patches, grad_text = split(grad_rows)
    vec1 = in_sums[:, 3 * model :].T
    vec2 = sums[:, units + model :].T
    return (
        out_patches,
        out_text,
        grad_patches,
        grad_text,
        vec1[GAIN1],
        vec1[SHIFT1],
        in_sums[:, : 3 * model],
        vec1[QBIAS],
        vec1[VBIAS],
        sums[:, units : units + model],
        vec2[BRANCH],
        vec2[GAIN2],
        vec2[SHIFT2],
        sums[:, :units],
        down_sums[:, model],
        down_sums[:, :model],
        vec2[DOWNB],
    )


def solution(mesh):
    both = ("dp", "seq")
    rows, slots, vector, matrix = P("dp", "seq", None), P("dp", None, None), P(both), P(both, None)
    weights = (vector, vector, matrix, vector, vector, matrix, vector, vector, vector, matrix, vector, matrix, vector)
    return jax.shard_map(
        functools.partial(per_device, mesh.shape["seq"], mesh.size),
        mesh=mesh,
        in_specs=(rows, slots, P("dp")) + weights + (rows, slots),
        out_specs=(rows, slots, rows, slots) + weights,
        check_vma=False,
    )
```

```python
import functools
import math

import jax
import jax.numpy as jnp
from jax import lax
from jax.experimental import pallas as pl
from jax.experimental.pallas import tpu as pltpu
from jax.sharding import PartitionSpec as P

HEADS = 8
EPSILON = 1e-05
NEG_FILL = -1e30
LOG2E = math.log2(math.e)
LN2 = math.log(2.0)
ROW_TILE = 16
LANES = 128
MESH = pl.DeviceIdType.MESH
f32, bf16 = jnp.float32, jnp.bfloat16

GAIN1, SHIFT1, QBIAS, VBIAS, BRANCH, GAIN2, SHIFT2, DOWNB = range(8)


def round_up(value, unit):
    return -(-value // unit) * unit


def mm(a, b):
    return lax.dot_general(a, b, (((1,), (0,)), ((), ())), preferred_element_type=f32)


def mm_t(a, b):
    return lax.dot_general(a, b, (((1,), (1,)), ((), ())), preferred_element_type=f32)


def t_mm(a, b):
    return lax.dot_general(a, b, (((0,), (0,)), ((), ())), preferred_element_type=f32)


def compiler_params(**more):
    return pltpu.CompilerParams(vmem_limit_bytes=60 * 2**20, **more)


WHOLE = pl.BlockSpec(memory_space=pltpu.VMEM)
ANY = pl.BlockSpec(memory_space=pl.ANY)


class Place:
    def __init__(self, depth, seq_size):
        self.depth, self.seq_size = depth, seq_size
        index = lax.axis_index("dp") * seq_size + lax.axis_index("seq")
        self.core = lax.rem(index, 2)
        self.x = lax.rem(index // 2, 2)
        self.y = lax.rem(index // 4, 2)
        self.z = index // 8
        core = self.core
        flip_x, flip_y = 1 - self.x, 1 - self.y
        x_first = self.x * core + flip_x * (1 - core)
        y_first = self.y * (1 - core) + flip_y * core
        x_second = self.x * (1 - core) + flip_x * core
        y_second = self.y * core + flip_y * (1 - core)
        self.columns = (
            (self.y, self.x),
            (y_first, x_first),
            (y_second, x_second),
            (flip_y, flip_x),
        )

    def device(self, z, y, x, core):
        index = ((z * 2 + y) * 2 + x) * 2 + core
        return (index // self.seq_size, lax.rem(index, self.seq_size))

    def layer(self, k):
        return lax.rem(self.z + self.depth - k, self.depth)

    def ahead(self, k):
        return lax.rem(self.z + k, self.depth)

    def first(self):
        return self.device(self.z, *self.columns[1], self.core)

    def second(self):
        return self.device(self.z, *self.columns[2], self.core)

    def other_core(self):
        return self.device(self.z, self.y, self.x, 1 - self.core)

    def above(self, k):
        return self.device(self.ahead(k), self.y, self.x, self.core)

    def mate(self, step):
        return (lax.axis_index("dp"), lax.rem(lax.axis_index("seq") + self.seq_size - step, self.seq_size))

    def octant(self, n):
        column, core = n % 4, n // 4
        y, x = self.columns[column]
        core = self.core * (1 - core) + (1 - self.core) * core
        return self.device(self.z, y, x, core), (y, x, core)

    def greet(self, corners=False):
        barrier = pltpu.get_barrier_semaphore()
        friends = [self.above(k) for k in range(1, self.depth)]
        friends += [self.octant(n)[0] for n in range(1, 8)] if corners else [self.first(), self.second(), self.other_core()]
        friends += [self.mate(step) for step in range(1, self.seq_size)]
        for friend in friends:
            pl.semaphore_signal(barrier, inc=1, device_id=friend, device_id_type=MESH)
        pl.semaphore_wait(barrier, len(friends))


def remote(src, dst, send, recv, device):
    return pltpu.make_async_remote_copy(
        src_ref=src, dst_ref=dst, send_sem=send, recv_sem=recv, device_id=device, device_id_type=MESH
    )


class Line:
    def __init__(self, place, shard, line, out, into, local):
        self.place, self.shard, self.line, self.out, self.into, self.local = place, shard, line, out, into, local

    def copy(self, k):
        return remote(self.shard, self.line.at[k], self.out.at[k], self.into.at[k], self.place.above(k))

    def start(self):
        pltpu.make_async_copy(self.shard, self.line.at[0], self.local).start()
        for k in range(1, self.place.depth):
            self.copy(k).start()

    def finish(self):
        pltpu.make_async_copy(self.shard, self.line.at[0], self.local).wait()
        for k in range(1, self.place.depth):
            self.copy(k).wait()


def line_sems(depth):
    sems = pltpu.SemaphoreType.DMA
    return [sems((depth,)), sems((depth,)), sems]


class Spread:
    def __init__(self, place, source, full, out, into, local):
        self.place, self.source, self.full, self.out, self.into, self.local = place, source, full, out, into, local

    def block(self, k, column, core):
        y, x = self.place.columns[column]
        return self.full.at[self.place.layer(k), y, x, core]

    def copy(self, src, dst, lane, k, device):
        return remote(src, dst, self.out.at[lane, k], self.into.at[lane, k], device)

    def arrived(self, lane, k, column, core):
        here = self.block(k, column, core)
        self.copy(here, here, lane, k, self.place.other_core()).wait_recv()
        return here

    def send_line(self, k):
        place, src, here = self.place, self.source(k), self.block(k, 0, self.place.core)
        self.copy(src, here, 0, k, place.first()).start()
        self.copy(src, here, 1, k, place.second()).start()
        self.copy(src, here, 3, k, place.other_core()).start()
        pltpu.make_async_copy(src, here, self.local.at[k]).start()

    def forward_first(self, k):
        here = self.arrived(0, k, 1, self.place.core)
        self.copy(here, here, 2, k, self.place.second()).start()
        self.copy(here, here, 4, k, self.place.other_core()).start()

    def forward_second(self, half, k):
        here = self.arrived(1 + half, k, 2 + half, self.place.core)
        self.copy(here, here, 5 + half, k, self.place.other_core()).start()

    def finish(self):
        for k in range(self.place.depth):
            src, here = self.source(k), self.block(k, 0, self.place.core)
            pltpu.make_async_copy(src, here, self.local.at[k]).wait()
            for column in range(4):
                self.arrived(3 + column, k, column, 1 - self.place.core)
            for lane in range(7):
                self.copy(here, here, lane, k, self.place.other_core()).wait_send()


def spread_sems(depth):
    sems = pltpu.SemaphoreType.DMA
    return [sems((7, depth)), sems((7, depth)), sems((depth,))]


class Reduce:
    def __init__(self, place, part, from_core, held, from_second, pair, from_first, line, from_line, out, into, local):
        self.place, self.part, self.local = place, part, local
        self.from_core, self.held, self.from_second, self.pair = from_core, held, from_second, pair
        self.from_first, self.line, self.from_line = from_first, line, from_line
        self.out, self.into = out, into

    def copy(self, src, dst, lane, device):
        return remote(src, dst, self.out.at[lane], self.into.at[lane], device)

    def own_copy(self):
        return pltpu.make_async_copy(self.part.at[:, :, :, self.place.core], self.held, self.local)

    def core_copy(self):
        return self.copy(self.part.at[:, :, :, 1 - self.place.core], self.from_core, 0, self.place.other_core())

    def second_copies(self):
        columns = self.place.columns
        return [
            self.copy(self.held.at[:, columns[2 + k][0], columns[2 + k][1]], self.from_second.at[k], 1 + k,
                      self.place.second())
            for k in range(2)
        ]

    def first_copy(self):
        return self.copy(self.pair.at[1], self.from_first, 3, self.place.first())

    def line_copies(self):
        place = self.place
        return [
            self.copy(self.line.at[place.ahead(k)], self.from_line.at[k - 1], 3 + k, place.above(k))
            for k in range(1, place.depth)
        ]

    def to_core(self):
        self.core_copy().start()
        self.own_copy().start()

    def to_second(self):
        self.own_copy().wait()
        self.core_copy().wait()
        self.held[...] = (self.held[...].astype(f32) + self.from_core[...].astype(f32)).astype(bf16)
        for copy in self.second_copies():
            copy.start()

    def to_first(self):
        for copy in self.second_copies():
            copy.wait()
        for k in range(2):
            y, x = self.place.columns[k]
            self.pair[k] = (self.held[:, y, x].astype(f32) + self.from_second[k].astype(f32)).astype(bf16)
        self.first_copy().start()

    def to_line(self):
        self.first_copy().wait()
        self.line[...] = (self.pair[0].astype(f32) + self.from_first[...].astype(f32)).astype(bf16)
        for copy in self.line_copies():
            copy.start()

    def last(self):
        for copy in self.line_copies():
            copy.wait()
        result = self.line[self.place.z].astype(f32)
        for k in range(self.place.depth - 1):
            result = result + self.from_line[k].astype(f32)
        return result


def reduce_scratch(depth, rows, cols):
    shapes = [(depth, 2, 2), (depth, 2, 2), (2, depth), (2, depth), (depth,), (depth,), (depth - 1,)]
    sems = pltpu.SemaphoreType.DMA
    return [pltpu.VMEM(shape + (rows, cols), bf16) for shape in shapes] + [sems((3 + depth,))] * 2 + [sems]


class ShortReduce:
    def __init__(self, place, part, from_octant, line, from_line, out, into):
        self.place, self.part, self.from_octant, self.line, self.from_line = place, part, from_octant, line, from_line
        self.out, self.into = out, into

    def octant_copy(self, n):
        device, (y, x, core) = self.place.octant(n)
        return remote(
            self.part.at[:, y, x, core], self.from_octant.at[n - 1], self.out.at[n - 1], self.into.at[n - 1], device
        )

    def line_copy(self, k):
        return remote(
            self.line.at[self.place.ahead(k)], self.from_line.at[k - 1], self.out.at[6 + k], self.into.at[6 + k],
            self.place.above(k)
        )

    def start(self):
        for n in range(1, 8):
            self.octant_copy(n).start()

    def to_line(self):
        place = self.place
        total = self.part[:, place.y, place.x, place.core].astype(f32)
        for n in range(1, 8):
            self.octant_copy(n).wait()
            total = total + self.from_octant[n - 1].astype(f32)
        self.line[...] = total.astype(bf16)
        for k in range(1, place.depth):
            self.line_copy(k).start()

    def last(self):
        total = self.line[self.place.z].astype(f32)
        for k in range(1, self.place.depth):
            self.line_copy(k).wait()
            total = total + self.from_line[k - 1].astype(f32)
        return total


def short_reduce_scratch(depth, rows, cols):
    sems = pltpu.SemaphoreType.DMA
    shapes = [(depth, 2, 2, 2), (7, depth), (depth,), (depth - 1,)]
    return [pltpu.VMEM(shape + (rows, cols), bf16) for shape in shapes] + [sems((6 + depth,))] * 2


def norm_rows(rows):
    centred = rows - jnp.mean(rows, axis=1, keepdims=True)
    inverse = lax.rsqrt(jnp.mean(centred * centred, axis=1, keepdims=True) + EPSILON)
    return centred * inverse, inverse


def norm_back(grad, scaled, inverse, gain):
    inner = grad * gain
    return inverse * (
        inner
        - jnp.mean(inner, axis=1, keepdims=True)
        - scaled * jnp.mean(inner * scaled, axis=1, keepdims=True)
    )


def gelu_both(v):
    power = jnp.exp2(v * v * (-0.5 * LOG2E))
    base = 1.0 + (0.3275911 / math.sqrt(2.0)) * jnp.abs(v)
    t = pl.reciprocal(base, approx=True)
    t = t * (2.0 - base * t)
    series = 0.5 * 1.061405429
    for factor in (-1.453152027, 1.421413741, -0.284496736, 0.254829592):
        series = series * t + 0.5 * factor
    tail = series * t * power
    cdf = jnp.where(v >= 0, 1.0 - tail, tail)
    return v * cdf, cdf + v * power * (1.0 / math.sqrt(2.0 * math.pi))


def column_sum(rows):
    return jnp.sum(rows.astype(f32), axis=0, keepdims=True)


def to_columns(rows):
    count, width = rows.shape
    return jnp.transpose(jnp.concatenate([rows, jnp.zeros((LANES - count, width), f32)], axis=0)).astype(bf16)


def own_text(ref, text, seq):
    slots, width = ref.shape
    own = jnp.zeros((text, width), ref.dtype)
    for r in range(-(-slots // text)):
        share = ref[r * text : min(slots, (r + 1) * text), :]
        if share.shape[0] < text:
            share = jnp.concatenate([share, jnp.zeros((text - share.shape[0], width), ref.dtype)], axis=0)
        own = jnp.where(seq == r, share, own)
    return own


def as_columns(vectors):
    length = vectors[0].shape[0]
    rows = [vector.reshape(1, length).astype(f32) for vector in vectors]
    rows = jnp.concatenate(rows + [jnp.zeros((LANES - len(rows), length), f32)], axis=0)
    rows = jnp.concatenate([rows, jnp.zeros((LANES, LANES - length), f32)], axis=1)
    return jnp.transpose(rows)[:length].astype(bf16)


def front_kernel(seq_size, text, width, *refs):
    shard_ref, vec_refs, up_ref, up_bias_ref, out_w_ref, down_ref, x_ref, slot_ref = (
        refs[0], refs[1:9], *refs[9:15]
    )
    outs, refs = refs[15 : 22 + 2 * seq_size], refs[22 + 2 * seq_size :]
    w_full, vecs, line_a, line_b, xtext_ref, first_ref, q_ref = outs[:7]
    k_refs, v_refs = outs[7 : 7 + seq_size], outs[7 + seq_size :]
    shard, shard_a, shard_b, line = refs[:4]
    sems, kv_out, kv_in = refs[4:-2], refs[-2], refs[-1]
    items, patch, model = x_ref.shape
    wide, units = shard_ref.shape[1], up_ref.shape[1]
    pairs = model // width
    place = Place(w_full.shape[0], seq_size)
    seq = lax.axis_index("seq")
    for p in range(pairs):
        for n in range(3):
            at = n * model + p * width
            to = (3 * p + n) * width
            shard[:, to : to + width] = shard_ref[:, at : at + width]
    shard[:, wide:] = as_columns([ref[...] for ref in vec_refs])
    place.greet()
    lines = Line(place, shard, line, *sems[:3])
    lines.start()

    def source(k):
        return line.at[k] if k else shard

    move = Spread(place, source, w_full, *sems[3:6])
    move.send_line(0)
    shard_a[:, :units] = up_ref[...]
    shard_a[:, units:] = out_w_ref[...]
    shard_b[:, :model] = down_ref[...]
    shard_b[:, model:] = as_columns([up_bias_ref[...]])
    more = [Line(place, shard_a, line_a, *sems[6:9]), Line(place, shard_b, line_b, *sems[9:12])]
    for i in range(items):
        xtext_ref[i] = own_text(slot_ref.at[i], text, seq)
    for k in range(1, place.depth):
        lines.copy(k).wait_recv()
        move.send_line(k)
    for each in more:
        each.start()
    for k in range(place.depth):
        move.forward_first(k)
    for half in range(2):
        for k in range(place.depth):
            move.forward_second(half, k)
    pltpu.make_async_copy(shard, line.at[0], lines.local).wait()
    for k in range(1, place.depth):
        lines.copy(k).wait_send()
    move.finish()
    weight = w_full[...].reshape(model, wide + LANES)
    table = jnp.transpose(weight[:, wide:].astype(f32))
    vecs[...] = table
    scale = LOG2E / math.sqrt(model // HEADS)
    copies = []
    for i in range(items):
        scaled, _ = norm_rows(jnp.concatenate([x_ref[i], xtext_ref[i]], axis=0).astype(f32))
        first_in = (scaled * table[GAIN1 : GAIN1 + 1] + table[SHIFT1 : SHIFT1 + 1]).astype(bf16)
        first_ref[i] = first_in
        for p in range(pairs):
            cols = slice(p * width, (p + 1) * width)
            projected = mm(first_in, weight[:, 3 * p * width : 3 * (p + 1) * width])
            q_ref[i, :, cols] = ((projected[:, :width] + table[QBIAS : QBIAS + 1, cols]) * scale).astype(bf16)
            k_refs[0][i, :, cols] = projected[:, width : 2 * width].astype(bf16)
            v_refs[0][i, :, cols] = (projected[:, 2 * width :] + table[VBIAS : VBIAS + 1, cols]).astype(bf16)
        for r in range(1, seq_size):
            for n, ref in enumerate((k_refs, v_refs)):
                at = (2 * i + n) * seq_size + r
                copies.append(remote(ref[0].at[i], ref[r].at[i], kv_out.at[at], kv_in.at[at], place.mate(r)))
                copies[-1].start()
    for each in more:
        each.finish()
    for copy in copies:
        copy.wait()


def front(in_weight, vectors, up_weight, up_bias, out_weight, down_weight, patches, text_rows, text, width, devices,
          seq_size):
    items, patch, model = patches.shape
    depth = devices // 8
    rows, cols = in_weight.shape
    shape_a = (rows, up_weight.shape[1] + model)
    shape_b = (down_weight.shape[0], model + LANES)
    tokens = jax.ShapeDtypeStruct((items, patch + text, model), bf16)
    sems = pltpu.SemaphoreType.DMA
    outs = pl.pallas_call(
        functools.partial(front_kernel, seq_size, text, width),
        in_specs=[WHOLE] * 15,
        out_specs=[WHOLE] * 2 + [ANY] * 2 + [WHOLE] * (3 + 2 * seq_size),
        out_shape=[
            jax.ShapeDtypeStruct((depth, 2, 2, 2, rows, cols + LANES), bf16),
            jax.ShapeDtypeStruct((LANES, model), f32),
            jax.ShapeDtypeStruct((depth,) + shape_a, bf16),
            jax.ShapeDtypeStruct((depth,) + shape_b, bf16),
            jax.ShapeDtypeStruct((items, text, model), bf16),
            tokens,
            tokens,
        ]
        + [tokens] * (2 * seq_size),
        scratch_shapes=[
            pltpu.VMEM((rows, cols + LANES), bf16),
            pltpu.VMEM(shape_a, bf16),
            pltpu.VMEM(shape_b, bf16),
            pltpu.VMEM((depth, rows, cols + LANES), bf16),
        ]
        + line_sems(depth)
        + spread_sems(depth)
        + line_sems(depth) * 2
        + [sems((2 * items * seq_size,)), sems((2 * items * seq_size,))],
        compiler_params=compiler_params(collective_id=0, has_side_effects=True),
        name="front",
    )(in_weight, *vectors, up_weight, up_bias, out_weight, down_weight, patches, text_rows)
    full = outs[0].reshape(model, cols + LANES)
    return full, outs[1], outs[2:4], outs[4], outs[5], outs[6], outs[7 : 7 + seq_size], outs[7 + seq_size :]


def collect(dst, refs, patch, text):
    count, width = len(refs), refs[0].shape[2]
    for r, ref in enumerate(refs):
        dst[r * patch : (r + 1) * patch, :width] = ref[0, :patch, :]
        at = count * patch + r * text
        dst[at : at + text, :width] = ref[0, patch:, :]
    filled = count * (patch + text)
    if dst.shape[0] > filled:
        dst[filled:, :width] = jnp.zeros((dst.shape[0] - filled, width), dst.dtype)


def spread_turns(move, depth):
    turns = {}

    def add(turn, *action):
        turns.setdefault(turn, []).append(action)

    for k in range(depth):
        quarter = 4 * k // depth
        add((2, 3, 4, 5)[quarter], move.forward_first, k)
        add((3, 4, 5, 6)[quarter], move.forward_second, 0, k)
        add((6, 7, 8, 9)[quarter], move.forward_second, 1, k)
    return turns


def attend_kernel(count, patch, head, seq_size, *refs):
    q_ref, k_refs, v_refs = refs[0], refs[1 : 1 + count], refs[1 + count : 1 + 2 * count]
    bias_ref, line_a, line_b, out_ref, rest_ref, log_ref, full_a, full_b = refs[1 + 2 * count : 9 + 2 * count]
    keys, values, *sems = refs[9 + 2 * count :]
    width = q_ref.shape[2]
    text = q_ref.shape[1] - patch
    place = Place(full_a.shape[0], seq_size)
    turn = pl.program_id(0) * pl.num_programs(1) + pl.program_id(1)
    last = pl.num_programs(0) * pl.num_programs(1) - 1
    moves = [
        Spread(place, lambda k: line_a.at[k], full_a, *sems[:3]),
        Spread(place, lambda k: line_b.at[k], full_b, *sems[3:]),
    ]

    @pl.when(turn == 0)
    def _():
        place.greet()
        for k in range(place.depth):
            for move in moves:
                move.send_line(k)

    turns = [spread_turns(move, place.depth) for move in moves]
    for at in sorted(turns[0]):

        @pl.when(turn == at)
        def _(at=at):
            for pair in zip(*[each[at] for each in turns]):
                for action in pair:
                    action[0](*action[1:])

    collect(keys, k_refs, patch, text)
    collect(values, v_refs, patch, text)
    values[:, width:] = jnp.ones((values.shape[0], values.shape[1] - width), bf16)
    q = q_ref[0]
    lane = lax.broadcasted_iota(jnp.int32, (1, width), 1) // head
    out = logs = None
    for h in range(width // head):
        q_head = jnp.where(lane == h, q, jnp.zeros_like(q))
        scores = mm_t(q_head, keys[...]) + bias_ref[0]
        top = jnp.max(scores, axis=1, keepdims=True)
        powers = jnp.exp2(scores - top).astype(bf16)
        mixed = mm(powers, values[...])
        total = mixed[:, width:]
        head_out = mixed[:, :width] * (1.0 / total)
        head_log = top + jnp.log2(total)
        out = head_out if out is None else jnp.where(lane == h, head_out, out)
        logs = head_log if logs is None else jnp.where(lane == h, head_log, logs)
    high = out.astype(bf16)
    out_ref[0] = high
    rest_ref[0] = (out - high.astype(f32)).astype(bf16)
    log_ref[0] = logs

    @pl.when(turn == last)
    def _():
        for move in moves:
            move.finish()


def attend(q, keys, values, bias, lines, patch, head, width, devices, seq_size):
    items, _, model = q.shape
    count, span = len(keys), bias.shape[-1]
    depth = devices // 8
    block = pl.BlockSpec((1, q.shape[1], width), lambda i, p: (i, 0, p))
    outs = pl.pallas_call(
        functools.partial(attend_kernel, count, patch, head, seq_size),
        grid=(items, model // width),
        in_specs=[block] * (1 + 2 * count) + [pl.BlockSpec((1, 1, span), lambda i, p: (i, 0, 0))] + [ANY] * 2,
        out_specs=[block, block, block, ANY, ANY],
        out_shape=[jax.ShapeDtypeStruct(q.shape, bf16)] * 2
        + [jax.ShapeDtypeStruct(q.shape, f32)]
        + [jax.ShapeDtypeStruct((depth, 2, 2, 2) + line.shape[1:], line.dtype) for line in lines],
        scratch_shapes=[pltpu.VMEM((span, width), bf16), pltpu.VMEM((span, 2 * width), bf16)]
        + spread_sems(depth) * 2,
        compiler_params=compiler_params(collective_id=1, has_side_effects=True),
        name="attend",
    )(q, *keys, *values, bias, *lines)
    return outs[0], outs[1], outs[2], [full.reshape(-1, full.shape[-1]) for full in outs[3:]]


def ffn_kernel(steps, chunk, seq_ref, x_ref, xtext_ref, at_ref, dy_ref, dy_slot_ref, w_ref, wd_ref, vec_ref,
               res_ref, restext_ref, gb_ref, ga_ref, part_ref, down_ref,
               second_s, hidden_s, pre_s, dy_s, sums_s, bias_s, out_s):
    step = pl.program_id(0)
    patch, model = x_ref.shape[1:]
    text = xtext_ref.shape[1]
    block, units = patch + text, wd_ref.shape[0]
    rows = pl.ds(pl.multiple_of(step * block, ROW_TILE), block)
    gain = vec_ref[GAIN2 : GAIN2 + 1]
    w_out = w_ref[:, units:]

    @pl.when(step == 0)
    def _():
        sums_s[...] = jnp.zeros_like(sums_s)
        bias_s[...] = jnp.transpose(wd_ref[:, model:].astype(f32))[:8]

    x = jnp.concatenate([x_ref[0], xtext_ref[0]], axis=0).astype(f32)
    dy = jnp.concatenate([dy_ref[0], own_text(dy_slot_ref.at[0], text, seq_ref[0])], axis=0)
    dy_s[rows, :] = dy
    middle = x + (mm(at_ref[0], w_out) + vec_ref[BRANCH : BRANCH + 1])
    scaled, inverse = norm_rows(middle)
    second_in = (scaled * gain + vec_ref[SHIFT2 : SHIFT2 + 1]).astype(bf16)
    second_s[rows, :] = second_in
    result = middle + vec_ref[DOWNB : DOWNB + 1]
    grad_second = jnp.zeros_like(middle)
    for c in range(units // chunk):
        cols = slice(c * chunk, (c + 1) * chunk)
        value, slope = gelu_both(mm(second_in, w_ref[:, cols]) + bias_s[:1, cols])
        hidden = value.astype(bf16)
        hidden_s[rows, cols] = hidden
        grad_pre = (mm_t(dy, wd_ref[cols, :model]) * slope).astype(bf16)
        pre_s[rows, cols] = grad_pre
        result = result + mm(hidden, wd_ref[cols, :model])
        grad_second = grad_second + mm_t(grad_pre, w_ref[:, cols])
    result = result.astype(bf16)
    res_ref[0] = result[:patch]
    restext_ref[0] = result[patch:]
    grad_branch = (dy.astype(f32) + norm_back(grad_second, scaled, inverse, gain)).astype(bf16)
    gb_ref[0] = grad_branch
    ga_ref[0] = mm_t(grad_branch, w_out).astype(bf16)
    out_grad = t_mm(at_ref[0], grad_branch)

    @pl.when(step == 0)
    def _():
        out_s[...] = out_grad

    @pl.when(step > 0)
    def _():
        out_s[...] += out_grad

    for at, grad in ((BRANCH, grad_branch), (GAIN2, grad_second * scaled), (SHIFT2, grad_second), (DOWNB, dy)):
        sums_s[at : at + 1, :] += column_sum(grad)

    @pl.when(step == steps - 1)
    def _():
        for c in range(units // model):
            cols = slice(c * model, (c + 1) * model)
            grad_pre = pre_s[:, cols]
            part_ref[:, cols] = t_mm(second_s[...], grad_pre).astype(bf16)
            down_ref[cols, :model] = jnp.transpose(t_mm(dy_s[...], hidden_s[:, cols])).astype(bf16)
            down_ref[cols, model:] = to_columns(column_sum(grad_pre))
        part_ref[:, units : units + model] = out_s[...].astype(bf16)
        part_ref[:, units + model :] = to_columns(sums_s[...])


def ffn(seq, patches, x_text, attended, patch_cotangent, text_cotangent, weights, w_down, vecs):
    items, patch, model = patches.shape
    units, rows, text, slots = w_down.shape[0], attended.shape[1], x_text.shape[1], text_cotangent.shape[1]

    def item(count):
        return pl.BlockSpec((1, count, model), lambda i: (i, 0, 0))

    def shape(count):
        return jax.ShapeDtypeStruct((items, count, model), bf16)

    return pl.pallas_call(
        functools.partial(ffn_kernel, items, 512),
        grid=(items,),
        in_specs=[pl.BlockSpec(memory_space=pltpu.SMEM)]
        + [item(patch), item(text), item(rows), item(patch), item(slots)]
        + [WHOLE] * 3,
        out_specs=[item(patch), item(text), item(rows), item(rows), WHOLE, WHOLE],
        out_shape=[shape(patch), shape(text), shape(rows), shape(rows)]
        + [
            jax.ShapeDtypeStruct((model, units + model + LANES), bf16),
            jax.ShapeDtypeStruct((units, model + LANES), bf16),
        ],
        scratch_shapes=[
            pltpu.VMEM((items * rows, model), bf16),
            pltpu.VMEM((items * rows, units), bf16),
            pltpu.VMEM((items * rows, units), bf16),
            pltpu.VMEM((items * rows, model), bf16),
            pltpu.VMEM((8, model), f32),
            pltpu.VMEM((8, units), f32),
            pltpu.VMEM((model, model), f32),
        ],
        compiler_params=compiler_params(),
        name="ffn",
    )(seq, patches, x_text, attended, patch_cotangent, text_cotangent, weights, w_down, vecs)


def back_kernel(count, patch, head, seq_size, pairs, items, *refs):
    refs = list(refs)

    def take(number):
        taken = refs[:number]
        del refs[:number]
        return taken

    (q_ref,), k_refs, v_refs = take(1), take(count), take(count)
    bias_ref, log_ref, at_ref, rest_ref, grad_ref = take(5)
    part_a, part_b, w_any, vec_ref, first_any, x_any, xtext_any, gb_any, restext_any = take(9)
    grad_out, text_grad_out, text_out, total_a, total_b, total_in, vec_out, vec2_out, upb_out = take(9)
    keys, values, mixed_s, own_s, dkv_out, dkv_in, sums_s, gacc_s = take(8)
    w_s, first_s, x_s, xtext_s, gb_s, text_s = take(6)
    fetch_sem, dkv_sem, dkv_in_sem, text_sem, text_in_sem = take(5)
    scratch_a, scratch_b = take(10), take(10)
    scratch_in = [take(11) for _ in range(pairs)]
    scratch_vec = take(6)

    width, rows = q_ref.shape[2], q_ref.shape[1]
    text, model = rows - patch, pairs * width
    place = Place(part_a.shape[0], seq_size)
    seq = lax.axis_index("seq")
    p, i = pl.program_id(0), pl.program_id(1)
    turn, last = p * items + i, pairs * items - 1
    sums_a, sums_b = Reduce(place, part_a, *scratch_a), Reduce(place, part_b, *scratch_b)
    sums_in = [Reduce(place, each[0], *each[1:]) for each in scratch_in]
    sums_vec = ShortReduce(place, *scratch_vec)
    fetches = [
        pltpu.make_async_copy(src, dst, fetch_sem.at[n])
        for n, (src, dst) in enumerate(
            ((w_any, w_s), (first_any, first_s), (x_any, x_s), (xtext_any, xtext_s), (gb_any, gb_s))
        )
    ]

    def text_copies(src, dst, row):
        to = dst.at[:, pl.ds(pl.multiple_of(seq * text, ROW_TILE), text)]
        own = pltpu.make_async_copy(src, to, text_sem.at[row, 0])
        away = [
            remote(src, to, text_sem.at[row, r], text_in_sem.at[row, r], place.mate(r)) for r in range(1, seq_size)
        ]
        return [own] + away

    def dkv_copy(slot, r):
        return remote(
            dkv_out.at[slot, r - 1], dkv_in.at[slot, r - 1], dkv_sem.at[slot, r - 1], dkv_in_sem.at[slot, r - 1],
            place.mate(-r)
        )

    def settle(of):
        slot, pair, item = lax.rem(of, 2), of // items, lax.rem(of, items)
        total = own_s[slot]
        for r in range(1, seq_size):
            dkv_copy(slot, r).wait_recv()
            total = total + dkv_in[slot, r - 1].astype(f32)
        at = pl.ds(pl.multiple_of(item * rows, ROW_TILE), rows)
        mixed_s[lax.rem(pair, 2), at, width:] = total.astype(bf16)

    def pair_done(pair):
        mixed = mixed_s[pair % 2]
        if pair == 0:
            fetches[0].wait()
            fetches[1].wait()
        grad = t_mm(first_s[...].reshape(items * rows, model), mixed).astype(bf16)
        sums_in[pair].part[...] = grad.reshape(sums_in[pair].part.shape)
        sums_in[pair].to_core()
        back = mm_t(mixed, w_s[:, 3 * pair * width : 3 * (pair + 1) * width])
        gacc_s[...] = back if pair == 0 else gacc_s[...] + back
        cols = slice(pair * width, (pair + 1) * width)
        sums_s[QBIAS : QBIAS + 1, cols] = column_sum(mixed[:, :width])
        sums_s[VBIAS : VBIAS + 1, cols] = column_sum(mixed[:, 2 * width :])

    def finish_in(pair):
        total = sums_in[pair].last()
        for n in range(3):
            at = n * model + pair * width
            total_in[:, at : at + width] = total[:, n * width : (n + 1) * width]

    def finish_a():
        total = sums_a.last()
        total_a[...] = total[:, : total_a.shape[1]]
        vec2_out[...] = total[:, total_a.shape[1] :]

    def finish_b():
        total = sums_b.last()
        total_b[...] = total[:, :model]
        upb_out[...] = total[:, model:]

    agenda = [(2, sums_a.to_second), (2, sums_b.to_second), (6, sums_a.to_first), (6, sums_b.to_first),
              (8, sums_a.to_line), (8, sums_b.to_line)]
    for pair in range(pairs):
        done = items * (pair + 1)
        steps = (sums_in[pair].to_second, sums_in[pair].to_first, sums_in[pair].to_line, functools.partial(finish_in, pair))
        agenda += [(done + 1 + n, step) for n, step in enumerate(steps)]
    agenda += [(last + 2, finish_a), (last + 3, finish_b)]
    agenda.sort(key=lambda entry: entry[0])

    @pl.when(turn == 0)
    def _():
        place.greet(corners=True)
        sums_a.to_core()
        sums_b.to_core()
        for copy in fetches:
            copy.start()
        for copy in text_copies(restext_any, text_out, 0):
            copy.start()
        sums_s[...] = jnp.zeros_like(sums_s)

    for at in sorted({at for at, _ in agenda if at <= last}):

        @pl.when(turn == at)
        def _(at=at):
            for when, step in agenda:
                if when == at:
                    step()

    collect(keys, k_refs, patch, text)
    collect(values, v_refs, patch, text)
    q, grad = q_ref[0], grad_ref[0]
    lane = lax.broadcasted_iota(jnp.int32, (1, width), 1) // head
    row = lax.broadcasted_iota(jnp.int32, (width, 1), 0) // head
    inner = grad.astype(f32) * (at_ref[0].astype(f32) + rest_ref[0].astype(f32))
    dq = dk = dv = None
    for h in range(width // head):
        mine = lane == h
        q_head = jnp.where(mine, q, jnp.zeros_like(q))
        grad_head = jnp.where(mine, grad, jnp.zeros_like(grad))
        delta = jnp.sum(jnp.where(mine, inner, 0.0), axis=1, keepdims=True)
        scores = mm_t(q_head, keys[...]) + bias_ref[0]
        probs = jnp.exp2(scores - log_ref[0, :, h * head : h * head + 1])
        grad_probs = mm_t(grad_head, values[...])
        grad_scores = (probs * (grad_probs - delta)).astype(bf16)
        dv_head = t_mm(grad, probs.astype(bf16))
        dk_head = t_mm(q, grad_scores)
        dq_head = mm(grad_scores, keys[...])
        dq = dq_head if dq is None else jnp.where(mine, dq_head, dq)
        dk = dk_head if dk is None else jnp.where(row == h, dk_head, dk)
        dv = dv_head if dv is None else jnp.where(row == h, dv_head, dv)
    dk, dv = jnp.transpose(dk * LN2), jnp.transpose(dv)
    slot = lax.rem(turn, 2)
    at = pl.ds(pl.multiple_of(i * rows, ROW_TILE), rows)
    mixed_s[lax.rem(p, 2), at, :width] = (dq * (1.0 / math.sqrt(head))).astype(bf16)
    own_s[slot, :patch, :width] = dk[:patch]
    own_s[slot, :patch, width:] = dv[:patch]
    first_text = count * patch
    own_s[slot, patch:, :width] = dk[first_text : first_text + text]
    own_s[slot, patch:, width:] = dv[first_text : first_text + text]

    @pl.when(turn > 0)
    def _():
        settle(turn - 1)

    @pl.when(turn > 1)
    def _():
        for r in range(1, seq_size):
            dkv_copy(slot, r).wait_send()

    for r in range(1, seq_size):
        at_text = first_text + r * text
        for n, part in enumerate((dk, dv)):
            cols = slice(n * width, (n + 1) * width)
            dkv_out[slot, r - 1, :patch, cols] = part[r * patch : (r + 1) * patch].astype(bf16)
            dkv_out[slot, r - 1, patch:, cols] = part[at_text : at_text + text].astype(bf16)
        dkv_copy(slot, r).start()

    for pair in range(pairs - 1):

        @pl.when(turn == items * (pair + 1))
        def _(pair=pair):
            pair_done(pair)

    @pl.when(turn == last)
    def _():
        left = [step for when, step in agenda if when > last]
        settle(last)
        pair_done(pairs - 1)
        for copy in fetches[2:]:
            copy.wait()
        gain = vec_ref[GAIN1 : GAIN1 + 1]
        for item in range(items):
            grad_first = gacc_s[item * rows : (item + 1) * rows, :]
            scaled, inverse = norm_rows(jnp.concatenate([x_s[item], xtext_s[item]], axis=0).astype(f32))
            grad_rows = gb_s[item].astype(f32) + norm_back(grad_first, scaled, inverse, gain)
            grad_rows = grad_rows.astype(bf16)
            grad_out[item] = grad_rows[:patch]
            text_s[item] = grad_rows[patch:]
            sums_s[GAIN1 : GAIN1 + 1, :] += column_sum(grad_first * scaled)
            sums_s[SHIFT1 : SHIFT1 + 1, :] += column_sum(grad_first)
            if left:
                left.pop(0)()
        for copy in text_copies(text_s, text_grad_out, 1):
            copy.start()
        sums_vec.part[...] = to_columns(sums_s[...]).reshape(sums_vec.part.shape)
        sums_vec.start()
        if left:
            left.pop(0)()
        sums_vec.to_line()
        for step in left:
            step()
        vec_out[...] = sums_vec.last()
        for copies in (text_copies(restext_any, text_out, 0), text_copies(text_s, text_grad_out, 1)):
            for copy in copies:
                copy.wait()
        for slot in range(2):
            for r in range(1, seq_size):
                dkv_copy(slot, r).wait_send()


def back(q, keys, values, bias, logs, attended, rest, grad_att, part_a, part_b, w_in, vecs, first_in, patches, x_text,
         grad_branch, res_text, head, width, devices, seq_size):
    items, patch, model = patches.shape
    rows, text = q.shape[1], x_text.shape[1]
    count, span, pairs, depth = len(keys), bias.shape[-1], model // width, devices // 8
    block = pl.BlockSpec((1, rows, width), lambda p, i: (i, 0, p))
    parts = [part.reshape((depth, 2, 2, 2, part.shape[0] // devices, part.shape[1])) for part in (part_a, part_b)]
    (rows_a, cols_a), (rows_b, cols_b) = parts[0].shape[4:], parts[1].shape[4:]
    sems = pltpu.SemaphoreType.DMA
    others = seq_size - 1
    slots = jax.ShapeDtypeStruct((items, seq_size * text, model), bf16)
    scratch_in = [pltpu.VMEM((depth, 2, 2, 2, rows_a, 3 * width), bf16)] + reduce_scratch(depth, rows_a, 3 * width)
    return pl.pallas_call(
        functools.partial(back_kernel, count, patch, head, seq_size, pairs, items),
        grid=(pairs, items),
        in_specs=[block] * (1 + 2 * count)
        + [pl.BlockSpec((1, 1, span), lambda p, i: (i, 0, 0))]
        + [block] * 4
        + [ANY] * 3
        + [WHOLE]
        + [ANY] * 5,
        out_specs=[WHOLE] + [ANY] * 2 + [WHOLE] * 6,
        out_shape=[
            jax.ShapeDtypeStruct(patches.shape, bf16),
            slots,
            slots,
            jax.ShapeDtypeStruct((rows_a, cols_a - LANES), f32),
            jax.ShapeDtypeStruct((rows_b, cols_b - LANES), f32),
            jax.ShapeDtypeStruct((rows_a, 3 * model), f32),
            jax.ShapeDtypeStruct((rows_a, LANES), f32),
            jax.ShapeDtypeStruct((rows_a, LANES), f32),
            jax.ShapeDtypeStruct((rows_b, LANES), f32),
        ],
        scratch_shapes=[
            pltpu.VMEM((span, width), bf16),
            pltpu.VMEM((span, width), bf16),
            pltpu.VMEM((2, items * rows, 3 * width), bf16),
            pltpu.VMEM((2, rows, 2 * width), f32),
            pltpu.VMEM((2, others, rows, 2 * width), bf16),
            pltpu.VMEM((2, others, rows, 2 * width), bf16),
            pltpu.VMEM((8, model), f32),
            pltpu.VMEM((items * rows, model), f32),
            pltpu.VMEM(w_in.shape, bf16),
            pltpu.VMEM(first_in.shape, bf16),
            pltpu.VMEM(patches.shape, bf16),
            pltpu.VMEM(x_text.shape, bf16),
            pltpu.VMEM(grad_branch.shape, bf16),
            pltpu.VMEM(x_text.shape, bf16),
            sems((5,)),
            sems((2, others)),
            sems((2, others)),
            sems((2, seq_size)),
            sems((2, seq_size)),
        ]
        + reduce_scratch(depth, rows_a, cols_a)
        + reduce_scratch(depth, rows_b, cols_b)
        + scratch_in * pairs
        + short_reduce_scratch(depth, rows_a, LANES),
        compiler_params=compiler_params(collective_id=2, has_side_effects=True),
        name="back",
    )(q, *keys, *values, bias, logs, attended, rest, grad_att, *parts, w_in, vecs, first_in, patches, x_text,
      grad_branch, res_text)


def per_device(
    seq_size,
    devices,
    patches,
    text_rows,
    lengths,
    first_gain,
    first_shift,
    in_weight,
    query_bias,
    value_bias,
    out_weight,
    branch_bias,
    second_gain,
    second_shift,
    up_weight,
    up_bias,
    down_weight,
    down_bias,
    patch_cotangent,
    text_cotangent,
):
    items, patch, model = patches.shape
    slots = text_rows.shape[1]
    units = up_weight.shape[1]
    head = model // HEADS
    width = min(LANES, model)
    text = round_up(-(-slots // seq_size), ROW_TILE)
    seq = lax.axis_index("seq")
    vectors = [first_gain, first_shift, query_bias, value_bias, branch_bias, second_gain, second_shift, down_bias]
    in_full, vecs, lines, x_text, first_in, q, keys, values = front(
        in_weight, vectors, up_weight, up_bias, out_weight, down_weight, patches, text_rows, text, width, devices,
        seq_size
    )

    spans = []
    for r in range(seq_size):
        slot = lax.rem(seq + r, seq_size) * text + jnp.arange(text)
        spans.append(slot[None, :] < lengths[:, None])
    valid = jnp.concatenate([jnp.ones((items, patch * seq_size), jnp.bool_)] + spans, axis=1)
    span = round_up(valid.shape[1], LANES)
    valid = jnp.pad(valid, ((0, 0), (0, span - valid.shape[1])))
    bias = jnp.where(valid, 0.0, NEG_FILL).astype(f32)[:, None, :]

    attended, rest, logs, (weights, w_down) = attend(
        q, keys, values, bias, lines, patch, head, width, devices, seq_size
    )
    out_patches, res_text, grad_branch, grad_att, part_a, part_b = ffn(
        seq[None], patches, x_text, attended, patch_cotangent, text_cotangent, weights, w_down, vecs
    )
    grad_patches, grad_text, out_text, sums, down_grad, in_grad, vec1, vec2, up_bias_grad = back(
        q, keys, values, bias, logs, attended, rest, grad_att, part_a, part_b, in_full, vecs, first_in, patches, x_text,
        grad_branch, res_text, head, width, devices, seq_size
    )
    return (
        out_patches,
        out_text[:, :slots],
        grad_patches,
        grad_text[:, :slots],
        vec1[:, GAIN1],
        vec1[:, SHIFT1],
        in_grad,
        vec1[:, QBIAS],
        vec1[:, VBIAS],
        sums[:, units:],
        vec2[:, BRANCH],
        vec2[:, GAIN2],
        vec2[:, SHIFT2],
        sums[:, :units],
        up_bias_grad[:, 0],
        down_grad,
        vec2[:, DOWNB],
    )


def solution(mesh):
    both = ("dp", "seq")
    rows, slots, vector, matrix = P("dp", "seq", None), P("dp", None, None), P(both), P(both, None)
    weights = (vector, vector, matrix, vector, vector, matrix, vector, vector, vector, matrix, vector, matrix, vector)
    return jax.shard_map(
        functools.partial(per_device, mesh.shape["seq"], mesh.size),
        mesh=mesh,
        in_specs=(rows, slots, P("dp")) + weights + (rows, slots),
        out_specs=(rows, slots, rows, slots) + weights,
        check_vma=False,
    )
```

```python
import functools
import math

import jax
import jax.numpy as jnp
from jax import lax
from jax.experimental import pallas as pl
from jax.experimental.pallas import tpu as pltpu
from jax.sharding import PartitionSpec as P

HEADS = 8
EPSILON = 1e-05
NEG_FILL = -1e30
LOG2E = math.log2(math.e)
LN2 = math.log(2.0)
ROW_TILE = 16
LANES = 128
MESH = pl.DeviceIdType.MESH
f32, bf16 = jnp.float32, jnp.bfloat16

GAIN1, SHIFT1, QBIAS, VBIAS, BRANCH, GAIN2, SHIFT2, DOWNB = range(8)


def round_up(value, unit):
    return -(-value // unit) * unit


def mm(a, b):
    return lax.dot_general(a, b, (((1,), (0,)), ((), ())), preferred_element_type=f32)


def mm_t(a, b):
    return lax.dot_general(a, b, (((1,), (1,)), ((), ())), preferred_element_type=f32)


def t_mm(a, b):
    return lax.dot_general(a, b, (((0,), (0,)), ((), ())), preferred_element_type=f32)


def compiler_params(**more):
    return pltpu.CompilerParams(vmem_limit_bytes=60 * 2**20, **more)


WHOLE = pl.BlockSpec(memory_space=pltpu.VMEM)
ANY = pl.BlockSpec(memory_space=pl.ANY)


class Place:
    def __init__(self, depth, seq_size):
        self.depth, self.seq_size = depth, seq_size
        index = lax.axis_index("dp") * seq_size + lax.axis_index("seq")
        self.core = lax.rem(index, 2)
        self.x = lax.rem(index // 2, 2)
        self.y = lax.rem(index // 4, 2)
        self.z = index // 8
        core = self.core
        flip_x, flip_y = 1 - self.x, 1 - self.y
        x_first = self.x * core + flip_x * (1 - core)
        y_first = self.y * (1 - core) + flip_y * core
        x_second = self.x * (1 - core) + flip_x * core
        y_second = self.y * core + flip_y * (1 - core)
        self.columns = (
            (self.y, self.x),
            (y_first, x_first),
            (y_second, x_second),
            (flip_y, flip_x),
        )

    def device(self, z, y, x, core):
        index = ((z * 2 + y) * 2 + x) * 2 + core
        return (index // self.seq_size, lax.rem(index, self.seq_size))

    def layer(self, k):
        return lax.rem(self.z + self.depth - k, self.depth)

    def ahead(self, k):
        return lax.rem(self.z + k, self.depth)

    def first(self):
        return self.device(self.z, *self.columns[1], self.core)

    def second(self):
        return self.device(self.z, *self.columns[2], self.core)

    def other_core(self):
        return self.device(self.z, self.y, self.x, 1 - self.core)

    def above(self, k):
        return self.device(self.ahead(k), self.y, self.x, self.core)

    def mate(self, step):
        return (lax.axis_index("dp"), lax.rem(lax.axis_index("seq") + self.seq_size - step, self.seq_size))

    def octant(self, n):
        column, core = n % 4, n // 4
        y, x = self.columns[column]
        core = self.core * (1 - core) + (1 - self.core) * core
        return self.device(self.z, y, x, core), (y, x, core)

    def greet(self, corners=False):
        barrier = pltpu.get_barrier_semaphore()
        friends = [self.above(k) for k in range(1, self.depth)]
        friends += [self.octant(n)[0] for n in range(1, 8)] if corners else [self.first(), self.second(), self.other_core()]
        friends += [self.mate(step) for step in range(1, self.seq_size)]
        for friend in friends:
            pl.semaphore_signal(barrier, inc=1, device_id=friend, device_id_type=MESH)
        pl.semaphore_wait(barrier, len(friends))


def remote(src, dst, send, recv, device):
    return pltpu.make_async_remote_copy(
        src_ref=src, dst_ref=dst, send_sem=send, recv_sem=recv, device_id=device, device_id_type=MESH
    )


class Spread:
    def __init__(self, place, shard, full, out, into, local):
        self.place, self.shard, self.full, self.out, self.into, self.local = place, shard, full, out, into, local

    def column(self, n, core=None):
        y, x = self.place.columns[n]
        return self.full.at[:, y, x, self.place.core if core is None else core]

    def line_copy(self, k):
        place = self.place
        here = self.full.at[place.z, place.y, place.x, place.core]
        return remote(self.shard, here, self.out.at[6 + k], self.into.at[6 + k], place.above(k))

    def own_copy(self):
        place = self.place
        return pltpu.make_async_copy(self.shard, self.full.at[place.z, place.y, place.x, place.core], self.local)

    def copy(self, n, lane):
        here = self.column(n)
        device = (self.place.first, self.place.second, self.place.second)[lane] if lane < 3 else self.place.other_core
        return remote(here, here, self.out.at[lane], self.into.at[lane], device())

    def arrive(self, n, lane):
        self.copy(n, lane).wait_recv()

    def start(self):
        self.own_copy().start()
        for k in range(1, self.place.depth):
            self.line_copy(k).start()

    def send_line(self):
        self.own_copy().wait()
        for k in range(1, self.place.depth):
            self.line_copy(k).wait_recv()
        for lane in (0, 1, 3):
            self.copy(0, lane).start()

    def forward_first(self):
        self.arrive(1, 0)
        self.copy(1, 2).start()
        self.copy(1, 4).start()

    def forward_second(self, half):
        self.arrive(2 + half, 1 + half)
        self.copy(2 + half, 5 + half).start()

    def finish(self):
        for n in range(4):
            self.arrive(n, 3 + n)
        for k in range(1, self.place.depth):
            self.line_copy(k).wait_send()
        for lane in range(7):
            self.copy(0, lane).wait_send()


def spread_sems(depth):
    sems = pltpu.SemaphoreType.DMA
    return [sems((6 + depth,)), sems((6 + depth,)), sems]


class Line:
    def __init__(self, place, shard, line, result, out, into, local):
        self.place, self.shard, self.line, self.result = place, shard, line, result
        self.out, self.into, self.local = out, into, local

    def line_copy(self, k):
        return remote(self.shard, self.line.at[self.place.z], self.out.at[k], self.into.at[k], self.place.above(k))

    def own_copy(self):
        return pltpu.make_async_copy(self.shard, self.line.at[self.place.z], self.local.at[0])

    def result_copy(self):
        return pltpu.make_async_copy(self.line, self.result, self.local.at[1])

    def start(self):
        self.own_copy().start()
        for k in range(1, self.place.depth):
            self.line_copy(k).start()

    def finish(self):
        self.own_copy().wait()
        for k in range(1, self.place.depth):
            self.line_copy(k).wait()
        self.result_copy().start()


def line_sems(depth):
    sems = pltpu.SemaphoreType.DMA
    return [sems((depth,)), sems((depth,)), sems((2,))]


class Early:
    def __init__(self, place, shard, quads, result, out, into, local):
        self.place, self.shard, self.quads, self.result = place, shard, quads, result
        self.out, self.into, self.local = out, into, local

    def line_copy(self, k):
        here = self.quads.at[0, self.place.z]
        return remote(self.shard, here, self.out.at[1 + k], self.into.at[1 + k], self.place.above(k))

    def own_copy(self):
        return pltpu.make_async_copy(self.shard, self.quads.at[0, self.place.z], self.local.at[3])

    def way_copy(self, way):
        device = (self.place.first, self.place.second)[way]()
        return remote(self.quads.at[0], self.quads.at[1 + way], self.out.at[way], self.into.at[way], device)

    def result_copy(self, n):
        return pltpu.make_async_copy(self.quads.at[n], self.result.at[n], self.local.at[n])

    def start(self):
        self.own_copy().start()
        for k in range(1, self.place.depth):
            self.line_copy(k).start()

    def send(self):
        self.own_copy().wait()
        for k in range(1, self.place.depth):
            self.line_copy(k).wait_recv()
        for way in range(2):
            self.way_copy(way).start()
        self.result_copy(0).start()

    def finish(self):
        for way in range(2):
            self.way_copy(way).wait_recv()
            self.result_copy(1 + way).start()
        for k in range(1, self.place.depth):
            self.line_copy(k).wait_send()
        for way in range(2):
            self.way_copy(way).wait_send()
        for n in range(3):
            self.result_copy(n).wait()


def early_sems(depth):
    sems = pltpu.SemaphoreType.DMA
    return [sems((1 + depth,)), sems((1 + depth,)), sems((4,))]


class Late:
    def __init__(self, place, quads, full, result, out, into, local):
        self.place, self.quads, self.full, self.result = place, quads, full, result
        self.out, self.into, self.local = out, into, local

    def column(self, n):
        y, x = self.place.columns[n]
        return self.full.at[:, y, x, self.place.core]

    def own_copy(self, n):
        return pltpu.make_async_copy(self.quads.at[n], self.column(n), self.local.at[n])

    def way_copy(self):
        here = self.column(1)
        return remote(here, here, self.out.at[4], self.into.at[4], self.place.second())

    def core_copy(self, n):
        here = self.column(n)
        return remote(here, here, self.out.at[n], self.into.at[n], self.place.other_core())

    def result_copy(self):
        return pltpu.make_async_copy(self.full, self.result, self.local.at[3])

    def start(self):
        for n in range(3):
            self.own_copy(n).start()

    def send(self):
        for n in (1, 0, 2):
            self.own_copy(n).wait()
            if n == 1:
                self.way_copy().start()
            self.core_copy(n).start()

    def forward(self):
        self.way_copy().wait_recv()
        self.core_copy(3).start()

    def finish(self):
        for n in range(4):
            self.core_copy(n).wait()
        self.way_copy().wait_send()
        self.result_copy().start()


def late_sems():
    sems = pltpu.SemaphoreType.DMA
    return [sems((5,)), sems((5,)), sems((4,))]


class LateLine(Spread):
    def __init__(self, place, line, full, result, out, into, local):
        super().__init__(place, line, full, out, into, local)
        self.result = result

    def own_copy(self):
        return pltpu.make_async_copy(self.shard, self.column(0), self.local.at[0])

    def result_copy(self):
        return pltpu.make_async_copy(self.full, self.result, self.local.at[1])

    def start(self):
        self.own_copy().start()

    def send(self):
        self.own_copy().wait()
        for lane in (0, 1, 3):
            self.copy(0, lane).start()

    def finish(self):
        for n in range(4):
            self.arrive(n, 3 + n)
        for lane in range(7):
            self.copy(0, lane).wait_send()
        self.result_copy().start()


def late_line_sems():
    sems = pltpu.SemaphoreType.DMA
    return [sems((7,)), sems((7,)), sems((2,))]


class Reduce:
    def __init__(self, place, part, from_core, held, from_second, pair, from_first, line, from_line, out, into, local):
        self.place, self.part, self.local = place, part, local
        self.from_core, self.held, self.from_second, self.pair = from_core, held, from_second, pair
        self.from_first, self.line, self.from_line = from_first, line, from_line
        self.out, self.into = out, into

    def copy(self, src, dst, lane, device):
        return remote(src, dst, self.out.at[lane], self.into.at[lane], device)

    def own_copy(self):
        return pltpu.make_async_copy(self.part.at[:, :, :, self.place.core], self.held, self.local)

    def core_copy(self):
        return self.copy(self.part.at[:, :, :, 1 - self.place.core], self.from_core, 0, self.place.other_core())

    def second_copies(self):
        columns = self.place.columns
        return [
            self.copy(self.held.at[:, columns[2 + k][0], columns[2 + k][1]], self.from_second.at[k], 1 + k,
                      self.place.second())
            for k in range(2)
        ]

    def first_copy(self):
        return self.copy(self.pair.at[1], self.from_first, 3, self.place.first())

    def line_copies(self):
        place = self.place
        return [
            self.copy(self.line.at[place.ahead(k)], self.from_line.at[k - 1], 3 + k, place.above(k))
            for k in range(1, place.depth)
        ]

    def to_core(self):
        self.core_copy().start()
        self.own_copy().start()

    def to_second(self):
        self.own_copy().wait()
        self.core_copy().wait()
        self.held[...] += self.from_core[...]
        for copy in self.second_copies():
            copy.start()

    def to_first(self):
        for copy in self.second_copies():
            copy.wait()
        for k in range(2):
            y, x = self.place.columns[k]
            self.pair[k] = self.held[:, y, x] + self.from_second[k]
        self.first_copy().start()

    def to_line(self):
        self.first_copy().wait()
        self.line[...] = self.pair[0] + self.from_first[...]
        for copy in self.line_copies():
            copy.start()

    def last(self):
        for copy in self.line_copies():
            copy.wait()
        result = self.line[self.place.z].astype(f32)
        for k in range(self.place.depth - 1):
            result = result + self.from_line[k].astype(f32)
        return result


def reduce_scratch(depth, rows, cols):
    shapes = [(depth, 2, 2), (depth, 2, 2), (2, depth), (2, depth), (depth,), (depth,), (depth - 1,)]
    sems = pltpu.SemaphoreType.DMA
    return [pltpu.VMEM(shape + (rows, cols), bf16) for shape in shapes] + [sems((3 + depth,))] * 2 + [sems]


class ShortReduce:
    def __init__(self, place, part, from_octant, line, from_line, out, into):
        self.place, self.part, self.from_octant, self.line, self.from_line = place, part, from_octant, line, from_line
        self.out, self.into = out, into

    def octant_copy(self, n):
        device, (y, x, core) = self.place.octant(n)
        return remote(
            self.part.at[:, y, x, core], self.from_octant.at[n - 1], self.out.at[n - 1], self.into.at[n - 1], device
        )

    def line_copy(self, k):
        return remote(
            self.line.at[self.place.ahead(k)], self.from_line.at[k - 1], self.out.at[6 + k], self.into.at[6 + k],
            self.place.above(k)
        )

    def start(self):
        for n in range(1, 8):
            self.octant_copy(n).start()

    def to_line(self):
        place = self.place
        total = self.part[:, place.y, place.x, place.core].astype(f32)
        for n in range(1, 8):
            self.octant_copy(n).wait()
            total = total + self.from_octant[n - 1].astype(f32)
        self.line[...] = total.astype(bf16)
        for k in range(1, place.depth):
            self.line_copy(k).start()

    def last(self):
        total = self.line[self.place.z].astype(f32)
        for k in range(1, self.place.depth):
            self.line_copy(k).wait()
            total = total + self.from_line[k - 1].astype(f32)
        return total


def short_reduce_scratch(depth, rows, cols):
    sems = pltpu.SemaphoreType.DMA
    shapes = [(depth, 2, 2, 2), (7, depth), (depth,), (depth - 1,)]
    return [pltpu.VMEM(shape + (rows, cols), bf16) for shape in shapes] + [sems((6 + depth,))] * 2


def norm_rows(rows):
    centred = rows - jnp.mean(rows, axis=1, keepdims=True)
    inverse = lax.rsqrt(jnp.mean(centred * centred, axis=1, keepdims=True) + EPSILON)
    return centred * inverse, inverse


def norm_back(grad, scaled, inverse, gain):
    inner = grad * gain
    return inverse * (
        inner
        - jnp.mean(inner, axis=1, keepdims=True)
        - scaled * jnp.mean(inner * scaled, axis=1, keepdims=True)
    )


def gelu_both(v):
    power = jnp.exp2(v * v * (-0.5 * LOG2E))
    cdf = 0.5 + 0.5 * lax.erf(v * math.sqrt(0.5))
    return v * cdf, cdf + v * power * (1.0 / math.sqrt(2.0 * math.pi))


def column_sum(rows):
    return jnp.sum(rows.astype(f32), axis=0, keepdims=True)


def to_columns(rows):
    count, width = rows.shape
    return jnp.transpose(jnp.concatenate([rows, jnp.zeros((LANES - count, width), f32)], axis=0)).astype(bf16)


def own_text(ref, text, seq):
    slots, width = ref.shape
    own = jnp.zeros((text, width), ref.dtype)
    for r in range(-(-slots // text)):
        share = ref[r * text : min(slots, (r + 1) * text), :]
        if share.shape[0] < text:
            share = jnp.concatenate([share, jnp.zeros((text - share.shape[0], width), ref.dtype)], axis=0)
        own = jnp.where(seq == r, share, own)
    return own


def as_columns(vectors):
    length = vectors[0].shape[0]
    rows = [vector.reshape(1, length).astype(f32) for vector in vectors]
    rows = jnp.concatenate(rows + [jnp.zeros((LANES - len(rows), length), f32)], axis=0)
    rows = jnp.concatenate([rows, jnp.zeros((LANES, LANES - length), f32)], axis=1)
    return jnp.transpose(rows)[:length].astype(bf16)


def front_kernel(seq_size, text, width, *refs):
    refs = list(refs)

    def take(number):
        taken = refs[:number]
        del refs[:number]
        return taken

    (shard_ref,), vec_refs = take(1), take(8)
    up_ref, up_bias_ref, out_w_ref, down_ref, x_any, slot_ref, length_ref = take(7)
    w_out, w2_out, vecs, bias_ref, quads_a, line_b, xtext_ref, first_out, q_out = take(9)
    k_outs, v_outs = take(seq_size), take(seq_size)
    shard, shard2, shard_a, shard_b, w_full, w2_full, own_a, own_b, x_s, n_s, first_s, q_s, k_s, v_s = take(14)
    sems, sems2, sems_a, sems_b = take(3), take(3), take(3), take(3)
    x_sem, w_sem, out_sem, kv_sem, kv_in_sem, kv_out_sem = take(6)
    items, patch, model = x_s.shape
    units, wide = up_ref.shape[1], shard2.shape[1]
    pairs = model // width
    place = Place(w_full.shape[0], seq_size)
    seq = lax.axis_index("seq")
    x_copies = [pltpu.make_async_copy(x_any.at[i], x_s.at[i], x_sem.at[i]) for i in range(items)]
    for copy in x_copies:
        copy.start()
    for p in range(pairs):
        half, to = divmod(3 * p * width, wide)
        for n in range(3):
            at = n * model + p * width
            (shard, shard2)[half][:, to + n * width : to + (n + 1) * width] = shard_ref[:, at : at + width]
    shard[:, wide:] = as_columns([ref[...] for ref in vec_refs])
    place.greet()
    halves = [Spread(place, shard, w_full, *sems), Spread(place, shard2, w2_full, *sems2)]
    for move in halves:
        move.start()
    shard_a[:, :units] = up_ref[...]
    shard_a[:, units:] = out_w_ref[...]
    shard_b[:, :model] = down_ref[...]
    shard_b[:, model:] = as_columns([up_bias_ref[...]])
    early, line = Early(place, shard_a, own_a, quads_a, *sems_a), Line(place, shard_b, own_b, line_b, *sems_b)
    tail = bias_ref.shape[2]
    col = lax.broadcasted_iota(jnp.int32, (1, tail), 1)
    slot = jnp.full((1, tail), seq_size * text, jnp.int32)
    for r in range(seq_size):
        begin = lax.rem(seq + r, seq_size) * text
        slot = jnp.where((col >= r * text) & (col < (r + 1) * text), begin + col - r * text, slot)
    for i in range(items):
        xtext_ref[i] = own_text(slot_ref.at[i], text, seq)
        bias_ref[i] = jnp.where(slot < length_ref[i], 0.0, NEG_FILL)
    halves[0].send_line()
    halves[1].send_line()
    early.start()
    line.start()
    for i in range(items):
        x_copies[i].wait()
        n_s[i], _ = norm_rows(jnp.concatenate([x_s[i], xtext_ref[i]], axis=0).astype(f32))
    halves[0].forward_first()
    halves[0].forward_second(0)
    halves[1].forward_first()
    halves[0].forward_second(1)
    halves[1].forward_second(0)
    halves[0].finish()
    w_copies = [pltpu.make_async_copy(src, dst, w_sem.at[n]) for n, (src, dst) in
                enumerate(((w_full, w_out), (w2_full, w2_out)))]
    w_copies[0].start()
    weight = w_full[...].reshape(model, wide + LANES)
    table = jnp.transpose(weight[:, wide:].astype(f32))
    vecs[...] = table
    scale = LOG2E / math.sqrt(model // HEADS)
    sends, outs = [], []

    def project(i, half, weight):
        for p in range(half * pairs // 2, (half + 1) * pairs // 2):
            cols = slice(p * width, (p + 1) * width)
            at = 3 * p * width - half * wide
            projected = mm(first_s[i], weight[:, at : at + 3 * width])
            q_s[i, :, cols] = ((projected[:, :width] + table[QBIAS : QBIAS + 1, cols]) * scale).astype(bf16)
            k_s[0, i, :, cols] = projected[:, width : 2 * width].astype(bf16)
            v_s[0, i, :, cols] = (projected[:, 2 * width :] + table[VBIAS : VBIAS + 1, cols]).astype(bf16)
        cols = pl.ds(half * (model // 2), model // 2)
        for r in range(1, seq_size):
            for n, ref in enumerate((k_s, v_s)):
                at = ((2 * i + n) * 2 + half) * seq_size + r
                src, dst = ref.at[0, i, :, cols], ref.at[r, i, :, cols]
                sends.append(remote(src, dst, kv_sem.at[at], kv_in_sem.at[at], place.mate(r)))
                sends[-1].start()

    def bring(n, src, dst, i):
        outs.append(pltpu.make_async_copy(src.at[i], dst.at[i], out_sem.at[n, i]))
        outs[-1].start()

    for i in range(items):
        first_s[i] = (n_s[i] * table[GAIN1 : GAIN1 + 1] + table[SHIFT1 : SHIFT1 + 1]).astype(bf16)
        bring(0, first_s, first_out, i)
        project(i, 0, weight)
        if i == 0:
            halves[1].forward_second(1)
    early.send()
    halves[1].finish()
    w_copies[1].start()
    weight = w2_full[...].reshape(model, wide)
    for i in range(items):
        project(i, 1, weight)
        for n, (src, dst) in enumerate(((q_s, q_out), (k_s.at[0], k_outs[0]), (v_s.at[0], v_outs[0]))):
            bring(1 + n, src, dst, i)
    line.finish()
    for copy in sends:
        copy.wait()
    for i in range(items):
        for r in range(1, seq_size):
            for n, (ref, dst) in enumerate(((k_s, k_outs), (v_s, v_outs))):
                at = (2 * i + n) * seq_size + r
                outs.append(pltpu.make_async_copy(ref.at[r, i], dst[r].at[i], kv_out_sem.at[at]))
                outs[-1].start()
    early.finish()
    line.result_copy().wait()
    for copy in w_copies + outs:
        copy.wait()


def front(in_weight, vectors, up_weight, up_bias, out_weight, down_weight, patches, text_rows, lengths, text, width,
          devices, seq_size):
    items, patch, model = patches.shape
    depth = devices // 8
    rows, cols = in_weight.shape
    shape_a = (rows, up_weight.shape[1] + model)
    shape_b = (down_weight.shape[0], model + LANES)
    shape_w = (depth, 2, 2, 2, rows, cols // 2 + LANES)
    shape_w2 = (depth, 2, 2, 2, rows, cols // 2)
    shape_x = (items, patch + text, model)
    tail = round_up(seq_size * text, LANES)
    tokens = jax.ShapeDtypeStruct(shape_x, bf16)
    sems = pltpu.SemaphoreType.DMA
    outs = pl.pallas_call(
        functools.partial(front_kernel, seq_size, text, width),
        in_specs=[WHOLE] * 13 + [ANY, WHOLE, pl.BlockSpec(memory_space=pltpu.SMEM)],
        out_specs=[ANY, ANY, WHOLE, WHOLE, ANY, ANY, WHOLE] + [ANY] * (2 + 2 * seq_size),
        out_shape=[
            jax.ShapeDtypeStruct(shape_w, bf16),
            jax.ShapeDtypeStruct(shape_w2, bf16),
            jax.ShapeDtypeStruct((LANES, model), f32),
            jax.ShapeDtypeStruct((items, 1, tail), f32),
            jax.ShapeDtypeStruct((3, depth) + shape_a, bf16),
            jax.ShapeDtypeStruct((depth,) + shape_b, bf16),
            jax.ShapeDtypeStruct((items, text, model), bf16),
            tokens,
            tokens,
        ]
        + [tokens] * (2 * seq_size),
        scratch_shapes=[
            pltpu.VMEM((rows, cols // 2 + LANES), bf16),
            pltpu.VMEM((rows, cols // 2), bf16),
            pltpu.VMEM(shape_a, bf16),
            pltpu.VMEM(shape_b, bf16),
            pltpu.VMEM(shape_w, bf16),
            pltpu.VMEM(shape_w2, bf16),
            pltpu.VMEM((3, depth) + shape_a, bf16),
            pltpu.VMEM((depth,) + shape_b, bf16),
            pltpu.VMEM(patches.shape, bf16),
            pltpu.VMEM(shape_x, f32),
            pltpu.VMEM(shape_x, bf16),
            pltpu.VMEM(shape_x, bf16),
            pltpu.VMEM((seq_size,) + shape_x, bf16),
            pltpu.VMEM((seq_size,) + shape_x, bf16),
        ]
        + spread_sems(depth) * 2
        + early_sems(depth)
        + line_sems(depth)
        + [sems((items,)), sems((2,)), sems((4, items))]
        + [sems((4 * items * seq_size,))] * 2
        + [sems((2 * items * seq_size,))],
        compiler_params=compiler_params(collective_id=0, has_side_effects=True),
        name="front",
    )(in_weight, *vectors, up_weight, up_bias, out_weight, down_weight, patches, text_rows, lengths)
    weights = [full.reshape(model, full.shape[-1]) for full in outs[:2]]
    return weights, *outs[2:4], outs[4:6], *outs[6:9], outs[9 : 9 + seq_size], outs[9 + seq_size :]


def collect(dst, refs, patch, text):
    count, width = len(refs), refs[0].shape[2]
    for r, ref in enumerate(refs):
        dst[r * patch : (r + 1) * patch, :width] = ref[0, :patch, :]
        at = count * patch + r * text
        dst[at : at + text, :width] = ref[0, patch:, :]
    filled = count * (patch + text)
    if dst.shape[0] > filled:
        dst[filled:, :width] = jnp.zeros((dst.shape[0] - filled, width), dst.dtype)


def by_head(dst, src, lane, heads, ones):
    count, width = src.shape
    for h in range(heads):
        rows = slice(h * count, (h + 1) * count)
        dst[rows, :width] = jnp.where(lane == h, src, jnp.zeros_like(src))
        if ones:
            dst[rows, width:] = jnp.where(lane == h, jnp.ones_like(src), jnp.zeros_like(src))


def attend_kernel(count, patch, head, seq_size, *refs):
    q_ref, k_refs, v_refs = refs[0], refs[1 : 1 + count], refs[1 + count : 1 + 2 * count]
    bias_ref, quads_a, line_b, out_ref, rest_ref, log_ref, full_a, full_b = refs[1 + 2 * count : 9 + 2 * count]
    keys, values, text_keys, text_values, into_a, into_b, *sems = refs[9 + 2 * count :]
    width = q_ref.shape[2]
    text, edge = q_ref.shape[1] - patch, count * patch
    heads, span = width // head, keys.shape[0] - edge
    place = Place(full_a.shape[0], seq_size)
    turn = pl.program_id(0) * pl.num_programs(1) + pl.program_id(1)
    last = pl.num_programs(0) * pl.num_programs(1) - 1
    move_a, move_b = Late(place, quads_a, into_a, full_a, *sems[:3]), LateLine(place, line_b, into_b, full_b, *sems[3:])

    @pl.when(turn == 0)
    def _():
        move_a.start()
        move_b.start()
        place.greet()
        move_a.send()
        move_b.send()

    agenda = (
        (4, move_a.forward),
        (4, move_b.forward_first),
        (6, functools.partial(move_b.forward_second, 0)),
        (7, functools.partial(move_b.forward_second, 1)),
        (9, move_a.finish),
        (9, move_b.finish),
    )
    for at in sorted({at for at, _ in agenda}):

        @pl.when(turn == at)
        def _(at=at):
            for when, step in agenda:
                if when == at:
                    step()

    collect(keys, k_refs, patch, text)
    collect(values, v_refs, patch, text)
    values[:, width:] = jnp.ones((values.shape[0], values.shape[1] - width), bf16)
    lane = lax.broadcasted_iota(jnp.int32, (1, width), 1) // head
    by_head(text_keys, keys[edge:], lane, heads, False)
    by_head(text_values, values[edge:, :width], lane, heads, True)
    q = q_ref[0]
    text_bias = jnp.concatenate([bias_ref[0]] * heads, axis=1)

    def scores_of(h):
        return mm_t(jnp.where(lane == h, q, jnp.zeros_like(q)), keys[:edge])

    text_scores = mm_t(q, text_keys[...]) + text_bias
    scores = scores_of(0)
    text_powers, mixed, total, tops = [], None, None, None
    for h in range(heads):
        following = scores_of(h + 1) if h + 1 < heads else None
        text_head = text_scores[:, h * span : (h + 1) * span]
        top = jnp.maximum(jnp.max(scores, axis=1, keepdims=True), jnp.max(text_head, axis=1, keepdims=True))
        powers = jnp.exp2(scores - top).astype(bf16)
        text_powers.append(jnp.exp2(text_head - top).astype(bf16))
        both = mm(powers, values[:edge])
        mixed = both[:, :width] if mixed is None else jnp.where(lane == h, both[:, :width], mixed)
        total = both[:, width:] if total is None else jnp.where(lane == h, both[:, width:], total)
        tops = jnp.broadcast_to(top, mixed.shape) if tops is None else jnp.where(lane == h, top, tops)
        scores = following
    both = mm(jnp.concatenate(text_powers, axis=1), text_values[...])
    total = total + both[:, width:]
    out = (mixed + both[:, :width]) * (1.0 / total)
    high = out.astype(bf16)
    out_ref[0] = high
    rest_ref[0] = (out - high.astype(f32)).astype(bf16)
    log_ref[0] = tops + jnp.log2(total)

    @pl.when(turn == last)
    def _():
        move_a.result_copy().wait()
        move_b.result_copy().wait()


def attend(q, keys, values, bias, halfway, patch, head, width, devices, seq_size):
    items, _, model = q.shape
    count, tail = len(keys), bias.shape[-1]
    depth, heads, span = devices // 8, width // head, count * patch + tail
    block = pl.BlockSpec((1, q.shape[1], width), lambda i, p: (i, 0, p))
    outs = pl.pallas_call(
        functools.partial(attend_kernel, count, patch, head, seq_size),
        grid=(items, model // width),
        in_specs=[block] * (1 + 2 * count) + [pl.BlockSpec((1, 1, tail), lambda i, p: (i, 0, 0))] + [ANY] * 2,
        out_specs=[block, block, block, ANY, ANY],
        out_shape=[jax.ShapeDtypeStruct(q.shape, bf16)] * 2
        + [jax.ShapeDtypeStruct(q.shape, f32)]
        + [jax.ShapeDtypeStruct((depth, 2, 2, 2) + part.shape[-2:], part.dtype) for part in halfway],
        scratch_shapes=[
            pltpu.VMEM((span, width), bf16),
            pltpu.VMEM((span, 2 * width), bf16),
            pltpu.VMEM((heads * tail, width), bf16),
            pltpu.VMEM((heads * tail, 2 * width), bf16),
        ]
        + [pltpu.VMEM((depth, 2, 2, 2) + part.shape[-2:], part.dtype) for part in halfway]
        + late_sems()
        + late_line_sems(),
        compiler_params=compiler_params(collective_id=1, has_side_effects=True),
        name="attend",
    )(q, *keys, *values, bias, *halfway)
    return outs[0], outs[1], outs[2], [full.reshape(-1, full.shape[-1]) for full in outs[3:]]


def ffn_kernel(steps, chunk, seq_ref, x_ref, xtext_ref, at_ref, dy_ref, dy_slot_ref, w_any, wd_any, vec_ref,
               res_ref, restext_ref, gb_ref, ga_ref, part_out, down_out,
               w_ref, wd_ref, part_ref, down_ref, second_s, hidden_s, pre_s, dy_s, sums_s, bias_s, out_s, dots_s,
               w_sem, wd_sem, part_sem, down_sem):
    step = pl.program_id(0)
    patch, model = x_ref.shape[1:]
    text = xtext_ref.shape[1]
    block, units = patch + text, wd_ref.shape[0]
    chunks = units // chunk
    rows = pl.ds(pl.multiple_of(step * block, ROW_TILE), block)
    gain = vec_ref[GAIN2 : GAIN2 + 1]
    w_out = w_ref.at[:, units:]

    def fetch(cols, at):
        if cols is None:
            return (
                pltpu.make_async_copy(w_any.at[:, units:], w_ref.at[:, units:], w_sem.at[at]),
                pltpu.make_async_copy(wd_any.at[:, model:], wd_ref.at[:, model:], wd_sem.at[at]),
            )
        return (
            pltpu.make_async_copy(w_any.at[:, cols], w_ref.at[:, cols], w_sem.at[at]),
            pltpu.make_async_copy(wd_any.at[cols, :model], wd_ref.at[cols, :model], wd_sem.at[at]),
        )

    @pl.when(step == 0)
    def _():
        others = fetch(None, chunks)
        for copy in others:
            copy.start()
        for c in range(chunks):
            for copy in fetch(pl.ds(c * chunk, chunk), c):
                copy.start()
        sums_s[...] = jnp.zeros_like(sums_s)
        for copy in others:
            copy.wait()
        bias_s[...] = jnp.transpose(wd_ref[:, model:].astype(f32))[:8]

    x = jnp.concatenate([x_ref[0], xtext_ref[0]], axis=0).astype(f32)
    dy = jnp.concatenate([dy_ref[0], own_text(dy_slot_ref.at[0], text, seq_ref[0])], axis=0)
    dy_s[rows, :] = dy
    middle = x + (mm(at_ref[0], w_out[...]) + vec_ref[BRANCH : BRANCH + 1])
    scaled, inverse = norm_rows(middle)
    second_in = (scaled * gain + vec_ref[SHIFT2 : SHIFT2 + 1]).astype(bf16)
    second_s[rows, :] = second_in
    dots_s[0] = middle + vec_ref[DOWNB : DOWNB + 1]
    dots_s[1] = jnp.zeros_like(middle)

    def part(c, _):
        cols = pl.ds(pl.multiple_of(c * chunk, chunk), chunk)

        @pl.when(step == 0)
        def _():
            for copy in fetch(cols, c):
                copy.wait()

        value, slope = gelu_both(mm(second_in, w_ref[:, cols]) + bias_s[:1, cols])
        hidden = value.astype(bf16)
        hidden_s[rows, cols] = hidden
        grad_pre = (mm_t(dy, wd_ref[cols, :model]) * slope).astype(bf16)
        pre_s[rows, cols] = grad_pre
        dots_s[0] += mm(hidden, wd_ref[cols, :model])
        dots_s[1] += mm_t(grad_pre, w_ref[:, cols])
        return 0

    lax.fori_loop(0, units // chunk, part, 0)
    result, grad_second = dots_s[0], dots_s[1]
    result = result.astype(bf16)
    res_ref[0] = result[:patch]
    restext_ref[0] = result[patch:]
    grad_branch = (dy.astype(f32) + norm_back(grad_second, scaled, inverse, gain)).astype(bf16)
    gb_ref[0] = grad_branch
    ga_ref[0] = mm_t(grad_branch, w_out[...]).astype(bf16)
    out_grad = t_mm(at_ref[0], grad_branch)

    @pl.when(step == 0)
    def _():
        out_s[...] = out_grad

    @pl.when(step > 0)
    def _():
        out_s[...] += out_grad

    for at, grad in ((BRANCH, grad_branch), (GAIN2, grad_second * scaled), (SHIFT2, grad_second), (DOWNB, dy)):
        sums_s[at : at + 1, :] += column_sum(grad)

    @pl.when(step == steps - 1)
    def _():
        groups = units // model
        copies = []
        part_ref[:, units : units + model] = out_s[...].astype(bf16)
        part_ref[:, units + model :] = to_columns(sums_s[...])
        copies.append(pltpu.make_async_copy(part_ref.at[:, units:], part_out.at[:, units:], part_sem.at[groups]))
        copies[-1].start()
        for c in range(groups):
            cols = slice(c * model, (c + 1) * model)
            at = pl.ds(c * model, model)
            grad_pre = pre_s[:, cols]
            part_ref[:, cols] = t_mm(second_s[...], grad_pre).astype(bf16)
            copies.append(pltpu.make_async_copy(part_ref.at[:, at], part_out.at[:, at], part_sem.at[c]))
            copies[-1].start()
            down_ref[cols, :model] = jnp.transpose(t_mm(dy_s[...], hidden_s[:, cols])).astype(bf16)
            down_ref[cols, model:] = to_columns(column_sum(grad_pre))
            copies.append(pltpu.make_async_copy(down_ref.at[at], down_out.at[at], down_sem.at[c]))
            copies[-1].start()
        for copy in copies:
            copy.wait()


def ffn(seq, patches, x_text, attended, patch_cotangent, text_cotangent, weights, w_down, vecs):
    items, patch, model = patches.shape
    units, rows, text, slots = w_down.shape[0], attended.shape[1], x_text.shape[1], text_cotangent.shape[1]

    def item(count):
        return pl.BlockSpec((1, count, model), lambda i: (i, 0, 0))

    def shape(count):
        return jax.ShapeDtypeStruct((items, count, model), bf16)

    return pl.pallas_call(
        functools.partial(ffn_kernel, items, 1024),
        grid=(items,),
        in_specs=[pl.BlockSpec(memory_space=pltpu.SMEM)]
        + [item(patch), item(text), item(rows), item(patch), item(slots)]
        + [ANY, ANY, WHOLE],
        out_specs=[item(patch), item(text), item(rows), item(rows), ANY, ANY],
        out_shape=[shape(patch), shape(text), shape(rows), shape(rows)]
        + [
            jax.ShapeDtypeStruct((model, units + model + LANES), bf16),
            jax.ShapeDtypeStruct((units, model + LANES), bf16),
        ],
        scratch_shapes=[
            pltpu.VMEM(weights.shape, bf16),
            pltpu.VMEM(w_down.shape, bf16),
            pltpu.VMEM((model, units + model + LANES), bf16),
            pltpu.VMEM((units, model + LANES), bf16),
            pltpu.VMEM((items * rows, model), bf16),
            pltpu.VMEM((items * rows, units), bf16),
            pltpu.VMEM((items * rows, units), bf16),
            pltpu.VMEM((items * rows, model), bf16),
            pltpu.VMEM((8, model), f32),
            pltpu.VMEM((8, units), f32),
            pltpu.VMEM((model, model), f32),
            pltpu.VMEM((2, rows, model), f32),
        ]
        + [pltpu.SemaphoreType.DMA((units // 1024 + 1,))] * 2
        + [pltpu.SemaphoreType.DMA((units // model + 1,))] * 2,
        compiler_params=compiler_params(),
        name="ffn",
    )(seq, patches, x_text, attended, patch_cotangent, text_cotangent, weights, w_down, vecs)


def back_kernel(count, patch, head, seq_size, pairs, items, *refs):
    refs = list(refs)

    def take(number):
        taken = refs[:number]
        del refs[:number]
        return taken

    (q_ref,), k_refs, v_refs = take(1), take(count), take(count)
    bias_ref, log_ref, at_ref, rest_ref, grad_ref = take(5)
    part_a, part_b, w_any, w2_any, vec_ref, first_any, x_any, xtext_any, gb_any, restext_any = take(10)
    grad_out, text_grad_out, text_out, total_a, total_b, total_in, vec_out, vec2_out, upb_out = take(9)
    keys, values, text_keys, text_values, probs_s, scores_s = take(6)
    mixed_s, own_s, dkv_out, dkv_in, sums_s = take(5)
    w_s, w2_s, first_s, x_s, xtext_s, gb_s, text_s, patch_s = take(8)
    fetch_sem, dkv_sem, dkv_in_sem, text_sem, text_in_sem, patch_sem = take(6)
    scratch_a, scratch_b = take(10), take(10)
    scratch_in = [take(11) for _ in range(pairs)]
    scratch_vec = take(6)

    width, rows = q_ref.shape[2], q_ref.shape[1]
    text, model = rows - patch, pairs * width
    place = Place(part_a.shape[0], seq_size)
    seq = lax.axis_index("seq")
    p, i = pl.program_id(0), pl.program_id(1)
    turn, last = p * items + i, pairs * items - 1
    sums_a, sums_b = Reduce(place, part_a, *scratch_a), Reduce(place, part_b, *scratch_b)
    sums_in = [Reduce(place, each[0], *each[1:]) for each in scratch_in]
    sums_vec = ShortReduce(place, *scratch_vec)
    fetches = [
        pltpu.make_async_copy(src, dst, fetch_sem.at[n])
        for n, (src, dst) in enumerate(
            ((first_any, first_s), (w_any, w_s), (w2_any, w2_s), (x_any, x_s), (xtext_any, xtext_s), (gb_any, gb_s))
        )
    ]

    def text_copies(src, dst, row):
        to = dst.at[:, pl.ds(pl.multiple_of(seq * text, ROW_TILE), text)]
        own = pltpu.make_async_copy(src, to, text_sem.at[row, 0])
        away = [
            remote(src, to, text_sem.at[row, r], text_in_sem.at[row, r], place.mate(r)) for r in range(1, seq_size)
        ]
        return [own] + away

    def dkv_copy(slot, r):
        return remote(
            dkv_out.at[slot, r - 1], dkv_in.at[slot, r - 1], dkv_sem.at[slot, r - 1], dkv_in_sem.at[slot, r - 1],
            place.mate(-r)
        )

    def settle(of):
        slot, pair, item = lax.rem(of, 2), of // items, lax.rem(of, items)
        total = own_s[slot]
        for r in range(1, seq_size):
            dkv_copy(slot, r).wait_recv()
            total = total + dkv_in[slot, r - 1].astype(f32)
        at = pl.ds(pl.multiple_of(item * rows, ROW_TILE), rows)
        mixed_s[pair, at, width:] = total.astype(bf16)

    def pair_done(pair):
        mixed = mixed_s[pair]
        if pair == 0:
            fetches[0].wait()
        grad = t_mm(first_s[...].reshape(items * rows, model), mixed).astype(bf16)
        sums_in[pair].part[...] = grad.reshape(sums_in[pair].part.shape)
        sums_in[pair].to_core()
        cols = slice(pair * width, (pair + 1) * width)
        sums_s[QBIAS : QBIAS + 1, cols] = column_sum(mixed[:, :width])
        sums_s[VBIAS : VBIAS + 1, cols] = column_sum(mixed[:, 2 * width :])

    def finish_in(pair):
        total = sums_in[pair].last()
        for n in range(3):
            at = n * model + pair * width
            total_in[:, at : at + width] = total[:, n * width : (n + 1) * width]

    def finish_a():
        total = sums_a.last()
        total_a[...] = total[:, : total_a.shape[1]]
        vec2_out[...] = total[:, total_a.shape[1] :]

    def finish_b():
        total = sums_b.last()
        total_b[...] = total[:, :model]
        upb_out[...] = total[:, model:]

    agenda = [(1, sums_a.to_second), (2, sums_b.to_second), (4, sums_a.to_first), (6, sums_b.to_first),
              (6, sums_a.to_line), (8, sums_b.to_line), (8, finish_a), (11, finish_b)]
    for pair in range(pairs):
        done = items * (pair + 1)
        steps = (sums_in[pair].to_second, sums_in[pair].to_first, sums_in[pair].to_line, functools.partial(finish_in, pair))
        agenda += [(done + 1 + n, step) for n, step in enumerate(steps)]
    agenda.sort(key=lambda entry: entry[0])

    @pl.when(turn == 0)
    def _():
        place.greet(corners=True)
        sums_a.to_core()
        sums_b.to_core()
        for copy in fetches:
            copy.start()
        for copy in text_copies(restext_any, text_out, 0):
            copy.start()
        sums_s[...] = jnp.zeros_like(sums_s)

    for at in sorted({at for at, _ in agenda if at <= last}):

        @pl.when(turn == at)
        def _(at=at):
            for when, step in agenda:
                if when == at:
                    step()

    collect(keys, k_refs, patch, text)
    collect(values, v_refs, patch, text)
    q, grad = q_ref[0], grad_ref[0]
    edge, heads, span = count * patch, width // head, keys.shape[0] - count * patch
    lane = lax.broadcasted_iota(jnp.int32, (1, width), 1) // head
    row = lax.broadcasted_iota(jnp.int32, (width, 1), 0) // head
    by_head(text_keys, keys[edge:], lane, heads, False)
    by_head(text_values, values[edge:], lane, heads, False)
    text_bias = jnp.concatenate([bias_ref[0]] * heads, axis=1)
    inner = grad.astype(f32) * (at_ref[0].astype(f32) + rest_ref[0].astype(f32))
    q_heads = [jnp.where(lane == h, q, jnp.zeros_like(q)) for h in range(heads)]
    grad_heads = [jnp.where(lane == h, grad, jnp.zeros_like(grad)) for h in range(heads)]
    deltas = [jnp.sum(jnp.where(lane == h, inner, 0.0), axis=1, keepdims=True) for h in range(heads)]
    logs = [log_ref[0, :, h * head : h * head + 1] for h in range(heads)]

    def first_dots(h):
        return mm_t(q_heads[h], keys[:edge]), mm_t(grad_heads[h], values[:edge])

    scores, grad_probs = first_dots(0)
    text_scores = mm_t(q, text_keys[...]) + text_bias
    text_grad_probs = mm_t(grad, text_values[...])
    dq, text_probs, text_grads = None, [], []
    for h in range(heads):
        following = first_dots(h + 1) if h + 1 < heads else (None, None)
        cols = slice(h * span, (h + 1) * span)
        text_head = jnp.exp2(text_scores[:, cols] - logs[h])
        text_probs.append(text_head.astype(bf16))
        text_grads.append((text_head * (text_grad_probs[:, cols] - deltas[h])).astype(bf16))
        probs = jnp.exp2(scores - logs[h])
        grad_scores = (probs * (grad_probs - deltas[h])).astype(bf16)
        probs_s[h * rows : (h + 1) * rows, :] = probs.astype(bf16)
        scores_s[h * rows : (h + 1) * rows, :] = grad_scores
        dq_head = mm(grad_scores, keys[:edge])
        dq = dq_head if dq is None else jnp.where(lane == h, dq_head, dq)
        scores, grad_probs = following
    text_probs, text_grads = jnp.concatenate(text_probs, axis=1), jnp.concatenate(text_grads, axis=1)
    dq = dq + mm(text_grads, text_keys[...])
    dv = jnp.transpose(t_mm(jnp.concatenate(grad_heads, axis=0), probs_s[...]))
    dk = jnp.transpose(t_mm(jnp.concatenate(q_heads, axis=0), scores_s[...])) * LN2

    def of_heads(wide):
        own = wide[:, :span]
        for h in range(1, heads):
            own = jnp.where(row == h, wide[:, h * span : (h + 1) * span], own)
        return jnp.transpose(own)

    text_dv, text_dk = of_heads(t_mm(grad, text_probs)), of_heads(t_mm(q, text_grads)) * LN2
    slot = lax.rem(turn, 2)
    at = pl.ds(pl.multiple_of(i * rows, ROW_TILE), rows)
    mixed_s[p, at, :width] = (dq * (1.0 / math.sqrt(head))).astype(bf16)
    own_s[slot, :patch, :width] = dk[:patch]
    own_s[slot, :patch, width:] = dv[:patch]
    own_s[slot, patch:, :width] = text_dk[:text]
    own_s[slot, patch:, width:] = text_dv[:text]

    @pl.when(turn > 0)
    def _():
        settle(turn - 1)

    @pl.when(turn > 1)
    def _():
        for r in range(1, seq_size):
            dkv_copy(slot, r).wait_send()

    for r in range(1, seq_size):
        for n, (part, text_part) in enumerate(((dk, text_dk), (dv, text_dv))):
            cols = slice(n * width, (n + 1) * width)
            dkv_out[slot, r - 1, :patch, cols] = part[r * patch : (r + 1) * patch].astype(bf16)
            dkv_out[slot, r - 1, patch:, cols] = text_part[r * text : (r + 1) * text].astype(bf16)
        dkv_copy(slot, r).start()

    for pair in range(pairs - 1):

        @pl.when(turn == items * (pair + 1))
        def _(pair=pair):
            pair_done(pair)

    @pl.when(turn == last)
    def _():
        left = [step for when, step in agenda if when > last]
        settle(last)
        pair_done(pairs - 1)
        for copy in fetches[1:]:
            copy.wait()
        patch_copies = [
            pltpu.make_async_copy(patch_s.at[item], grad_out.at[item], patch_sem.at[item]) for item in range(items)
        ]
        gain = vec_ref[GAIN1 : GAIN1 + 1]
        for item in range(items):
            half, at = pairs // 2, slice(item * rows, (item + 1) * rows)
            grad_first = sum(
                mm_t(jnp.concatenate([mixed_s[n * half + m, at, :] for m in range(half)], axis=1), ref[...])
                for n, ref in enumerate((w_s.at[:, : 3 * half * width], w2_s))
            )
            scaled, inverse = norm_rows(jnp.concatenate([x_s[item], xtext_s[item]], axis=0).astype(f32))
            grad_rows = gb_s[item].astype(f32) + norm_back(grad_first, scaled, inverse, gain)
            grad_rows = grad_rows.astype(bf16)
            patch_s[item] = grad_rows[:patch]
            patch_copies[item].start()
            text_s[item] = grad_rows[patch:]
            sums_s[GAIN1 : GAIN1 + 1, :] += column_sum(grad_first * scaled)
            sums_s[SHIFT1 : SHIFT1 + 1, :] += column_sum(grad_first)
            if left:
                left.pop(0)()
        for copy in text_copies(text_s, text_grad_out, 1):
            copy.start()
        sums_vec.part[...] = to_columns(sums_s[...]).reshape(sums_vec.part.shape)
        sums_vec.start()
        if left:
            left.pop(0)()
        sums_vec.to_line()
        for step in left:
            step()
        vec_out[...] = sums_vec.last()
        for copies in (text_copies(restext_any, text_out, 0), text_copies(text_s, text_grad_out, 1)):
            for copy in copies:
                copy.wait()
        for slot in range(2):
            for r in range(1, seq_size):
                dkv_copy(slot, r).wait_send()
        for copy in patch_copies:
            copy.wait()


def back(q, keys, values, bias, logs, attended, rest, grad_att, part_a, part_b, w_in, vecs, first_in, patches, x_text,
         grad_branch, res_text, head, width, devices, seq_size):
    items, patch, model = patches.shape
    rows, text = q.shape[1], x_text.shape[1]
    count, tail, pairs, depth = len(keys), bias.shape[-1], model // width, devices // 8
    span = count * patch + tail
    block = pl.BlockSpec((1, rows, width), lambda p, i: (i, 0, p))
    parts = [part.reshape((depth, 2, 2, 2, part.shape[0] // devices, part.shape[1])) for part in (part_a, part_b)]
    (rows_a, cols_a), (rows_b, cols_b) = parts[0].shape[4:], parts[1].shape[4:]
    sems = pltpu.SemaphoreType.DMA
    others = seq_size - 1
    slots = jax.ShapeDtypeStruct((items, seq_size * text, model), bf16)
    scratch_in = [pltpu.VMEM((depth, 2, 2, 2, rows_a, 3 * width), bf16)] + reduce_scratch(depth, rows_a, 3 * width)
    return pl.pallas_call(
        functools.partial(back_kernel, count, patch, head, seq_size, pairs, items),
        grid=(pairs, items),
        in_specs=[block] * (1 + 2 * count)
        + [pl.BlockSpec((1, 1, tail), lambda p, i: (i, 0, 0))]
        + [block] * 4
        + [ANY] * 4
        + [WHOLE]
        + [ANY] * 5,
        out_specs=[ANY] * 3 + [WHOLE] * 6,
        out_shape=[
            jax.ShapeDtypeStruct(patches.shape, bf16),
            slots,
            slots,
            jax.ShapeDtypeStruct((rows_a, cols_a - LANES), f32),
            jax.ShapeDtypeStruct((rows_b, cols_b - LANES), f32),
            jax.ShapeDtypeStruct((rows_a, 3 * model), f32),
            jax.ShapeDtypeStruct((rows_a, LANES), f32),
            jax.ShapeDtypeStruct((rows_a, LANES), f32),
            jax.ShapeDtypeStruct((rows_b, LANES), f32),
        ],
        scratch_shapes=[
            pltpu.VMEM((span, width), bf16),
            pltpu.VMEM((span, width), bf16),
            pltpu.VMEM((width // head * tail, width), bf16),
            pltpu.VMEM((width // head * tail, width), bf16),
            pltpu.VMEM((width // head * rows, count * patch), bf16),
            pltpu.VMEM((width // head * rows, count * patch), bf16),
            pltpu.VMEM((pairs, items * rows, 3 * width), bf16),
            pltpu.VMEM((2, rows, 2 * width), f32),
            pltpu.VMEM((2, others, rows, 2 * width), bf16),
            pltpu.VMEM((2, others, rows, 2 * width), bf16),
            pltpu.VMEM((8, model), f32),
            pltpu.VMEM(w_in[0].shape, bf16),
            pltpu.VMEM(w_in[1].shape, bf16),
            pltpu.VMEM(first_in.shape, bf16),
            pltpu.VMEM(patches.shape, bf16),
            pltpu.VMEM(x_text.shape, bf16),
            pltpu.VMEM(grad_branch.shape, bf16),
            pltpu.VMEM(x_text.shape, bf16),
            pltpu.VMEM(patches.shape, bf16),
            sems((6,)),
            sems((2, others)),
            sems((2, others)),
            sems((2, seq_size)),
            sems((2, seq_size)),
            sems((items,)),
        ]
        + reduce_scratch(depth, rows_a, cols_a)
        + reduce_scratch(depth, rows_b, cols_b)
        + scratch_in * pairs
        + short_reduce_scratch(depth, rows_a, LANES),
        compiler_params=compiler_params(collective_id=2, has_side_effects=True),
        name="back",
    )(q, *keys, *values, bias, logs, attended, rest, grad_att, *parts, *w_in, vecs, first_in, patches, x_text,
      grad_branch, res_text)


def outputs_kernel(*refs):
    text_ref, patch_grad, text_grad, total_a, total_b, total_in, vec1, vec2, upb = refs[:9]
    outs = list(refs[9:])
    out_text, grad_patches, grad_text = outs[:3]
    first_gain, first_shift, in_weight, query_bias, value_bias, out_weight, branch_bias = outs[3:10]
    second_gain, second_shift, up_weight, up_bias, down_weight, down_bias = outs[10:]
    slots, units = out_text.shape[1], up_weight.shape[1]
    out_text[...] = text_ref[:, :slots]
    grad_text[...] = text_grad[:, :slots]
    grad_patches[...] = patch_grad[...]

    def row_of(ref, at):
        count = ref.shape[0]
        tall = jnp.concatenate([ref[...], jnp.zeros((LANES - count, LANES), f32)], axis=0)
        return jnp.transpose(tall)[at, :count]

    @pl.when(pl.program_id(0) == 0)
    def _():
        in_weight[...] = total_in[...]
        out_weight[...] = total_a[:, units:]
        up_weight[...] = total_a[:, :units]
        down_weight[...] = total_b[...]
        for ref, at in ((first_gain, GAIN1), (first_shift, SHIFT1), (query_bias, QBIAS), (value_bias, VBIAS)):
            ref[...] = row_of(vec1, at)
        for ref, at in ((branch_bias, BRANCH), (second_gain, GAIN2), (second_shift, SHIFT2), (down_bias, DOWNB)):
            ref[...] = row_of(vec2, at)
        up_bias[...] = row_of(upb, 0)


def outputs(text, patch_grad, text_grad, total_a, total_b, total_in, vec1, vec2, upb, slots, units):
    items, patch, model = patch_grad.shape
    padded = text.shape[1]

    def item(count):
        return pl.BlockSpec((1, count, model), lambda i: (i, 0, 0))

    def shape(*dims):
        return jax.ShapeDtypeStruct(dims, f32)

    count = total_in.shape[0]
    vector, texts = shape(count), jax.ShapeDtypeStruct((items, slots, model), bf16)
    return pl.pallas_call(
        outputs_kernel,
        grid=(items,),
        in_specs=[item(padded), item(patch), item(padded)] + [WHOLE] * 6,
        out_specs=[item(slots), item(patch), item(slots)] + [WHOLE] * 13,
        out_shape=[texts, jax.ShapeDtypeStruct(patch_grad.shape, bf16), texts]
        + [vector, vector, shape(count, 3 * model), vector, vector, shape(count, model), vector, vector, vector]
        + [shape(count, units), shape(upb.shape[0]), shape(*total_b.shape), vector],
        compiler_params=compiler_params(),
        name="outputs",
    )(text, patch_grad, text_grad, total_a, total_b, total_in, vec1, vec2, upb)


def per_device(
    seq_size,
    devices,
    patches,
    text_rows,
    lengths,
    first_gain,
    first_shift,
    in_weight,
    query_bias,
    value_bias,
    out_weight,
    branch_bias,
    second_gain,
    second_shift,
    up_weight,
    up_bias,
    down_weight,
    down_bias,
    patch_cotangent,
    text_cotangent,
):
    items, patch, model = patches.shape
    slots = text_rows.shape[1]
    units = up_weight.shape[1]
    head = model // HEADS
    width = min(LANES, model)
    text = round_up(-(-slots // seq_size), ROW_TILE)
    seq = lax.axis_index("seq")
    vectors = [first_gain, first_shift, query_bias, value_bias, branch_bias, second_gain, second_shift, down_bias]
    w_in, vecs, bias, halfway, x_text, first_in, q, keys, values = front(
        in_weight, vectors, up_weight, up_bias, out_weight, down_weight, patches, text_rows, lengths, text, width,
        devices, seq_size
    )
    attended, rest, logs, (weights, w_down) = attend(
        q, keys, values, bias, halfway, patch, head, width, devices, seq_size
    )
    out_patches, res_text, grad_branch, grad_att, part_a, part_b = ffn(
        seq[None], patches, x_text, attended, patch_cotangent, text_cotangent, weights, w_down, vecs
    )
    grad_patches, grad_text, out_text, sums, down_grad, in_grad, vec1, vec2, up_bias_grad = back(
        q, keys, values, bias, logs, attended, rest, grad_att, part_a, part_b, w_in, vecs, first_in, patches, x_text,
        grad_branch, res_text, head, width, devices, seq_size
    )
    rest = outputs(
        out_text, grad_patches, grad_text, sums, down_grad, in_grad, vec1, vec2, up_bias_grad, slots, units
    )
    return (out_patches, *rest)


def solution(mesh):
    both = ("dp", "seq")
    rows, slots, vector, matrix = P("dp", "seq", None), P("dp", None, None), P(both), P(both, None)
    weights = (vector, vector, matrix, vector, vector, matrix, vector, vector, vector, matrix, vector, matrix, vector)
    return jax.shard_map(
        functools.partial(per_device, mesh.shape["seq"], mesh.size),
        mesh=mesh,
        in_specs=(rows, slots, P("dp")) + weights + (rows, slots),
        out_specs=(rows, slots, rows, slots) + weights,
        check_vma=False,
    )
```

```python
import functools
import math

import jax
import jax.numpy as jnp
from jax import lax
from jax.experimental import pallas as pl
from jax.experimental.pallas import tpu as pltpu
from jax.sharding import PartitionSpec as P

HEADS = 8
EPSILON = 1e-05
NEG_FILL = -1e30
LOG2E = math.log2(math.e)
LN2 = math.log(2.0)
ROW_TILE = 16
LANES = 128
MESH = pl.DeviceIdType.MESH
f32, bf16 = jnp.float32, jnp.bfloat16

GAIN1, SHIFT1, QBIAS, VBIAS, BRANCH, GAIN2, SHIFT2, DOWNB = range(8)


def round_up(value, unit):
    return -(-value // unit) * unit


def mm(a, b):
    return lax.dot_general(a, b, (((1,), (0,)), ((), ())), preferred_element_type=f32)


def mm_t(a, b):
    return lax.dot_general(a, b, (((1,), (1,)), ((), ())), preferred_element_type=f32)


def t_mm(a, b):
    return lax.dot_general(a, b, (((0,), (0,)), ((), ())), preferred_element_type=f32)


def compiler_params(**more):
    return pltpu.CompilerParams(vmem_limit_bytes=60 * 2**20, **more)


WHOLE = pl.BlockSpec(memory_space=pltpu.VMEM)
ANY = pl.BlockSpec(memory_space=pl.ANY)


class Place:
    def __init__(self, depth, seq_size):
        self.depth, self.seq_size = depth, seq_size
        index = lax.axis_index("dp") * seq_size + lax.axis_index("seq")
        self.core = lax.rem(index, 2)
        self.x = lax.rem(index // 2, 2)
        self.y = lax.rem(index // 4, 2)
        self.z = index // 8
        core = self.core
        flip_x, flip_y = 1 - self.x, 1 - self.y
        x_first = self.x * core + flip_x * (1 - core)
        y_first = self.y * (1 - core) + flip_y * core
        x_second = self.x * (1 - core) + flip_x * core
        y_second = self.y * core + flip_y * (1 - core)
        self.columns = (
            (self.y, self.x),
            (y_first, x_first),
            (y_second, x_second),
            (flip_y, flip_x),
        )

    def device(self, z, y, x, core):
        index = ((z * 2 + y) * 2 + x) * 2 + core
        return (index // self.seq_size, lax.rem(index, self.seq_size))

    def layer(self, k):
        return lax.rem(self.z + self.depth - k, self.depth)

    def ahead(self, k):
        return lax.rem(self.z + k, self.depth)

    def first(self):
        return self.device(self.z, *self.columns[1], self.core)

    def second(self):
        return self.device(self.z, *self.columns[2], self.core)

    def other_core(self):
        return self.device(self.z, self.y, self.x, 1 - self.core)

    def above(self, k):
        return self.device(self.ahead(k), self.y, self.x, self.core)

    def mate(self, step):
        return (lax.axis_index("dp"), lax.rem(lax.axis_index("seq") + self.seq_size - step, self.seq_size))

    def octant(self, n):
        column, core = n % 4, n // 4
        y, x = self.columns[column]
        core = self.core * (1 - core) + (1 - self.core) * core
        return self.device(self.z, y, x, core), (y, x, core)

    def friends(self, corners):
        friends = [self.above(k) for k in range(1, self.depth)]
        friends += [self.octant(n)[0] for n in range(1, 8)] if corners else [self.first(), self.second(), self.other_core()]
        return friends + [self.mate(step) for step in range(1, self.seq_size)]

    def greet(self, corners=False):
        barrier = pltpu.get_barrier_semaphore()
        for friend in self.friends(corners):
            pl.semaphore_signal(barrier, inc=1, device_id=friend, device_id_type=MESH)

    def meet(self, corners=False):
        pl.semaphore_wait(pltpu.get_barrier_semaphore(), len(self.friends(corners)))


def remote(src, dst, send, recv, device):
    return pltpu.make_async_remote_copy(
        src_ref=src, dst_ref=dst, send_sem=send, recv_sem=recv, device_id=device, device_id_type=MESH
    )


class Spread:
    def __init__(self, place, shard, full, out, into, local):
        self.place, self.shard, self.full, self.out, self.into, self.local = place, shard, full, out, into, local

    def column(self, n, core=None):
        y, x = self.place.columns[n]
        return self.full.at[:, y, x, self.place.core if core is None else core]

    def line_copy(self, k):
        place = self.place
        here = self.full.at[place.z, place.y, place.x, place.core]
        return remote(self.shard, here, self.out.at[6 + k], self.into.at[6 + k], place.above(k))

    def own_copy(self):
        place = self.place
        return pltpu.make_async_copy(self.shard, self.full.at[place.z, place.y, place.x, place.core], self.local)

    def copy(self, n, lane):
        here = self.column(n)
        device = (self.place.first, self.place.second, self.place.second)[lane] if lane < 3 else self.place.other_core
        return remote(here, here, self.out.at[lane], self.into.at[lane], device())

    def arrive(self, n, lane):
        self.copy(n, lane).wait_recv()

    def start(self):
        self.own_copy().start()
        for k in range(1, self.place.depth):
            self.line_copy(k).start()

    def send_line(self):
        self.own_copy().wait()
        for k in range(1, self.place.depth):
            self.line_copy(k).wait_recv()
        for lane in (0, 1, 3):
            self.copy(0, lane).start()

    def forward_first(self):
        self.arrive(1, 0)
        self.copy(1, 2).start()
        self.copy(1, 4).start()

    def forward_second(self, half):
        self.arrive(2 + half, 1 + half)
        self.copy(2 + half, 5 + half).start()

    def finish(self):
        for n in range(4):
            self.arrive(n, 3 + n)
        for k in range(1, self.place.depth):
            self.line_copy(k).wait_send()
        for lane in range(7):
            self.copy(0, lane).wait_send()


def spread_sems(depth):
    sems = pltpu.SemaphoreType.DMA
    return [sems((6 + depth,)), sems((6 + depth,)), sems]


class Line:
    def __init__(self, place, shard, line, result, out, into, local):
        self.place, self.shard, self.line, self.result = place, shard, line, result
        self.out, self.into, self.local = out, into, local

    def line_copy(self, k):
        return remote(self.shard, self.line.at[self.place.z], self.out.at[k], self.into.at[k], self.place.above(k))

    def own_copy(self):
        return pltpu.make_async_copy(self.shard, self.line.at[self.place.z], self.local.at[0])

    def result_copy(self):
        return pltpu.make_async_copy(self.line, self.result, self.local.at[1])

    def start(self):
        self.own_copy().start()
        for k in range(1, self.place.depth):
            self.line_copy(k).start()

    def finish(self):
        self.own_copy().wait()
        for k in range(1, self.place.depth):
            self.line_copy(k).wait()
        self.result_copy().start()


def line_sems(depth):
    sems = pltpu.SemaphoreType.DMA
    return [sems((depth,)), sems((depth,)), sems((2,))]


class Early:
    def __init__(self, place, shard, quads, result, out, into, local):
        self.place, self.shard, self.quads, self.result = place, shard, quads, result
        self.out, self.into, self.local = out, into, local

    def line_copy(self, k):
        here = self.quads.at[0, self.place.z]
        return remote(self.shard, here, self.out.at[k], self.into.at[k], self.place.above(k))

    def own_copy(self):
        return pltpu.make_async_copy(self.shard, self.quads.at[0, self.place.z], self.local.at[2])

    def way_copy(self):
        return remote(self.quads.at[0], self.quads.at[1], self.out.at[0], self.into.at[0], self.place.first())

    def result_copy(self, n):
        return pltpu.make_async_copy(self.quads.at[n], self.result.at[n], self.local.at[n])

    def start(self):
        self.own_copy().start()
        for k in range(1, self.place.depth):
            self.line_copy(k).start()

    def send(self):
        self.own_copy().wait()
        for k in range(1, self.place.depth):
            self.line_copy(k).wait_recv()
        self.way_copy().start()
        self.result_copy(0).start()

    def finish(self):
        self.way_copy().wait_recv()
        self.result_copy(1).start()
        for k in range(1, self.place.depth):
            self.line_copy(k).wait_send()
        self.way_copy().wait_send()
        for n in range(2):
            self.result_copy(n).wait()


def early_sems(depth):
    sems = pltpu.SemaphoreType.DMA
    return [sems((depth,)), sems((depth,)), sems((3,))]


class Results:
    def result_copy(self, n, other):
        y, x = self.place.columns[(0, 2, 1, 3)[n] if other else n]
        core = 1 - self.place.core if other else self.place.core
        here = (slice(None), y, x, core)
        return pltpu.make_async_copy(self.full.at[here], self.result.at[here], self.results.at[n, other])

    def land(self, n):
        self.arrive_core(n)
        for other in range(2):
            self.result_copy(n, other).start()

    def finish(self):
        for n in range(4):
            for other in range(2):
                self.result_copy(n, other).wait()
        self.sent()


class Late(Results):
    def __init__(self, place, quads, full, result, out, into, local, results):
        self.place, self.quads, self.full, self.result = place, quads, full, result
        self.out, self.into, self.local, self.results = out, into, local, results

    def column(self, n):
        y, x = self.place.columns[n]
        return self.full.at[:, y, x, self.place.core]

    def own_copy(self, n):
        return pltpu.make_async_copy(self.quads.at[n], self.column(n), self.local.at[n])

    def way_copy(self, n):
        here = self.column(n)
        return remote(here, here, self.out.at[4 + n], self.into.at[4 + n], self.place.second())

    def core_copy(self, n):
        here = self.column(n)
        return remote(here, here, self.out.at[n], self.into.at[n], self.place.other_core())

    def arrive_core(self, n):
        self.core_copy(n).wait_recv()

    def start(self):
        for n in range(2):
            self.own_copy(n).start()

    def send(self):
        for n in range(2):
            self.own_copy(n).wait()
            self.way_copy(n).start()
            self.core_copy(n).start()

    def forward(self, n):
        self.way_copy(n).wait_recv()
        self.core_copy(2 + n).start()

    def sent(self):
        for n in range(4):
            self.core_copy(n).wait_send()
        for n in range(2):
            self.way_copy(n).wait_send()


def late_sems():
    sems = pltpu.SemaphoreType.DMA
    return [sems((6,)), sems((6,)), sems((2,)), sems((4, 2))]


class LateLine(Results, Spread):
    def __init__(self, place, line, full, result, out, into, local, results):
        Spread.__init__(self, place, line, full, out, into, local)
        self.result, self.results = result, results

    def own_copy(self):
        return pltpu.make_async_copy(self.shard, self.column(0), self.local)

    def arrive_core(self, n):
        self.arrive(n, 3 + n)

    def start(self):
        self.own_copy().start()

    def send(self):
        self.own_copy().wait()
        for lane in (0, 1, 3):
            self.copy(0, lane).start()

    def sent(self):
        for lane in range(7):
            self.copy(0, lane).wait_send()


def late_line_sems():
    sems = pltpu.SemaphoreType.DMA
    return [sems((7,)), sems((7,)), sems, sems((4, 2))]


class Reduce:
    def __init__(self, place, part, from_core, held, from_second, pair, from_first, line, from_line, out, into, local):
        self.place, self.part, self.local = place, part, local
        self.from_core, self.held, self.from_second, self.pair = from_core, held, from_second, pair
        self.from_first, self.line, self.from_line = from_first, line, from_line
        self.out, self.into = out, into

    def copy(self, src, dst, lane, device):
        return remote(src, dst, self.out.at[lane], self.into.at[lane], device)

    def own_copy(self):
        return pltpu.make_async_copy(self.part.at[:, :, :, self.place.core], self.held, self.local)

    def core_copy(self):
        return self.copy(self.part.at[:, :, :, 1 - self.place.core], self.from_core, 0, self.place.other_core())

    def second_copies(self):
        columns = self.place.columns
        return [
            self.copy(self.held.at[:, columns[2 + k][0], columns[2 + k][1]], self.from_second.at[k], 1 + k,
                      self.place.second())
            for k in range(2)
        ]

    def first_copy(self):
        return self.copy(self.pair.at[1], self.from_first, 3, self.place.first())

    def line_copies(self):
        place = self.place
        return [
            self.copy(self.line.at[place.ahead(k)], self.from_line.at[k - 1], 3 + k, place.above(k))
            for k in range(1, place.depth)
        ]

    def to_core(self):
        self.core_copy().start()
        self.own_copy().start()

    def to_second(self):
        self.own_copy().wait()
        self.core_copy().wait()
        self.held[...] += self.from_core[...]
        for copy in self.second_copies():
            copy.start()

    def to_first(self):
        for copy in self.second_copies():
            copy.wait()
        for k in range(2):
            y, x = self.place.columns[k]
            self.pair[k] = self.held[:, y, x] + self.from_second[k]
        self.first_copy().start()

    def to_line(self):
        self.first_copy().wait()
        self.line[...] = self.pair[0] + self.from_first[...]
        for copy in self.line_copies():
            copy.start()

    def last(self):
        for copy in self.line_copies():
            copy.wait()
        result = self.line[self.place.z].astype(f32)
        for k in range(self.place.depth - 1):
            result = result + self.from_line[k].astype(f32)
        return result


def reduce_scratch(depth, rows, cols):
    shapes = [(depth, 2, 2), (depth, 2, 2), (2, depth), (2, depth), (depth,), (depth,), (depth - 1,)]
    sems = pltpu.SemaphoreType.DMA
    return [pltpu.VMEM(shape + (rows, cols), bf16) for shape in shapes] + [sems((3 + depth,))] * 2 + [sems]


class ShortReduce:
    def __init__(self, place, part, from_octant, line, from_line, out, into):
        self.place, self.part, self.from_octant, self.line, self.from_line = place, part, from_octant, line, from_line
        self.out, self.into = out, into

    def octant_copy(self, n):
        device, (y, x, core) = self.place.octant(n)
        return remote(
            self.part.at[:, y, x, core], self.from_octant.at[n - 1], self.out.at[n - 1], self.into.at[n - 1], device
        )

    def line_copy(self, k):
        return remote(
            self.line.at[self.place.ahead(k)], self.from_line.at[k - 1], self.out.at[6 + k], self.into.at[6 + k],
            self.place.above(k)
        )

    def start(self):
        for n in range(1, 8):
            self.octant_copy(n).start()

    def to_line(self):
        place = self.place
        total = self.part[:, place.y, place.x, place.core].astype(f32)
        for n in range(1, 8):
            self.octant_copy(n).wait()
            total = total + self.from_octant[n - 1].astype(f32)
        self.line[...] = total.astype(bf16)
        for k in range(1, place.depth):
            self.line_copy(k).start()

    def last(self):
        total = self.line[self.place.z].astype(f32)
        for k in range(1, self.place.depth):
            self.line_copy(k).wait()
            total = total + self.from_line[k - 1].astype(f32)
        return total


def short_reduce_scratch(depth, rows, cols):
    sems = pltpu.SemaphoreType.DMA
    shapes = [(depth, 2, 2, 2), (7, depth), (depth,), (depth - 1,)]
    return [pltpu.VMEM(shape + (rows, cols), bf16) for shape in shapes] + [sems((6 + depth,))] * 2


def norm_rows(rows):
    centred = rows - jnp.mean(rows, axis=1, keepdims=True)
    inverse = lax.rsqrt(jnp.mean(centred * centred, axis=1, keepdims=True) + EPSILON)
    return centred * inverse, inverse


def norm_back(grad, scaled, inverse, gain):
    inner = grad * gain
    return inverse * (
        inner
        - jnp.mean(inner, axis=1, keepdims=True)
        - scaled * jnp.mean(inner * scaled, axis=1, keepdims=True)
    )


def gelu_both(v):
    power = jnp.exp2(v * v * (-0.5 * LOG2E))
    cdf = 0.5 + 0.5 * lax.erf(v * math.sqrt(0.5))
    return v * cdf, cdf + v * power * (1.0 / math.sqrt(2.0 * math.pi))


def column_sum(rows):
    return jnp.sum(rows.astype(f32), axis=0, keepdims=True)


def to_columns(rows):
    count, width = rows.shape
    return jnp.transpose(jnp.concatenate([rows, jnp.zeros((LANES - count, width), f32)], axis=0)).astype(bf16)


def own_text(ref, text, seq):
    slots, width = ref.shape
    own = jnp.zeros((text, width), ref.dtype)
    for r in range(-(-slots // text)):
        share = ref[r * text : min(slots, (r + 1) * text), :]
        if share.shape[0] < text:
            share = jnp.concatenate([share, jnp.zeros((text - share.shape[0], width), ref.dtype)], axis=0)
        own = jnp.where(seq == r, share, own)
    return own


def as_columns(vectors):
    length = vectors[0].shape[0]
    rows = [vector.reshape(1, length).astype(f32) for vector in vectors]
    rows = jnp.concatenate(rows + [jnp.zeros((LANES - len(rows), length), f32)], axis=0)
    rows = jnp.concatenate([rows, jnp.zeros((LANES, LANES - length), f32)], axis=1)
    return jnp.transpose(rows)[:length].astype(bf16)


def front_kernel(seq_size, text, width, *refs):
    refs = list(refs)

    def take(number):
        taken = refs[:number]
        del refs[:number]
        return taken

    (shard_ref,), vec_refs = take(1), take(8)
    up_ref, up_bias_ref, out_w_ref, down_ref, x_any, slot_ref, length_ref = take(7)
    w_out, w2_out, vecs, bias_ref, quads_a, line_b, xtext_ref, first_out, q_out = take(9)
    k_outs, v_outs = take(seq_size), take(seq_size)
    shard, shard2, shard_a, shard_b, w_full, w2_full, own_a, own_b, x_s, n_s, first_s, q_s, k_s, v_s = take(14)
    sems, sems2, sems_a, sems_b = take(3), take(3), take(3), take(3)
    x_sem, w_sem, out_sem, kv_sem, kv_in_sem, kv_out_sem = take(6)
    items, patch, model = x_s.shape
    units, wide = up_ref.shape[1], shard2.shape[1]
    pairs = model // width
    place = Place(w_full.shape[0], seq_size)
    seq = lax.axis_index("seq")
    x_copies = [pltpu.make_async_copy(x_any.at[i], x_s.at[i], x_sem.at[i]) for i in range(items)]
    for copy in x_copies:
        copy.start()
    place.greet()
    for half, to in enumerate((shard, shard2)):
        for n in range(3):
            at = (n + 1) % 3 * model + half * (model // 2)
            to[:, n * (model // 2) : (n + 1) * (model // 2)] = shard_ref[:, at : at + model // 2]
    shard[:, wide:] = as_columns([ref[...] for ref in vec_refs])
    place.meet()
    halves = [Spread(place, shard, w_full, *sems), Spread(place, shard2, w2_full, *sems2)]
    for move in halves:
        move.start()
    shard_a[:, :units] = up_ref[...]
    shard_a[:, units:] = out_w_ref[...]
    shard_b[:, :model] = down_ref[...]
    shard_b[:, model:] = as_columns([up_bias_ref[...]])
    early, line = Early(place, shard_a, own_a, quads_a, *sems_a), Line(place, shard_b, own_b, line_b, *sems_b)
    tail = bias_ref.shape[2]
    col = lax.broadcasted_iota(jnp.int32, (1, tail), 1)
    slot = jnp.full((1, tail), seq_size * text, jnp.int32)
    for r in range(seq_size):
        begin = lax.rem(seq + r, seq_size) * text
        slot = jnp.where((col >= r * text) & (col < (r + 1) * text), begin + col - r * text, slot)
    for i in range(items):
        xtext_ref[i] = own_text(slot_ref.at[i], text, seq)
        bias_ref[i] = jnp.where(slot < length_ref[i], 0.0, NEG_FILL)
    halves[0].send_line()
    halves[1].send_line()
    early.start()
    line.start()
    for i in range(items):
        x_copies[i].wait()
        n_s[i], _ = norm_rows(jnp.concatenate([x_s[i], xtext_ref[i]], axis=0).astype(f32))
    halves[0].forward_first()
    halves[0].forward_second(0)
    halves[1].forward_first()
    halves[0].forward_second(1)
    halves[1].forward_second(0)
    halves[0].finish()
    w_copies = [pltpu.make_async_copy(src, dst, w_sem.at[n]) for n, (src, dst) in
                enumerate(((w_full, w_out), (w2_full, w2_out)))]
    w_copies[0].start()
    weight = w_full[...].reshape(model, wide + LANES)
    table = jnp.transpose(weight[:, wide:].astype(f32))
    vecs[...] = table
    scale = LOG2E / math.sqrt(model // HEADS)
    sends, outs = [], []

    def keys_and_values(i, half, weight):
        span = model // 2
        cols = pl.ds(half * span, span)
        projected = mm(first_s[i], weight[:, : 2 * span])
        k_s[0, i, :, cols] = projected[:, :span].astype(bf16)
        v_s[0, i, :, cols] = (projected[:, span:] + table[VBIAS : VBIAS + 1, half * span : (half + 1) * span]).astype(bf16)
        for r in range(1, seq_size):
            for n, ref in enumerate((k_s, v_s)):
                at = ((2 * i + n) * 2 + half) * seq_size + r
                src, dst = ref.at[0, i, :, cols], ref.at[r, i, :, cols]
                sends.append(remote(src, dst, kv_sem.at[at], kv_in_sem.at[at], place.mate(r)))
                sends[-1].start()

    def queries(i, half, weight):
        span = model // 2
        q = mm(first_s[i], weight[:, 2 * span : 3 * span]) + table[QBIAS : QBIAS + 1, half * span : (half + 1) * span]
        q_s[i, :, half * span : (half + 1) * span] = (q * scale).astype(bf16)

    def bring(n, src, dst, i):
        outs.append(pltpu.make_async_copy(src.at[i], dst.at[i], out_sem.at[n, i]))
        outs[-1].start()

    for i in range(items):
        first_s[i] = (n_s[i] * table[GAIN1 : GAIN1 + 1] + table[SHIFT1 : SHIFT1 + 1]).astype(bf16)
        bring(0, first_s, first_out, i)
        keys_and_values(i, 0, weight)
        if i == 0:
            halves[1].forward_second(1)
    early.send()
    halves[1].finish()
    w_copies[1].start()
    weight2 = w2_full[...].reshape(model, wide)
    for i in range(items):
        keys_and_values(i, 1, weight2)
        bring(1, k_s.at[0], k_outs[0], i)
        bring(2, v_s.at[0], v_outs[0], i)
    for i in range(items):
        queries(i, 0, weight)
        queries(i, 1, weight2)
        bring(3, q_s, q_out, i)
    line.finish()
    for copy in sends:
        copy.wait()
    for i in range(items):
        for r in range(1, seq_size):
            for n, (ref, dst) in enumerate(((k_s, k_outs), (v_s, v_outs))):
                at = (2 * i + n) * seq_size + r
                outs.append(pltpu.make_async_copy(ref.at[r, i], dst[r].at[i], kv_out_sem.at[at]))
                outs[-1].start()
    early.finish()
    line.result_copy().wait()
    for copy in w_copies + outs:
        copy.wait()


def front(in_weight, vectors, up_weight, up_bias, out_weight, down_weight, patches, text_rows, lengths, text, width,
          devices, seq_size):
    items, patch, model = patches.shape
    depth = devices // 8
    rows, cols = in_weight.shape
    shape_a = (rows, up_weight.shape[1] + model)
    shape_b = (down_weight.shape[0], model + LANES)
    shape_w = (depth, 2, 2, 2, rows, cols // 2 + LANES)
    shape_w2 = (depth, 2, 2, 2, rows, cols // 2)
    shape_x = (items, patch + text, model)
    tail = round_up(seq_size * text, LANES)
    tokens = jax.ShapeDtypeStruct(shape_x, bf16)
    sems = pltpu.SemaphoreType.DMA
    outs = pl.pallas_call(
        functools.partial(front_kernel, seq_size, text, width),
        in_specs=[WHOLE] * 13 + [ANY, WHOLE, pl.BlockSpec(memory_space=pltpu.SMEM)],
        out_specs=[ANY, ANY, WHOLE, WHOLE, ANY, ANY, WHOLE] + [ANY] * (2 + 2 * seq_size),
        out_shape=[
            jax.ShapeDtypeStruct(shape_w, bf16),
            jax.ShapeDtypeStruct(shape_w2, bf16),
            jax.ShapeDtypeStruct((LANES, model), f32),
            jax.ShapeDtypeStruct((items, 1, tail), f32),
            jax.ShapeDtypeStruct((2, depth) + shape_a, bf16),
            jax.ShapeDtypeStruct((depth,) + shape_b, bf16),
            jax.ShapeDtypeStruct((items, text, model), bf16),
            tokens,
            tokens,
        ]
        + [tokens] * (2 * seq_size),
        scratch_shapes=[
            pltpu.VMEM((rows, cols // 2 + LANES), bf16),
            pltpu.VMEM((rows, cols // 2), bf16),
            pltpu.VMEM(shape_a, bf16),
            pltpu.VMEM(shape_b, bf16),
            pltpu.VMEM(shape_w, bf16),
            pltpu.VMEM(shape_w2, bf16),
            pltpu.VMEM((2, depth) + shape_a, bf16),
            pltpu.VMEM((depth,) + shape_b, bf16),
            pltpu.VMEM(patches.shape, bf16),
            pltpu.VMEM(shape_x, f32),
            pltpu.VMEM(shape_x, bf16),
            pltpu.VMEM(shape_x, bf16),
            pltpu.VMEM((seq_size,) + shape_x, bf16),
            pltpu.VMEM((seq_size,) + shape_x, bf16),
        ]
        + spread_sems(depth) * 2
        + early_sems(depth)
        + line_sems(depth)
        + [sems((items,)), sems((2,)), sems((4, items))]
        + [sems((4 * items * seq_size,))] * 2
        + [sems((2 * items * seq_size,))],
        compiler_params=compiler_params(collective_id=0, has_side_effects=True),
        name="front",
    )(in_weight, *vectors, up_weight, up_bias, out_weight, down_weight, patches, text_rows, lengths)
    weights = [full.reshape(model, full.shape[-1]) for full in outs[:2]]
    return weights, *outs[2:4], outs[4:6], *outs[6:9], outs[9 : 9 + seq_size], outs[9 + seq_size :]


def collect(dst, refs, patch, text):
    count, width = len(refs), refs[0].shape[2]
    for r, ref in enumerate(refs):
        dst[r * patch : (r + 1) * patch, :width] = ref[0, :patch, :]
        at = count * patch + r * text
        dst[at : at + text, :width] = ref[0, patch:, :]
    filled = count * (patch + text)
    if dst.shape[0] > filled:
        dst[filled:, :width] = jnp.zeros((dst.shape[0] - filled, width), dst.dtype)


def by_head(dst, src, lane, heads, ones):
    count, width = src.shape
    for h in range(heads):
        rows = slice(h * count, (h + 1) * count)
        dst[rows, :width] = jnp.where(lane == h, src, jnp.zeros_like(src))
        if ones:
            dst[rows, width:] = jnp.where(lane == h, jnp.ones_like(src), jnp.zeros_like(src))


def attend_kernel(count, patch, head, seq_size, *refs):
    q_ref, k_refs, v_refs = refs[0], refs[1 : 1 + count], refs[1 + count : 1 + 2 * count]
    bias_ref, quads_a, line_b, out_ref, rest_ref, log_ref, full_a, full_b = refs[1 + 2 * count : 9 + 2 * count]
    keys, values, text_keys, text_values, into_a, into_b, *sems = refs[9 + 2 * count :]
    width = q_ref.shape[2]
    text, edge = q_ref.shape[1] - patch, count * patch
    heads, span = width // head, keys.shape[0] - edge
    place = Place(full_a.shape[0], seq_size)
    turn = pl.program_id(0) * pl.num_programs(1) + pl.program_id(1)
    last = pl.num_programs(0) * pl.num_programs(1) - 1
    move_a, move_b = Late(place, quads_a, into_a, full_a, *sems[:4]), LateLine(place, line_b, into_b, full_b, *sems[4:])

    @pl.when(turn == 0)
    def _():
        place.greet()
        move_a.start()
        move_b.start()

    agenda = (
        (1, place.meet),
        (1, move_b.send),
        (1, move_a.send),
        (5, move_b.forward_first),
        (6, functools.partial(move_b.forward_second, 0)),
        (6, functools.partial(move_b.land, 0)),
        (7, functools.partial(move_a.land, 0)),
        (7, functools.partial(move_a.land, 1)),
        (8, functools.partial(move_a.forward, 0)),
        (8, functools.partial(move_a.forward, 1)),
        (9, functools.partial(move_b.land, 1)),
        (9, functools.partial(move_b.land, 2)),
        (10, functools.partial(move_a.land, 2)),
        (10, functools.partial(move_a.land, 3)),
        (10, functools.partial(move_b.forward_second, 1)),
    )
    for at in sorted({at for at, _ in agenda}):

        @pl.when(turn == at)
        def _(at=at):
            for when, step in agenda:
                if when == at:
                    step()

    collect(keys, k_refs, patch, text)
    collect(values, v_refs, patch, text)
    values[:, width:] = jnp.ones((values.shape[0], values.shape[1] - width), bf16)
    lane = lax.broadcasted_iota(jnp.int32, (1, width), 1) // head
    by_head(text_keys, keys[edge:], lane, heads, False)
    by_head(text_values, values[edge:, :width], lane, heads, True)
    q = q_ref[0]
    text_bias = jnp.concatenate([bias_ref[0]] * heads, axis=1)

    def scores_of(h):
        return mm_t(jnp.where(lane == h, q, jnp.zeros_like(q)), keys[:edge])

    text_scores = mm_t(q, text_keys[...]) + text_bias
    scores = scores_of(0)
    text_powers, mixed, total, tops = [], None, None, None
    for h in range(heads):
        following = scores_of(h + 1) if h + 1 < heads else None
        text_head = text_scores[:, h * span : (h + 1) * span]
        top = jnp.maximum(jnp.max(scores, axis=1, keepdims=True), jnp.max(text_head, axis=1, keepdims=True))
        powers = jnp.exp2(scores - top).astype(bf16)
        text_powers.append(jnp.exp2(text_head - top).astype(bf16))
        both = mm(powers, values[:edge])
        mixed = both[:, :width] if mixed is None else jnp.where(lane == h, both[:, :width], mixed)
        total = both[:, width:] if total is None else jnp.where(lane == h, both[:, width:], total)
        tops = jnp.broadcast_to(top, mixed.shape) if tops is None else jnp.where(lane == h, top, tops)
        scores = following
    both = mm(jnp.concatenate(text_powers, axis=1), text_values[...])
    total = total + both[:, width:]
    out = (mixed + both[:, :width]) * (1.0 / total)
    high = out.astype(bf16)
    out_ref[0] = high
    rest_ref[0] = (out - high.astype(f32)).astype(bf16)
    log_ref[0] = tops + jnp.log2(total)

    @pl.when(turn == last)
    def _():
        move_b.land(3)
        move_a.finish()
        move_b.finish()


def attend(q, keys, values, bias, halfway, patch, head, width, devices, seq_size):
    items, _, model = q.shape
    count, tail = len(keys), bias.shape[-1]
    depth, heads, span = devices // 8, width // head, count * patch + tail
    block = pl.BlockSpec((1, q.shape[1], width), lambda i, p: (i, 0, p))
    outs = pl.pallas_call(
        functools.partial(attend_kernel, count, patch, head, seq_size),
        grid=(items, model // width),
        in_specs=[block] * (1 + 2 * count) + [pl.BlockSpec((1, 1, tail), lambda i, p: (i, 0, 0))] + [ANY] * 2,
        out_specs=[block, block, block, ANY, ANY],
        out_shape=[jax.ShapeDtypeStruct(q.shape, bf16)] * 2
        + [jax.ShapeDtypeStruct(q.shape, f32)]
        + [jax.ShapeDtypeStruct((depth, 2, 2, 2) + part.shape[-2:], part.dtype) for part in halfway],
        scratch_shapes=[
            pltpu.VMEM((span, width), bf16),
            pltpu.VMEM((span, 2 * width), bf16),
            pltpu.VMEM((heads * tail, width), bf16),
            pltpu.VMEM((heads * tail, 2 * width), bf16),
        ]
        + [pltpu.VMEM((depth, 2, 2, 2) + part.shape[-2:], part.dtype) for part in halfway]
        + late_sems()
        + late_line_sems(),
        compiler_params=compiler_params(collective_id=1, has_side_effects=True),
        name="attend",
    )(q, *keys, *values, bias, *halfway)
    return outs[0], outs[1], outs[2], [full.reshape(-1, full.shape[-1]) for full in outs[3:]]


def ffn_kernel(steps, chunk, seq_ref, x_ref, xtext_ref, at_ref, dy_ref, dy_slot_ref, w_any, wd_any, vec_ref,
               res_ref, restext_ref, gb_ref, ga_ref, part_out, down_out,
               w_ref, wd_ref, part_ref, down_ref, second_s, hidden_s, pre_s, dy_s, sums_s, bias_s, out_s, dots_s,
               w_sem, wd_sem, part_sem, down_sem):
    step = pl.program_id(0)
    patch, model = x_ref.shape[1:]
    text = xtext_ref.shape[1]
    block, units = patch + text, wd_ref.shape[0]
    chunks = units // chunk
    rows = pl.ds(pl.multiple_of(step * block, ROW_TILE), block)
    gain = vec_ref[GAIN2 : GAIN2 + 1]
    w_out = w_ref.at[:, units:]

    def fetch(cols, at):
        if cols is None:
            return (
                pltpu.make_async_copy(w_any.at[:, units:], w_ref.at[:, units:], w_sem.at[at]),
                pltpu.make_async_copy(wd_any.at[:, model:], wd_ref.at[:, model:], wd_sem.at[at]),
            )
        return (
            pltpu.make_async_copy(w_any.at[:, cols], w_ref.at[:, cols], w_sem.at[at]),
            pltpu.make_async_copy(wd_any.at[cols, :model], wd_ref.at[cols, :model], wd_sem.at[at]),
        )

    @pl.when(step == 0)
    def _():
        others = fetch(None, chunks)
        for copy in others:
            copy.start()
        for c in range(chunks):
            for copy in fetch(pl.ds(c * chunk, chunk), c):
                copy.start()
        sums_s[...] = jnp.zeros_like(sums_s)
        for copy in others:
            copy.wait()
        bias_s[...] = jnp.transpose(wd_ref[:, model:].astype(f32))[:8]

    x = jnp.concatenate([x_ref[0], xtext_ref[0]], axis=0).astype(f32)
    dy = jnp.concatenate([dy_ref[0], own_text(dy_slot_ref.at[0], text, seq_ref[0])], axis=0)
    dy_s[rows, :] = dy
    middle = x + (mm(at_ref[0], w_out[...]) + vec_ref[BRANCH : BRANCH + 1])
    scaled, inverse = norm_rows(middle)
    second_in = (scaled * gain + vec_ref[SHIFT2 : SHIFT2 + 1]).astype(bf16)
    second_s[rows, :] = second_in
    dots_s[0] = middle + vec_ref[DOWNB : DOWNB + 1]
    dots_s[1] = jnp.zeros_like(middle)

    def part(c, _):
        cols = pl.ds(pl.multiple_of(c * chunk, chunk), chunk)

        @pl.when(step == 0)
        def _():
            for copy in fetch(cols, c):
                copy.wait()

        value, slope = gelu_both(mm(second_in, w_ref[:, cols]) + bias_s[:1, cols])
        hidden = value.astype(bf16)
        hidden_s[rows, cols] = hidden
        grad_pre = (mm_t(dy, wd_ref[cols, :model]) * slope).astype(bf16)
        pre_s[rows, cols] = grad_pre
        dots_s[0] += mm(hidden, wd_ref[cols, :model])
        dots_s[1] += mm_t(grad_pre, w_ref[:, cols])
        return 0

    lax.fori_loop(0, units // chunk, part, 0)
    result, grad_second = dots_s[0], dots_s[1]
    result = result.astype(bf16)
    res_ref[0] = result[:patch]
    restext_ref[0] = result[patch:]
    grad_branch = (dy.astype(f32) + norm_back(grad_second, scaled, inverse, gain)).astype(bf16)
    gb_ref[0] = grad_branch
    ga_ref[0] = mm_t(grad_branch, w_out[...]).astype(bf16)
    out_grad = t_mm(at_ref[0], grad_branch)

    @pl.when(step == 0)
    def _():
        out_s[...] = out_grad

    @pl.when(step > 0)
    def _():
        out_s[...] += out_grad

    for at, grad in ((BRANCH, grad_branch), (GAIN2, grad_second * scaled), (SHIFT2, grad_second), (DOWNB, dy)):
        sums_s[at : at + 1, :] += column_sum(grad)

    @pl.when(step == steps - 1)
    def _():
        groups = units // model
        copies = []
        part_ref[:, units : units + model] = out_s[...].astype(bf16)
        part_ref[:, units + model :] = to_columns(sums_s[...])
        copies.append(pltpu.make_async_copy(part_ref.at[:, units:], part_out.at[:, units:], part_sem.at[groups]))
        copies[-1].start()
        for c in range(groups):
            cols = slice(c * model, (c + 1) * model)
            at = pl.ds(c * model, model)
            grad_pre = pre_s[:, cols]
            part_ref[:, cols] = t_mm(second_s[...], grad_pre).astype(bf16)
            copies.append(pltpu.make_async_copy(part_ref.at[:, at], part_out.at[:, at], part_sem.at[c]))
            copies[-1].start()
            down_ref[cols, :model] = jnp.transpose(t_mm(dy_s[...], hidden_s[:, cols])).astype(bf16)
            down_ref[cols, model:] = to_columns(column_sum(grad_pre))
            copies.append(pltpu.make_async_copy(down_ref.at[at], down_out.at[at], down_sem.at[c]))
            copies[-1].start()
        for copy in copies:
            copy.wait()


def ffn(seq, patches, x_text, attended, patch_cotangent, text_cotangent, weights, w_down, vecs):
    items, patch, model = patches.shape
    units, rows, text, slots = w_down.shape[0], attended.shape[1], x_text.shape[1], text_cotangent.shape[1]

    def item(count):
        return pl.BlockSpec((1, count, model), lambda i: (i, 0, 0))

    def shape(count):
        return jax.ShapeDtypeStruct((items, count, model), bf16)

    return pl.pallas_call(
        functools.partial(ffn_kernel, items, 1024),
        grid=(items,),
        in_specs=[pl.BlockSpec(memory_space=pltpu.SMEM)]
        + [item(patch), item(text), item(rows), item(patch), item(slots)]
        + [ANY, ANY, WHOLE],
        out_specs=[item(patch), item(text), item(rows), item(rows), ANY, ANY],
        out_shape=[shape(patch), shape(text), shape(rows), shape(rows)]
        + [
            jax.ShapeDtypeStruct((model, units + model + LANES), bf16),
            jax.ShapeDtypeStruct((units, model + LANES), bf16),
        ],
        scratch_shapes=[
            pltpu.VMEM(weights.shape, bf16),
            pltpu.VMEM(w_down.shape, bf16),
            pltpu.VMEM((model, units + model + LANES), bf16),
            pltpu.VMEM((units, model + LANES), bf16),
            pltpu.VMEM((items * rows, model), bf16),
            pltpu.VMEM((items * rows, units), bf16),
            pltpu.VMEM((items * rows, units), bf16),
            pltpu.VMEM((items * rows, model), bf16),
            pltpu.VMEM((8, model), f32),
            pltpu.VMEM((8, units), f32),
            pltpu.VMEM((model, model), f32),
            pltpu.VMEM((2, rows, model), f32),
        ]
        + [pltpu.SemaphoreType.DMA((units // 1024 + 1,))] * 2
        + [pltpu.SemaphoreType.DMA((units // model + 1,))] * 2,
        compiler_params=compiler_params(),
        name="ffn",
    )(seq, patches, x_text, attended, patch_cotangent, text_cotangent, weights, w_down, vecs)


def back_kernel(count, patch, head, seq_size, pairs, items, *refs):
    refs = list(refs)

    def take(number):
        taken = refs[:number]
        del refs[:number]
        return taken

    (q_ref,), k_refs, v_refs = take(1), take(count), take(count)
    bias_ref, log_ref, at_ref, rest_ref, grad_ref = take(5)
    part_a, part_b, w_any, w2_any, vec_ref, first_any, x_any, xtext_any, gb_any, restext_any = take(10)
    grad_out, text_grad_out, text_out, total_a, total_b, total_in, vec_out, vec2_out, upb_out = take(9)
    keys, values, text_keys, text_values, probs_s, scores_s = take(6)
    mixed_s, own_s, dkv_out, dkv_in, sums_s = take(5)
    w_s, w2_s, first_s, x_s, xtext_s, gb_s, text_s, patch_s = take(8)
    first_grad_s, scaled_s, inverse_s = take(3)
    fetch_sem, dkv_sem, dkv_in_sem, text_sem, text_in_sem, patch_sem = take(6)
    scratch_a, scratch_b = take(10), take(10)
    scratch_in = [take(11) for _ in range(2)]
    scratch_last, scratch_vec = take(6), take(6)

    width, rows = q_ref.shape[2], q_ref.shape[1]
    text, model = rows - patch, pairs * width
    place = Place(part_a.shape[0], seq_size)
    seq = lax.axis_index("seq")
    p, i = pl.program_id(0), pl.program_id(1)
    turn, last = p * items + i, pairs * items - 1
    sums_a, sums_b = Reduce(place, part_a, *scratch_a), Reduce(place, part_b, *scratch_b)
    chunks = ((0, pairs - 2), (pairs - 2, pairs - 1), (pairs - 1, pairs))
    sums_in = [Reduce(place, each[0], *each[1:]) for each in scratch_in]
    sums_in.append(ShortReduce(place, *scratch_last))
    sums_vec = ShortReduce(place, *scratch_vec)
    fetches = [
        pltpu.make_async_copy(src, dst, fetch_sem.at[n])
        for n, (src, dst) in enumerate(
            ((first_any, first_s), (w_any, w_s), (w2_any, w2_s), (x_any, x_s), (xtext_any, xtext_s), (gb_any, gb_s))
        )
    ]

    def text_copies(src, dst, row):
        to = dst.at[:, pl.ds(pl.multiple_of(seq * text, ROW_TILE), text)]
        own = pltpu.make_async_copy(src, to, text_sem.at[row, 0])
        away = [
            remote(src, to, text_sem.at[row, r], text_in_sem.at[row, r], place.mate(r)) for r in range(1, seq_size)
        ]
        return [own] + away

    def begin():
        place.meet(corners=True)
        sums_a.to_core()
        sums_b.to_core()
        for copy in text_copies(restext_any, text_out, 0):
            copy.start()

    def dkv_copy(slot, r):
        return remote(
            dkv_out.at[slot, r - 1], dkv_in.at[slot, r - 1], dkv_sem.at[slot, r - 1], dkv_in_sem.at[slot, r - 1],
            place.mate(-r)
        )

    def settle(of):
        slot, pair, item = lax.rem(of, 2), of // items, lax.rem(of, items)
        total = own_s[slot]
        for r in range(1, seq_size):
            dkv_copy(slot, r).wait_recv()
            total = total + dkv_in[slot, r - 1].astype(f32)
        at = pl.ds(pl.multiple_of(item * rows, ROW_TILE), rows)
        mixed_s[pair, at, width:] = total.astype(bf16)

    def pair_done(pair):
        mixed = mixed_s[pair]
        if pair == 0:
            fetches[0].wait()
        grad = t_mm(first_s[...].reshape(items * rows, model), mixed).astype(bf16)
        chunk = sum(pair >= first for first, _ in chunks) - 1
        first, end = chunks[chunk]
        part = sums_in[chunk].part
        part[..., 3 * (pair - first) * width : 3 * (pair - first + 1) * width] = grad.reshape(
            part.shape[:-1] + (3 * width,)
        )
        if pair == end - 1:
            (sums_in[chunk].start if end == pairs else sums_in[chunk].to_core)()
        cols = slice(pair * width, (pair + 1) * width)
        sums_s[QBIAS : QBIAS + 1, cols] = column_sum(mixed[:, :width])
        sums_s[VBIAS : VBIAS + 1, cols] = column_sum(mixed[:, 2 * width :])

    def finish_in(chunk):
        total = sums_in[chunk].last()
        first, end = chunks[chunk]
        for m in range(end - first):
            for n in range(3):
                at, of = n * model + (first + m) * width, (3 * m + n) * width
                total_in[:, at : at + width] = total[:, of : of + width]

    def finish_a():
        total = sums_a.last()
        total_a[...] = total[:, : total_a.shape[1]]
        vec2_out[...] = total[:, total_a.shape[1] :]

    def finish_b():
        total = sums_b.last()
        total_b[...] = total[:, :model]
        upb_out[...] = total[:, model:]

    tail_at = last + 1
    agenda = [(2, sums_a.to_second), (3, sums_b.to_second), (5, sums_a.to_first), (7, sums_b.to_first),
              (8, sums_a.to_line), (9, sums_b.to_line), (11, finish_a), (tail_at + 1, finish_b)]
    turns_in = ((9, 10, 11, tail_at + 1), (11, tail_at, tail_at + 1, tail_at + 2))
    for chunk, turns in enumerate(turns_in):
        steps = (sums_in[chunk].to_second, sums_in[chunk].to_first, sums_in[chunk].to_line)
        steps += (functools.partial(finish_in, chunk),)
        agenda += [(max(at, items * chunks[chunk][1] + 2), step) for at, step in zip(turns, steps)]
    agenda += [(tail_at + 1, sums_in[2].to_line), (tail_at + 3, functools.partial(finish_in, 2))]
    agenda.sort(key=lambda entry: entry[0])

    @pl.when(turn == 0)
    def _():
        place.greet(corners=True)
        for copy in fetches:
            copy.start()
        sums_s[...] = jnp.zeros_like(sums_s)

    collect(keys, k_refs, patch, text)
    collect(values, v_refs, patch, text)
    q, grad = q_ref[0], grad_ref[0]
    edge, heads, span = count * patch, width // head, keys.shape[0] - count * patch
    lane = lax.broadcasted_iota(jnp.int32, (1, width), 1) // head
    row = lax.broadcasted_iota(jnp.int32, (width, 1), 0) // head
    by_head(text_keys, keys[edge:], lane, heads, False)
    by_head(text_values, values[edge:], lane, heads, False)
    text_bias = jnp.concatenate([bias_ref[0]] * heads, axis=1)
    inner = grad.astype(f32) * (at_ref[0].astype(f32) + rest_ref[0].astype(f32))
    q_heads = [jnp.where(lane == h, q, jnp.zeros_like(q)) for h in range(heads)]
    grad_heads = [jnp.where(lane == h, grad, jnp.zeros_like(grad)) for h in range(heads)]
    deltas = [jnp.sum(jnp.where(lane == h, inner, 0.0), axis=1, keepdims=True) for h in range(heads)]
    logs = [log_ref[0, :, h * head : h * head + 1] for h in range(heads)]

    def first_dots(h):
        return mm_t(q_heads[h], keys[:edge]), mm_t(grad_heads[h], values[:edge])

    scores, grad_probs = first_dots(0)
    text_scores = mm_t(q, text_keys[...]) + text_bias
    text_grad_probs = mm_t(grad, text_values[...])
    dq, text_probs, text_grads = None, [], []
    for h in range(heads):
        following = first_dots(h + 1) if h + 1 < heads else (None, None)
        cols = slice(h * span, (h + 1) * span)
        text_head = jnp.exp2(text_scores[:, cols] - logs[h])
        text_probs.append(text_head.astype(bf16))
        text_grads.append((text_head * (text_grad_probs[:, cols] - deltas[h])).astype(bf16))
        probs = jnp.exp2(scores - logs[h])
        grad_scores = (probs * (grad_probs - deltas[h])).astype(bf16)
        probs_s[h * rows : (h + 1) * rows, :] = probs.astype(bf16)
        scores_s[h * rows : (h + 1) * rows, :] = grad_scores
        dq_head = mm(grad_scores, keys[:edge])
        dq = dq_head if dq is None else jnp.where(lane == h, dq_head, dq)
        scores, grad_probs = following
    text_probs, text_grads = jnp.concatenate(text_probs, axis=1), jnp.concatenate(text_grads, axis=1)
    dq = dq + mm(text_grads, text_keys[...])
    dv = jnp.transpose(t_mm(jnp.concatenate(grad_heads, axis=0), probs_s[...]))
    dk = jnp.transpose(t_mm(jnp.concatenate(q_heads, axis=0), scores_s[...])) * LN2

    def of_heads(wide):
        own = wide[:, :span]
        for h in range(1, heads):
            own = jnp.where(row == h, wide[:, h * span : (h + 1) * span], own)
        return jnp.transpose(own)

    text_dv, text_dk = of_heads(t_mm(grad, text_probs)), of_heads(t_mm(q, text_grads)) * LN2
    slot = lax.rem(turn, 2)

    @pl.when(turn == 0)
    def _():
        begin()

    for at in sorted({at for at, _ in agenda if at <= last}):

        @pl.when(turn == at - 1)
        def _(at=at):
            for when, step in agenda:
                if when == at:
                    step()

    at = pl.ds(pl.multiple_of(i * rows, ROW_TILE), rows)
    mixed_s[p, at, :width] = (dq * (1.0 / math.sqrt(head))).astype(bf16)
    own_s[slot, :patch, :width] = dk[:patch]
    own_s[slot, :patch, width:] = dv[:patch]
    own_s[slot, patch:, :width] = text_dk[:text]
    own_s[slot, patch:, width:] = text_dv[:text]

    @pl.when(turn > 0)
    def _():
        settle(turn - 1)

    @pl.when(turn > 1)
    def _():
        for r in range(1, seq_size):
            dkv_copy(slot, r).wait_send()

    for r in range(1, seq_size):
        for n, (part, text_part) in enumerate(((dk, text_dk), (dv, text_dv))):
            cols = slice(n * width, (n + 1) * width)
            dkv_out[slot, r - 1, :patch, cols] = part[r * patch : (r + 1) * patch].astype(bf16)
            dkv_out[slot, r - 1, patch:, cols] = text_part[r * text : (r + 1) * text].astype(bf16)
        dkv_copy(slot, r).start()

    for pair in range(pairs - 1):

        @pl.when(turn == items * (pair + 1))
        def _(pair=pair):
            pair_done(pair)

    @pl.when(turn == last)
    def _():
        left = [[step for when, step in agenda if when == at] for at in sorted({at for at, _ in agenda if at > last})]

        def more():
            if left:
                for step in left.pop(0):
                    step()

        half = pairs // 2
        sides = (w_s.at[:, : 3 * half * width], w2_s)

        def grad_first(item, side):
            at = slice(item * rows, (item + 1) * rows)
            mixed = [
                mixed_s[side * half + m, at, n * width : (n + 1) * width] for n in (1, 2, 0) for m in range(half)
            ]
            return mm_t(jnp.concatenate(mixed, axis=1), sides[side][...])

        for copy in fetches[1:]:
            copy.wait()
        for item in range(items):
            first_grad_s[item] = grad_first(item, 0)
        settle(last)
        pair_done(pairs - 1)
        for item in range(items):
            grad = first_grad_s[item] + grad_first(item, 1)
            first_grad_s[item] = grad
            scaled, inverse = norm_rows(jnp.concatenate([x_s[item], xtext_s[item]], axis=0).astype(f32))
            scaled_s[item] = scaled
            inverse_s[item] = jnp.broadcast_to(inverse, (rows, LANES))
            sums_s[GAIN1 : GAIN1 + 1, :] += column_sum(grad * scaled)
            sums_s[SHIFT1 : SHIFT1 + 1, :] += column_sum(grad)
        sums_vec.part[...] = to_columns(sums_s[...]).reshape(sums_vec.part.shape)
        sums_vec.start()
        more()
        gain = vec_ref[GAIN1 : GAIN1 + 1]
        patch_copies = [
            pltpu.make_async_copy(patch_s.at[item], grad_out.at[item], patch_sem.at[item]) for item in range(items)
        ]
        for item in range(items):
            grad_rows = norm_back(first_grad_s[item], scaled_s[item], inverse_s[item][:, :1], gain)
            grad_rows = (gb_s[item].astype(f32) + grad_rows).astype(bf16)
            patch_s[item] = grad_rows[:patch]
            patch_copies[item].start()
            text_s[item] = grad_rows[patch:]
            if item == 0:
                sums_vec.to_line()
            more()
        for copy in text_copies(text_s, text_grad_out, 1):
            copy.start()
        while left:
            more()
        vec_out[...] = sums_vec.last()
        for copies in (text_copies(restext_any, text_out, 0), text_copies(text_s, text_grad_out, 1)):
            for copy in copies:
                copy.wait()
        for slot in range(2):
            for r in range(1, seq_size):
                dkv_copy(slot, r).wait_send()
        for copy in patch_copies:
            copy.wait()


def back(q, keys, values, bias, logs, attended, rest, grad_att, part_a, part_b, w_in, vecs, first_in, patches, x_text,
         grad_branch, res_text, head, width, devices, seq_size):
    items, patch, model = patches.shape
    rows, text = q.shape[1], x_text.shape[1]
    count, tail, pairs, depth = len(keys), bias.shape[-1], model // width, devices // 8
    span = count * patch + tail
    block = pl.BlockSpec((1, rows, width), lambda p, i: (i, 0, p))
    parts = [part.reshape((depth, 2, 2, 2, part.shape[0] // devices, part.shape[1])) for part in (part_a, part_b)]
    (rows_a, cols_a), (rows_b, cols_b) = parts[0].shape[4:], parts[1].shape[4:]
    sems = pltpu.SemaphoreType.DMA
    others = seq_size - 1
    slots = jax.ShapeDtypeStruct((items, seq_size * text, model), bf16)
    scratch_in = []
    for cols in (3 * (pairs - 2) * width, 3 * width):
        scratch_in += [pltpu.VMEM((depth, 2, 2, 2, rows_a, cols), bf16)] + reduce_scratch(depth, rows_a, cols)
    scratch_in += short_reduce_scratch(depth, rows_a, 3 * width)
    return pl.pallas_call(
        functools.partial(back_kernel, count, patch, head, seq_size, pairs, items),
        grid=(pairs, items),
        in_specs=[block] * (1 + 2 * count)
        + [pl.BlockSpec((1, 1, tail), lambda p, i: (i, 0, 0))]
        + [block] * 4
        + [ANY] * 4
        + [WHOLE]
        + [ANY] * 5,
        out_specs=[ANY] * 3 + [WHOLE] * 6,
        out_shape=[
            jax.ShapeDtypeStruct(patches.shape, bf16),
            slots,
            slots,
            jax.ShapeDtypeStruct((rows_a, cols_a - LANES), f32),
            jax.ShapeDtypeStruct((rows_b, cols_b - LANES), f32),
            jax.ShapeDtypeStruct((rows_a, 3 * model), f32),
            jax.ShapeDtypeStruct((rows_a, LANES), f32),
            jax.ShapeDtypeStruct((rows_a, LANES), f32),
            jax.ShapeDtypeStruct((rows_b, LANES), f32),
        ],
        scratch_shapes=[
            pltpu.VMEM((span, width), bf16),
            pltpu.VMEM((span, width), bf16),
            pltpu.VMEM((width // head * tail, width), bf16),
            pltpu.VMEM((width // head * tail, width), bf16),
            pltpu.VMEM((width // head * rows, count * patch), bf16),
            pltpu.VMEM((width // head * rows, count * patch), bf16),
            pltpu.VMEM((pairs, items * rows, 3 * width), bf16),
            pltpu.VMEM((2, rows, 2 * width), f32),
            pltpu.VMEM((2, others, rows, 2 * width), bf16),
            pltpu.VMEM((2, others, rows, 2 * width), bf16),
            pltpu.VMEM((8, model), f32),
            pltpu.VMEM(w_in[0].shape, bf16),
            pltpu.VMEM(w_in[1].shape, bf16),
            pltpu.VMEM(first_in.shape, bf16),
            pltpu.VMEM(patches.shape, bf16),
            pltpu.VMEM(x_text.shape, bf16),
            pltpu.VMEM(grad_branch.shape, bf16),
            pltpu.VMEM(x_text.shape, bf16),
            pltpu.VMEM(patches.shape, bf16),
            pltpu.VMEM(q.shape, f32),
            pltpu.VMEM(q.shape, f32),
            pltpu.VMEM((items, rows, LANES), f32),
            sems((6,)),
            sems((2, others)),
            sems((2, others)),
            sems((2, seq_size)),
            sems((2, seq_size)),
            sems((items,)),
        ]
        + reduce_scratch(depth, rows_a, cols_a)
        + reduce_scratch(depth, rows_b, cols_b)
        + scratch_in
        + short_reduce_scratch(depth, rows_a, LANES),
        compiler_params=compiler_params(collective_id=2, has_side_effects=True),
        name="back",
    )(q, *keys, *values, bias, logs, attended, rest, grad_att, *parts, *w_in, vecs, first_in, patches, x_text,
      grad_branch, res_text)


def outputs_kernel(*refs):
    text_ref, patch_grad, text_grad, total_a, total_b, total_in, vec1, vec2, upb = refs[:9]
    outs = list(refs[9:])
    out_text, grad_patches, grad_text = outs[:3]
    first_gain, first_shift, in_weight, query_bias, value_bias, out_weight, branch_bias = outs[3:10]
    second_gain, second_shift, up_weight, up_bias, down_weight, down_bias = outs[10:]
    slots, units = out_text.shape[1], up_weight.shape[1]
    out_text[...] = text_ref[:, :slots]
    grad_text[...] = text_grad[:, :slots]
    grad_patches[...] = patch_grad[...]

    def row_of(ref, at):
        count = ref.shape[0]
        tall = jnp.concatenate([ref[...], jnp.zeros((LANES - count, LANES), f32)], axis=0)
        return jnp.transpose(tall)[at, :count]

    @pl.when(pl.program_id(0) == 0)
    def _():
        in_weight[...] = total_in[...]
        out_weight[...] = total_a[:, units:]
        up_weight[...] = total_a[:, :units]
        down_weight[...] = total_b[...]
        for ref, at in ((first_gain, GAIN1), (first_shift, SHIFT1), (query_bias, QBIAS), (value_bias, VBIAS)):
            ref[...] = row_of(vec1, at)
        for ref, at in ((branch_bias, BRANCH), (second_gain, GAIN2), (second_shift, SHIFT2), (down_bias, DOWNB)):
            ref[...] = row_of(vec2, at)
        up_bias[...] = row_of(upb, 0)


def outputs(text, patch_grad, text_grad, total_a, total_b, total_in, vec1, vec2, upb, slots, units):
    items, patch, model = patch_grad.shape
    padded = text.shape[1]

    def item(count):
        return pl.BlockSpec((1, count, model), lambda i: (i, 0, 0))

    def shape(*dims):
        return jax.ShapeDtypeStruct(dims, f32)

    count = total_in.shape[0]
    vector, texts = shape(count), jax.ShapeDtypeStruct((items, slots, model), bf16)
    return pl.pallas_call(
        outputs_kernel,
        grid=(items,),
        in_specs=[item(padded), item(patch), item(padded)] + [WHOLE] * 6,
        out_specs=[item(slots), item(patch), item(slots)] + [WHOLE] * 13,
        out_shape=[texts, jax.ShapeDtypeStruct(patch_grad.shape, bf16), texts]
        + [vector, vector, shape(count, 3 * model), vector, vector, shape(count, model), vector, vector, vector]
        + [shape(count, units), shape(upb.shape[0]), shape(*total_b.shape), vector],
        compiler_params=compiler_params(),
        name="outputs",
    )(text, patch_grad, text_grad, total_a, total_b, total_in, vec1, vec2, upb)


def per_device(
    seq_size,
    devices,
    patches,
    text_rows,
    lengths,
    first_gain,
    first_shift,
    in_weight,
    query_bias,
    value_bias,
    out_weight,
    branch_bias,
    second_gain,
    second_shift,
    up_weight,
    up_bias,
    down_weight,
    down_bias,
    patch_cotangent,
    text_cotangent,
):
    items, patch, model = patches.shape
    slots = text_rows.shape[1]
    units = up_weight.shape[1]
    head = model // HEADS
    width = min(LANES, model)
    text = round_up(-(-slots // seq_size), ROW_TILE)
    seq = lax.axis_index("seq")
    vectors = [first_gain, first_shift, query_bias, value_bias, branch_bias, second_gain, second_shift, down_bias]
    w_in, vecs, bias, halfway, x_text, first_in, q, keys, values = front(
        in_weight, vectors, up_weight, up_bias, out_weight, down_weight, patches, text_rows, lengths, text, width,
        devices, seq_size
    )
    attended, rest, logs, (weights, w_down) = attend(
        q, keys, values, bias, halfway, patch, head, width, devices, seq_size
    )
    out_patches, res_text, grad_branch, grad_att, part_a, part_b = ffn(
        seq[None], patches, x_text, attended, patch_cotangent, text_cotangent, weights, w_down, vecs
    )
    grad_patches, grad_text, out_text, sums, down_grad, in_grad, vec1, vec2, up_bias_grad = back(
        q, keys, values, bias, logs, attended, rest, grad_att, part_a, part_b, w_in, vecs, first_in, patches, x_text,
        grad_branch, res_text, head, width, devices, seq_size
    )
    rest = outputs(
        out_text, grad_patches, grad_text, sums, down_grad, in_grad, vec1, vec2, up_bias_grad, slots, units
    )
    return (out_patches, *rest)


def solution(mesh):
    both = ("dp", "seq")
    rows, slots, vector, matrix = P("dp", "seq", None), P("dp", None, None), P(both), P(both, None)
    weights = (vector, vector, matrix, vector, vector, matrix, vector, vector, vector, matrix, vector, matrix, vector)
    return jax.shard_map(
        functools.partial(per_device, mesh.shape["seq"], mesh.size),
        mesh=mesh,
        in_specs=(rows, slots, P("dp")) + weights + (rows, slots),
        out_specs=(rows, slots, rows, slots) + weights,
        check_vma=False,
    )
```

```python
import functools
import math

import jax
import jax.numpy as jnp
from jax import lax
from jax.experimental import pallas as pl
from jax.experimental.pallas import tpu as pltpu
from jax.sharding import PartitionSpec as P

HEADS = 8
EPSILON = 1e-05
NEG_FILL = -1e30
LOG2E = math.log2(math.e)
LN2 = math.log(2.0)
ROW_TILE = 16
LANES = 128
MESH = pl.DeviceIdType.MESH
f32, bf16 = jnp.float32, jnp.bfloat16

GAIN1, SHIFT1, QBIAS, VBIAS, BRANCH, GAIN2, SHIFT2, DOWNB = range(8)


def round_up(value, unit):
    return -(-value // unit) * unit


def mm(a, b):
    return lax.dot_general(a, b, (((1,), (0,)), ((), ())), preferred_element_type=f32)


def mm_t(a, b):
    return lax.dot_general(a, b, (((1,), (1,)), ((), ())), preferred_element_type=f32)


def t_mm(a, b):
    return lax.dot_general(a, b, (((0,), (0,)), ((), ())), preferred_element_type=f32)


def compiler_params(**more):
    return pltpu.CompilerParams(vmem_limit_bytes=60 * 2**20, **more)


WHOLE = pl.BlockSpec(memory_space=pltpu.VMEM)
ANY = pl.BlockSpec(memory_space=pl.ANY)


class Place:
    def __init__(self, depth, seq_size):
        self.depth, self.seq_size = depth, seq_size
        index = lax.axis_index("dp") * seq_size + lax.axis_index("seq")
        self.core = lax.rem(index, 2)
        self.x = lax.rem(index // 2, 2)
        self.y = lax.rem(index // 4, 2)
        self.z = index // 8
        core = self.core
        flip_x, flip_y = 1 - self.x, 1 - self.y
        x_first = self.x * core + flip_x * (1 - core)
        y_first = self.y * (1 - core) + flip_y * core
        x_second = self.x * (1 - core) + flip_x * core
        y_second = self.y * core + flip_y * (1 - core)
        self.columns = (
            (self.y, self.x),
            (y_first, x_first),
            (y_second, x_second),
            (flip_y, flip_x),
        )

    def device(self, z, y, x, core):
        index = ((z * 2 + y) * 2 + x) * 2 + core
        return (index // self.seq_size, lax.rem(index, self.seq_size))

    def layer(self, k):
        return lax.rem(self.z + self.depth - k, self.depth)

    def ahead(self, k):
        return lax.rem(self.z + k, self.depth)

    def first(self):
        return self.device(self.z, *self.columns[1], self.core)

    def second(self):
        return self.device(self.z, *self.columns[2], self.core)

    def other_core(self):
        return self.device(self.z, self.y, self.x, 1 - self.core)

    def above(self, k):
        return self.device(self.ahead(k), self.y, self.x, self.core)

    def mate(self, step):
        return (lax.axis_index("dp"), lax.rem(lax.axis_index("seq") + self.seq_size - step, self.seq_size))

    def octant(self, n):
        column, core = n % 4, n // 4
        y, x = self.columns[column]
        core = self.core * (1 - core) + (1 - self.core) * core
        return self.device(self.z, y, x, core), (y, x, core)

    def friends(self, corners):
        friends = [self.above(k) for k in range(1, self.depth)]
        friends += [self.octant(n)[0] for n in range(1, 8)] if corners else [self.first(), self.second(), self.other_core()]
        return friends + [self.mate(step) for step in range(1, self.seq_size)]

    def greet(self, corners=False):
        barrier = pltpu.get_barrier_semaphore()
        for friend in self.friends(corners):
            pl.semaphore_signal(barrier, inc=1, device_id=friend, device_id_type=MESH)

    def meet(self, corners=False):
        pl.semaphore_wait(pltpu.get_barrier_semaphore(), len(self.friends(corners)))


def remote(src, dst, send, recv, device):
    return pltpu.make_async_remote_copy(
        src_ref=src, dst_ref=dst, send_sem=send, recv_sem=recv, device_id=device, device_id_type=MESH
    )


class Spread:
    def __init__(self, place, shard, full, out, into, local):
        self.place, self.shard, self.full, self.out, self.into, self.local = place, shard, full, out, into, local

    def column(self, n, core=None):
        y, x = self.place.columns[n]
        return self.full.at[:, y, x, self.place.core if core is None else core]

    def line_copy(self, k):
        place = self.place
        here = self.full.at[place.z, place.y, place.x, place.core]
        return remote(self.shard, here, self.out.at[6 + k], self.into.at[6 + k], place.above(k))

    def own_copy(self):
        place = self.place
        return pltpu.make_async_copy(self.shard, self.full.at[place.z, place.y, place.x, place.core], self.local)

    def copy(self, n, lane):
        here = self.column(n)
        device = (self.place.first, self.place.second, self.place.second)[lane] if lane < 3 else self.place.other_core
        return remote(here, here, self.out.at[lane], self.into.at[lane], device())

    def arrive(self, n, lane):
        self.copy(n, lane).wait_recv()

    def start(self):
        self.own_copy().start()
        for k in range(1, self.place.depth):
            self.line_copy(k).start()

    def send_line(self):
        self.own_copy().wait()
        for k in range(1, self.place.depth):
            self.line_copy(k).wait_recv()
        for lane in (0, 1, 3):
            self.copy(0, lane).start()

    def forward_first(self):
        self.arrive(1, 0)
        self.copy(1, 2).start()
        self.copy(1, 4).start()

    def forward_second(self, half):
        self.arrive(2 + half, 1 + half)
        self.copy(2 + half, 5 + half).start()

    def finish(self):
        for n in range(4):
            self.arrive(n, 3 + n)
        for k in range(1, self.place.depth):
            self.line_copy(k).wait_send()
        for lane in range(7):
            self.copy(0, lane).wait_send()


def spread_sems(depth):
    sems = pltpu.SemaphoreType.DMA
    return [sems((6 + depth,)), sems((6 + depth,)), sems]


class Results:
    def result_copy(self, n, other):
        y, x = self.place.columns[(0, 2, 1, 3)[n] if other else n]
        core = 1 - self.place.core if other else self.place.core
        here = (slice(None), y, x, core)
        return pltpu.make_async_copy(self.full.at[here], self.result.at[here], self.results.at[n, other])

    def land(self, n):
        self.arrive_core(n)
        for other in range(2):
            self.result_copy(n, other).start()

    def finish(self):
        for n in range(4):
            for other in range(2):
                self.result_copy(n, other).wait()
        self.sent()


class Gather(Results, Spread):
    def __init__(self, place, shard, full, result, out, into, local, results):
        Spread.__init__(self, place, shard, full, out, into, local)
        self.result, self.results = result, results

    def arrive_core(self, n):
        self.arrive(n, 3 + n)

    def sent(self):
        for k in range(1, self.place.depth):
            self.line_copy(k).wait_send()
        for lane in range(7):
            self.copy(0, lane).wait_send()


def gather_sems(depth):
    return spread_sems(depth) + [pltpu.SemaphoreType.DMA((4, 2))]


class Reduce:
    def __init__(self, place, part, from_core, held, from_second, pair, from_first, line, from_line, out, into, local):
        self.place, self.part, self.local = place, part, local
        self.from_core, self.held, self.from_second, self.pair = from_core, held, from_second, pair
        self.from_first, self.line, self.from_line = from_first, line, from_line
        self.out, self.into = out, into

    def copy(self, src, dst, lane, device):
        return remote(src, dst, self.out.at[lane], self.into.at[lane], device)

    def own_copy(self):
        return pltpu.make_async_copy(self.part.at[:, :, :, self.place.core], self.held, self.local)

    def core_copy(self):
        return self.copy(self.part.at[:, :, :, 1 - self.place.core], self.from_core, 0, self.place.other_core())

    def second_copies(self):
        columns = self.place.columns
        return [
            self.copy(self.held.at[:, columns[2 + k][0], columns[2 + k][1]], self.from_second.at[k], 1 + k,
                      self.place.second())
            for k in range(2)
        ]

    def first_copy(self):
        return self.copy(self.pair.at[1], self.from_first, 3, self.place.first())

    def line_copies(self):
        place = self.place
        return [
            self.copy(self.line.at[place.ahead(k)], self.from_line.at[k - 1], 3 + k, place.above(k))
            for k in range(1, place.depth)
        ]

    def to_core(self):
        self.core_copy().start()
        self.own_copy().start()

    def to_second(self):
        self.own_copy().wait()
        self.core_copy().wait()
        self.held[...] += self.from_core[...]
        for copy in self.second_copies():
            copy.start()

    def to_first(self):
        for copy in self.second_copies():
            copy.wait()
        for k in range(2):
            y, x = self.place.columns[k]
            self.pair[k] = self.held[:, y, x] + self.from_second[k]
        self.first_copy().start()

    def to_line(self):
        self.first_copy().wait()
        self.line[...] = self.pair[0] + self.from_first[...]
        for copy in self.line_copies():
            copy.start()

    def last(self):
        for copy in self.line_copies():
            copy.wait()
        result = self.line[self.place.z].astype(f32)
        for k in range(self.place.depth - 1):
            result = result + self.from_line[k].astype(f32)
        return result


def reduce_scratch(depth, rows, cols):
    shapes = [(depth, 2, 2), (depth, 2, 2), (2, depth), (2, depth), (depth,), (depth,), (depth - 1,)]
    sems = pltpu.SemaphoreType.DMA
    return [pltpu.VMEM(shape + (rows, cols), bf16) for shape in shapes] + [sems((3 + depth,))] * 2 + [sems]


class ShortReduce:
    def __init__(self, place, part, from_octant, line, from_line, out, into):
        self.place, self.part, self.from_octant, self.line, self.from_line = place, part, from_octant, line, from_line
        self.out, self.into = out, into

    def octant_copy(self, n):
        device, (y, x, core) = self.place.octant(n)
        return remote(
            self.part.at[:, y, x, core], self.from_octant.at[n - 1], self.out.at[n - 1], self.into.at[n - 1], device
        )

    def line_copy(self, k):
        return remote(
            self.line.at[self.place.ahead(k)], self.from_line.at[k - 1], self.out.at[6 + k], self.into.at[6 + k],
            self.place.above(k)
        )

    def start(self):
        for n in range(1, 8):
            self.octant_copy(n).start()

    def to_line(self):
        place = self.place
        total = self.part[:, place.y, place.x, place.core].astype(f32)
        for n in range(1, 8):
            self.octant_copy(n).wait()
            total = total + self.from_octant[n - 1].astype(f32)
        self.line[...] = total.astype(bf16)
        for k in range(1, place.depth):
            self.line_copy(k).start()

    def last(self):
        total = self.line[self.place.z].astype(f32)
        for k in range(1, self.place.depth):
            self.line_copy(k).wait()
            total = total + self.from_line[k - 1].astype(f32)
        return total


def short_reduce_scratch(depth, rows, cols):
    sems = pltpu.SemaphoreType.DMA
    shapes = [(depth, 2, 2, 2), (7, depth), (depth,), (depth - 1,)]
    return [pltpu.VMEM(shape + (rows, cols), bf16) for shape in shapes] + [sems((6 + depth,))] * 2


def norm_rows(rows):
    centred = rows - jnp.mean(rows, axis=1, keepdims=True)
    inverse = lax.rsqrt(jnp.mean(centred * centred, axis=1, keepdims=True) + EPSILON)
    return centred * inverse, inverse


def norm_back(grad, scaled, inverse, gain):
    inner = grad * gain
    return inverse * (
        inner
        - jnp.mean(inner, axis=1, keepdims=True)
        - scaled * jnp.mean(inner * scaled, axis=1, keepdims=True)
    )


def gelu_both(v):
    power = jnp.exp2(v * v * (-0.5 * LOG2E))
    cdf = 0.5 + 0.5 * lax.erf(v * math.sqrt(0.5))
    return v * cdf, cdf + v * power * (1.0 / math.sqrt(2.0 * math.pi))


def column_sum(rows):
    return jnp.sum(rows.astype(f32), axis=0, keepdims=True)


def to_columns(rows):
    count, width = rows.shape
    return jnp.transpose(jnp.concatenate([rows, jnp.zeros((LANES - count, width), f32)], axis=0)).astype(bf16)


def own_text(ref, text, seq):
    slots, width = ref.shape
    own = jnp.zeros((text, width), ref.dtype)
    for r in range(-(-slots // text)):
        share = ref[r * text : min(slots, (r + 1) * text), :]
        if share.shape[0] < text:
            share = jnp.concatenate([share, jnp.zeros((text - share.shape[0], width), ref.dtype)], axis=0)
        own = jnp.where(seq == r, share, own)
    return own


def as_columns(vectors):
    length = vectors[0].shape[0]
    rows = [vector.reshape(1, length).astype(f32) for vector in vectors]
    rows = jnp.concatenate(rows + [jnp.zeros((LANES - len(rows), length), f32)], axis=0)
    rows = jnp.concatenate([rows, jnp.zeros((LANES, LANES - length), f32)], axis=1)
    return jnp.transpose(rows)[:length].astype(bf16)


def collect(dst, blocks, patch, text):
    count, width = len(blocks), blocks[0].shape[1]
    for r, block in enumerate(blocks):
        dst[r * patch : (r + 1) * patch, :width] = block[:patch]
        at = count * patch + r * text
        dst[at : at + text, :width] = block[patch:]
    filled = count * (patch + text)
    if dst.shape[0] > filled:
        dst[filled:, :width] = jnp.zeros((dst.shape[0] - filled, width), dst.dtype)


def by_head(dst, src, lane, heads, ones):
    count, width = src.shape
    for h in range(heads):
        rows = slice(h * count, (h + 1) * count)
        dst[rows, :width] = jnp.where(lane == h, src, jnp.zeros_like(src))
        if ones:
            dst[rows, width:] = jnp.where(lane == h, jnp.ones_like(src), jnp.zeros_like(src))


def forward_kernel(seq_size, text, width, head, *refs):
    refs = list(refs)

    def take(number):
        taken = refs[:number]
        del refs[:number]
        return taken

    (shard_ref,), vec_refs = take(1), take(8)
    up_ref, up_bias_ref, out_w_ref, down_ref, x_any, slot_ref, length_ref = take(7)
    w_out, w2_out, vecs, bias_ref, full_a, full_b, xtext_ref, first_out, q_out, out_out, rest_out, log_out = take(12)
    k_outs, v_outs = take(seq_size), take(seq_size)
    shard, shard2, shard_a, shard_b, w_full, w2_full, into_a, into_b, x_s, n_s, first_s, q_s, k_s, v_s = take(14)
    keys, values, text_keys, text_values, out_s, rest_s, log_s = take(7)
    sems, sems2, sems_a, sems_b = take(3), take(3), take(4), take(4)
    x_sem, w_sem, out_sem, kv_sem, kv_in_sem, kv_out_sem, turn_sem = take(7)
    items, patch, model = x_s.shape
    units, wide = up_ref.shape[1], shard2.shape[1]
    pairs = model // width
    place = Place(w_full.shape[0], seq_size)
    seq = lax.axis_index("seq")
    x_copies = [pltpu.make_async_copy(x_any.at[i], x_s.at[i], x_sem.at[i]) for i in range(items)]
    for copy in x_copies:
        copy.start()
    place.greet()
    for half, to in enumerate((shard, shard2)):
        for n in range(3):
            at = (n + 1) % 3 * model + half * (model // 2)
            to[:, n * (model // 2) : (n + 1) * (model // 2)] = shard_ref[:, at : at + model // 2]
    shard[:, wide:] = as_columns([ref[...] for ref in vec_refs])
    place.meet()
    halves = [Spread(place, shard, w_full, *sems), Spread(place, shard2, w2_full, *sems2)]
    for move in halves:
        move.start()
    shard_a[:, :units] = up_ref[...]
    shard_a[:, units:] = out_w_ref[...]
    shard_b[:, :model] = down_ref[...]
    shard_b[:, model:] = as_columns([up_bias_ref[...]])
    move_a, move_b = Gather(place, shard_a, into_a, full_a, *sems_a), Gather(place, shard_b, into_b, full_b, *sems_b)
    tail = bias_ref.shape[2]
    col = lax.broadcasted_iota(jnp.int32, (1, tail), 1)
    slot = jnp.full((1, tail), seq_size * text, jnp.int32)
    for r in range(seq_size):
        begin = lax.rem(seq + r, seq_size) * text
        slot = jnp.where((col >= r * text) & (col < (r + 1) * text), begin + col - r * text, slot)
    for i in range(items):
        xtext_ref[i] = own_text(slot_ref.at[i], text, seq)
        bias_ref[i] = jnp.where(slot < length_ref[i], 0.0, NEG_FILL)
    halves[0].send_line()
    halves[1].send_line()
    move_a.start()
    move_b.start()
    for i in range(items):
        x_copies[i].wait()
        n_s[i], _ = norm_rows(jnp.concatenate([x_s[i], xtext_ref[i]], axis=0).astype(f32))
    halves[0].forward_first()
    halves[0].forward_second(0)
    halves[1].forward_first()
    halves[0].forward_second(1)
    halves[1].forward_second(0)
    halves[0].finish()
    move_a.send_line()
    w_copies = [pltpu.make_async_copy(src, dst, w_sem.at[n]) for n, (src, dst) in
                enumerate(((w_full, w_out), (w2_full, w2_out)))]
    w_copies[0].start()
    weight = w_full[...].reshape(model, wide + LANES)
    table = jnp.transpose(weight[:, wide:].astype(f32))
    vecs[...] = table
    scale = LOG2E / math.sqrt(model // HEADS)
    sends, outs = [], []

    def keys_and_values(i, half, weight):
        span = model // 2
        cols = pl.ds(half * span, span)
        projected = mm(first_s[i], weight[:, : 2 * span])
        k_s[0, i, :, cols] = projected[:, :span].astype(bf16)
        v_s[0, i, :, cols] = (projected[:, span:] + table[VBIAS : VBIAS + 1, half * span : (half + 1) * span]).astype(bf16)
        for r in range(1, seq_size):
            for n, ref in enumerate((k_s, v_s)):
                at = ((2 * i + n) * 2 + half) * seq_size + r
                src, dst = ref.at[0, i, :, cols], ref.at[r, i, :, cols]
                sends.append(remote(src, dst, kv_sem.at[at], kv_in_sem.at[at], place.mate(r)))
                sends[-1].start()

    def queries(i, half, weight):
        span = model // 2
        q = mm(first_s[i], weight[:, 2 * span : 3 * span]) + table[QBIAS : QBIAS + 1, half * span : (half + 1) * span]
        q_s[i, :, half * span : (half + 1) * span] = (q * scale).astype(bf16)

    def bring(n, src, dst, i):
        outs.append(pltpu.make_async_copy(src.at[i], dst.at[i], out_sem.at[n, i]))
        outs[-1].start()

    for i in range(items):
        first_s[i] = (n_s[i] * table[GAIN1 : GAIN1 + 1] + table[SHIFT1 : SHIFT1 + 1]).astype(bf16)
        bring(0, first_s, first_out, i)
        keys_and_values(i, 0, weight)
        if i == 0:
            halves[1].forward_second(1)
    halves[1].finish()
    move_b.send_line()
    w_copies[1].start()
    weight2 = w2_full[...].reshape(model, wide)
    for i in range(items):
        keys_and_values(i, 1, weight2)
        bring(1, k_s.at[0], k_outs[0], i)
        bring(2, v_s.at[0], v_outs[0], i)
    for i in range(items):
        queries(i, 0, weight)
        queries(i, 1, weight2)
        bring(3, q_s, q_out, i)

    edge, heads, span = seq_size * patch, width // head, keys.shape[0] - seq_size * patch
    lane = lax.broadcasted_iota(jnp.int32, (1, width), 1) // head
    values[:, width:] = jnp.ones((values.shape[0], values.shape[1] - width), bf16)
    last = items * pairs - 1

    def turn_copies(slot, i, cols):
        return [
            pltpu.make_async_copy(src.at[slot], dst.at[i, :, cols], turn_sem.at[slot, n])
            for n, (src, dst) in enumerate(((out_s, out_out), (rest_s, rest_out), (log_s, log_out)))
        ]

    def kv_out_copies(i):
        return [
            pltpu.make_async_copy(ref.at[r, i], dst[r].at[i], kv_out_sem.at[(2 * i + n) * seq_size + r])
            for n, (ref, dst) in enumerate(((k_s, k_outs), (v_s, v_outs)))
            for r in range(1, seq_size)
        ]

    def exchanged(i):
        for n, ref in enumerate((k_s, v_s)):
            for half in range(2):
                cols = pl.ds(half * (model // 2), model // 2)
                for r in range(1, seq_size):
                    at = ((2 * i + n) * 2 + half) * seq_size + r
                    src, dst = ref.at[0, i, :, cols], ref.at[r, i, :, cols]
                    remote(src, dst, kv_sem.at[at], kv_in_sem.at[at], place.mate(r)).wait_recv()
        for copy in kv_out_copies(i):
            copy.start()

    agenda = (
        (3, move_a.forward_first),
        (3, functools.partial(move_a.forward_second, 0)),
        (5, move_b.forward_first),
        (5, functools.partial(move_b.forward_second, 0)),
        (7, functools.partial(move_a.land, 0)),
        (7, functools.partial(move_a.land, 1)),
        (8, functools.partial(move_a.forward_second, 1)),
        (9, functools.partial(move_a.land, 2)),
        (9, functools.partial(move_b.land, 0)),
        (9, functools.partial(move_b.land, 1)),
        (10, functools.partial(move_b.forward_second, 1)),
        (10, functools.partial(move_b.land, 2)),
        (11, functools.partial(move_a.land, 3)),
        (13, functools.partial(move_b.land, 3)),
    )

    def attend(turn, _):
        i, p = turn // pairs, lax.rem(turn, pairs)
        slot = lax.rem(turn, 2)
        cols = pl.ds(pl.multiple_of(p * width, width), width)

        @pl.when(p == 0)
        def _():
            exchanged(i)

        for at in sorted({at for at, _ in agenda if at <= last}):

            @pl.when(turn == at)
            def _(at=at):
                for when, step in agenda:
                    if when == at:
                        step()

        collect(keys, [k_s[r, i, :, cols] for r in range(seq_size)], patch, text)
        collect(values, [v_s[r, i, :, cols] for r in range(seq_size)], patch, text)
        by_head(text_keys, keys[edge:], lane, heads, False)
        by_head(text_values, values[edge:, :width], lane, heads, True)
        q = q_s[i, :, cols]
        text_bias = jnp.concatenate([bias_ref[i]] * heads, axis=1)

        def scores_of(h):
            return mm_t(jnp.where(lane == h, q, jnp.zeros_like(q)), keys[:edge])

        text_scores = mm_t(q, text_keys[...]) + text_bias
        scores = scores_of(0)
        text_powers, mixed, total, tops = [], None, None, None
        for h in range(heads):
            following = scores_of(h + 1) if h + 1 < heads else None
            text_head = text_scores[:, h * span : (h + 1) * span]
            top = jnp.maximum(jnp.max(scores, axis=1, keepdims=True), jnp.max(text_head, axis=1, keepdims=True))
            powers = jnp.exp2(scores - top).astype(bf16)
            text_powers.append(jnp.exp2(text_head - top).astype(bf16))
            both = mm(powers, values[:edge])
            mixed = both[:, :width] if mixed is None else jnp.where(lane == h, both[:, :width], mixed)
            total = both[:, width:] if total is None else jnp.where(lane == h, both[:, width:], total)
            tops = jnp.broadcast_to(top, mixed.shape) if tops is None else jnp.where(lane == h, top, tops)
            scores = following
        both = mm(jnp.concatenate(text_powers, axis=1), text_values[...])
        total = total + both[:, width:]
        out = (mixed + both[:, :width]) * (1.0 / total)
        high = out.astype(bf16)

        @pl.when(turn > 1)
        def _():
            for copy in turn_copies(slot, i, cols):
                copy.wait()

        out_s[slot] = high
        rest_s[slot] = (out - high.astype(f32)).astype(bf16)
        log_s[slot] = tops + jnp.log2(total)
        for copy in turn_copies(slot, i, cols):
            copy.start()
        return 0

    lax.fori_loop(0, last + 1, attend, 0)
    for when, step in agenda:
        if when > last:
            step()
    move_a.finish()
    move_b.finish()
    for slot in range(2):
        for copy in turn_copies(slot, 0, pl.ds(0, width)):
            copy.wait()
    for copy in sends:
        copy.wait_send()
    for i in range(items):
        for copy in kv_out_copies(i):
            copy.wait()
    for copy in w_copies + outs:
        copy.wait()


def forward(in_weight, vectors, up_weight, up_bias, out_weight, down_weight, patches, text_rows, lengths, text, width,
            head, devices, seq_size):
    items, patch, model = patches.shape
    depth, heads = devices // 8, width // head
    rows, cols = in_weight.shape
    shape_a = (depth, 2, 2, 2, rows, up_weight.shape[1] + model)
    shape_b = (depth, 2, 2, 2, down_weight.shape[0], model + LANES)
    shape_w = (depth, 2, 2, 2, rows, cols // 2 + LANES)
    shape_w2 = (depth, 2, 2, 2, rows, cols // 2)
    shape_x = (items, patch + text, model)
    tail = round_up(seq_size * text, LANES)
    span = seq_size * patch + tail
    tokens = jax.ShapeDtypeStruct(shape_x, bf16)
    sems = pltpu.SemaphoreType.DMA
    outs = pl.pallas_call(
        functools.partial(forward_kernel, seq_size, text, width, head),
        in_specs=[WHOLE] * 13 + [ANY, WHOLE, pl.BlockSpec(memory_space=pltpu.SMEM)],
        out_specs=[ANY, ANY, WHOLE, WHOLE, ANY, ANY, WHOLE] + [ANY] * (5 + 2 * seq_size),
        out_shape=[
            jax.ShapeDtypeStruct(shape_w, bf16),
            jax.ShapeDtypeStruct(shape_w2, bf16),
            jax.ShapeDtypeStruct((LANES, model), f32),
            jax.ShapeDtypeStruct((items, 1, tail), f32),
            jax.ShapeDtypeStruct(shape_a, bf16),
            jax.ShapeDtypeStruct(shape_b, bf16),
            jax.ShapeDtypeStruct((items, text, model), bf16),
            tokens,
            tokens,
            tokens,
            tokens,
            jax.ShapeDtypeStruct(shape_x, f32),
        ]
        + [tokens] * (2 * seq_size),
        scratch_shapes=[
            pltpu.VMEM(shape_w[4:], bf16),
            pltpu.VMEM(shape_w2[4:], bf16),
            pltpu.VMEM(shape_a[4:], bf16),
            pltpu.VMEM(shape_b[4:], bf16),
            pltpu.VMEM(shape_w, bf16),
            pltpu.VMEM(shape_w2, bf16),
            pltpu.VMEM(shape_a, bf16),
            pltpu.VMEM(shape_b, bf16),
            pltpu.VMEM(patches.shape, bf16),
            pltpu.VMEM(shape_x, f32),
            pltpu.VMEM(shape_x, bf16),
            pltpu.VMEM(shape_x, bf16),
            pltpu.VMEM((seq_size,) + shape_x, bf16),
            pltpu.VMEM((seq_size,) + shape_x, bf16),
            pltpu.VMEM((span, width), bf16),
            pltpu.VMEM((span, 2 * width), bf16),
            pltpu.VMEM((heads * tail, width), bf16),
            pltpu.VMEM((heads * tail, 2 * width), bf16),
            pltpu.VMEM((2, patch + text, width), bf16),
            pltpu.VMEM((2, patch + text, width), bf16),
            pltpu.VMEM((2, patch + text, width), f32),
        ]
        + spread_sems(depth) * 2
        + gather_sems(depth) * 2
        + [sems((items,)), sems((2,)), sems((4, items))]
        + [sems((4 * items * seq_size,))] * 2
        + [sems((2 * items * seq_size,)), sems((2, 3))],
        compiler_params=compiler_params(collective_id=0, has_side_effects=True),
        name="forward",
    )(in_weight, *vectors, up_weight, up_bias, out_weight, down_weight, patches, text_rows, lengths)
    w_in, weights = ([full.reshape(-1, full.shape[-1]) for full in pair] for pair in (outs[:2], outs[4:6]))
    return w_in, *outs[2:4], weights, *outs[6:12], outs[12 : 12 + seq_size], outs[12 + seq_size :]


def ffn_kernel(steps, chunk, part, seq_ref, x_ref, xtext_ref, at_ref, dy_ref, dy_slot_ref, w_any, wd_any, vec_ref,
               res_ref, restext_ref, gb_ref, ga_ref, part_out, down_out,
               w_ref, wd_ref, part_ref, down_ref, second_s, hidden_s, pre_s, dy_s, sums_s, bias_s, out_s,
               w_sem, wd_sem, part_sem, down_sem):
    step = pl.program_id(0)
    patch, model = x_ref.shape[1:]
    text = xtext_ref.shape[1]
    block, units = patch + text, wd_ref.shape[0]
    chunks = units // chunk
    rows = pl.ds(pl.multiple_of(step * block, ROW_TILE), block)
    gain = vec_ref[GAIN2 : GAIN2 + 1]
    w_out = w_ref.at[:, units:]

    def fetch(cols, at):
        if cols is None:
            return (
                pltpu.make_async_copy(w_any.at[:, units:], w_ref.at[:, units:], w_sem.at[at]),
                pltpu.make_async_copy(wd_any.at[:, model:], wd_ref.at[:, model:], wd_sem.at[at]),
            )
        return (
            pltpu.make_async_copy(w_any.at[:, cols], w_ref.at[:, cols], w_sem.at[at]),
            pltpu.make_async_copy(wd_any.at[cols, :model], wd_ref.at[cols, :model], wd_sem.at[at]),
        )

    @pl.when(step == 0)
    def _():
        others = fetch(None, chunks)
        for copy in others:
            copy.start()
        for c in range(chunks):
            for copy in fetch(pl.ds(c * chunk, chunk), c):
                copy.start()
        sums_s[...] = jnp.zeros_like(sums_s)
        for copy in others:
            copy.wait()
        bias_s[...] = jnp.transpose(wd_ref[:, model:].astype(f32))[:8]

    x = jnp.concatenate([x_ref[0], xtext_ref[0]], axis=0).astype(f32)
    dy = jnp.concatenate([dy_ref[0], own_text(dy_slot_ref.at[0], text, seq_ref[0])], axis=0)
    dy_s[rows, :] = dy
    middle = x + (mm(at_ref[0], w_out[...]) + vec_ref[BRANCH : BRANCH + 1])
    scaled, inverse = norm_rows(middle)
    second_in = (scaled * gain + vec_ref[SHIFT2 : SHIFT2 + 1]).astype(bf16)
    second_s[rows, :] = second_in
    @pl.when(step == 0)
    def _():
        for c in range(chunks):
            for copy in fetch(pl.ds(c * chunk, chunk), c):
                copy.wait()

    def first_dots(c):
        cols = slice(c * part, (c + 1) * part)
        return mm(second_in, w_ref[:, cols]) + bias_s[:1, cols], mm_t(dy, wd_ref[cols, :model])

    result, grad_second = middle + vec_ref[DOWNB : DOWNB + 1], None
    pre, grad_hidden = first_dots(0)
    for c in range(units // part):
        following = first_dots(c + 1) if c + 1 < units // part else (None, None)
        cols = slice(c * part, (c + 1) * part)
        value, slope = gelu_both(pre)
        hidden = value.astype(bf16)
        hidden_s[rows, cols] = hidden
        grad_pre = (grad_hidden * slope).astype(bf16)
        pre_s[rows, cols] = grad_pre
        result = result + mm(hidden, wd_ref[cols, :model])
        back_part = mm_t(grad_pre, w_ref[:, cols])
        grad_second = back_part if grad_second is None else grad_second + back_part
        pre, grad_hidden = following
    result = result.astype(bf16)
    res_ref[0] = result[:patch]
    restext_ref[0] = result[patch:]
    grad_branch = (dy.astype(f32) + norm_back(grad_second, scaled, inverse, gain)).astype(bf16)
    gb_ref[0] = grad_branch
    ga_ref[0] = mm_t(grad_branch, w_out[...]).astype(bf16)
    out_grad = t_mm(at_ref[0], grad_branch)

    @pl.when(step == 0)
    def _():
        out_s[...] = out_grad

    @pl.when(step > 0)
    def _():
        out_s[...] += out_grad

    for at, grad in ((BRANCH, grad_branch), (GAIN2, grad_second * scaled), (SHIFT2, grad_second), (DOWNB, dy)):
        sums_s[at : at + 1, :] += column_sum(grad)

    @pl.when(step == steps - 1)
    def _():
        groups = units // model
        copies = []
        part_ref[:, units : units + model] = out_s[...].astype(bf16)
        part_ref[:, units + model :] = to_columns(sums_s[...])
        copies.append(pltpu.make_async_copy(part_ref.at[:, units:], part_out.at[:, units:], part_sem.at[groups]))
        copies[-1].start()
        for c in range(groups):
            cols = slice(c * model, (c + 1) * model)
            at = pl.ds(c * model, model)
            grad_pre = pre_s[:, cols]
            part_ref[:, cols] = t_mm(second_s[...], grad_pre).astype(bf16)
            copies.append(pltpu.make_async_copy(part_ref.at[:, at], part_out.at[:, at], part_sem.at[c]))
            copies[-1].start()
            down_ref[cols, :model] = jnp.transpose(t_mm(dy_s[...], hidden_s[:, cols])).astype(bf16)
            down_ref[cols, model:] = to_columns(column_sum(grad_pre))
            copies.append(pltpu.make_async_copy(down_ref.at[at], down_out.at[at], down_sem.at[c]))
            copies[-1].start()
        for copy in copies:
            copy.wait()


def ffn(seq, patches, x_text, attended, patch_cotangent, text_cotangent, weights, w_down, vecs):
    items, patch, model = patches.shape
    units, rows, text, slots = w_down.shape[0], attended.shape[1], x_text.shape[1], text_cotangent.shape[1]

    def item(count):
        return pl.BlockSpec((1, count, model), lambda i: (i, 0, 0))

    def shape(count):
        return jax.ShapeDtypeStruct((items, count, model), bf16)

    return pl.pallas_call(
        functools.partial(ffn_kernel, items, 1024, 256),
        grid=(items,),
        in_specs=[pl.BlockSpec(memory_space=pltpu.SMEM)]
        + [item(patch), item(text), item(rows), item(patch), item(slots)]
        + [ANY, ANY, WHOLE],
        out_specs=[item(patch), item(text), item(rows), item(rows), ANY, ANY],
        out_shape=[shape(patch), shape(text), shape(rows), shape(rows)]
        + [
            jax.ShapeDtypeStruct((model, units + model + LANES), bf16),
            jax.ShapeDtypeStruct((units, model + LANES), bf16),
        ],
        scratch_shapes=[
            pltpu.VMEM(weights.shape, bf16),
            pltpu.VMEM(w_down.shape, bf16),
            pltpu.VMEM((model, units + model + LANES), bf16),
            pltpu.VMEM((units, model + LANES), bf16),
            pltpu.VMEM((items * rows, model), bf16),
            pltpu.VMEM((items * rows, units), bf16),
            pltpu.VMEM((items * rows, units), bf16),
            pltpu.VMEM((items * rows, model), bf16),
            pltpu.VMEM((8, model), f32),
            pltpu.VMEM((8, units), f32),
            pltpu.VMEM((model, model), f32),
        ]
        + [pltpu.SemaphoreType.DMA((units // 1024 + 1,))] * 2
        + [pltpu.SemaphoreType.DMA((units // model + 1,))] * 2,
        compiler_params=compiler_params(),
        name="ffn",
    )(seq, patches, x_text, attended, patch_cotangent, text_cotangent, weights, w_down, vecs)


def back_kernel(count, patch, head, seq_size, pairs, items, *refs):
    refs = list(refs)

    def take(number):
        taken = refs[:number]
        del refs[:number]
        return taken

    (q_ref,), k_refs, v_refs = take(1), take(count), take(count)
    bias_ref, log_ref, at_ref, rest_ref, grad_ref = take(5)
    part_a, part_b, w_any, w2_any, vec_ref, first_any, x_any, xtext_any, gb_any, restext_any = take(10)
    grad_out, text_grad_out, text_out, total_a, total_b, total_in, vec_out, vec2_out, upb_out = take(9)
    keys, values, text_keys, text_values, probs_s, scores_s = take(6)
    mixed_s, own_s, dkv_out, dkv_in, sums_s = take(5)
    w_s, w2_s, first_s, x_s, xtext_s, gb_s, text_s, patch_s = take(8)
    first_grad_s, scaled_s, inverse_s = take(3)
    fetch_sem, dkv_sem, dkv_in_sem, text_sem, text_in_sem, patch_sem = take(6)
    scratch_a, scratch_b = take(10), take(10)
    scratch_in = [take(11) for _ in range(2)]
    scratch_last, scratch_vec = take(6), take(6)

    width, rows = q_ref.shape[2], q_ref.shape[1]
    text, model = rows - patch, pairs * width
    place = Place(part_a.shape[0], seq_size)
    seq = lax.axis_index("seq")
    p, i = pl.program_id(0), pl.program_id(1)
    turn, last = p * items + i, pairs * items - 1
    sums_a, sums_b = Reduce(place, part_a, *scratch_a), Reduce(place, part_b, *scratch_b)
    chunks = ((0, pairs - 2), (pairs - 2, pairs - 1), (pairs - 1, pairs))
    sums_in = [Reduce(place, each[0], *each[1:]) for each in scratch_in]
    sums_in.append(ShortReduce(place, *scratch_last))
    sums_vec = ShortReduce(place, *scratch_vec)
    fetches = [
        pltpu.make_async_copy(src, dst, fetch_sem.at[n])
        for n, (src, dst) in enumerate(
            ((first_any, first_s), (w_any, w_s), (w2_any, w2_s), (x_any, x_s), (xtext_any, xtext_s), (gb_any, gb_s))
        )
    ]

    def text_copies(src, dst, row):
        to = dst.at[:, pl.ds(pl.multiple_of(seq * text, ROW_TILE), text)]
        own = pltpu.make_async_copy(src, to, text_sem.at[row, 0])
        away = [
            remote(src, to, text_sem.at[row, r], text_in_sem.at[row, r], place.mate(r)) for r in range(1, seq_size)
        ]
        return [own] + away

    def begin():
        place.meet(corners=True)
        sums_a.to_core()
        sums_b.to_core()
        for copy in text_copies(restext_any, text_out, 0):
            copy.start()

    def dkv_copy(slot, r):
        return remote(
            dkv_out.at[slot, r - 1], dkv_in.at[slot, r - 1], dkv_sem.at[slot, r - 1], dkv_in_sem.at[slot, r - 1],
            place.mate(-r)
        )

    def settle(of):
        slot, pair, item = lax.rem(of, 2), of // items, lax.rem(of, items)
        total = own_s[slot]
        for r in range(1, seq_size):
            dkv_copy(slot, r).wait_recv()
            total = total + dkv_in[slot, r - 1].astype(f32)
        at = pl.ds(pl.multiple_of(item * rows, ROW_TILE), rows)
        mixed_s[pair, at, width:] = total.astype(bf16)

    def pair_done(pair):
        mixed = mixed_s[pair]
        if pair == 0:
            fetches[0].wait()
        grad = t_mm(first_s[...].reshape(items * rows, model), mixed).astype(bf16)
        chunk = sum(pair >= first for first, _ in chunks) - 1
        first, end = chunks[chunk]
        part = sums_in[chunk].part
        part[..., 3 * (pair - first) * width : 3 * (pair - first + 1) * width] = grad.reshape(
            part.shape[:-1] + (3 * width,)
        )
        if pair == end - 1:
            (sums_in[chunk].start if end == pairs else sums_in[chunk].to_core)()
        cols = slice(pair * width, (pair + 1) * width)
        sums_s[QBIAS : QBIAS + 1, cols] = column_sum(mixed[:, :width])
        sums_s[VBIAS : VBIAS + 1, cols] = column_sum(mixed[:, 2 * width :])

    def finish_in(chunk):
        total = sums_in[chunk].last()
        first, end = chunks[chunk]
        for m in range(end - first):
            for n in range(3):
                at, of = n * model + (first + m) * width, (3 * m + n) * width
                total_in[:, at : at + width] = total[:, of : of + width]

    def finish_a():
        total = sums_a.last()
        total_a[...] = total[:, : total_a.shape[1]]
        vec2_out[...] = total[:, total_a.shape[1] :]

    def finish_b():
        total = sums_b.last()
        total_b[...] = total[:, :model]
        upb_out[...] = total[:, model:]

    tail_at = last + 1
    agenda = [(2, sums_a.to_second), (3, sums_b.to_second), (6, sums_a.to_first), (7, sums_b.to_first),
              (9, sums_a.to_line), (10, sums_b.to_line), (tail_at, finish_a), (tail_at + 2, finish_b)]
    turns_in = ((9, 11, tail_at, tail_at + 1), (11, tail_at, tail_at + 1, tail_at + 2))
    for chunk, turns in enumerate(turns_in):
        steps = (sums_in[chunk].to_second, sums_in[chunk].to_first, sums_in[chunk].to_line)
        steps += (functools.partial(finish_in, chunk),)
        agenda += [(max(at, items * chunks[chunk][1] + 2), step) for at, step in zip(turns, steps)]
    agenda += [(tail_at + 1, sums_in[2].to_line), (tail_at + 3, functools.partial(finish_in, 2))]
    agenda.sort(key=lambda entry: entry[0])

    @pl.when(turn == 0)
    def _():
        place.greet(corners=True)
        for copy in fetches:
            copy.start()
        sums_s[...] = jnp.zeros_like(sums_s)

    collect(keys, [ref[0] for ref in k_refs], patch, text)
    collect(values, [ref[0] for ref in v_refs], patch, text)
    q, grad = q_ref[0], grad_ref[0]
    edge, heads, span = count * patch, width // head, keys.shape[0] - count * patch
    lane = lax.broadcasted_iota(jnp.int32, (1, width), 1) // head
    row = lax.broadcasted_iota(jnp.int32, (width, 1), 0) // head
    by_head(text_keys, keys[edge:], lane, heads, False)
    by_head(text_values, values[edge:], lane, heads, False)
    text_bias = jnp.concatenate([bias_ref[0]] * heads, axis=1)
    inner = grad.astype(f32) * (at_ref[0].astype(f32) + rest_ref[0].astype(f32))
    q_heads = [jnp.where(lane == h, q, jnp.zeros_like(q)) for h in range(heads)]
    grad_heads = [jnp.where(lane == h, grad, jnp.zeros_like(grad)) for h in range(heads)]
    deltas = [jnp.sum(jnp.where(lane == h, inner, 0.0), axis=1, keepdims=True) for h in range(heads)]
    logs = [log_ref[0, :, h * head : h * head + 1] for h in range(heads)]

    def first_dots(h):
        return mm_t(q_heads[h], keys[:edge]), mm_t(grad_heads[h], values[:edge])

    scores, grad_probs = first_dots(0)
    text_scores = mm_t(q, text_keys[...]) + text_bias
    text_grad_probs = mm_t(grad, text_values[...])
    dq, text_probs, text_grads = None, [], []
    for h in range(heads):
        following = first_dots(h + 1) if h + 1 < heads else (None, None)
        cols = slice(h * span, (h + 1) * span)
        text_head = jnp.exp2(text_scores[:, cols] - logs[h])
        text_probs.append(text_head.astype(bf16))
        text_grads.append((text_head * (text_grad_probs[:, cols] - deltas[h])).astype(bf16))
        probs = jnp.exp2(scores - logs[h])
        grad_scores = (probs * (grad_probs - deltas[h])).astype(bf16)
        probs_s[h * rows : (h + 1) * rows, :] = probs.astype(bf16)
        scores_s[h * rows : (h + 1) * rows, :] = grad_scores
        dq_head = mm(grad_scores, keys[:edge])
        dq = dq_head if dq is None else jnp.where(lane == h, dq_head, dq)
        scores, grad_probs = following
    text_probs, text_grads = jnp.concatenate(text_probs, axis=1), jnp.concatenate(text_grads, axis=1)
    dq = dq + mm(text_grads, text_keys[...])
    dv = jnp.transpose(t_mm(jnp.concatenate(grad_heads, axis=0), probs_s[...]))
    dk = jnp.transpose(t_mm(jnp.concatenate(q_heads, axis=0), scores_s[...])) * LN2

    def of_heads(wide):
        own = wide[:, :span]
        for h in range(1, heads):
            own = jnp.where(row == h, wide[:, h * span : (h + 1) * span], own)
        return jnp.transpose(own)

    text_dv, text_dk = of_heads(t_mm(grad, text_probs)), of_heads(t_mm(q, text_grads)) * LN2
    slot = lax.rem(turn, 2)

    @pl.when(turn == 0)
    def _():
        begin()

    for at in sorted({at for at, _ in agenda if at <= last}):

        @pl.when(turn == at - 1)
        def _(at=at):
            for when, step in agenda:
                if when == at:
                    step()

    at = pl.ds(pl.multiple_of(i * rows, ROW_TILE), rows)
    mixed_s[p, at, :width] = (dq * (1.0 / math.sqrt(head))).astype(bf16)
    own_s[slot, :patch, :width] = dk[:patch]
    own_s[slot, :patch, width:] = dv[:patch]
    own_s[slot, patch:, :width] = text_dk[:text]
    own_s[slot, patch:, width:] = text_dv[:text]

    @pl.when(turn > 0)
    def _():
        settle(turn - 1)

    @pl.when(turn > 1)
    def _():
        for r in range(1, seq_size):
            dkv_copy(slot, r).wait_send()

    for r in range(1, seq_size):
        for n, (part, text_part) in enumerate(((dk, text_dk), (dv, text_dv))):
            cols = slice(n * width, (n + 1) * width)
            dkv_out[slot, r - 1, :patch, cols] = part[r * patch : (r + 1) * patch].astype(bf16)
            dkv_out[slot, r - 1, patch:, cols] = text_part[r * text : (r + 1) * text].astype(bf16)
        dkv_copy(slot, r).start()

    for pair in range(pairs - 1):

        @pl.when(turn == items * (pair + 1))
        def _(pair=pair):
            pair_done(pair)

    @pl.when(turn == last)
    def _():
        left = [[step for when, step in agenda if when == at] for at in sorted({at for at, _ in agenda if at > last})]

        def more():
            if left:
                for step in left.pop(0):
                    step()

        half = pairs // 2
        sides = (w_s.at[:, : 3 * half * width], w2_s)

        def grad_first(item, side):
            at = slice(item * rows, (item + 1) * rows)
            mixed = [
                mixed_s[side * half + m, at, n * width : (n + 1) * width] for n in (1, 2, 0) for m in range(half)
            ]
            return mm_t(jnp.concatenate(mixed, axis=1), sides[side][...])

        for copy in fetches[1:]:
            copy.wait()
        for item in range(items):
            first_grad_s[item] = grad_first(item, 0)
        settle(last)
        pair_done(pairs - 1)
        for item in range(items):
            grad = first_grad_s[item] + grad_first(item, 1)
            first_grad_s[item] = grad
            scaled, inverse = norm_rows(jnp.concatenate([x_s[item], xtext_s[item]], axis=0).astype(f32))
            scaled_s[item] = scaled
            inverse_s[item] = jnp.broadcast_to(inverse, (rows, LANES))
            sums_s[GAIN1 : GAIN1 + 1, :] += column_sum(grad * scaled)
            sums_s[SHIFT1 : SHIFT1 + 1, :] += column_sum(grad)
        sums_vec.part[...] = to_columns(sums_s[...]).reshape(sums_vec.part.shape)
        sums_vec.start()
        more()
        gain = vec_ref[GAIN1 : GAIN1 + 1]
        patch_copies = [
            pltpu.make_async_copy(patch_s.at[item], grad_out.at[item], patch_sem.at[item]) for item in range(items)
        ]
        for item in range(items):
            grad_rows = norm_back(first_grad_s[item], scaled_s[item], inverse_s[item][:, :1], gain)
            grad_rows = (gb_s[item].astype(f32) + grad_rows).astype(bf16)
            patch_s[item] = grad_rows[:patch]
            patch_copies[item].start()
            text_s[item] = grad_rows[patch:]
            if item == 0:
                sums_vec.to_line()
            more()
        for copy in text_copies(text_s, text_grad_out, 1):
            copy.start()
        while left:
            more()
        vec_out[...] = sums_vec.last()
        for copies in (text_copies(restext_any, text_out, 0), text_copies(text_s, text_grad_out, 1)):
            for copy in copies:
                copy.wait()
        for slot in range(2):
            for r in range(1, seq_size):
                dkv_copy(slot, r).wait_send()
        for copy in patch_copies:
            copy.wait()


def back(q, keys, values, bias, logs, attended, rest, grad_att, part_a, part_b, w_in, vecs, first_in, patches, x_text,
         grad_branch, res_text, head, width, devices, seq_size):
    items, patch, model = patches.shape
    rows, text = q.shape[1], x_text.shape[1]
    count, tail, pairs, depth = len(keys), bias.shape[-1], model // width, devices // 8
    span = count * patch + tail
    block = pl.BlockSpec((1, rows, width), lambda p, i: (i, 0, p))
    parts = [part.reshape((depth, 2, 2, 2, part.shape[0] // devices, part.shape[1])) for part in (part_a, part_b)]
    (rows_a, cols_a), (rows_b, cols_b) = parts[0].shape[4:], parts[1].shape[4:]
    sems = pltpu.SemaphoreType.DMA
    others = seq_size - 1
    slots = jax.ShapeDtypeStruct((items, seq_size * text, model), bf16)
    scratch_in = []
    for cols in (3 * (pairs - 2) * width, 3 * width):
        scratch_in += [pltpu.VMEM((depth, 2, 2, 2, rows_a, cols), bf16)] + reduce_scratch(depth, rows_a, cols)
    scratch_in += short_reduce_scratch(depth, rows_a, 3 * width)
    return pl.pallas_call(
        functools.partial(back_kernel, count, patch, head, seq_size, pairs, items),
        grid=(pairs, items),
        in_specs=[block] * (1 + 2 * count)
        + [pl.BlockSpec((1, 1, tail), lambda p, i: (i, 0, 0))]
        + [block] * 4
        + [ANY] * 4
        + [WHOLE]
        + [ANY] * 5,
        out_specs=[ANY] * 3 + [WHOLE] * 6,
        out_shape=[
            jax.ShapeDtypeStruct(patches.shape, bf16),
            slots,
            slots,
            jax.ShapeDtypeStruct((rows_a, cols_a - LANES), f32),
            jax.ShapeDtypeStruct((rows_b, cols_b - LANES), f32),
            jax.ShapeDtypeStruct((rows_a, 3 * model), f32),
            jax.ShapeDtypeStruct((rows_a, LANES), f32),
            jax.ShapeDtypeStruct((rows_a, LANES), f32),
            jax.ShapeDtypeStruct((rows_b, LANES), f32),
        ],
        scratch_shapes=[
            pltpu.VMEM((span, width), bf16),
            pltpu.VMEM((span, width), bf16),
            pltpu.VMEM((width // head * tail, width), bf16),
            pltpu.VMEM((width // head * tail, width), bf16),
            pltpu.VMEM((width // head * rows, count * patch), bf16),
            pltpu.VMEM((width // head * rows, count * patch), bf16),
            pltpu.VMEM((pairs, items * rows, 3 * width), bf16),
            pltpu.VMEM((2, rows, 2 * width), f32),
            pltpu.VMEM((2, others, rows, 2 * width), bf16),
            pltpu.VMEM((2, others, rows, 2 * width), bf16),
            pltpu.VMEM((8, model), f32),
            pltpu.VMEM(w_in[0].shape, bf16),
            pltpu.VMEM(w_in[1].shape, bf16),
            pltpu.VMEM(first_in.shape, bf16),
            pltpu.VMEM(patches.shape, bf16),
            pltpu.VMEM(x_text.shape, bf16),
            pltpu.VMEM(grad_branch.shape, bf16),
            pltpu.VMEM(x_text.shape, bf16),
            pltpu.VMEM(patches.shape, bf16),
            pltpu.VMEM(q.shape, f32),
            pltpu.VMEM(q.shape, f32),
            pltpu.VMEM((items, rows, LANES), f32),
            sems((6,)),
            sems((2, others)),
            sems((2, others)),
            sems((2, seq_size)),
            sems((2, seq_size)),
            sems((items,)),
        ]
        + reduce_scratch(depth, rows_a, cols_a)
        + reduce_scratch(depth, rows_b, cols_b)
        + scratch_in
        + short_reduce_scratch(depth, rows_a, LANES),
        compiler_params=compiler_params(collective_id=2, has_side_effects=True),
        name="back",
    )(q, *keys, *values, bias, logs, attended, rest, grad_att, *parts, *w_in, vecs, first_in, patches, x_text,
      grad_branch, res_text)


def outputs_kernel(*refs):
    text_any, patch_any, text_grad_any, total_a, total_b, total_in, vec1, vec2, upb = refs[:9]
    outs = list(refs[9:25])
    out_text, patch_out, grad_text = outs[:3]
    first_gain, first_shift, in_weight, query_bias, value_bias, out_weight, branch_bias = outs[3:10]
    second_gain, second_shift, up_weight, up_bias, down_weight, down_bias = outs[10:]
    patch_s, text_s, text_grad_s, sem = refs[25:]
    items, slots, units = patch_s.shape[0], out_text.shape[1], up_weight.shape[1]
    fetches = [pltpu.make_async_copy(patch_any.at[i], patch_s.at[i], sem.at[0, i]) for i in range(items)]
    stores = [pltpu.make_async_copy(patch_s.at[i], patch_out.at[i], sem.at[1, i]) for i in range(items)]
    texts = [
        pltpu.make_async_copy(text_any, text_s, sem.at[2, 0]),
        pltpu.make_async_copy(text_grad_any, text_grad_s, sem.at[2, 1]),
    ]
    for copy in fetches + texts:
        copy.start()

    count, wide = vec1.shape[0], upb.shape[0]
    empty = jnp.zeros((LANES - 2 * count - wide, LANES), f32)
    table = jnp.transpose(jnp.concatenate([upb[...], vec1[...], vec2[...], empty], axis=0))
    in_weight[...] = total_in[...]
    out_weight[...] = total_a[:, units:]
    up_weight[...] = total_a[:, :units]
    down_weight[...] = total_b[...]
    for ref, at in ((first_gain, GAIN1), (first_shift, SHIFT1), (query_bias, QBIAS), (value_bias, VBIAS)):
        ref[...] = table[at, wide : wide + count]
    for ref, at in ((branch_bias, BRANCH), (second_gain, GAIN2), (second_shift, SHIFT2), (down_bias, DOWNB)):
        ref[...] = table[at, wide + count : wide + 2 * count]
    up_bias[...] = table[0, :wide]
    for fetch, store in zip(fetches, stores):
        fetch.wait()
        store.start()
    for copy in texts:
        copy.wait()
    out_text[...] = text_s[:, :slots]
    grad_text[...] = text_grad_s[:, :slots]
    for copy in stores:
        copy.wait()


def outputs(text, patch_grad, text_grad, total_a, total_b, total_in, vec1, vec2, upb, slots, units):
    items, patch, model = patch_grad.shape

    def shape(*dims):
        return jax.ShapeDtypeStruct(dims, f32)

    count = total_in.shape[0]
    vector, texts = shape(count), jax.ShapeDtypeStruct((items, slots, model), bf16)
    return pl.pallas_call(
        outputs_kernel,
        in_specs=[ANY] * 3 + [WHOLE] * 6,
        out_specs=[WHOLE, ANY, WHOLE] + [WHOLE] * 13,
        out_shape=[texts, jax.ShapeDtypeStruct(patch_grad.shape, bf16), texts]
        + [vector, vector, shape(count, 3 * model), vector, vector, shape(count, model), vector, vector, vector]
        + [shape(count, units), shape(upb.shape[0]), shape(*total_b.shape), vector],
        scratch_shapes=[
            pltpu.VMEM(patch_grad.shape, bf16),
            pltpu.VMEM(text.shape, bf16),
            pltpu.VMEM(text.shape, bf16),
            pltpu.SemaphoreType.DMA((3, max(items, 2))),
        ],
        compiler_params=compiler_params(),
        name="outputs",
    )(text, patch_grad, text_grad, total_a, total_b, total_in, vec1, vec2, upb)


def per_device(
    seq_size,
    devices,
    patches,
    text_rows,
    lengths,
    first_gain,
    first_shift,
    in_weight,
    query_bias,
    value_bias,
    out_weight,
    branch_bias,
    second_gain,
    second_shift,
    up_weight,
    up_bias,
    down_weight,
    down_bias,
    patch_cotangent,
    text_cotangent,
):
    items, patch, model = patches.shape
    slots = text_rows.shape[1]
    units = up_weight.shape[1]
    head = model // HEADS
    width = min(LANES, model)
    text = round_up(-(-slots // seq_size), ROW_TILE)
    seq = lax.axis_index("seq")
    vectors = [first_gain, first_shift, query_bias, value_bias, branch_bias, second_gain, second_shift, down_bias]
    w_in, vecs, bias, (weights, w_down), x_text, first_in, q, attended, rest, logs, keys, values = forward(
        in_weight, vectors, up_weight, up_bias, out_weight, down_weight, patches, text_rows, lengths, text, width, head,
        devices, seq_size
    )
    out_patches, res_text, grad_branch, grad_att, part_a, part_b = ffn(
        seq[None], patches, x_text, attended, patch_cotangent, text_cotangent, weights, w_down, vecs
    )
    grad_patches, grad_text, out_text, sums, down_grad, in_grad, vec1, vec2, up_bias_grad = back(
        q, keys, values, bias, logs, attended, rest, grad_att, part_a, part_b, w_in, vecs, first_in, patches, x_text,
        grad_branch, res_text, head, width, devices, seq_size
    )
    rest = outputs(
        out_text, grad_patches, grad_text, sums, down_grad, in_grad, vec1, vec2, up_bias_grad, slots, units
    )
    return (out_patches, *rest)


def solution(mesh):
    both = ("dp", "seq")
    rows, slots, vector, matrix = P("dp", "seq", None), P("dp", None, None), P(both), P(both, None)
    weights = (vector, vector, matrix, vector, vector, matrix, vector, vector, vector, matrix, vector, matrix, vector)
    return jax.shard_map(
        functools.partial(per_device, mesh.shape["seq"], mesh.size),
        mesh=mesh,
        in_specs=(rows, slots, P("dp")) + weights + (rows, slots),
        out_specs=(rows, slots, rows, slots) + weights,
        check_vma=False,
    )
```

```python
import functools
import math

import jax
import jax.numpy as jnp
from jax import lax
from jax.experimental import pallas as pl
from jax.experimental.pallas import tpu as pltpu
from jax.sharding import PartitionSpec as P

HEADS = 8
EPSILON = 1e-05
NEG_FILL = -1e30
LOG2E = math.log2(math.e)
LN2 = math.log(2.0)
ROW_TILE = 16
LANES = 128
MESH = pl.DeviceIdType.MESH
f32, bf16 = jnp.float32, jnp.bfloat16

GAIN1, SHIFT1, QBIAS, VBIAS, BRANCH, GAIN2, SHIFT2, DOWNB = range(8)


def round_up(value, unit):
    return -(-value // unit) * unit


def mm(a, b):
    return lax.dot_general(a, b, (((1,), (0,)), ((), ())), preferred_element_type=f32)


def mm_t(a, b):
    return lax.dot_general(a, b, (((1,), (1,)), ((), ())), preferred_element_type=f32)


def t_mm(a, b):
    return lax.dot_general(a, b, (((0,), (0,)), ((), ())), preferred_element_type=f32)


def compiler_params(**more):
    return pltpu.CompilerParams(vmem_limit_bytes=60 * 2**20, **more)


WHOLE = pl.BlockSpec(memory_space=pltpu.VMEM)
ANY = pl.BlockSpec(memory_space=pl.ANY)


class Place:
    def __init__(self, depth, seq_size):
        self.depth, self.seq_size = depth, seq_size
        index = lax.axis_index("dp") * seq_size + lax.axis_index("seq")
        self.core = lax.rem(index, 2)
        self.x = lax.rem(index // 2, 2)
        self.y = lax.rem(index // 4, 2)
        self.z = index // 8
        core = self.core
        flip_x, flip_y = 1 - self.x, 1 - self.y
        x_first = self.x * core + flip_x * (1 - core)
        y_first = self.y * (1 - core) + flip_y * core
        x_second = self.x * (1 - core) + flip_x * core
        y_second = self.y * core + flip_y * (1 - core)
        self.columns = (
            (self.y, self.x),
            (y_first, x_first),
            (y_second, x_second),
            (flip_y, flip_x),
        )

    def device(self, z, y, x, core):
        index = ((z * 2 + y) * 2 + x) * 2 + core
        return (index // self.seq_size, lax.rem(index, self.seq_size))

    def layer(self, k):
        return lax.rem(self.z + self.depth - k, self.depth)

    def ahead(self, k):
        return lax.rem(self.z + k, self.depth)

    def first(self):
        return self.device(self.z, *self.columns[1], self.core)

    def second(self):
        return self.device(self.z, *self.columns[2], self.core)

    def other_core(self):
        return self.device(self.z, self.y, self.x, 1 - self.core)

    def above(self, k):
        return self.device(self.ahead(k), self.y, self.x, self.core)

    def mate(self, step):
        return (lax.axis_index("dp"), lax.rem(lax.axis_index("seq") + self.seq_size - step, self.seq_size))

    def octant(self, n):
        column, core = n % 4, n // 4
        y, x = self.columns[column]
        core = self.core * (1 - core) + (1 - self.core) * core
        return self.device(self.z, y, x, core), (y, x, core)

    def friends(self, corners):
        friends = [self.above(k) for k in range(1, self.depth)]
        friends += [self.octant(n)[0] for n in range(1, 8)] if corners else [self.first(), self.second(), self.other_core()]
        return friends + [self.mate(step) for step in range(1, self.seq_size)]

    def greet(self, corners=False):
        barrier = pltpu.get_barrier_semaphore()
        for friend in self.friends(corners):
            pl.semaphore_signal(barrier, inc=1, device_id=friend, device_id_type=MESH)

    def meet(self, corners=False):
        pl.semaphore_wait(pltpu.get_barrier_semaphore(), len(self.friends(corners)))


def remote(src, dst, send, recv, device):
    return pltpu.make_async_remote_copy(
        src_ref=src, dst_ref=dst, send_sem=send, recv_sem=recv, device_id=device, device_id_type=MESH
    )


class Spread:
    def __init__(self, place, shard, full, out, into, local):
        self.place, self.shard, self.full, self.out, self.into, self.local = place, shard, full, out, into, local

    def column(self, n, core=None):
        y, x = self.place.columns[n]
        return self.full.at[:, y, x, self.place.core if core is None else core]

    def line_copy(self, k):
        place = self.place
        here = self.full.at[place.z, place.y, place.x, place.core]
        return remote(self.shard, here, self.out.at[6 + k], self.into.at[6 + k], place.above(k))

    def own_copy(self):
        place = self.place
        return pltpu.make_async_copy(self.shard, self.full.at[place.z, place.y, place.x, place.core], self.local)

    def copy(self, n, lane):
        here = self.column(n)
        device = (self.place.first, self.place.second, self.place.second)[lane] if lane < 3 else self.place.other_core
        return remote(here, here, self.out.at[lane], self.into.at[lane], device())

    def arrive(self, n, lane):
        self.copy(n, lane).wait_recv()

    def start(self):
        self.own_copy().start()
        for k in range(1, self.place.depth):
            self.line_copy(k).start()

    def send_line(self):
        self.own_copy().wait()
        for k in range(1, self.place.depth):
            self.line_copy(k).wait_recv()
        for lane in (0, 1, 3):
            self.copy(0, lane).start()

    def forward_first(self):
        self.arrive(1, 0)
        self.copy(1, 2).start()
        self.copy(1, 4).start()

    def forward_second(self, half):
        self.arrive(2 + half, 1 + half)
        self.copy(2 + half, 5 + half).start()

    def finish(self):
        for n in range(4):
            self.arrive(n, 3 + n)
        for k in range(1, self.place.depth):
            self.line_copy(k).wait_send()
        for lane in range(7):
            self.copy(0, lane).wait_send()


def spread_sems(depth):
    sems = pltpu.SemaphoreType.DMA
    return [sems((6 + depth,)), sems((6 + depth,)), sems]


class Results:
    def result_copy(self, n, other):
        y, x = self.place.columns[(0, 2, 1, 3)[n] if other else n]
        core = 1 - self.place.core if other else self.place.core
        here = (slice(None), y, x, core)
        return pltpu.make_async_copy(self.full.at[here], self.result.at[here], self.results.at[n, other])

    def land(self, n):
        self.arrive_core(n)
        for other in range(2):
            self.result_copy(n, other).start()

    def finish(self):
        for n in range(4):
            for other in range(2):
                self.result_copy(n, other).wait()
        self.sent()


class Gather(Results, Spread):
    def __init__(self, place, shard, full, result, out, into, local, results):
        Spread.__init__(self, place, shard, full, out, into, local)
        self.result, self.results = result, results

    def arrive_core(self, n):
        self.arrive(n, 3 + n)

    def sent(self):
        for k in range(1, self.place.depth):
            self.line_copy(k).wait_send()
        for lane in range(7):
            self.copy(0, lane).wait_send()


def gather_sems(depth):
    return spread_sems(depth) + [pltpu.SemaphoreType.DMA((4, 2))]


class Reduce:
    def __init__(self, place, part, from_core, held, from_second, pair, from_first, line, from_line, out, into, local):
        self.place, self.part, self.local = place, part, local
        self.from_core, self.held, self.from_second, self.pair = from_core, held, from_second, pair
        self.from_first, self.line, self.from_line = from_first, line, from_line
        self.out, self.into = out, into

    def copy(self, src, dst, lane, device):
        return remote(src, dst, self.out.at[lane], self.into.at[lane], device)

    def own_copy(self):
        return pltpu.make_async_copy(self.part.at[:, :, :, self.place.core], self.held, self.local)

    def core_copy(self):
        return self.copy(self.part.at[:, :, :, 1 - self.place.core], self.from_core, 0, self.place.other_core())

    def second_copies(self):
        columns = self.place.columns
        return [
            self.copy(self.held.at[:, columns[2 + k][0], columns[2 + k][1]], self.from_second.at[k], 1 + k,
                      self.place.second())
            for k in range(2)
        ]

    def first_copy(self):
        return self.copy(self.pair.at[1], self.from_first, 3, self.place.first())

    def line_copies(self):
        place = self.place
        return [
            self.copy(self.line.at[place.ahead(k)], self.from_line.at[k - 1], 3 + k, place.above(k))
            for k in range(1, place.depth)
        ]

    def to_core(self):
        self.core_copy().start()
        self.own_copy().start()

    def to_second(self):
        self.own_copy().wait()
        self.core_copy().wait()
        self.held[...] += self.from_core[...]
        for copy in self.second_copies():
            copy.start()

    def to_first(self):
        for copy in self.second_copies():
            copy.wait()
        for k in range(2):
            y, x = self.place.columns[k]
            self.pair[k] = self.held[:, y, x] + self.from_second[k]
        self.first_copy().start()

    def to_line(self):
        self.first_copy().wait()
        self.line[...] = self.pair[0] + self.from_first[...]
        for copy in self.line_copies():
            copy.start()

    def last(self):
        for copy in self.line_copies():
            copy.wait()
        result = self.line[self.place.z].astype(f32)
        for k in range(self.place.depth - 1):
            result = result + self.from_line[k].astype(f32)
        return result


def reduce_scratch(depth, rows, cols):
    shapes = [(depth, 2, 2), (depth, 2, 2), (2, depth), (2, depth), (depth,), (depth,), (depth - 1,)]
    sems = pltpu.SemaphoreType.DMA
    return [pltpu.VMEM(shape + (rows, cols), bf16) for shape in shapes] + [sems((3 + depth,))] * 2 + [sems]


class ShortReduce:
    def __init__(self, place, part, from_octant, line, from_line, out, into):
        self.place, self.part, self.from_octant, self.line, self.from_line = place, part, from_octant, line, from_line
        self.out, self.into = out, into

    def octant_copy(self, n):
        device, (y, x, core) = self.place.octant(n)
        return remote(
            self.part.at[:, y, x, core], self.from_octant.at[n - 1], self.out.at[n - 1], self.into.at[n - 1], device
        )

    def line_copy(self, k):
        return remote(
            self.line.at[self.place.ahead(k)], self.from_line.at[k - 1], self.out.at[6 + k], self.into.at[6 + k],
            self.place.above(k)
        )

    def start(self):
        for n in range(1, 8):
            self.octant_copy(n).start()

    def to_line(self):
        place = self.place
        total = self.part[:, place.y, place.x, place.core].astype(f32)
        for n in range(1, 8):
            self.octant_copy(n).wait()
            total = total + self.from_octant[n - 1].astype(f32)
        self.line[...] = total.astype(bf16)
        for k in range(1, place.depth):
            self.line_copy(k).start()

    def last(self):
        total = self.line[self.place.z].astype(f32)
        for k in range(1, self.place.depth):
            self.line_copy(k).wait()
            total = total + self.from_line[k - 1].astype(f32)
        return total


def short_reduce_scratch(depth, rows, cols):
    sems = pltpu.SemaphoreType.DMA
    shapes = [(depth, 2, 2, 2), (7, depth), (depth,), (depth - 1,)]
    return [pltpu.VMEM(shape + (rows, cols), bf16) for shape in shapes] + [sems((6 + depth,))] * 2


def norm_rows(rows):
    centred = rows - jnp.mean(rows, axis=1, keepdims=True)
    inverse = lax.rsqrt(jnp.mean(centred * centred, axis=1, keepdims=True) + EPSILON)
    return centred * inverse, inverse


def norm_back(grad, scaled, inverse, gain):
    inner = grad * gain
    return inverse * (
        inner
        - jnp.mean(inner, axis=1, keepdims=True)
        - scaled * jnp.mean(inner * scaled, axis=1, keepdims=True)
    )


def gelu_both(v):
    power = jnp.exp2(v * v * (-0.5 * LOG2E))
    cdf = 0.5 + 0.5 * lax.erf(v * math.sqrt(0.5))
    return v * cdf, cdf + v * power * (1.0 / math.sqrt(2.0 * math.pi))


def column_sum(rows):
    return jnp.sum(rows.astype(f32), axis=0, keepdims=True)


def to_columns(rows):
    count, width = rows.shape
    return jnp.transpose(jnp.concatenate([rows, jnp.zeros((LANES - count, width), f32)], axis=0)).astype(bf16)


def own_text(ref, text, seq):
    slots, width = ref.shape
    own = jnp.zeros((text, width), ref.dtype)
    for r in range(-(-slots // text)):
        share = ref[r * text : min(slots, (r + 1) * text), :]
        if share.shape[0] < text:
            share = jnp.concatenate([share, jnp.zeros((text - share.shape[0], width), ref.dtype)], axis=0)
        own = jnp.where(seq == r, share, own)
    return own


def as_columns(vectors):
    length = vectors[0].shape[0]
    rows = [vector.reshape(1, length).astype(f32) for vector in vectors]
    rows = jnp.concatenate(rows + [jnp.zeros((LANES - len(rows), length), f32)], axis=0)
    rows = jnp.concatenate([rows, jnp.zeros((LANES, LANES - length), f32)], axis=1)
    return jnp.transpose(rows)[:length].astype(bf16)


def collect(dst, blocks, patch, text):
    count, width = len(blocks), blocks[0].shape[1]
    for r, block in enumerate(blocks):
        dst[r * patch : (r + 1) * patch, :width] = block[:patch]
        at = count * patch + r * text
        dst[at : at + text, :width] = block[patch:]
    filled = count * (patch + text)
    if dst.shape[0] > filled:
        dst[filled:, :width] = jnp.zeros((dst.shape[0] - filled, width), dst.dtype)


def by_head(dst, src, lane, heads, ones):
    count, width = src.shape
    for h in range(heads):
        rows = slice(h * count, (h + 1) * count)
        dst[rows, :width] = jnp.where(lane == h, src, jnp.zeros_like(src))
        if ones:
            dst[rows, width:] = jnp.where(lane == h, jnp.ones_like(src), jnp.zeros_like(src))


def forward_kernel(seq_size, text, width, head, *refs):
    refs = list(refs)

    def take(number):
        taken = refs[:number]
        del refs[:number]
        return taken

    given, x_any, length_ref = take(14), *take(2)
    w_out, w2_out, vecs, bias_ref, full_a, full_b, xtext_ref, first_out, q_out, out_out, rest_out, log_out = take(12)
    k_outs, v_outs = take(seq_size), take(seq_size)
    shard, shard2, shard_a, shard_b, w_full, w2_full, into_a, into_b, x_s, n_s, first_s, q_s, k_s, v_s = take(14)
    keys, values, text_keys, text_values, out_s, rest_s, log_s = take(7)
    sems, sems2, sems_a, sems_b = take(3), take(3), take(4), take(4)
    x_sem, w_sem, out_sem, kv_sem, kv_in_sem, kv_out_sem, turn_sem = take(7)
    held, given_sem = take(14), *take(1)
    fetches = [pltpu.make_async_copy(src, dst, given_sem.at[n]) for n, (src, dst) in enumerate(zip(given, held))]
    (shard_ref,), vec_refs, (up_ref, up_bias_ref, out_w_ref, down_ref, slot_ref) = held[:1], held[1:9], held[9:]
    items, patch, model = x_s.shape
    units, wide = up_ref.shape[1], shard2.shape[1]
    pairs = model // width
    place = Place(w_full.shape[0], seq_size)
    seq = lax.axis_index("seq")
    x_copies = [pltpu.make_async_copy(x_any.at[i], x_s.at[i], x_sem.at[i]) for i in range(items)]
    place.greet()
    for copy in fetches + x_copies:
        copy.start()
    for copy in fetches[:9]:
        copy.wait()
    for half, to in enumerate((shard, shard2)):
        for n in range(3):
            at = (n + 1) % 3 * model + half * (model // 2)
            to[:, n * (model // 2) : (n + 1) * (model // 2)] = shard_ref[:, at : at + model // 2]
    shard[:, wide:] = as_columns([ref[...] for ref in vec_refs])
    place.meet()
    halves = [Spread(place, shard, w_full, *sems), Spread(place, shard2, w2_full, *sems2)]
    for move in halves:
        move.start()
    for copy in fetches[9:]:
        copy.wait()
    shard_a[:, :units] = up_ref[...]
    shard_a[:, units:] = out_w_ref[...]
    shard_b[:, :model] = down_ref[...]
    shard_b[:, model:] = as_columns([up_bias_ref[...]])
    move_a, move_b = Gather(place, shard_a, into_a, full_a, *sems_a), Gather(place, shard_b, into_b, full_b, *sems_b)
    tail = bias_ref.shape[2]
    col = lax.broadcasted_iota(jnp.int32, (1, tail), 1)
    slot = jnp.full((1, tail), seq_size * text, jnp.int32)
    for r in range(seq_size):
        begin = lax.rem(seq + r, seq_size) * text
        slot = jnp.where((col >= r * text) & (col < (r + 1) * text), begin + col - r * text, slot)
    for i in range(items):
        xtext_ref[i] = own_text(slot_ref.at[i], text, seq)
        bias_ref[i] = jnp.where(slot < length_ref[i], 0.0, NEG_FILL)
    halves[0].send_line()
    halves[1].send_line()
    move_a.start()
    move_b.start()
    for i in range(items):
        x_copies[i].wait()
        n_s[i], _ = norm_rows(jnp.concatenate([x_s[i], xtext_ref[i]], axis=0).astype(f32))
    halves[0].forward_first()
    halves[0].forward_second(0)
    halves[1].forward_first()
    halves[0].forward_second(1)
    halves[1].forward_second(0)
    halves[0].finish()
    move_a.send_line()
    w_copies = [pltpu.make_async_copy(src, dst, w_sem.at[n]) for n, (src, dst) in
                enumerate(((w_full, w_out), (w2_full, w2_out)))]
    w_copies[0].start()
    weight = w_full[...].reshape(model, wide + LANES)
    table = jnp.transpose(weight[:, wide:].astype(f32))
    vecs[...] = table
    scale = LOG2E / math.sqrt(model // HEADS)
    sends, outs = [], []

    def keys_and_values(i, half, weight):
        span = model // 2
        cols = pl.ds(half * span, span)
        projected = mm(first_s[i], weight[:, : 2 * span])
        k_s[0, i, :, cols] = projected[:, :span].astype(bf16)
        v_s[0, i, :, cols] = (projected[:, span:] + table[VBIAS : VBIAS + 1, half * span : (half + 1) * span]).astype(bf16)
        for r in range(1, seq_size):
            for n, ref in enumerate((k_s, v_s)):
                at = ((2 * i + n) * 2 + half) * seq_size + r
                src, dst = ref.at[0, i, :, cols], ref.at[r, i, :, cols]
                sends.append(remote(src, dst, kv_sem.at[at], kv_in_sem.at[at], place.mate(r)))
                sends[-1].start()

    def queries(i, half, weight):
        span = model // 2
        q = mm(first_s[i], weight[:, 2 * span : 3 * span]) + table[QBIAS : QBIAS + 1, half * span : (half + 1) * span]
        q_s[i, :, half * span : (half + 1) * span] = (q * scale).astype(bf16)

    def bring(n, src, dst, i):
        outs.append(pltpu.make_async_copy(src.at[i], dst.at[i], out_sem.at[n, i]))
        outs[-1].start()

    for i in range(items):
        first_s[i] = (n_s[i] * table[GAIN1 : GAIN1 + 1] + table[SHIFT1 : SHIFT1 + 1]).astype(bf16)
        bring(0, first_s, first_out, i)
        keys_and_values(i, 0, weight)
        if i == 0:
            halves[1].forward_second(1)
    halves[1].finish()
    move_b.send_line()
    w_copies[1].start()
    weight2 = w2_full[...].reshape(model, wide)
    for i in range(items):
        keys_and_values(i, 1, weight2)
        bring(1, k_s.at[0], k_outs[0], i)
        bring(2, v_s.at[0], v_outs[0], i)
    for i in range(items):
        queries(i, 0, weight)
        queries(i, 1, weight2)
        bring(3, q_s, q_out, i)

    edge, heads, span = seq_size * patch, width // head, keys.shape[0] - seq_size * patch
    lane = lax.broadcasted_iota(jnp.int32, (1, width), 1) // head
    values[:, width:] = jnp.ones((values.shape[0], values.shape[1] - width), bf16)
    last = items * pairs - 1

    def turn_copies(slot, i, cols):
        return [
            pltpu.make_async_copy(src.at[slot], dst.at[i, :, cols], turn_sem.at[slot, n])
            for n, (src, dst) in enumerate(((out_s, out_out), (rest_s, rest_out), (log_s, log_out)))
        ]

    def kv_out_copies(i):
        return [
            pltpu.make_async_copy(ref.at[r, i], dst[r].at[i], kv_out_sem.at[(2 * i + n) * seq_size + r])
            for n, (ref, dst) in enumerate(((k_s, k_outs), (v_s, v_outs)))
            for r in range(1, seq_size)
        ]

    def exchanged(i):
        for n, ref in enumerate((k_s, v_s)):
            for half in range(2):
                cols = pl.ds(half * (model // 2), model // 2)
                for r in range(1, seq_size):
                    at = ((2 * i + n) * 2 + half) * seq_size + r
                    src, dst = ref.at[0, i, :, cols], ref.at[r, i, :, cols]
                    remote(src, dst, kv_sem.at[at], kv_in_sem.at[at], place.mate(r)).wait_recv()
        for copy in kv_out_copies(i):
            copy.start()

    agenda = (
        (4, move_a.forward_first),
        (4, functools.partial(move_a.forward_second, 0)),
        (6, move_b.forward_first),
        (6, functools.partial(move_b.forward_second, 0)),
        (8, functools.partial(move_a.land, 0)),
        (8, functools.partial(move_a.land, 1)),
        (9, functools.partial(move_a.forward_second, 1)),
        (10, functools.partial(move_a.land, 2)),
        (10, functools.partial(move_b.land, 0)),
        (10, functools.partial(move_b.land, 1)),
        (11, functools.partial(move_b.forward_second, 1)),
        (11, functools.partial(move_b.land, 2)),
        (13, functools.partial(move_a.land, 3)),
        (13, functools.partial(move_b.land, 3)),
    )

    def attend(turn, _):
        i, p = turn // pairs, lax.rem(turn, pairs)
        slot = lax.rem(turn, 2)
        cols = pl.ds(pl.multiple_of(p * width, width), width)

        @pl.when(p == 0)
        def _():
            exchanged(i)

        for at in sorted({at for at, _ in agenda if at <= last}):

            @pl.when(turn == at)
            def _(at=at):
                for when, step in agenda:
                    if when == at:
                        step()

        collect(keys, [k_s[r, i, :, cols] for r in range(seq_size)], patch, text)
        collect(values, [v_s[r, i, :, cols] for r in range(seq_size)], patch, text)
        by_head(text_keys, keys[edge:], lane, heads, False)
        by_head(text_values, values[edge:, :width], lane, heads, True)
        q = q_s[i, :, cols]
        text_bias = jnp.concatenate([bias_ref[i]] * heads, axis=1)

        def scores_of(h):
            return mm_t(jnp.where(lane == h, q, jnp.zeros_like(q)), keys[:edge])

        text_scores = mm_t(q, text_keys[...]) + text_bias
        scores = scores_of(0)
        text_powers, mixed, total, tops = [], None, None, None
        for h in range(heads):
            following = scores_of(h + 1) if h + 1 < heads else None
            text_head = text_scores[:, h * span : (h + 1) * span]
            top = jnp.maximum(jnp.max(scores, axis=1, keepdims=True), jnp.max(text_head, axis=1, keepdims=True))
            powers = jnp.exp2(scores - top).astype(bf16)
            text_powers.append(jnp.exp2(text_head - top).astype(bf16))
            both = mm(powers, values[:edge])
            mixed = both[:, :width] if mixed is None else jnp.where(lane == h, both[:, :width], mixed)
            total = both[:, width:] if total is None else jnp.where(lane == h, both[:, width:], total)
            tops = jnp.broadcast_to(top, mixed.shape) if tops is None else jnp.where(lane == h, top, tops)
            scores = following
        both = mm(jnp.concatenate(text_powers, axis=1), text_values[...])
        total = total + both[:, width:]
        out = (mixed + both[:, :width]) * (1.0 / total)
        high = out.astype(bf16)

        @pl.when(turn > 1)
        def _():
            for copy in turn_copies(slot, i, cols):
                copy.wait()

        out_s[slot] = high
        rest_s[slot] = (out - high.astype(f32)).astype(bf16)
        log_s[slot] = tops + jnp.log2(total)
        for copy in turn_copies(slot, i, cols):
            copy.start()
        return 0

    lax.fori_loop(0, last + 1, attend, 0)
    for when, step in agenda:
        if when > last:
            step()
    move_a.finish()
    move_b.finish()
    for slot in range(2):
        for copy in turn_copies(slot, 0, pl.ds(0, width)):
            copy.wait()
    for copy in sends:
        copy.wait_send()
    for i in range(items):
        for copy in kv_out_copies(i):
            copy.wait()
    for copy in w_copies + outs:
        copy.wait()


def forward(in_weight, vectors, up_weight, up_bias, out_weight, down_weight, patches, text_rows, lengths, text, width,
            head, devices, seq_size):
    items, patch, model = patches.shape
    depth, heads = devices // 8, width // head
    rows, cols = in_weight.shape
    shape_a = (depth, 2, 2, 2, rows, up_weight.shape[1] + model)
    shape_b = (depth, 2, 2, 2, down_weight.shape[0], model + LANES)
    shape_w = (depth, 2, 2, 2, rows, cols // 2 + LANES)
    shape_w2 = (depth, 2, 2, 2, rows, cols // 2)
    shape_x = (items, patch + text, model)
    tail = round_up(seq_size * text, LANES)
    span = seq_size * patch + tail
    tokens = jax.ShapeDtypeStruct(shape_x, bf16)
    sems = pltpu.SemaphoreType.DMA
    given = (in_weight, *vectors, up_weight, up_bias, out_weight, down_weight, text_rows)
    outs = pl.pallas_call(
        functools.partial(forward_kernel, seq_size, text, width, head),
        in_specs=[ANY] * 15 + [pl.BlockSpec(memory_space=pltpu.SMEM)],
        out_specs=[ANY, ANY, WHOLE, WHOLE, ANY, ANY, WHOLE] + [ANY] * (5 + 2 * seq_size),
        out_shape=[
            jax.ShapeDtypeStruct(shape_w, bf16),
            jax.ShapeDtypeStruct(shape_w2, bf16),
            jax.ShapeDtypeStruct((LANES, model), f32),
            jax.ShapeDtypeStruct((items, 1, tail), f32),
            jax.ShapeDtypeStruct(shape_a, bf16),
            jax.ShapeDtypeStruct(shape_b, bf16),
            jax.ShapeDtypeStruct((items, text, model), bf16),
            tokens,
            tokens,
            tokens,
            tokens,
            jax.ShapeDtypeStruct(shape_x, f32),
        ]
        + [tokens] * (2 * seq_size),
        scratch_shapes=[
            pltpu.VMEM(shape_w[4:], bf16),
            pltpu.VMEM(shape_w2[4:], bf16),
            pltpu.VMEM(shape_a[4:], bf16),
            pltpu.VMEM(shape_b[4:], bf16),
            pltpu.VMEM(shape_w, bf16),
            pltpu.VMEM(shape_w2, bf16),
            pltpu.VMEM(shape_a, bf16),
            pltpu.VMEM(shape_b, bf16),
            pltpu.VMEM(patches.shape, bf16),
            pltpu.VMEM(shape_x, f32),
            pltpu.VMEM(shape_x, bf16),
            pltpu.VMEM(shape_x, bf16),
            pltpu.VMEM((seq_size,) + shape_x, bf16),
            pltpu.VMEM((seq_size,) + shape_x, bf16),
            pltpu.VMEM((span, width), bf16),
            pltpu.VMEM((span, 2 * width), bf16),
            pltpu.VMEM((heads * tail, width), bf16),
            pltpu.VMEM((heads * tail, 2 * width), bf16),
            pltpu.VMEM((2, patch + text, width), bf16),
            pltpu.VMEM((2, patch + text, width), bf16),
            pltpu.VMEM((2, patch + text, width), f32),
        ]
        + spread_sems(depth) * 2
        + gather_sems(depth) * 2
        + [sems((items,)), sems((2,)), sems((4, items))]
        + [sems((4 * items * seq_size,))] * 2
        + [sems((2 * items * seq_size,)), sems((2, 3))]
        + [pltpu.VMEM(array.shape, array.dtype) for array in given]
        + [sems((len(given),))],
        compiler_params=compiler_params(collective_id=0, has_side_effects=True),
        name="forward",
    )(*given, patches, lengths)
    w_in, weights = ([full.reshape(-1, full.shape[-1]) for full in pair] for pair in (outs[:2], outs[4:6]))
    return w_in, *outs[2:4], weights, *outs[6:12], outs[12 : 12 + seq_size], outs[12 + seq_size :]


def ffn_kernel(steps, chunk, part, seq_ref, x_ref, xtext_ref, at_ref, dy_ref, dy_slot_ref, w_any, wd_any, vec_ref,
               res_ref, restext_ref, gb_ref, ga_ref, part_out, down_out,
               w_ref, wd_ref, part_ref, down_ref, second_s, hidden_s, pre_s, dy_s, sums_s, bias_s, at_s, gb_s,
               w_sem, wd_sem, part_sem, down_sem):
    step = pl.program_id(0)
    patch, model = x_ref.shape[1:]
    text = xtext_ref.shape[1]
    block, units = patch + text, wd_ref.shape[0]
    chunks = units // chunk
    rows = pl.ds(pl.multiple_of(step * block, ROW_TILE), block)
    gain = vec_ref[GAIN2 : GAIN2 + 1]
    w_out = w_ref.at[:, units:]

    def fetch(cols, at):
        if cols is None:
            return (
                pltpu.make_async_copy(w_any.at[:, units:], w_ref.at[:, units:], w_sem.at[at]),
                pltpu.make_async_copy(wd_any.at[:, model:], wd_ref.at[:, model:], wd_sem.at[at]),
            )
        return (
            pltpu.make_async_copy(w_any.at[:, cols], w_ref.at[:, cols], w_sem.at[at]),
            pltpu.make_async_copy(wd_any.at[cols, :model], wd_ref.at[cols, :model], wd_sem.at[at]),
        )

    @pl.when(step == 0)
    def _():
        others = fetch(None, chunks)
        for copy in others:
            copy.start()
        for c in range(chunks):
            for copy in fetch(pl.ds(c * chunk, chunk), c):
                copy.start()
        sums_s[...] = jnp.zeros_like(sums_s)
        for copy in others:
            copy.wait()
        bias_s[...] = jnp.transpose(wd_ref[:, model:].astype(f32))[:8]

    x = jnp.concatenate([x_ref[0], xtext_ref[0]], axis=0).astype(f32)
    dy = jnp.concatenate([dy_ref[0], own_text(dy_slot_ref.at[0], text, seq_ref[0])], axis=0)
    dy_s[rows, :] = dy
    middle = x + (mm(at_ref[0], w_out[...]) + vec_ref[BRANCH : BRANCH + 1])
    scaled, inverse = norm_rows(middle)
    second_in = (scaled * gain + vec_ref[SHIFT2 : SHIFT2 + 1]).astype(bf16)
    second_s[rows, :] = second_in
    @pl.when(step == 0)
    def _():
        for c in range(chunks):
            for copy in fetch(pl.ds(c * chunk, chunk), c):
                copy.wait()

    def first_dots(c):
        cols = slice(c * part, (c + 1) * part)
        return mm(second_in, w_ref[:, cols]) + bias_s[:1, cols], mm_t(dy, wd_ref[cols, :model])

    result, grad_second = middle + vec_ref[DOWNB : DOWNB + 1], None
    pre, grad_hidden = first_dots(0)
    for c in range(units // part):
        following = first_dots(c + 1) if c + 1 < units // part else (None, None)
        cols = slice(c * part, (c + 1) * part)
        value, slope = gelu_both(pre)
        hidden = value.astype(bf16)
        hidden_s[rows, cols] = hidden
        grad_pre = (grad_hidden * slope).astype(bf16)
        pre_s[rows, cols] = grad_pre
        result = result + mm(hidden, wd_ref[cols, :model])
        back_part = mm_t(grad_pre, w_ref[:, cols])
        grad_second = back_part if grad_second is None else grad_second + back_part
        pre, grad_hidden = following
    result = result.astype(bf16)
    res_ref[0] = result[:patch]
    restext_ref[0] = result[patch:]
    grad_branch = (dy.astype(f32) + norm_back(grad_second, scaled, inverse, gain)).astype(bf16)
    gb_ref[0] = grad_branch
    ga_ref[0] = mm_t(grad_branch, w_out[...]).astype(bf16)
    at_s[rows, :] = at_ref[0]
    gb_s[rows, :] = grad_branch
    for at, grad in ((BRANCH, grad_branch), (GAIN2, grad_second * scaled), (SHIFT2, grad_second), (DOWNB, dy)):
        sums_s[at : at + 1, :] += column_sum(grad)

    @pl.when(step == steps - 1)
    def _():
        groups = units // model
        copies = []
        part_ref[:, units : units + model] = t_mm(at_s[...], gb_s[...]).astype(bf16)
        part_ref[:, units + model :] = to_columns(sums_s[...])
        copies.append(pltpu.make_async_copy(part_ref.at[:, units:], part_out.at[:, units:], part_sem.at[groups]))
        copies[-1].start()
        for c in range(groups):
            cols = slice(c * model, (c + 1) * model)
            at = pl.ds(c * model, model)
            grad_pre = pre_s[:, cols]
            part_ref[:, cols] = t_mm(second_s[...], grad_pre).astype(bf16)
            copies.append(pltpu.make_async_copy(part_ref.at[:, at], part_out.at[:, at], part_sem.at[c]))
            copies[-1].start()
            down_ref[cols, :model] = jnp.transpose(t_mm(dy_s[...], hidden_s[:, cols])).astype(bf16)
            down_ref[cols, model:] = to_columns(column_sum(grad_pre))
            copies.append(pltpu.make_async_copy(down_ref.at[at], down_out.at[at], down_sem.at[c]))
            copies[-1].start()
        for copy in copies:
            copy.wait()


def ffn(seq, patches, x_text, attended, patch_cotangent, text_cotangent, weights, w_down, vecs):
    items, patch, model = patches.shape
    units, rows, text, slots = w_down.shape[0], attended.shape[1], x_text.shape[1], text_cotangent.shape[1]

    def item(count):
        return pl.BlockSpec((1, count, model), lambda i: (i, 0, 0))

    def shape(count):
        return jax.ShapeDtypeStruct((items, count, model), bf16)

    return pl.pallas_call(
        functools.partial(ffn_kernel, items, 1024, 256),
        grid=(items,),
        in_specs=[pl.BlockSpec(memory_space=pltpu.SMEM)]
        + [item(patch), item(text), item(rows), item(patch), item(slots)]
        + [ANY, ANY, WHOLE],
        out_specs=[item(patch), item(text), item(rows), item(rows), ANY, ANY],
        out_shape=[shape(patch), shape(text), shape(rows), shape(rows)]
        + [
            jax.ShapeDtypeStruct((model, units + model + LANES), bf16),
            jax.ShapeDtypeStruct((units, model + LANES), bf16),
        ],
        scratch_shapes=[
            pltpu.VMEM(weights.shape, bf16),
            pltpu.VMEM(w_down.shape, bf16),
            pltpu.VMEM((model, units + model + LANES), bf16),
            pltpu.VMEM((units, model + LANES), bf16),
            pltpu.VMEM((items * rows, model), bf16),
            pltpu.VMEM((items * rows, units), bf16),
            pltpu.VMEM((items * rows, units), bf16),
            pltpu.VMEM((items * rows, model), bf16),
            pltpu.VMEM((8, model), f32),
            pltpu.VMEM((8, units), f32),
            pltpu.VMEM((items * rows, model), bf16),
            pltpu.VMEM((items * rows, model), bf16),
        ]
        + [pltpu.SemaphoreType.DMA((units // 1024 + 1,))] * 2
        + [pltpu.SemaphoreType.DMA((units // model + 1,))] * 2,
        compiler_params=compiler_params(),
        name="ffn",
    )(seq, patches, x_text, attended, patch_cotangent, text_cotangent, weights, w_down, vecs)


def back_kernel(count, patch, head, seq_size, pairs, items, *refs):
    refs = list(refs)

    def take(number):
        taken = refs[:number]
        del refs[:number]
        return taken

    (q_ref,), k_refs, v_refs = take(1), take(count), take(count)
    bias_ref, log_ref, at_ref, rest_ref, grad_ref = take(5)
    part_a, part_b, w_any, w2_any, vec_ref, first_any, x_any, xtext_any, gb_any, restext_any = take(10)
    grad_out, text_grad_out, text_out, total_a, total_b, total_in, vec_out, vec2_out, upb_out = take(9)
    keys, values, text_keys, text_values, probs_s, scores_s = take(6)
    mixed_s, own_s, dkv_out, dkv_in, sums_s = take(5)
    w_s, w2_s, first_s, x_s, xtext_s, gb_s, text_s, patch_s = take(8)
    first_grad_s, scaled_s, inverse_s = take(3)
    fetch_sem, dkv_sem, dkv_in_sem, text_sem, text_in_sem, patch_sem = take(6)
    scratch_a, scratch_b = take(10), take(10)
    scratch_in, scratch_last, scratch_vec = take(11), [take(6), take(6)], take(6)

    width, rows = q_ref.shape[2], q_ref.shape[1]
    text, model = rows - patch, pairs * width
    place = Place(part_a.shape[0], seq_size)
    seq = lax.axis_index("seq")
    p, i = pl.program_id(0), pl.program_id(1)
    turn, last = p * items + i, pairs * items - 1
    sums_a, sums_b = Reduce(place, part_a, *scratch_a), Reduce(place, part_b, *scratch_b)
    chunks = ((0, pairs - 2), (pairs - 2, pairs - 1), (pairs - 1, pairs))
    sums_in = [Reduce(place, *scratch_in)]
    sums_in += [ShortReduce(place, *each) for each in scratch_last]
    sums_vec = ShortReduce(place, *scratch_vec)
    fetches = [
        pltpu.make_async_copy(src, dst, fetch_sem.at[n])
        for n, (src, dst) in enumerate(
            ((first_any, first_s), (w_any, w_s), (w2_any, w2_s), (x_any, x_s), (xtext_any, xtext_s), (gb_any, gb_s))
        )
    ]

    def text_copies(src, dst, row):
        to = dst.at[:, pl.ds(pl.multiple_of(seq * text, ROW_TILE), text)]
        own = pltpu.make_async_copy(src, to, text_sem.at[row, 0])
        away = [
            remote(src, to, text_sem.at[row, r], text_in_sem.at[row, r], place.mate(r)) for r in range(1, seq_size)
        ]
        return [own] + away

    def begin():
        place.meet(corners=True)
        sums_a.to_core()
        sums_b.to_core()
        for copy in text_copies(restext_any, text_out, 0):
            copy.start()

    def dkv_copy(slot, r):
        return remote(
            dkv_out.at[slot, r - 1], dkv_in.at[slot, r - 1], dkv_sem.at[slot, r - 1], dkv_in_sem.at[slot, r - 1],
            place.mate(-r)
        )

    def settle(of):
        slot, pair, item = lax.rem(of, 2), of // items, lax.rem(of, items)
        total = own_s[slot].astype(f32)
        for r in range(1, seq_size):
            dkv_copy(slot, r).wait_recv()
            total = total + dkv_in[slot, r - 1].astype(f32)
        at = pl.ds(pl.multiple_of(item * rows, ROW_TILE), rows)
        mixed_s[pair, at, width:] = total.astype(bf16)

    def pair_done(pair):
        mixed = mixed_s[pair]
        if pair == 0:
            fetches[0].wait()
        grad = t_mm(first_s[...].reshape(items * rows, model), mixed).astype(bf16)
        chunk = sum(pair >= first for first, _ in chunks) - 1
        first, end = chunks[chunk]
        part = sums_in[chunk].part
        part[..., 3 * (pair - first) * width : 3 * (pair - first + 1) * width] = grad.reshape(
            part.shape[:-1] + (3 * width,)
        )
        if pair == end - 1:
            (sums_in[chunk].start if chunk else sums_in[chunk].to_core)()
        cols = slice(pair * width, (pair + 1) * width)
        sums_s[QBIAS : QBIAS + 1, cols] = column_sum(mixed[:, :width])
        sums_s[VBIAS : VBIAS + 1, cols] = column_sum(mixed[:, 2 * width :])

    def finish_in(chunk):
        total = sums_in[chunk].last()
        first, end = chunks[chunk]
        for m in range(end - first):
            for n in range(3):
                at, of = n * model + (first + m) * width, (3 * m + n) * width
                total_in[:, at : at + width] = total[:, of : of + width]

    def finish_a():
        total = sums_a.last()
        total_a[...] = total[:, : total_a.shape[1]]
        vec2_out[...] = total[:, total_a.shape[1] :]

    def finish_b():
        total = sums_b.last()
        total_b[...] = total[:, :model]
        upb_out[...] = total[:, model:]

    tail_at = last + 1
    agenda = [(2, sums_a.to_second), (3, sums_b.to_second), (6, sums_a.to_first), (7, sums_b.to_first),
              (9, sums_a.to_line), (10, sums_b.to_line), (tail_at, finish_a), (tail_at + 2, finish_b)]
    steps = (sums_in[0].to_second, sums_in[0].to_first, sums_in[0].to_line, functools.partial(finish_in, 0))
    agenda += [(max(at, items * chunks[0][1] + 2), step) for at, step in zip((9, 11, tail_at, tail_at + 1), steps)]
    agenda += [(tail_at, sums_in[1].to_line), (tail_at + 2, functools.partial(finish_in, 1))]
    agenda += [(tail_at + 1, sums_in[2].to_line), (tail_at + 3, functools.partial(finish_in, 2))]
    agenda.sort(key=lambda entry: entry[0])

    @pl.when(turn == 0)
    def _():
        place.greet(corners=True)
        for copy in fetches:
            copy.start()
        sums_s[...] = jnp.zeros_like(sums_s)

    collect(keys, [ref[0] for ref in k_refs], patch, text)
    collect(values, [ref[0] for ref in v_refs], patch, text)
    q, grad = q_ref[0], grad_ref[0]
    edge, heads, span = count * patch, width // head, keys.shape[0] - count * patch
    lane = lax.broadcasted_iota(jnp.int32, (1, width), 1) // head
    row = lax.broadcasted_iota(jnp.int32, (width, 1), 0) // head
    by_head(text_keys, keys[edge:], lane, heads, False)
    by_head(text_values, values[edge:], lane, heads, False)
    text_bias = jnp.concatenate([bias_ref[0]] * heads, axis=1)
    inner = grad.astype(f32) * (at_ref[0].astype(f32) + rest_ref[0].astype(f32))
    q_heads = [jnp.where(lane == h, q, jnp.zeros_like(q)) for h in range(heads)]
    grad_heads = [jnp.where(lane == h, grad, jnp.zeros_like(grad)) for h in range(heads)]
    deltas = [jnp.sum(jnp.where(lane == h, inner, 0.0), axis=1, keepdims=True) for h in range(heads)]
    logs = [log_ref[0, :, h * head : h * head + 1] for h in range(heads)]

    def first_dots(h):
        return mm_t(q_heads[h], keys[:edge]), mm_t(grad_heads[h], values[:edge])

    scores, grad_probs = first_dots(0)
    text_scores = mm_t(q, text_keys[...]) + text_bias
    text_grad_probs = mm_t(grad, text_values[...])
    dq, text_probs, text_grads = None, [], []
    for h in range(heads):
        following = first_dots(h + 1) if h + 1 < heads else (None, None)
        cols = slice(h * span, (h + 1) * span)
        text_head = jnp.exp2(text_scores[:, cols] - logs[h])
        text_probs.append(text_head.astype(bf16))
        text_grads.append((text_head * (text_grad_probs[:, cols] - deltas[h])).astype(bf16))
        probs = jnp.exp2(scores - logs[h])
        grad_scores = (probs * (grad_probs - deltas[h])).astype(bf16)
        probs_s[h * rows : (h + 1) * rows, :] = probs.astype(bf16)
        scores_s[h * rows : (h + 1) * rows, :] = grad_scores
        dq_head = mm(grad_scores, keys[:edge])
        dq = dq_head if dq is None else jnp.where(lane == h, dq_head, dq)
        scores, grad_probs = following
    text_probs, text_grads = jnp.concatenate(text_probs, axis=1), jnp.concatenate(text_grads, axis=1)
    dq = dq + mm(text_grads, text_keys[...])
    dv = jnp.transpose(t_mm(jnp.concatenate(grad_heads, axis=0), probs_s[...]).astype(bf16))
    dk = jnp.transpose((t_mm(jnp.concatenate(q_heads, axis=0), scores_s[...]) * LN2).astype(bf16))

    def of_heads(wide):
        own = wide[:, :span]
        for h in range(1, heads):
            own = jnp.where(row == h, wide[:, h * span : (h + 1) * span], own)
        return jnp.transpose(own.astype(bf16))

    text_dv, text_dk = of_heads(t_mm(grad, text_probs)), of_heads(t_mm(q, text_grads) * LN2)
    slot = lax.rem(turn, 2)

    @pl.when(turn == 0)
    def _():
        begin()

    for at in sorted({at for at, _ in agenda if at <= last}):

        @pl.when(turn == at - 1)
        def _(at=at):
            for when, step in agenda:
                if when == at:
                    step()

    at = pl.ds(pl.multiple_of(i * rows, ROW_TILE), rows)
    mixed_s[p, at, :width] = (dq * (1.0 / math.sqrt(head))).astype(bf16)
    own_s[slot, :patch, :width] = dk[:patch]
    own_s[slot, :patch, width:] = dv[:patch]
    own_s[slot, patch:, :width] = text_dk[:text]
    own_s[slot, patch:, width:] = text_dv[:text]

    @pl.when(turn > 0)
    def _():
        settle(turn - 1)

    @pl.when(turn > 1)
    def _():
        for r in range(1, seq_size):
            dkv_copy(slot, r).wait_send()

    for r in range(1, seq_size):
        for n, (part, text_part) in enumerate(((dk, text_dk), (dv, text_dv))):
            cols = slice(n * width, (n + 1) * width)
            dkv_out[slot, r - 1, :patch, cols] = part[r * patch : (r + 1) * patch]
            dkv_out[slot, r - 1, patch:, cols] = text_part[r * text : (r + 1) * text]
        dkv_copy(slot, r).start()

    for pair in range(pairs - 1):

        @pl.when(turn == items * (pair + 1))
        def _(pair=pair):
            pair_done(pair)

    @pl.when(turn == last)
    def _():
        left = [[step for when, step in agenda if when == at] for at in sorted({at for at, _ in agenda if at > last})]

        def more():
            if left:
                for step in left.pop(0):
                    step()

        half = pairs // 2
        sides = (w_s.at[:, : 3 * half * width], w2_s)

        def grad_first(item, side):
            at = slice(item * rows, (item + 1) * rows)
            mixed = [
                mixed_s[side * half + m, at, n * width : (n + 1) * width] for n in (1, 2, 0) for m in range(half)
            ]
            return mm_t(jnp.concatenate(mixed, axis=1), sides[side][...])

        for copy in fetches[1:]:
            copy.wait()
        for item in range(items):
            first_grad_s[item] = grad_first(item, 0)
        settle(last)
        pair_done(pairs - 1)
        for item in range(items):
            grad = first_grad_s[item] + grad_first(item, 1)
            first_grad_s[item] = grad
            scaled, inverse = norm_rows(jnp.concatenate([x_s[item], xtext_s[item]], axis=0).astype(f32))
            scaled_s[item] = scaled
            inverse_s[item] = jnp.broadcast_to(inverse, (rows, LANES))
            sums_s[GAIN1 : GAIN1 + 1, :] += column_sum(grad * scaled)
            sums_s[SHIFT1 : SHIFT1 + 1, :] += column_sum(grad)
        sums_vec.part[...] = to_columns(sums_s[...]).reshape(sums_vec.part.shape)
        sums_vec.start()
        more()
        gain = vec_ref[GAIN1 : GAIN1 + 1]
        patch_copies = [
            pltpu.make_async_copy(patch_s.at[item], grad_out.at[item], patch_sem.at[item]) for item in range(items)
        ]
        for item in range(items):
            grad_rows = norm_back(first_grad_s[item], scaled_s[item], inverse_s[item][:, :1], gain)
            grad_rows = (gb_s[item].astype(f32) + grad_rows).astype(bf16)
            patch_s[item] = grad_rows[:patch]
            patch_copies[item].start()
            text_s[item] = grad_rows[patch:]
            if item == 0:
                sums_vec.to_line()
            more()
        for copy in text_copies(text_s, text_grad_out, 1):
            copy.start()
        while left:
            more()
        vec_out[...] = sums_vec.last()
        for copies in (text_copies(restext_any, text_out, 0), text_copies(text_s, text_grad_out, 1)):
            for copy in copies:
                copy.wait()
        for slot in range(2):
            for r in range(1, seq_size):
                dkv_copy(slot, r).wait_send()
        for copy in patch_copies:
            copy.wait()


def back(q, keys, values, bias, logs, attended, rest, grad_att, part_a, part_b, w_in, vecs, first_in, patches, x_text,
         grad_branch, res_text, head, width, devices, seq_size):
    items, patch, model = patches.shape
    rows, text = q.shape[1], x_text.shape[1]
    count, tail, pairs, depth = len(keys), bias.shape[-1], model // width, devices // 8
    span = count * patch + tail
    block = pl.BlockSpec((1, rows, width), lambda p, i: (i, 0, p))
    parts = [part.reshape((depth, 2, 2, 2, part.shape[0] // devices, part.shape[1])) for part in (part_a, part_b)]
    (rows_a, cols_a), (rows_b, cols_b) = parts[0].shape[4:], parts[1].shape[4:]
    sems = pltpu.SemaphoreType.DMA
    others = seq_size - 1
    slots = jax.ShapeDtypeStruct((items, seq_size * text, model), bf16)
    cols = 3 * (pairs - 2) * width
    scratch_in = [pltpu.VMEM((depth, 2, 2, 2, rows_a, cols), bf16)] + reduce_scratch(depth, rows_a, cols)
    scratch_in += short_reduce_scratch(depth, rows_a, 3 * width) * 2
    return pl.pallas_call(
        functools.partial(back_kernel, count, patch, head, seq_size, pairs, items),
        grid=(pairs, items),
        in_specs=[block] * (1 + 2 * count)
        + [pl.BlockSpec((1, 1, tail), lambda p, i: (i, 0, 0))]
        + [block] * 4
        + [ANY] * 4
        + [WHOLE]
        + [ANY] * 5,
        out_specs=[ANY] * 3 + [WHOLE] * 6,
        out_shape=[
            jax.ShapeDtypeStruct(patches.shape, bf16),
            slots,
            slots,
            jax.ShapeDtypeStruct((rows_a, cols_a - LANES), f32),
            jax.ShapeDtypeStruct((rows_b, cols_b - LANES), f32),
            jax.ShapeDtypeStruct((rows_a, 3 * model), f32),
            jax.ShapeDtypeStruct((rows_a, LANES), f32),
            jax.ShapeDtypeStruct((rows_a, LANES), f32),
            jax.ShapeDtypeStruct((rows_b, LANES), f32),
        ],
        scratch_shapes=[
            pltpu.VMEM((span, width), bf16),
            pltpu.VMEM((span, width), bf16),
            pltpu.VMEM((width // head * tail, width), bf16),
            pltpu.VMEM((width // head * tail, width), bf16),
            pltpu.VMEM((width // head * rows, count * patch), bf16),
            pltpu.VMEM((width // head * rows, count * patch), bf16),
            pltpu.VMEM((pairs, items * rows, 3 * width), bf16),
            pltpu.VMEM((2, rows, 2 * width), bf16),
            pltpu.VMEM((2, others, rows, 2 * width), bf16),
            pltpu.VMEM((2, others, rows, 2 * width), bf16),
            pltpu.VMEM((8, model), f32),
            pltpu.VMEM(w_in[0].shape, bf16),
            pltpu.VMEM(w_in[1].shape, bf16),
            pltpu.VMEM(first_in.shape, bf16),
            pltpu.VMEM(patches.shape, bf16),
            pltpu.VMEM(x_text.shape, bf16),
            pltpu.VMEM(grad_branch.shape, bf16),
            pltpu.VMEM(x_text.shape, bf16),
            pltpu.VMEM(patches.shape, bf16),
            pltpu.VMEM(q.shape, f32),
            pltpu.VMEM(q.shape, f32),
            pltpu.VMEM((items, rows, LANES), f32),
            sems((6,)),
            sems((2, others)),
            sems((2, others)),
            sems((2, seq_size)),
            sems((2, seq_size)),
            sems((items,)),
        ]
        + reduce_scratch(depth, rows_a, cols_a)
        + reduce_scratch(depth, rows_b, cols_b)
        + scratch_in
        + short_reduce_scratch(depth, rows_a, LANES),
        compiler_params=compiler_params(collective_id=2, has_side_effects=True),
        name="back",
    )(q, *keys, *values, bias, logs, attended, rest, grad_att, *parts, *w_in, vecs, first_in, patches, x_text,
      grad_branch, res_text)


def outputs_kernel(*refs):
    text_any, patch_any, text_grad_any, total_a, total_b, total_in, vec1, vec2, upb = refs[:9]
    outs = list(refs[9:25])
    out_text, patch_out, grad_text = outs[:3]
    first_gain, first_shift, in_weight, query_bias, value_bias, out_weight, branch_bias = outs[3:10]
    second_gain, second_shift, up_weight, up_bias, down_weight, down_bias = outs[10:]
    patch_s, text_s, text_grad_s, sem = refs[25:]
    items, slots, units = patch_s.shape[0], out_text.shape[1], up_weight.shape[1]
    fetches = [pltpu.make_async_copy(patch_any.at[i], patch_s.at[i], sem.at[0, i]) for i in range(items)]
    stores = [pltpu.make_async_copy(patch_s.at[i], patch_out.at[i], sem.at[1, i]) for i in range(items)]
    texts = [
        pltpu.make_async_copy(text_any, text_s, sem.at[2, 0]),
        pltpu.make_async_copy(text_grad_any, text_grad_s, sem.at[2, 1]),
    ]
    for copy in fetches + texts:
        copy.start()

    count, wide = vec1.shape[0], upb.shape[0]
    empty = jnp.zeros((LANES - 2 * count - wide, LANES), f32)
    table = jnp.transpose(jnp.concatenate([upb[...], vec1[...], vec2[...], empty], axis=0))
    in_weight[...] = total_in[...]
    out_weight[...] = total_a[:, units:]
    up_weight[...] = total_a[:, :units]
    down_weight[...] = total_b[...]
    for ref, at in ((first_gain, GAIN1), (first_shift, SHIFT1), (query_bias, QBIAS), (value_bias, VBIAS)):
        ref[...] = table[at, wide : wide + count]
    for ref, at in ((branch_bias, BRANCH), (second_gain, GAIN2), (second_shift, SHIFT2), (down_bias, DOWNB)):
        ref[...] = table[at, wide + count : wide + 2 * count]
    up_bias[...] = table[0, :wide]
    for fetch, store in zip(fetches, stores):
        fetch.wait()
        store.start()
    for copy in texts:
        copy.wait()
    out_text[...] = text_s[:, :slots]
    grad_text[...] = text_grad_s[:, :slots]
    for copy in stores:
        copy.wait()


def outputs(text, patch_grad, text_grad, total_a, total_b, total_in, vec1, vec2, upb, slots, units):
    items, patch, model = patch_grad.shape

    def shape(*dims):
        return jax.ShapeDtypeStruct(dims, f32)

    count = total_in.shape[0]
    vector, texts = shape(count), jax.ShapeDtypeStruct((items, slots, model), bf16)
    return pl.pallas_call(
        outputs_kernel,
        in_specs=[ANY] * 3 + [WHOLE] * 6,
        out_specs=[WHOLE, ANY, WHOLE] + [WHOLE] * 13,
        out_shape=[texts, jax.ShapeDtypeStruct(patch_grad.shape, bf16), texts]
        + [vector, vector, shape(count, 3 * model), vector, vector, shape(count, model), vector, vector, vector]
        + [shape(count, units), shape(upb.shape[0]), shape(*total_b.shape), vector],
        scratch_shapes=[
            pltpu.VMEM(patch_grad.shape, bf16),
            pltpu.VMEM(text.shape, bf16),
            pltpu.VMEM(text.shape, bf16),
            pltpu.SemaphoreType.DMA((3, max(items, 2))),
        ],
        compiler_params=compiler_params(),
        name="outputs",
    )(text, patch_grad, text_grad, total_a, total_b, total_in, vec1, vec2, upb)


def per_device(
    seq_size,
    devices,
    patches,
    text_rows,
    lengths,
    first_gain,
    first_shift,
    in_weight,
    query_bias,
    value_bias,
    out_weight,
    branch_bias,
    second_gain,
    second_shift,
    up_weight,
    up_bias,
    down_weight,
    down_bias,
    patch_cotangent,
    text_cotangent,
):
    items, patch, model = patches.shape
    slots = text_rows.shape[1]
    units = up_weight.shape[1]
    head = model // HEADS
    width = min(LANES, model)
    text = round_up(-(-slots // seq_size), ROW_TILE)
    seq = lax.axis_index("seq")
    vectors = [first_gain, first_shift, query_bias, value_bias, branch_bias, second_gain, second_shift, down_bias]
    w_in, vecs, bias, (weights, w_down), x_text, first_in, q, attended, rest, logs, keys, values = forward(
        in_weight, vectors, up_weight, up_bias, out_weight, down_weight, patches, text_rows, lengths, text, width, head,
        devices, seq_size
    )
    out_patches, res_text, grad_branch, grad_att, part_a, part_b = ffn(
        seq[None], patches, x_text, attended, patch_cotangent, text_cotangent, weights, w_down, vecs
    )
    grad_patches, grad_text, out_text, sums, down_grad, in_grad, vec1, vec2, up_bias_grad = back(
        q, keys, values, bias, logs, attended, rest, grad_att, part_a, part_b, w_in, vecs, first_in, patches, x_text,
        grad_branch, res_text, head, width, devices, seq_size
    )
    rest = outputs(
        out_text, grad_patches, grad_text, sums, down_grad, in_grad, vec1, vec2, up_bias_grad, slots, units
    )
    return (out_patches, *rest)


def solution(mesh):
    both = ("dp", "seq")
    rows, slots, vector, matrix = P("dp", "seq", None), P("dp", None, None), P(both), P(both, None)
    weights = (vector, vector, matrix, vector, vector, matrix, vector, vector, vector, matrix, vector, matrix, vector)
    return jax.shard_map(
        functools.partial(per_device, mesh.shape["seq"], mesh.size),
        mesh=mesh,
        in_specs=(rows, slots, P("dp")) + weights + (rows, slots),
        out_specs=(rows, slots, rows, slots) + weights,
        check_vma=False,
    )
```

```python
import functools
import math

import jax
import jax.numpy as jnp
from jax import lax
from jax.experimental import pallas as pl
from jax.experimental.pallas import tpu as pltpu
from jax.sharding import PartitionSpec as P

HEADS = 8
EPSILON = 1e-05
NEG_FILL = -1e30
LOG2E = math.log2(math.e)
LN2 = math.log(2.0)
ROW_TILE = 16
LANES = 128
SIDE = 64
MESH = pl.DeviceIdType.MESH
f32, bf16 = jnp.float32, jnp.bfloat16

GAIN1, SHIFT1, QBIAS, VBIAS, BRANCH, GAIN2, SHIFT2, DOWNB = range(8)


def round_up(value, unit):
    return -(-value // unit) * unit


def mm(a, b):
    return lax.dot_general(a, b, (((1,), (0,)), ((), ())), preferred_element_type=f32)


def mm_t(a, b):
    return lax.dot_general(a, b, (((1,), (1,)), ((), ())), preferred_element_type=f32)


def t_mm(a, b):
    return lax.dot_general(a, b, (((0,), (0,)), ((), ())), preferred_element_type=f32)


def compiler_params(**more):
    return pltpu.CompilerParams(vmem_limit_bytes=60 * 2**20, **more)


WHOLE = pl.BlockSpec(memory_space=pltpu.VMEM)
ANY = pl.BlockSpec(memory_space=pl.ANY)


class Place:
    def __init__(self, depth, seq_size):
        self.depth, self.seq_size = depth, seq_size
        index = lax.axis_index("dp") * seq_size + lax.axis_index("seq")
        self.core = lax.rem(index, 2)
        self.x = lax.rem(index // 2, 2)
        self.y = lax.rem(index // 4, 2)
        self.z = index // 8
        core = self.core
        flip_x, flip_y = 1 - self.x, 1 - self.y
        x_first = self.x * core + flip_x * (1 - core)
        y_first = self.y * (1 - core) + flip_y * core
        x_second = self.x * (1 - core) + flip_x * core
        y_second = self.y * core + flip_y * (1 - core)
        self.columns = (
            (self.y, self.x),
            (y_first, x_first),
            (y_second, x_second),
            (flip_y, flip_x),
        )

    def device(self, z, y, x, core):
        index = ((z * 2 + y) * 2 + x) * 2 + core
        return (index // self.seq_size, lax.rem(index, self.seq_size))

    def layer(self, k):
        return lax.rem(self.z + self.depth - k, self.depth)

    def ahead(self, k):
        return lax.rem(self.z + k, self.depth)

    def first(self):
        return self.device(self.z, *self.columns[1], self.core)

    def second(self):
        return self.device(self.z, *self.columns[2], self.core)

    def other_core(self):
        return self.device(self.z, self.y, self.x, 1 - self.core)

    def above(self, k):
        return self.device(self.ahead(k), self.y, self.x, self.core)

    def mate(self, step):
        return (lax.axis_index("dp"), lax.rem(lax.axis_index("seq") + self.seq_size - step, self.seq_size))

    def octant(self, n):
        column, core = n % 4, n // 4
        y, x = self.columns[column]
        core = self.core * (1 - core) + (1 - self.core) * core
        return self.device(self.z, y, x, core), (y, x, core)

    def friends(self, corners):
        friends = [self.above(k) for k in range(1, self.depth)]
        friends += [self.octant(n)[0] for n in range(1, 8)] if corners else [self.first(), self.second(), self.other_core()]
        return friends + [self.mate(step) for step in range(1, self.seq_size)]

    def greet(self, corners=False):
        barrier = pltpu.get_barrier_semaphore()
        for friend in self.friends(corners):
            pl.semaphore_signal(barrier, inc=1, device_id=friend, device_id_type=MESH)

    def meet(self, corners=False):
        pl.semaphore_wait(pltpu.get_barrier_semaphore(), len(self.friends(corners)))


def remote(src, dst, send, recv, device):
    return pltpu.make_async_remote_copy(
        src_ref=src, dst_ref=dst, send_sem=send, recv_sem=recv, device_id=device, device_id_type=MESH
    )


class Spread:
    def __init__(self, place, shard, full, out, into, local):
        self.place, self.shard, self.full, self.out, self.into, self.local = place, shard, full, out, into, local

    def column(self, n, core=None):
        y, x = self.place.columns[n]
        return self.full.at[:, y, x, self.place.core if core is None else core]

    def line_copy(self, k):
        place = self.place
        here = self.full.at[place.z, place.y, place.x, place.core]
        return remote(self.shard, here, self.out.at[6 + k], self.into.at[6 + k], place.above(k))

    def own_copy(self):
        place = self.place
        return pltpu.make_async_copy(self.shard, self.full.at[place.z, place.y, place.x, place.core], self.local)

    def copy(self, n, lane):
        here = self.column(n)
        device = (self.place.first, self.place.second, self.place.second)[lane] if lane < 3 else self.place.other_core
        return remote(here, here, self.out.at[lane], self.into.at[lane], device())

    def arrive(self, n, lane):
        self.copy(n, lane).wait_recv()

    def start(self):
        self.own_copy().start()
        for k in range(1, self.place.depth):
            self.line_copy(k).start()

    def send_line(self):
        self.own_copy().wait()
        for k in range(1, self.place.depth):
            self.line_copy(k).wait_recv()
        for lane in (0, 1, 3):
            self.copy(0, lane).start()

    def forward_first(self):
        self.arrive(1, 0)
        self.copy(1, 2).start()
        self.copy(1, 4).start()

    def forward_second(self, half):
        self.arrive(2 + half, 1 + half)
        self.copy(2 + half, 5 + half).start()

    def finish(self):
        for n in range(4):
            self.arrive(n, 3 + n)
        for k in range(1, self.place.depth):
            self.line_copy(k).wait_send()
        for lane in range(7):
            self.copy(0, lane).wait_send()


def spread_sems(depth):
    sems = pltpu.SemaphoreType.DMA
    return [sems((6 + depth,)), sems((6 + depth,)), sems]


class Results:
    def result_copy(self, n, other):
        y, x = self.place.columns[(0, 2, 1, 3)[n] if other else n]
        core = 1 - self.place.core if other else self.place.core
        here = (slice(None), y, x, core)
        return pltpu.make_async_copy(self.full.at[here], self.result.at[here], self.results.at[n, other])

    def land(self, n):
        self.arrive_core(n)
        for other in range(2):
            self.result_copy(n, other).start()

    def finish(self):
        for n in range(4):
            for other in range(2):
                self.result_copy(n, other).wait()
        self.sent()


class Gather(Results, Spread):
    def __init__(self, place, shard, full, result, out, into, local, results):
        Spread.__init__(self, place, shard, full, out, into, local)
        self.result, self.results = result, results

    def arrive_core(self, n):
        self.arrive(n, 3 + n)

    def sent(self):
        for k in range(1, self.place.depth):
            self.line_copy(k).wait_send()
        for lane in range(7):
            self.copy(0, lane).wait_send()


def gather_sems(depth):
    return spread_sems(depth) + [pltpu.SemaphoreType.DMA((4, 2))]


class Reduce:
    def __init__(self, place, part, from_core, held, from_second, pair, from_first, line, from_line, out, into, local):
        self.place, self.part, self.local = place, part, local
        self.from_core, self.held, self.from_second, self.pair = from_core, held, from_second, pair
        self.from_first, self.line, self.from_line = from_first, line, from_line
        self.out, self.into = out, into

    def copy(self, src, dst, lane, device):
        return remote(src, dst, self.out.at[lane], self.into.at[lane], device)

    def own_copy(self):
        return pltpu.make_async_copy(self.part.at[:, :, :, self.place.core], self.held, self.local)

    def core_copy(self):
        return self.copy(self.part.at[:, :, :, 1 - self.place.core], self.from_core, 0, self.place.other_core())

    def second_copies(self):
        columns = self.place.columns
        return [
            self.copy(self.held.at[:, columns[2 + k][0], columns[2 + k][1]], self.from_second.at[k], 1 + k,
                      self.place.second())
            for k in range(2)
        ]

    def first_copy(self):
        return self.copy(self.pair.at[1], self.from_first, 3, self.place.first())

    def line_copies(self):
        place = self.place
        return [
            self.copy(self.line.at[place.ahead(k)], self.from_line.at[k - 1], 3 + k, place.above(k))
            for k in range(1, place.depth)
        ]

    def to_core(self):
        self.core_copy().start()
        self.own_copy().start()

    def to_second(self):
        self.own_copy().wait()
        self.core_copy().wait()
        self.held[...] += self.from_core[...]
        for copy in self.second_copies():
            copy.start()

    def to_first(self):
        for copy in self.second_copies():
            copy.wait()
        for k in range(2):
            y, x = self.place.columns[k]
            self.pair[k] = self.held[:, y, x] + self.from_second[k]
        self.first_copy().start()

    def to_line(self):
        self.first_copy().wait()
        self.line[...] = self.pair[0] + self.from_first[...]
        for copy in self.line_copies():
            copy.start()

    def last(self):
        for copy in self.line_copies():
            copy.wait()
        result = self.line[self.place.z].astype(f32)
        for k in range(self.place.depth - 1):
            result = result + self.from_line[k].astype(f32)
        return result


def reduce_scratch(depth, rows, cols):
    shapes = [(depth, 2, 2), (depth, 2, 2), (2, depth), (2, depth), (depth,), (depth,), (depth - 1,)]
    sems = pltpu.SemaphoreType.DMA
    return [pltpu.VMEM(shape + (rows, cols), bf16) for shape in shapes] + [sems((3 + depth,))] * 2 + [sems]


class ShortReduce:
    def __init__(self, place, part, from_octant, line, from_line, out, into):
        self.place, self.part, self.from_octant, self.line, self.from_line = place, part, from_octant, line, from_line
        self.out, self.into = out, into

    def octant_copy(self, n):
        device, (y, x, core) = self.place.octant(n)
        return remote(
            self.part.at[:, y, x, core], self.from_octant.at[n - 1], self.out.at[n - 1], self.into.at[n - 1], device
        )

    def line_copy(self, k):
        return remote(
            self.line.at[self.place.ahead(k)], self.from_line.at[k - 1], self.out.at[6 + k], self.into.at[6 + k],
            self.place.above(k)
        )

    def start(self):
        for n in range(1, 8):
            self.octant_copy(n).start()

    def to_line(self):
        place = self.place
        total = self.part[:, place.y, place.x, place.core].astype(f32)
        for n in range(1, 8):
            self.octant_copy(n).wait()
            total = total + self.from_octant[n - 1].astype(f32)
        self.line[...] = total.astype(bf16)
        for k in range(1, place.depth):
            self.line_copy(k).start()

    def last(self):
        total = self.line[self.place.z].astype(f32)
        for k in range(1, self.place.depth):
            self.line_copy(k).wait()
            total = total + self.from_line[k - 1].astype(f32)
        return total


def short_reduce_scratch(depth, rows, cols):
    sems = pltpu.SemaphoreType.DMA
    shapes = [(depth, 2, 2, 2), (7, depth), (depth,), (depth - 1,)]
    return [pltpu.VMEM(shape + (rows, cols), bf16) for shape in shapes] + [sems((6 + depth,))] * 2


def norm_rows(rows):
    centred = rows - jnp.mean(rows, axis=1, keepdims=True)
    inverse = lax.rsqrt(jnp.mean(centred * centred, axis=1, keepdims=True) + EPSILON)
    return centred * inverse, inverse


def norm_back(grad, scaled, inverse, gain):
    inner = grad * gain
    return inverse * (
        inner
        - jnp.mean(inner, axis=1, keepdims=True)
        - scaled * jnp.mean(inner * scaled, axis=1, keepdims=True)
    )


def gelu_both(v):
    power = jnp.exp2(v * v * (-0.5 * LOG2E))
    cdf = 0.5 + 0.5 * lax.erf(v * math.sqrt(0.5))
    return v * cdf, cdf + v * power * (1.0 / math.sqrt(2.0 * math.pi))


def column_sum(rows):
    return jnp.sum(rows.astype(f32), axis=0, keepdims=True)


def to_columns(rows):
    count, width = rows.shape
    return jnp.transpose(jnp.concatenate([rows, jnp.zeros((LANES - count, width), f32)], axis=0)).astype(bf16)


def own_text(ref, text, seq):
    slots, width = ref.shape
    own = jnp.zeros((text, width), ref.dtype)
    for r in range(-(-slots // text)):
        share = ref[r * text : min(slots, (r + 1) * text), :]
        if share.shape[0] < text:
            share = jnp.concatenate([share, jnp.zeros((text - share.shape[0], width), ref.dtype)], axis=0)
        own = jnp.where(seq == r, share, own)
    return own


def as_columns(vectors):
    length = vectors[0].shape[0]
    rows = [vector.reshape(1, length).astype(f32) for vector in vectors]
    rows = jnp.concatenate(rows + [jnp.zeros((LANES - len(rows), length), f32)], axis=0)
    rows = jnp.concatenate([rows, jnp.zeros((LANES, LANES - length), f32)], axis=1)
    return jnp.transpose(rows)[:length].astype(bf16)


def collect(dst, blocks, patch, text):
    count, width = len(blocks), blocks[0].shape[1]
    for r, block in enumerate(blocks):
        dst[r * patch : (r + 1) * patch, :width] = block[:patch]
        at = count * patch + r * text
        dst[at : at + text, :width] = block[patch:]
    filled = count * (patch + text)
    if dst.shape[0] > filled:
        dst[filled:, :width] = jnp.zeros((dst.shape[0] - filled, width), dst.dtype)


def by_head(dst, src, lane, heads, ones):
    count, width = src.shape
    for h in range(heads):
        rows = slice(h * count, (h + 1) * count)
        dst[rows, :width] = jnp.where(lane == h, src, jnp.zeros_like(src))
        if ones:
            dst[rows, width:] = jnp.where(lane == h, jnp.ones_like(src), jnp.zeros_like(src))


def forward_kernel(seq_size, text, width, head, *refs):
    refs = list(refs)

    def take(number):
        taken = refs[:number]
        del refs[:number]
        return taken

    given, x_any, length_ref = take(14), *take(2)
    w_out, w2_out, vecs, bias_ref, full_a, full_b, xtext_ref, first_out, q_out, out_out, rest_out, log_out = take(12)
    k_outs, v_outs = take(seq_size), take(seq_size)
    shard, shard2, shard_a, shard_b, w_full, w2_full, into_a, into_b, x_s, n_s, first_s, q_s, k_s, v_s = take(14)
    keys, values, text_keys, text_values, out_s, rest_s, log_s = take(7)
    sems, sems2, sems_a, sems_b = take(3), take(3), take(4), take(4)
    x_sem, w_sem, out_sem, kv_sem, kv_in_sem, kv_out_sem, turn_sem = take(7)
    held, given_sem = take(14), *take(1)
    fetches = [pltpu.make_async_copy(src, dst, given_sem.at[n]) for n, (src, dst) in enumerate(zip(given, held))]
    (shard_ref,), vec_refs, (up_ref, up_bias_ref, out_w_ref, down_ref, slot_ref) = held[:1], held[1:9], held[9:]
    items, patch, model = x_s.shape
    units, wide = up_ref.shape[1], shard2.shape[1]
    pairs = model // width
    place = Place(w_full.shape[0], seq_size)
    seq = lax.axis_index("seq")
    x_copies = [pltpu.make_async_copy(x_any.at[i], x_s.at[i], x_sem.at[i]) for i in range(items)]
    place.greet()
    for copy in fetches + x_copies:
        copy.start()
    for copy in fetches[:9]:
        copy.wait()
    for half, to in enumerate((shard, shard2)):
        for n in range(3):
            at = (n + 1) % 3 * model + half * (model // 2)
            to[:, n * (model // 2) : (n + 1) * (model // 2)] = shard_ref[:, at : at + model // 2]
    shard[:, wide:] = as_columns([ref[...] for ref in vec_refs])
    place.meet()
    halves = [Spread(place, shard, w_full, *sems), Spread(place, shard2, w2_full, *sems2)]
    for move in halves:
        move.start()
    for copy in fetches[9:]:
        copy.wait()
    shard_a[:, :units] = up_ref[...]
    shard_a[:, units:] = out_w_ref[...]
    shard_b[:, :model] = down_ref[...]
    shard_b[:, model:] = as_columns([up_bias_ref[...]])
    move_a, move_b = Gather(place, shard_a, into_a, full_a, *sems_a), Gather(place, shard_b, into_b, full_b, *sems_b)
    tail = bias_ref.shape[2]
    col = lax.broadcasted_iota(jnp.int32, (1, tail), 1)
    slot = jnp.full((1, tail), seq_size * text, jnp.int32)
    for r in range(seq_size):
        begin = lax.rem(seq + r, seq_size) * text
        slot = jnp.where((col >= r * text) & (col < (r + 1) * text), begin + col - r * text, slot)
    for i in range(items):
        xtext_ref[i] = own_text(slot_ref.at[i], text, seq)
        bias_ref[i] = jnp.where(slot < length_ref[i], 0.0, NEG_FILL)
    halves[0].send_line()
    halves[1].send_line()
    move_a.start()
    move_b.start()
    for i in range(items):
        x_copies[i].wait()
        n_s[i], _ = norm_rows(jnp.concatenate([x_s[i], xtext_ref[i]], axis=0).astype(f32))
    halves[0].forward_first()
    halves[0].forward_second(0)
    halves[1].forward_first()
    halves[0].forward_second(1)
    halves[1].forward_second(0)
    halves[0].finish()
    move_a.send_line()
    w_copies = [pltpu.make_async_copy(src, dst, w_sem.at[n]) for n, (src, dst) in
                enumerate(((w_full, w_out), (w2_full, w2_out)))]
    w_copies[0].start()
    weight = w_full[...].reshape(model, wide + LANES)
    table = jnp.transpose(weight[:, wide:].astype(f32))
    vecs[...] = table
    scale = LOG2E / math.sqrt(model // HEADS)
    sends, outs = [], []

    def keys_and_values(i, half, weight):
        span = model // 2
        cols = pl.ds(half * span, span)
        projected = mm(first_s[i], weight[:, : 2 * span])
        k_s[0, i, :, cols] = projected[:, :span].astype(bf16)
        v_s[0, i, :, cols] = (projected[:, span:] + table[VBIAS : VBIAS + 1, half * span : (half + 1) * span]).astype(bf16)
        for r in range(1, seq_size):
            for n, ref in enumerate((k_s, v_s)):
                at = ((2 * i + n) * 2 + half) * seq_size + r
                src, dst = ref.at[0, i, :, cols], ref.at[r, i, :, cols]
                sends.append(remote(src, dst, kv_sem.at[at], kv_in_sem.at[at], place.mate(r)))
                sends[-1].start()

    def queries(i, half, weight):
        span = model // 2
        q = mm(first_s[i], weight[:, 2 * span : 3 * span]) + table[QBIAS : QBIAS + 1, half * span : (half + 1) * span]
        q_s[i, :, half * span : (half + 1) * span] = (q * scale).astype(bf16)

    def bring(n, src, dst, i):
        outs.append(pltpu.make_async_copy(src.at[i], dst.at[i], out_sem.at[n, i]))
        outs[-1].start()

    for i in range(items):
        first_s[i] = (n_s[i] * table[GAIN1 : GAIN1 + 1] + table[SHIFT1 : SHIFT1 + 1]).astype(bf16)
        bring(0, first_s, first_out, i)
        keys_and_values(i, 0, weight)
        if i == 0:
            halves[1].forward_second(1)
    halves[1].finish()
    move_b.send_line()
    w_copies[1].start()
    weight2 = w2_full[...].reshape(model, wide)
    for i in range(items):
        keys_and_values(i, 1, weight2)
        bring(1, k_s.at[0], k_outs[0], i)
        bring(2, v_s.at[0], v_outs[0], i)
    for i in range(items):
        queries(i, 0, weight)
        queries(i, 1, weight2)
        bring(3, q_s, q_out, i)

    edge, heads, span = seq_size * patch, width // head, keys.shape[0] - seq_size * patch
    lane = lax.broadcasted_iota(jnp.int32, (1, width), 1) // head
    values[:, width:] = jnp.ones((values.shape[0], values.shape[1] - width), bf16)
    last = items * pairs - 1

    def turn_copies(slot, i, cols):
        return [
            pltpu.make_async_copy(src.at[slot], dst.at[i, :, cols], turn_sem.at[slot, n])
            for n, (src, dst) in enumerate(((out_s, out_out), (rest_s, rest_out), (log_s, log_out)))
        ]

    def kv_out_copies(i):
        return [
            pltpu.make_async_copy(ref.at[r, i], dst[r].at[i], kv_out_sem.at[(2 * i + n) * seq_size + r])
            for n, (ref, dst) in enumerate(((k_s, k_outs), (v_s, v_outs)))
            for r in range(1, seq_size)
        ]

    def exchanged(i):
        for n, ref in enumerate((k_s, v_s)):
            for half in range(2):
                cols = pl.ds(half * (model // 2), model // 2)
                for r in range(1, seq_size):
                    at = ((2 * i + n) * 2 + half) * seq_size + r
                    src, dst = ref.at[0, i, :, cols], ref.at[r, i, :, cols]
                    remote(src, dst, kv_sem.at[at], kv_in_sem.at[at], place.mate(r)).wait_recv()
        for copy in kv_out_copies(i):
            copy.start()

    agenda = (
        (4, move_a.forward_first),
        (4, functools.partial(move_a.forward_second, 0)),
        (6, move_b.forward_first),
        (6, functools.partial(move_b.forward_second, 0)),
        (8, functools.partial(move_a.land, 0)),
        (8, functools.partial(move_a.land, 1)),
        (9, functools.partial(move_a.forward_second, 1)),
        (10, functools.partial(move_a.land, 2)),
        (10, functools.partial(move_b.land, 0)),
        (10, functools.partial(move_b.land, 1)),
        (11, functools.partial(move_b.forward_second, 1)),
        (11, functools.partial(move_b.land, 2)),
        (13, functools.partial(move_a.land, 3)),
        (13, functools.partial(move_b.land, 3)),
    )

    def attend(turn, _):
        i, p = turn // pairs, lax.rem(turn, pairs)
        slot = lax.rem(turn, 2)
        cols = pl.ds(pl.multiple_of(p * width, width), width)

        @pl.when(p == 0)
        def _():
            exchanged(i)

        for at in sorted({at for at, _ in agenda if at <= last}):

            @pl.when(turn == at)
            def _(at=at):
                for when, step in agenda:
                    if when == at:
                        step()

        collect(keys, [k_s[r, i, :, cols] for r in range(seq_size)], patch, text)
        collect(values, [v_s[r, i, :, cols] for r in range(seq_size)], patch, text)
        by_head(text_keys, keys[edge:], lane, heads, False)
        by_head(text_values, values[edge:, :width], lane, heads, True)
        q = q_s[i, :, cols]
        text_bias = jnp.concatenate([bias_ref[i]] * heads, axis=1)

        def scores_of(h):
            return mm_t(jnp.where(lane == h, q, jnp.zeros_like(q)), keys[:edge])

        text_scores = mm_t(q, text_keys[...]) + text_bias
        scores = scores_of(0)
        text_powers, mixed, total, tops = [], None, None, None
        for h in range(heads):
            following = scores_of(h + 1) if h + 1 < heads else None
            text_head = text_scores[:, h * span : (h + 1) * span]
            top = jnp.maximum(jnp.max(scores, axis=1, keepdims=True), jnp.max(text_head, axis=1, keepdims=True))
            powers = jnp.exp2(scores - top).astype(bf16)
            text_powers.append(jnp.exp2(text_head - top).astype(bf16))
            both = mm(powers, values[:edge])
            mixed = both[:, :width] if mixed is None else jnp.where(lane == h, both[:, :width], mixed)
            total = both[:, width:] if total is None else jnp.where(lane == h, both[:, width:], total)
            tops = jnp.broadcast_to(top, mixed.shape) if tops is None else jnp.where(lane == h, top, tops)
            scores = following
        both = mm(jnp.concatenate(text_powers, axis=1), text_values[...])
        total = total + both[:, width:]
        out = (mixed + both[:, :width]) * (1.0 / total)
        high = out.astype(bf16)

        @pl.when(turn > 1)
        def _():
            for copy in turn_copies(slot, i, cols):
                copy.wait()

        out_s[slot] = high
        rest_s[slot] = (out - high.astype(f32)).astype(bf16)
        log_s[slot] = tops + jnp.log2(total)
        for copy in turn_copies(slot, i, cols):
            copy.start()
        return 0

    lax.fori_loop(0, last + 1, attend, 0)
    for when, step in agenda:
        if when > last:
            step()
    move_a.finish()
    move_b.finish()
    for slot in range(2):
        for copy in turn_copies(slot, 0, pl.ds(0, width)):
            copy.wait()
    for copy in sends:
        copy.wait_send()
    for i in range(items):
        for copy in kv_out_copies(i):
            copy.wait()
    for copy in w_copies + outs:
        copy.wait()


def forward(in_weight, vectors, up_weight, up_bias, out_weight, down_weight, patches, text_rows, lengths, text, width,
            head, devices, seq_size):
    items, patch, model = patches.shape
    depth, heads = devices // 8, width // head
    rows, cols = in_weight.shape
    shape_a = (depth, 2, 2, 2, rows, up_weight.shape[1] + model)
    shape_b = (depth, 2, 2, 2, down_weight.shape[0], model + LANES)
    shape_w = (depth, 2, 2, 2, rows, cols // 2 + LANES)
    shape_w2 = (depth, 2, 2, 2, rows, cols // 2)
    shape_x = (items, patch + text, model)
    tail = round_up(seq_size * text, LANES)
    span = seq_size * patch + tail
    tokens = jax.ShapeDtypeStruct(shape_x, bf16)
    sems = pltpu.SemaphoreType.DMA
    given = (in_weight, *vectors, up_weight, up_bias, out_weight, down_weight, text_rows)
    outs = pl.pallas_call(
        functools.partial(forward_kernel, seq_size, text, width, head),
        in_specs=[ANY] * 15 + [pl.BlockSpec(memory_space=pltpu.SMEM)],
        out_specs=[ANY, ANY, WHOLE, WHOLE, ANY, ANY, WHOLE] + [ANY] * (5 + 2 * seq_size),
        out_shape=[
            jax.ShapeDtypeStruct(shape_w, bf16),
            jax.ShapeDtypeStruct(shape_w2, bf16),
            jax.ShapeDtypeStruct((LANES, model), f32),
            jax.ShapeDtypeStruct((items, 1, tail), f32),
            jax.ShapeDtypeStruct(shape_a, bf16),
            jax.ShapeDtypeStruct(shape_b, bf16),
            jax.ShapeDtypeStruct((items, text, model), bf16),
            tokens,
            tokens,
            tokens,
            tokens,
            jax.ShapeDtypeStruct(shape_x, f32),
        ]
        + [tokens] * (2 * seq_size),
        scratch_shapes=[
            pltpu.VMEM(shape_w[4:], bf16),
            pltpu.VMEM(shape_w2[4:], bf16),
            pltpu.VMEM(shape_a[4:], bf16),
            pltpu.VMEM(shape_b[4:], bf16),
            pltpu.VMEM(shape_w, bf16),
            pltpu.VMEM(shape_w2, bf16),
            pltpu.VMEM(shape_a, bf16),
            pltpu.VMEM(shape_b, bf16),
            pltpu.VMEM(patches.shape, bf16),
            pltpu.VMEM(shape_x, f32),
            pltpu.VMEM(shape_x, bf16),
            pltpu.VMEM(shape_x, bf16),
            pltpu.VMEM((seq_size,) + shape_x, bf16),
            pltpu.VMEM((seq_size,) + shape_x, bf16),
            pltpu.VMEM((span, width), bf16),
            pltpu.VMEM((span, 2 * width), bf16),
            pltpu.VMEM((heads * tail, width), bf16),
            pltpu.VMEM((heads * tail, 2 * width), bf16),
            pltpu.VMEM((2, patch + text, width), bf16),
            pltpu.VMEM((2, patch + text, width), bf16),
            pltpu.VMEM((2, patch + text, width), f32),
        ]
        + spread_sems(depth) * 2
        + gather_sems(depth) * 2
        + [sems((items,)), sems((2,)), sems((4, items))]
        + [sems((4 * items * seq_size,))] * 2
        + [sems((2 * items * seq_size,)), sems((2, 3))]
        + [pltpu.VMEM(array.shape, array.dtype) for array in given]
        + [sems((len(given),))],
        compiler_params=compiler_params(collective_id=0, has_side_effects=True),
        name="forward",
    )(*given, patches, lengths)
    w_in, weights = ([full.reshape(-1, full.shape[-1]) for full in pair] for pair in (outs[:2], outs[4:6]))
    return w_in, *outs[2:4], weights, *outs[6:12], outs[12 : 12 + seq_size], outs[12 + seq_size :]


def ffn_kernel(steps, chunk, part, devices, seq_ref, x_ref, xtext_ref, at_ref, dy_ref, dy_slot_ref, w_any, wd_any, vec_ref,
               res_ref, restext_ref, gb_ref, ga_ref, part_out, down_out,
               w_ref, wd_ref, part_ref, down_ref, second_s, hidden_s, pre_s, dy_s, sums_s, bias_s, at_s, gb_s,
               w_sem, wd_sem, part_sem, down_sem):
    step = pl.program_id(0)
    patch, model = x_ref.shape[1:]
    text = xtext_ref.shape[1]
    block, units = patch + text, wd_ref.shape[0]
    chunks = units // chunk
    rows = pl.ds(pl.multiple_of(step * block, ROW_TILE), block)
    gain = vec_ref[GAIN2 : GAIN2 + 1]
    w_out = w_ref.at[:, units:]

    def fetch(cols, at):
        if cols is None:
            return (
                pltpu.make_async_copy(w_any.at[:, units:], w_ref.at[:, units:], w_sem.at[at]),
                pltpu.make_async_copy(wd_any.at[:, model:], wd_ref.at[:, model:], wd_sem.at[at]),
            )
        return (
            pltpu.make_async_copy(w_any.at[:, cols], w_ref.at[:, cols], w_sem.at[at]),
            pltpu.make_async_copy(wd_any.at[cols, :model], wd_ref.at[cols, :model], wd_sem.at[at]),
        )

    @pl.when(step == 0)
    def _():
        others = fetch(None, chunks)
        for copy in others:
            copy.start()
        for c in range(chunks):
            for copy in fetch(pl.ds(c * chunk, chunk), c):
                copy.start()
        sums_s[...] = jnp.zeros_like(sums_s)
        for copy in others:
            copy.wait()
        bias_s[...] = jnp.transpose(wd_ref[:, model:].astype(f32))[:8]

    x = jnp.concatenate([x_ref[0], xtext_ref[0]], axis=0).astype(f32)
    dy = jnp.concatenate([dy_ref[0], own_text(dy_slot_ref.at[0], text, seq_ref[0])], axis=0)
    dy_s[rows, :] = dy
    middle = x + (mm(at_ref[0], w_out[...]) + vec_ref[BRANCH : BRANCH + 1])
    scaled, inverse = norm_rows(middle)
    second_in = (scaled * gain + vec_ref[SHIFT2 : SHIFT2 + 1]).astype(bf16)
    second_s[rows, :] = second_in
    @pl.when(step == 0)
    def _():
        for c in range(chunks):
            for copy in fetch(pl.ds(c * chunk, chunk), c):
                copy.wait()

    def first_dots(c):
        cols = slice(c * part, (c + 1) * part)
        return mm(second_in, w_ref[:, cols]) + bias_s[:1, cols], mm_t(dy, wd_ref[cols, :model])

    result, grad_second = middle + vec_ref[DOWNB : DOWNB + 1], None
    pre, grad_hidden = first_dots(0)
    for c in range(units // part):
        following = first_dots(c + 1) if c + 1 < units // part else (None, None)
        cols = slice(c * part, (c + 1) * part)
        value, slope = gelu_both(pre)
        hidden = value.astype(bf16)
        hidden_s[rows, cols] = hidden
        grad_pre = (grad_hidden * slope).astype(bf16)
        pre_s[rows, cols] = grad_pre
        result = result + mm(hidden, wd_ref[cols, :model])
        back_part = mm_t(grad_pre, w_ref[:, cols])
        grad_second = back_part if grad_second is None else grad_second + back_part
        pre, grad_hidden = following
    result = result.astype(bf16)
    res_ref[0] = result[:patch]
    restext_ref[0] = result[patch:]
    grad_branch = (dy.astype(f32) + norm_back(grad_second, scaled, inverse, gain)).astype(bf16)
    gb_ref[0] = grad_branch
    ga_ref[0] = mm_t(grad_branch, w_out[...]).astype(bf16)
    at_s[rows, :] = at_ref[0]
    gb_s[rows, :] = grad_branch
    for at, grad in ((BRANCH, grad_branch), (GAIN2, grad_second * scaled), (SHIFT2, grad_second), (DOWNB, dy)):
        sums_s[at : at + 1, :] += column_sum(grad)

    @pl.when(step == steps - 1)
    def _():
        groups = units // model
        copies = []
        part_ref[:, units : units + model] = t_mm(at_s[...], gb_s[...]).astype(bf16)
        side = units + model
        part_ref[:, side:] = to_columns(sums_s[...])
        step_rows, count = model // devices, units // devices
        for c in range(groups):
            bias_sum = column_sum(pre_s[:, c * model : (c + 1) * model])
            for m in range(model // count):
                at = (c * model // count + m) * step_rows
                part_ref[at : at + 1, side + SIDE : side + SIDE + count] = bias_sum[
                    :, m * count : (m + 1) * count
                ].astype(bf16)
        copies.append(pltpu.make_async_copy(part_ref.at[:, units:], part_out.at[:, units:], part_sem.at[groups]))
        copies[-1].start()
        for c in range(groups):
            cols = slice(c * model, (c + 1) * model)
            at = pl.ds(c * model, model)
            grad_pre = pre_s[:, cols]
            part_ref[:, cols] = t_mm(second_s[...], grad_pre).astype(bf16)
            copies.append(pltpu.make_async_copy(part_ref.at[:, at], part_out.at[:, at], part_sem.at[c]))
            copies[-1].start()
            down_ref[cols, :] = jnp.transpose(t_mm(dy_s[...], hidden_s[:, cols])).astype(bf16)
            copies.append(pltpu.make_async_copy(down_ref.at[at], down_out.at[at], down_sem.at[c]))
            copies[-1].start()
        for copy in copies:
            copy.wait()


def ffn(seq, patches, x_text, attended, patch_cotangent, text_cotangent, weights, w_down, vecs, devices):
    items, patch, model = patches.shape
    units, rows, text, slots = w_down.shape[0], attended.shape[1], x_text.shape[1], text_cotangent.shape[1]

    def item(count):
        return pl.BlockSpec((1, count, model), lambda i: (i, 0, 0))

    def shape(count):
        return jax.ShapeDtypeStruct((items, count, model), bf16)

    return pl.pallas_call(
        functools.partial(ffn_kernel, items, 1024, 256, devices),
        grid=(items,),
        in_specs=[pl.BlockSpec(memory_space=pltpu.SMEM)]
        + [item(patch), item(text), item(rows), item(patch), item(slots)]
        + [ANY, ANY, WHOLE],
        out_specs=[item(patch), item(text), item(rows), item(rows), ANY, ANY],
        out_shape=[shape(patch), shape(text), shape(rows), shape(rows)]
        + [
            jax.ShapeDtypeStruct((model, units + model + LANES), bf16),
            jax.ShapeDtypeStruct((units, model), bf16),
        ],
        scratch_shapes=[
            pltpu.VMEM(weights.shape, bf16),
            pltpu.VMEM(w_down.shape, bf16),
            pltpu.VMEM((model, units + model + LANES), bf16),
            pltpu.VMEM((units, model), bf16),
            pltpu.VMEM((items * rows, model), bf16),
            pltpu.VMEM((items * rows, units), bf16),
            pltpu.VMEM((items * rows, units), bf16),
            pltpu.VMEM((items * rows, model), bf16),
            pltpu.VMEM((8, model), f32),
            pltpu.VMEM((8, units), f32),
            pltpu.VMEM((items * rows, model), bf16),
            pltpu.VMEM((items * rows, model), bf16),
        ]
        + [pltpu.SemaphoreType.DMA((units // 1024 + 1,))] * 2
        + [pltpu.SemaphoreType.DMA((units // model + 1,))] * 2,
        compiler_params=compiler_params(),
        name="ffn",
    )(seq, patches, x_text, attended, patch_cotangent, text_cotangent, weights, w_down, vecs)


def back_kernel(count, patch, head, seq_size, pairs, items, *refs):
    refs = list(refs)

    def take(number):
        taken = refs[:number]
        del refs[:number]
        return taken

    (q_ref,), k_refs, v_refs = take(1), take(count), take(count)
    bias_ref, log_ref, at_ref, rest_ref, grad_ref = take(5)
    part_a, part_b, w_any, w2_any, vec_ref, first_any, x_any, xtext_any, gb_any, restext_any = take(10)
    grad_out, text_grad_out, text_out, total_a, total_b, total_in, vec_out, vec2_out = take(8)
    keys, values, text_keys, text_values, probs_s, scores_s = take(6)
    mixed_s, own_s, dkv_out, dkv_in, sums_s = take(5)
    w_s, w2_s, first_s, x_s, xtext_s, gb_s, text_s, patch_s = take(8)
    first_grad_s, scaled_s, inverse_s = take(3)
    fetch_sem, dkv_sem, dkv_in_sem, text_sem, text_in_sem, patch_sem = take(6)
    scratch_a, scratch_b = take(10), take(10)
    scratch_in, scratch_last, scratch_vec = take(11), [take(6), take(6)], take(6)

    width, rows = q_ref.shape[2], q_ref.shape[1]
    text, model = rows - patch, pairs * width
    place = Place(part_a.shape[0], seq_size)
    seq = lax.axis_index("seq")
    p, i = pl.program_id(0), pl.program_id(1)
    turn, last = p * items + i, pairs * items - 1
    sums_a, sums_b = Reduce(place, part_a, *scratch_a), Reduce(place, part_b, *scratch_b)
    chunks = ((0, pairs - 2), (pairs - 2, pairs - 1), (pairs - 1, pairs))
    sums_in = [Reduce(place, *scratch_in)]
    sums_in += [ShortReduce(place, *each) for each in scratch_last]
    sums_vec = ShortReduce(place, *scratch_vec)
    fetches = [
        pltpu.make_async_copy(src, dst, fetch_sem.at[n])
        for n, (src, dst) in enumerate(
            ((first_any, first_s), (w_any, w_s), (w2_any, w2_s), (x_any, x_s), (xtext_any, xtext_s), (gb_any, gb_s))
        )
    ]

    def text_copies(src, dst, row):
        to = dst.at[:, pl.ds(pl.multiple_of(seq * text, ROW_TILE), text)]
        own = pltpu.make_async_copy(src, to, text_sem.at[row, 0])
        away = [
            remote(src, to, text_sem.at[row, r], text_in_sem.at[row, r], place.mate(r)) for r in range(1, seq_size)
        ]
        return [own] + away

    def begin():
        place.meet(corners=True)
        sums_a.to_core()
        sums_b.to_core()
        for copy in text_copies(restext_any, text_out, 0):
            copy.start()

    def dkv_copy(slot, r):
        return remote(
            dkv_out.at[slot, r - 1], dkv_in.at[slot, r - 1], dkv_sem.at[slot, r - 1], dkv_in_sem.at[slot, r - 1],
            place.mate(-r)
        )

    def settle(of):
        slot, pair, item = lax.rem(of, 2), of // items, lax.rem(of, items)
        total = own_s[slot].astype(f32)
        for r in range(1, seq_size):
            dkv_copy(slot, r).wait_recv()
            total = total + dkv_in[slot, r - 1].astype(f32)
        at = pl.ds(pl.multiple_of(item * rows, ROW_TILE), rows)
        mixed_s[pair, at, width:] = total.astype(bf16)

    def pair_done(pair):
        mixed = mixed_s[pair]
        if pair == 0:
            fetches[0].wait()
        grad = t_mm(first_s[...].reshape(items * rows, model), mixed).astype(bf16)
        chunk = sum(pair >= first for first, _ in chunks) - 1
        first, end = chunks[chunk]
        part = sums_in[chunk].part
        part[..., 3 * (pair - first) * width : 3 * (pair - first + 1) * width] = grad.reshape(
            part.shape[:-1] + (3 * width,)
        )
        if pair == end - 1:
            (sums_in[chunk].start if chunk else sums_in[chunk].to_core)()
        cols = slice(pair * width, (pair + 1) * width)
        sums_s[QBIAS : QBIAS + 1, cols] = column_sum(mixed[:, :width])
        sums_s[VBIAS : VBIAS + 1, cols] = column_sum(mixed[:, 2 * width :])

    def finish_in(chunk):
        total = sums_in[chunk].last()
        first, end = chunks[chunk]
        for m in range(end - first):
            for n in range(3):
                at, of = n * model + (first + m) * width, (3 * m + n) * width
                total_in[:, at : at + width] = total[:, of : of + width]

    def finish_a():
        total = sums_a.last()
        total_a[...] = total[:, : total_a.shape[1]]
        vec2_out[...] = total[:, total_a.shape[1] :]

    def finish_b():
        total_b[...] = sums_b.last()

    tail_at = last + 1
    agenda = [(2, sums_a.to_second), (3, sums_b.to_second), (6, sums_a.to_first), (7, sums_b.to_first),
              (9, sums_a.to_line), (10, sums_b.to_line), (tail_at, finish_a), (tail_at + 2, finish_b)]
    steps = (sums_in[0].to_second, sums_in[0].to_first, sums_in[0].to_line, functools.partial(finish_in, 0))
    agenda += [(max(at, items * chunks[0][1] + 2), step) for at, step in zip((9, 11, tail_at, tail_at + 1), steps)]
    agenda += [(tail_at, sums_in[1].to_line), (tail_at + 2, functools.partial(finish_in, 1))]
    agenda += [(tail_at + 1, sums_in[2].to_line), (tail_at + 3, functools.partial(finish_in, 2))]
    agenda.sort(key=lambda entry: entry[0])

    @pl.when(turn == 0)
    def _():
        place.greet(corners=True)
        for copy in fetches:
            copy.start()
        sums_s[...] = jnp.zeros_like(sums_s)

    collect(keys, [ref[0] for ref in k_refs], patch, text)
    collect(values, [ref[0] for ref in v_refs], patch, text)
    q, grad = q_ref[0], grad_ref[0]
    edge, heads, span = count * patch, width // head, keys.shape[0] - count * patch
    lane = lax.broadcasted_iota(jnp.int32, (1, width), 1) // head
    row = lax.broadcasted_iota(jnp.int32, (width, 1), 0) // head
    by_head(text_keys, keys[edge:], lane, heads, False)
    by_head(text_values, values[edge:], lane, heads, False)
    text_bias = jnp.concatenate([bias_ref[0]] * heads, axis=1)
    inner = grad.astype(f32) * (at_ref[0].astype(f32) + rest_ref[0].astype(f32))
    q_heads = [jnp.where(lane == h, q, jnp.zeros_like(q)) for h in range(heads)]
    grad_heads = [jnp.where(lane == h, grad, jnp.zeros_like(grad)) for h in range(heads)]
    deltas = [jnp.sum(jnp.where(lane == h, inner, 0.0), axis=1, keepdims=True) for h in range(heads)]
    logs = [log_ref[0, :, h * head : h * head + 1] for h in range(heads)]

    def first_dots(h):
        return mm_t(q_heads[h], keys[:edge]), mm_t(grad_heads[h], values[:edge])

    scores, grad_probs = first_dots(0)
    text_scores = mm_t(q, text_keys[...]) + text_bias
    text_grad_probs = mm_t(grad, text_values[...])
    dq, text_probs, text_grads = None, [], []
    for h in range(heads):
        following = first_dots(h + 1) if h + 1 < heads else (None, None)
        cols = slice(h * span, (h + 1) * span)
        text_head = jnp.exp2(text_scores[:, cols] - logs[h])
        text_probs.append(text_head.astype(bf16))
        text_grads.append((text_head * (text_grad_probs[:, cols] - deltas[h])).astype(bf16))
        probs = jnp.exp2(scores - logs[h])
        grad_scores = (probs * (grad_probs - deltas[h])).astype(bf16)
        probs_s[h * rows : (h + 1) * rows, :] = probs.astype(bf16)
        scores_s[h * rows : (h + 1) * rows, :] = grad_scores
        dq_head = mm(grad_scores, keys[:edge])
        dq = dq_head if dq is None else jnp.where(lane == h, dq_head, dq)
        scores, grad_probs = following
    text_probs, text_grads = jnp.concatenate(text_probs, axis=1), jnp.concatenate(text_grads, axis=1)
    dq = dq + mm(text_grads, text_keys[...])
    dv = jnp.transpose(t_mm(jnp.concatenate(grad_heads, axis=0), probs_s[...]).astype(bf16))
    dk = jnp.transpose((t_mm(jnp.concatenate(q_heads, axis=0), scores_s[...]) * LN2).astype(bf16))

    def of_heads(wide):
        own = wide[:, :span]
        for h in range(1, heads):
            own = jnp.where(row == h, wide[:, h * span : (h + 1) * span], own)
        return jnp.transpose(own.astype(bf16))

    text_dv, text_dk = of_heads(t_mm(grad, text_probs)), of_heads(t_mm(q, text_grads) * LN2)
    slot = lax.rem(turn, 2)

    @pl.when(turn == 0)
    def _():
        begin()

    for at in sorted({at for at, _ in agenda if at <= last}):

        @pl.when(turn == at - 1)
        def _(at=at):
            for when, step in agenda:
                if when == at:
                    step()

    at = pl.ds(pl.multiple_of(i * rows, ROW_TILE), rows)
    mixed_s[p, at, :width] = (dq * (1.0 / math.sqrt(head))).astype(bf16)
    own_s[slot, :patch, :width] = dk[:patch]
    own_s[slot, :patch, width:] = dv[:patch]
    own_s[slot, patch:, :width] = text_dk[:text]
    own_s[slot, patch:, width:] = text_dv[:text]

    @pl.when(turn > 0)
    def _():
        settle(turn - 1)

    @pl.when(turn > 1)
    def _():
        for r in range(1, seq_size):
            dkv_copy(slot, r).wait_send()

    for r in range(1, seq_size):
        for n, (part, text_part) in enumerate(((dk, text_dk), (dv, text_dv))):
            cols = slice(n * width, (n + 1) * width)
            dkv_out[slot, r - 1, :patch, cols] = part[r * patch : (r + 1) * patch]
            dkv_out[slot, r - 1, patch:, cols] = text_part[r * text : (r + 1) * text]
        dkv_copy(slot, r).start()

    for pair in range(pairs - 1):

        @pl.when(turn == items * (pair + 1))
        def _(pair=pair):
            pair_done(pair)

    @pl.when(turn == last)
    def _():
        left = [[step for when, step in agenda if when == at] for at in sorted({at for at, _ in agenda if at > last})]

        def more():
            if left:
                for step in left.pop(0):
                    step()

        half = pairs // 2
        sides = (w_s.at[:, : 3 * half * width], w2_s)

        def grad_first(item, side):
            at = slice(item * rows, (item + 1) * rows)
            mixed = [
                mixed_s[side * half + m, at, n * width : (n + 1) * width] for n in (1, 2, 0) for m in range(half)
            ]
            return mm_t(jnp.concatenate(mixed, axis=1), sides[side][...])

        for copy in fetches[1:]:
            copy.wait()
        for item in range(items):
            first_grad_s[item] = grad_first(item, 0)
        settle(last)
        pair_done(pairs - 1)
        for item in range(items):
            grad = first_grad_s[item] + grad_first(item, 1)
            first_grad_s[item] = grad
            scaled, inverse = norm_rows(jnp.concatenate([x_s[item], xtext_s[item]], axis=0).astype(f32))
            scaled_s[item] = scaled
            inverse_s[item] = jnp.broadcast_to(inverse, (rows, LANES))
            sums_s[GAIN1 : GAIN1 + 1, :] += column_sum(grad * scaled)
            sums_s[SHIFT1 : SHIFT1 + 1, :] += column_sum(grad)
        sums_vec.part[...] = to_columns(sums_s[...]).reshape(sums_vec.part.shape)
        sums_vec.start()
        more()
        gain = vec_ref[GAIN1 : GAIN1 + 1]
        patch_copies = [
            pltpu.make_async_copy(patch_s.at[item], grad_out.at[item], patch_sem.at[item]) for item in range(items)
        ]
        for item in range(items):
            grad_rows = norm_back(first_grad_s[item], scaled_s[item], inverse_s[item][:, :1], gain)
            grad_rows = (gb_s[item].astype(f32) + grad_rows).astype(bf16)
            patch_s[item] = grad_rows[:patch]
            patch_copies[item].start()
            text_s[item] = grad_rows[patch:]
            if item == 0:
                sums_vec.to_line()
            more()
        for copy in text_copies(text_s, text_grad_out, 1):
            copy.start()
        while left:
            more()
        vec_out[...] = sums_vec.last()
        for copies in (text_copies(restext_any, text_out, 0), text_copies(text_s, text_grad_out, 1)):
            for copy in copies:
                copy.wait()
        for slot in range(2):
            for r in range(1, seq_size):
                dkv_copy(slot, r).wait_send()
        for copy in patch_copies:
            copy.wait()


def back(q, keys, values, bias, logs, attended, rest, grad_att, part_a, part_b, w_in, vecs, first_in, patches, x_text,
         grad_branch, res_text, head, width, devices, seq_size):
    items, patch, model = patches.shape
    rows, text = q.shape[1], x_text.shape[1]
    count, tail, pairs, depth = len(keys), bias.shape[-1], model // width, devices // 8
    span = count * patch + tail
    block = pl.BlockSpec((1, rows, width), lambda p, i: (i, 0, p))
    parts = [part.reshape((depth, 2, 2, 2, part.shape[0] // devices, part.shape[1])) for part in (part_a, part_b)]
    (rows_a, cols_a), (rows_b, cols_b) = parts[0].shape[4:], parts[1].shape[4:]
    sems = pltpu.SemaphoreType.DMA
    others = seq_size - 1
    slots = jax.ShapeDtypeStruct((items, seq_size * text, model), bf16)
    cols = 3 * (pairs - 2) * width
    scratch_in = [pltpu.VMEM((depth, 2, 2, 2, rows_a, cols), bf16)] + reduce_scratch(depth, rows_a, cols)
    scratch_in += short_reduce_scratch(depth, rows_a, 3 * width) * 2
    return pl.pallas_call(
        functools.partial(back_kernel, count, patch, head, seq_size, pairs, items),
        grid=(pairs, items),
        in_specs=[block] * (1 + 2 * count)
        + [pl.BlockSpec((1, 1, tail), lambda p, i: (i, 0, 0))]
        + [block] * 4
        + [ANY] * 4
        + [WHOLE]
        + [ANY] * 5,
        out_specs=[ANY] * 3 + [WHOLE] * 5,
        out_shape=[
            jax.ShapeDtypeStruct(patches.shape, bf16),
            slots,
            slots,
            jax.ShapeDtypeStruct((rows_a, cols_a - LANES), f32),
            jax.ShapeDtypeStruct((rows_b, cols_b), f32),
            jax.ShapeDtypeStruct((rows_a, 3 * model), f32),
            jax.ShapeDtypeStruct((rows_a, LANES), f32),
            jax.ShapeDtypeStruct((rows_a, LANES), f32),
        ],
        scratch_shapes=[
            pltpu.VMEM((span, width), bf16),
            pltpu.VMEM((span, width), bf16),
            pltpu.VMEM((width // head * tail, width), bf16),
            pltpu.VMEM((width // head * tail, width), bf16),
            pltpu.VMEM((width // head * rows, count * patch), bf16),
            pltpu.VMEM((width // head * rows, count * patch), bf16),
            pltpu.VMEM((pairs, items * rows, 3 * width), bf16),
            pltpu.VMEM((2, rows, 2 * width), bf16),
            pltpu.VMEM((2, others, rows, 2 * width), bf16),
            pltpu.VMEM((2, others, rows, 2 * width), bf16),
            pltpu.VMEM((8, model), f32),
            pltpu.VMEM(w_in[0].shape, bf16),
            pltpu.VMEM(w_in[1].shape, bf16),
            pltpu.VMEM(first_in.shape, bf16),
            pltpu.VMEM(patches.shape, bf16),
            pltpu.VMEM(x_text.shape, bf16),
            pltpu.VMEM(grad_branch.shape, bf16),
            pltpu.VMEM(x_text.shape, bf16),
            pltpu.VMEM(patches.shape, bf16),
            pltpu.VMEM(q.shape, f32),
            pltpu.VMEM(q.shape, f32),
            pltpu.VMEM((items, rows, LANES), f32),
            sems((6,)),
            sems((2, others)),
            sems((2, others)),
            sems((2, seq_size)),
            sems((2, seq_size)),
            sems((items,)),
        ]
        + reduce_scratch(depth, rows_a, cols_a)
        + reduce_scratch(depth, rows_b, cols_b)
        + scratch_in
        + short_reduce_scratch(depth, rows_a, LANES),
        compiler_params=compiler_params(collective_id=2, has_side_effects=True),
        name="back",
    )(q, *keys, *values, bias, logs, attended, rest, grad_att, *parts, *w_in, vecs, first_in, patches, x_text,
      grad_branch, res_text)


def outputs_kernel(*refs):
    text_any, patch_any, text_grad_any, total_a, total_b, total_in, vec1, vec2 = refs[:8]
    outs = list(refs[8:24])
    out_text, patch_out, grad_text = outs[:3]
    first_gain, first_shift, in_weight, query_bias, value_bias, out_weight, branch_bias = outs[3:10]
    second_gain, second_shift, up_weight, up_bias, down_weight, down_bias = outs[10:]
    patch_s, text_s, text_grad_s, sem = refs[24:]
    items, slots, units = patch_s.shape[0], out_text.shape[1], up_weight.shape[1]
    fetches = [pltpu.make_async_copy(patch_any.at[i], patch_s.at[i], sem.at[0, i]) for i in range(items)]
    stores = [pltpu.make_async_copy(patch_s.at[i], patch_out.at[i], sem.at[1, i]) for i in range(items)]
    texts = [
        pltpu.make_async_copy(text_any, text_s, sem.at[2, 0]),
        pltpu.make_async_copy(text_grad_any, text_grad_s, sem.at[2, 1]),
    ]
    for copy in fetches + texts:
        copy.start()

    count = vec1.shape[0]
    empty = jnp.zeros((LANES - 2 * count, LANES), f32)
    table = jnp.transpose(jnp.concatenate([vec1[...], vec2[...], empty], axis=0))
    in_weight[...] = total_in[...]
    out_weight[...] = total_a[:, units:]
    up_weight[...] = total_a[:, :units]
    down_weight[...] = total_b[...]
    for ref, at in ((first_gain, GAIN1), (first_shift, SHIFT1), (query_bias, QBIAS), (value_bias, VBIAS)):
        ref[...] = table[at, :count]
    for ref, at in ((branch_bias, BRANCH), (second_gain, GAIN2), (second_shift, SHIFT2), (down_bias, DOWNB)):
        ref[...] = table[at, count : 2 * count]
    up_bias[...] = vec2[:1, SIDE : SIDE + up_bias.shape[0]].reshape(up_bias.shape)
    for fetch, store in zip(fetches, stores):
        fetch.wait()
        store.start()
    for copy in texts:
        copy.wait()
    out_text[...] = text_s[:, :slots]
    grad_text[...] = text_grad_s[:, :slots]
    for copy in stores:
        copy.wait()


def outputs(text, patch_grad, text_grad, total_a, total_b, total_in, vec1, vec2, slots, units, hidden):
    items, patch, model = patch_grad.shape

    def shape(*dims):
        return jax.ShapeDtypeStruct(dims, f32)

    count = total_in.shape[0]
    vector, texts = shape(count), jax.ShapeDtypeStruct((items, slots, model), bf16)
    return pl.pallas_call(
        outputs_kernel,
        in_specs=[ANY] * 3 + [WHOLE] * 5,
        out_specs=[WHOLE, ANY, WHOLE] + [WHOLE] * 13,
        out_shape=[texts, jax.ShapeDtypeStruct(patch_grad.shape, bf16), texts]
        + [vector, vector, shape(count, 3 * model), vector, vector, shape(count, model), vector, vector, vector]
        + [shape(count, units), shape(hidden), shape(*total_b.shape), vector],
        scratch_shapes=[
            pltpu.VMEM(patch_grad.shape, bf16),
            pltpu.VMEM(text.shape, bf16),
            pltpu.VMEM(text.shape, bf16),
            pltpu.SemaphoreType.DMA((3, max(items, 2))),
        ],
        compiler_params=compiler_params(),
        name="outputs",
    )(text, patch_grad, text_grad, total_a, total_b, total_in, vec1, vec2)


def per_device(
    seq_size,
    devices,
    patches,
    text_rows,
    lengths,
    first_gain,
    first_shift,
    in_weight,
    query_bias,
    value_bias,
    out_weight,
    branch_bias,
    second_gain,
    second_shift,
    up_weight,
    up_bias,
    down_weight,
    down_bias,
    patch_cotangent,
    text_cotangent,
):
    items, patch, model = patches.shape
    slots = text_rows.shape[1]
    units = up_weight.shape[1]
    head = model // HEADS
    width = min(LANES, model)
    text = round_up(-(-slots // seq_size), ROW_TILE)
    seq = lax.axis_index("seq")
    vectors = [first_gain, first_shift, query_bias, value_bias, branch_bias, second_gain, second_shift, down_bias]
    w_in, vecs, bias, (weights, w_down), x_text, first_in, q, attended, rest, logs, keys, values = forward(
        in_weight, vectors, up_weight, up_bias, out_weight, down_weight, patches, text_rows, lengths, text, width, head,
        devices, seq_size
    )
    out_patches, res_text, grad_branch, grad_att, part_a, part_b = ffn(
        seq[None], patches, x_text, attended, patch_cotangent, text_cotangent, weights, w_down, vecs, devices
    )
    grad_patches, grad_text, out_text, sums, down_grad, in_grad, vec1, vec2 = back(
        q, keys, values, bias, logs, attended, rest, grad_att, part_a, part_b, w_in, vecs, first_in, patches, x_text,
        grad_branch, res_text, head, width, devices, seq_size
    )
    rest = outputs(
        out_text, grad_patches, grad_text, sums, down_grad, in_grad, vec1, vec2, slots, units, up_bias.shape[0]
    )
    return (out_patches, *rest)


def solution(mesh):
    both = ("dp", "seq")
    rows, slots, vector, matrix = P("dp", "seq", None), P("dp", None, None), P(both), P(both, None)
    weights = (vector, vector, matrix, vector, vector, matrix, vector, vector, vector, matrix, vector, matrix, vector)
    return jax.shard_map(
        functools.partial(per_device, mesh.shape["seq"], mesh.size),
        mesh=mesh,
        in_specs=(rows, slots, P("dp")) + weights + (rows, slots),
        out_specs=(rows, slots, rows, slots) + weights,
        check_vma=False,
    )
```
